32 devices in a mesh: dp: 8 (over z, x), group: 4 (over y, core).
Axes of the slice: x: 2, y: 2, z: 4, core: 2. Of those that a mesh axis runs over, the one named last changes fastest.
Arguments:
- token_ids: int32 [16384], P(('dp', 'group')), may hold values from 0 to 30527
- seq_lengths: int32 [32, 4], P(('dp', 'group')), may hold values from 1 to 320, 512 in all within a row
- valid_mask: int32 [16384], P(('dp', 'group')), may hold values 0 or 1
- deal_order: int32 [128], replicated, may hold values from 0 to 127, each once
- log_scale: float32 [1], replicated, may hold values from 2.5 to 3.5
- embed_master: float32 [30528, 512], P('dp'), may hold values from -6 to 6
- attn_in: float32 [2, 512, 1536], P(None, 'dp'), may hold values from -0.25 to 0.25
- attn_out: float32 [2, 512, 512], P(None, 'dp'), may hold values from -0.75 to 0.75
- ffn_in: float32 [2, 512, 4096], P(None, 'dp'), may hold values from -0.25 to 0.25
- ffn_out: float32 [2, 2048, 512], P(None, 'dp'), may hold values from -0.125 to 0.125
- head_master: float32 [512, 512], P('dp'), may hold values from -0.25 to 0.25
- norm_master: float32 [5, 2, 512], P(None, None, 'dp'), may hold values from -1.2 to 1.4, as said below
- embed_rows: float32 [30528], P('dp'), as said below
- head_rows: float32 [512], P('dp'), as said below
- layer_rows: float32 [2, 3, 512], P(None, None, 'dp'), as said below
- ffn_out_rows: float32 [2, 2048], P(None, 'dp'), as said below
- layer_cols: float32 [2, 6656], replicated, as said below
- embed_head_cols: float32 [2, 512], replicated, as said below
- norm_state: float32 [5, 2, 512], P(None, None, 'dp'), as said below
- scale_state: float32 [1], replicated, as said below
Outputs:
- pair_loss: float32 [], replicated
- new_embed: float32 [30528, 512], P('dp')
- new_attn_in: float32 [2, 512, 1536], P(None, 'dp')
- new_attn_out: float32 [2, 512, 512], P(None, 'dp')
- new_ffn_in: float32 [2, 512, 4096], P(None, 'dp')
- new_ffn_out: float32 [2, 2048, 512], P(None, 'dp')
- new_head: float32 [512, 512], P('dp')
- new_norm: float32 [5, 2, 512], P(None, None, 'dp')
- new_log_scale: float32 [1], replicated
- new_embed_rows: float32 [30528], P('dp')
- new_head_rows: float32 [512], P('dp')
- new_layer_rows: float32 [2, 3, 512], P(None, None, 'dp')
- new_ffn_out_rows: float32 [2, 2048], P(None, 'dp')
- new_layer_cols: float32 [2, 6656], replicated
- new_embed_cols: float32 [512], replicated
- new_head_cols: float32 [512], replicated
- new_norm_state: float32 [5, 2, 512], P(None, None, 'dp')
- new_scale_state: float32 [1], replicated
- update_rms: float32 [10], replicated
The draws below stay inside these ranges and needn't reach their ends.
Inputs may be any that keep to these rules, and one draw needn't show every extreme that they name: `seq_lengths`: each row holds 4 lengths that sum to 512. `deal_order`: a permutation; sequence j < 64 is a query whose document is sequence 64 + j. `norm_master`: gains near one, biases near zero. `embed_rows`: positive. `head_rows`: positive. `layer_rows`: positive. `ffn_out_rows`: positive. `layer_cols`: positive. `embed_head_cols`: positive. `norm_state`: positive. `scale_state`: positive.
All inputs are finite; a program needn't handle non-finite values. No bound on the sum of `valid_mask` on one device may be relied on, other than what follows from the above.
Results may differ from the reference program's by a relative error of at most 0.0085.
The reference program's roundings to bfloat16 on the way count: a program that leaves them out, or rounds other values in their place, can miss the bound.
Values may be sent and summed in bfloat16 or wider, within the bound.
A program may use at most 256 MiB of HBM per device.

```python
import math
import jax
import jax.numpy as jnp
import numpy as np
from jax import lax

D = 512
HEADS = 8
HEAD_DIM = 64
FF = 2048
VOCAB = 30528
LAYERS = 2
SEQ_DEV = 4
TOK_DEV = 512
LONGEST = 320
NSEQ = 128
PAIRS = 64
TOKENS = 16384
N_DP = 8
N_GROUP = 4


def draw_norm_master(key, part):
    noise = jax.random.truncated_normal(key, -4.0, 4.0, (2 * LAYERS + 1, 2, D), jnp.float32)
    center = jnp.array([1.0, 0.0], jnp.float32)[None, :, None]
    spread = jnp.array([0.1, 0.3], jnp.float32)[None, :, None]
    return center + spread * noise


def layer_level():
    return 12.0 / D


def head_level():
    return 4.0 * NSEQ ** 0.5 / D


def state_like(key, shape, level):
    count = shape[-1]
    index = jnp.arange(count, dtype=jnp.float32) / max(count - 1, 1)
    ramp = jnp.exp(jnp.log(0.7) + jnp.log(2.0) * index)
    factor = jnp.exp(jax.random.uniform(key, shape, jnp.float32, jnp.log(0.7), jnp.log(1.4)))
    return 2.0 * level * level * factor * ramp


def draw_embed_rows(key, part):
    return state_like(jax.random.fold_in(key, 11), (VOCAB,), 0.3 * layer_level())


def draw_head_rows(key, part):
    return state_like(jax.random.fold_in(key, 12), (D,), head_level())


def draw_layer_rows(key, part):
    return state_like(jax.random.fold_in(key, 13), (LAYERS, 3, D), layer_level())


def draw_ffn_out_rows(key, part):
    return state_like(jax.random.fold_in(key, 14), (LAYERS, FF), layer_level())


def draw_layer_cols(key, part):
    return state_like(jax.random.fold_in(key, 15), (LAYERS, 5 * D + 2 * FF), layer_level())


def draw_embed_head_cols(key, part):
    table_part = state_like(jax.random.fold_in(key, 16), (1, D), 0.1 * layer_level())
    head_part = state_like(jax.random.fold_in(key, 17), (1, D), head_level())
    return jnp.concatenate([table_part, head_part], axis=0)


def draw_norm_state(key, part):
    key = jax.random.fold_in(key, 18)
    shape = (2 * LAYERS + 1, 2, D)
    level = layer_level()
    factor = jnp.exp(jax.random.uniform(key, shape, jnp.float32, jnp.log(0.1), jnp.log(10.0)))
    return 37.0 * level * level * factor


def draw_scale_state(key, part):
    return state_like(jax.random.fold_in(key, 19), (1,), 2.0 * PAIRS ** 0.5)


def set_ends(values, key, least, high):
    index_at = [jax.random.randint(jax.random.fold_in(key, axis), (), 0, length) for axis, length in enumerate(values.shape)]
    main_axis = values.shape.index(max(values.shape))
    next_to = index_at[:main_axis] + [(index_at[main_axis] + 1) % values.shape[main_axis]] + index_at[main_axis + 1:]
    return values.at[tuple(index_at)].set(least).at[tuple(next_to)].set(high)


def levels(own_key, extent, shards, smallest, high):
    def one(dim, blocks):
        draws = jax.random.uniform(jax.random.fold_in(jax.random.fold_in(own_key, 6), dim), (blocks,), jnp.float32, smallest / len(shards), high / len(shards))
        return jnp.repeat(jnp.exp(draws), extent[dim] // blocks).reshape((-1,) + (1,) * (len(extent) - dim - 1))

    level = one(*shards[0])
    for cut in shards[1:]:
        level = level * one(*cut)
    return level


def cumulative_ranks(count, skew):
    weights = [(1 << 20) // math.isqrt(standing ** skew) + 1 for standing in range(1, count + 1)]
    deviation = 1 + sum(weights) // (1 << 30)
    return np.cumsum(np.array([max(1, weight // deviation) for weight in weights]))


def ranked_ids(own_key, extent, count, slope):
    grid = cumulative_ranks(count, slope)
    pick = jax.random.randint(jax.random.fold_in(own_key, 1), extent, 0, int(grid[count - 1]))
    grade = jnp.searchsorted(jnp.asarray(grid, jnp.int32), pick, side="right")
    return jax.random.permutation(jax.random.fold_in(own_key, 2), count)[grade].astype(jnp.int32)


def split_up(amount, total, reach, skew):
    loads = [(1 << 20) // math.isqrt(rank ** skew) + 1 for rank in range(2, amount + 1)]
    surplus, given = total - reach - (amount - 1), [1] * (amount - 1)
    while surplus > 0:
        movable = [i for i in range(amount - 1) if given[i] < reach]
        pool, left = sum([loads[i] for i in movable]), surplus
        for i in movable:
            extra = min(reach - given[i], max(1, left * loads[i] // pool), surplus)
            given[i] = given[i] + extra
            surplus = surplus - extra
    return np.array([reach] + given)


def uneven_parts(key, amount, total, most, lean):
    if amount == 2:
        one = jax.random.randint(key, (), max(1, total - most), min(most, total - 1) + 1)
        return jnp.stack([one, total - one])
    sizes = jnp.asarray(split_up(amount, total, most, lean), jnp.int32)
    pairs = (amount - 1) // 2
    giver, taker = sizes[1:1 + 2 * pairs:2], sizes[2:2 + 2 * pairs:2]
    margin = jnp.minimum(giver - 1, most - taker)
    shifted = jax.random.randint(jax.random.fold_in(key, 1), (pairs,), 0, 1 << 20) % (margin + 1)
    sizes = sizes.at[1:1 + 2 * pairs:2].set(giver - shifted).at[2:2 + 2 * pairs:2].set(taker + shifted)
    return sizes[jax.random.permutation(jax.random.fold_in(key, 2), amount)]


def centred(stream_key, extent, scale, bound, split=(), held_as=jnp.bfloat16):
    drawn = scale * jax.random.normal(stream_key, extent, jnp.float32)
    if split:
        drawn = drawn * levels(stream_key, extent, split, -0.22, 0.18)
    return jnp.clip(drawn, -bound, bound).astype(held_as)


def setup_inputs(seed: int = 0) -> dict:
    arg_keys = jax.random.split(jax.random.key(seed), 21)
    return {
        "token_ids": set_ends(ranked_ids(arg_keys[0], (TOKENS,), VOCAB, 2), jax.random.fold_in(arg_keys[0], 3), 0, VOCAB - 1).astype(jnp.int32),
        "seq_lengths": jax.vmap(lambda own: uneven_parts(own, SEQ_DEV, TOK_DEV, LONGEST, 2))(jax.random.split(arg_keys[1], (N_DP * N_GROUP))).reshape((N_DP * N_GROUP, SEQ_DEV)).astype(jnp.int32),
        "valid_mask": set_ends((jax.random.randint(arg_keys[2], (TOKENS,), 0, 8) < 7).astype(jnp.int32), jax.random.fold_in(arg_keys[2], 1), 0, 1),
        "deal_order": jax.random.permutation(arg_keys[3], NSEQ).astype(jnp.int32),
        "log_scale": jnp.clip(jax.random.uniform(arg_keys[4], (1,), jnp.float32, 2.5, 3.5), 2.5, 3.5),
        "embed_master": centred(arg_keys[5], (VOCAB, D), 1.0, 6.0, ((0, 8),), jnp.float32),
        "attn_in": centred(arg_keys[6], (LAYERS, D, 3 * D), D ** -0.5, 0.25, ((1, 8),), jnp.float32),
        "attn_out": centred(arg_keys[7], (LAYERS, D, D), (D // 8) ** -0.5, 0.75, ((1, 8),), jnp.float32),
        "ffn_in": centred(arg_keys[8], (LAYERS, D, 2 * FF), D ** -0.5, 0.25, ((1, 8),), jnp.float32),
        "ffn_out": centred(arg_keys[9], (LAYERS, FF, D), FF ** -0.5, 0.125, ((1, 8),), jnp.float32),
        "head_master": centred(arg_keys[10], (D, D), D ** -0.5, 0.25, ((0, 8),), jnp.float32),
        "norm_master": draw_norm_master(jax.random.fold_in(arg_keys[20], 71), 0),
        "embed_rows": draw_embed_rows(jax.random.fold_in(arg_keys[20], 71), 0),
        "head_rows": draw_head_rows(jax.random.fold_in(arg_keys[20], 71), 0),
        "layer_rows": draw_layer_rows(jax.random.fold_in(arg_keys[20], 71), 0),
        "ffn_out_rows": draw_ffn_out_rows(jax.random.fold_in(arg_keys[20], 71), 0),
        "layer_cols": draw_layer_cols(jax.random.fold_in(arg_keys[20], 71), 0),
        "embed_head_cols": draw_embed_head_cols(jax.random.fold_in(arg_keys[20], 71), 0),
        "norm_state": draw_norm_state(jax.random.fold_in(arg_keys[20], 71), 0),
        "scale_state": draw_scale_state(jax.random.fold_in(arg_keys[20], 71), 0),
    }


@jax.custom_vjp
def low(v):
    return lax.optimization_barrier(v.astype(jnp.bfloat16)).astype(jnp.float32)

@jax.custom_vjp
def low_back(v):
    return v

def low_keep(v):
    return (low(v), None)

def low_pass(kept, grad):
    return (grad,)

def back_keep(v):
    return (v, None)

def back_low(kept, grad):
    return (low(grad),)
low.defvjp(low_keep, low_pass)
low_back.defvjp(back_keep, back_low)
NORM_EPS = 1e-06
UNIT_EPS = 1e-06
STATE_EPS = 1e-30
DECAY_RATE = 0.5
CLIP_LEVEL = 0.05
RATE_SCALE = 10.0
NORM_RATE = 0.1

def matmul_high(left, right):
    return jnp.matmul(left, right, precision=lax.Precision.HIGHEST)

def layer_norm(values, gain_vec, shift_vec):
    center = values - lax.optimization_barrier(jnp.mean(values, axis=-1, keepdims=True))
    spread = lax.optimization_barrier(jnp.mean(center * center, axis=-1, keepdims=True))
    return center * lax.rsqrt(spread + NORM_EPS) * gain_vec + shift_vec

def geglu(joined):
    half_width = joined.shape[-1] // 2
    return jax.nn.gelu(joined[:, :half_width]) * joined[:, half_width:]

def alibi_slopes(head_count):
    return 2.0 ** (-8.0 * (jnp.arange(head_count).astype(jnp.float32) + 1.0) / head_count)

def normalize(vectors):
    return vectors * lax.rsqrt(lax.optimization_barrier(jnp.sum(vectors * vectors, axis=-1, keepdims=True)) + UNIT_EPS)

def contrast(unit_all, scale_arg, deal_order):
    pair_count = deal_order.shape[0] // 2
    queries = jnp.take(unit_all, deal_order[:pair_count], axis=0)
    documents = jnp.take(unit_all, deal_order[pair_count:], axis=0)
    logits = jnp.exp(scale_arg[0]) * jnp.matmul(queries, documents.T, precision=lax.Precision.HIGHEST)
    by_row = jax.nn.logsumexp(logits, axis=1)
    by_column = jax.nn.logsumexp(logits, axis=0)
    return jnp.sum(0.5 * (by_row + by_column) - jnp.diagonal(logits))

def pack_units(weights, stream, pack_lengths, pack_valid):
    qkv_weight = weights[1]
    out_weight = weights[2]
    up_weight = weights[3]
    down_weight = weights[4]
    head_weight = weights[5]
    norm_low = weights[6]
    tokens = stream.shape[0]
    position = jnp.arange(tokens, dtype=jnp.int32)
    bounds = jnp.cumsum(pack_lengths).astype(jnp.int32)
    segment = lax.optimization_barrier(jnp.sum((position[:, None] >= bounds[None, :]).astype(jnp.int32), axis=1))
    same_seq = segment[:, None] == segment[None, :]
    distance = jnp.abs(position[:, None] - position[None, :]).astype(jnp.float32)
    alibi_bias = -alibi_slopes(HEADS)[:, None, None] * distance[None]
    for layer_idx in range(LAYERS):
        qkv_low = low(low_back(matmul_high(low(stream), qkv_weight[layer_idx])))
        split_heads = qkv_low.reshape(tokens, 3, HEADS, HEAD_DIM)
        raw_scores = low_back(jnp.einsum('thc,shc->hts', split_heads[:, 0], split_heads[:, 1], precision=lax.Precision.HIGHEST))
        scores = jnp.where(same_seq[None], raw_scores * HEAD_DIM ** (-0.5) + alibi_bias, -jnp.inf)
        prob_low = low(jax.nn.softmax(scores, axis=-1))
        mixed_heads = jnp.einsum('hts,shc->thc', prob_low, split_heads[:, 2], precision=lax.Precision.HIGHEST).reshape(tokens, D)
        attended = low_back(matmul_high(low(low_back(mixed_heads)), out_weight[layer_idx]))
        normed = layer_norm(stream + attended, norm_low[2 * layer_idx, 0], norm_low[2 * layer_idx, 1])
        joined = low_back(matmul_high(low(normed), up_weight[layer_idx]))
        branch = low_back(matmul_high(low(geglu(joined)), down_weight[layer_idx]))
        stream = layer_norm(normed + branch, norm_low[2 * layer_idx + 1, 0], norm_low[2 * layer_idx + 1, 1])
    final = layer_norm(stream, norm_low[2 * LAYERS, 0], norm_low[2 * LAYERS, 1])
    member = ((segment[None, :] == jnp.arange(SEQ_DEV, dtype=jnp.int32)[:, None]) & (pack_valid[None, :] > 0)).astype(jnp.float32)
    counts = jnp.maximum(lax.optimization_barrier(jnp.sum(member, axis=1)), 1.0)
    pooled = matmul_high(member, final) / counts[:, None]
    return normalize(low_back(matmul_high(low(pooled), head_weight)))

def total_loss(masters, scale_arg, token_ids, seq_lengths, valid_mask, deal_order):
    weights = tuple((low(master) for master in masters))
    devices = N_DP * N_GROUP
    batch_packs = 8
    batches = devices // batch_packs
    stream_all = jnp.take(weights[0], token_ids, axis=0)

    def one_pack(stream, pack_lengths, pack_valid):
        return pack_units(weights, stream, pack_lengths, pack_valid)
    many_packs = jax.checkpoint(jax.vmap(one_pack))

    def one_batch(batch_args):
        return many_packs(batch_args[0], batch_args[1], batch_args[2])
    unit_all = lax.map(one_batch, (stream_all.reshape(batches, batch_packs, TOK_DEV, D), seq_lengths.reshape(batches, batch_packs, SEQ_DEV), valid_mask.reshape(batches, batch_packs, TOK_DEV)))
    return contrast(unit_all.reshape(devices * SEQ_DEV, D), scale_arg, deal_order)

def factored(grad_full, row_state, col_state, rate):
    squares = grad_full * grad_full
    row_new = DECAY_RATE * row_state + (1.0 - DECAY_RATE) * (lax.optimization_barrier(jnp.mean(squares, axis=-1)) + STATE_EPS)
    col_new = DECAY_RATE * col_state + (1.0 - DECAY_RATE) * (lax.optimization_barrier(jnp.mean(squares, axis=-2)) + STATE_EPS)
    row_mean = lax.optimization_barrier(jnp.mean(row_new, axis=-1))
    step_dir = grad_full * lax.rsqrt(row_new[:, :, None] * col_new[:, None, :] / row_mean[:, None, None])
    step_rms = jnp.sqrt(lax.optimization_barrier(jnp.mean(step_dir * step_dir, axis=(1, 2))))
    delta = -rate * step_dir / jnp.maximum(1.0, step_rms / CLIP_LEVEL)[:, None, None]
    return (delta, row_new, col_new, step_rms)

def unfactored(grad_full, state):
    state_new = DECAY_RATE * state + (1.0 - DECAY_RATE) * (grad_full * grad_full + STATE_EPS)
    return (-NORM_RATE * grad_full * lax.rsqrt(state_new), state_new)

def reference(token_ids, seq_lengths, valid_mask, deal_order, log_scale, embed_master, attn_in, attn_out, ffn_in, ffn_out, head_master, norm_master, embed_rows, head_rows, layer_rows, ffn_out_rows, layer_cols, embed_head_cols, norm_state, scale_state):
    masters = (embed_master, attn_in, attn_out, ffn_in, ffn_out, head_master, norm_master)

    def loss_of(weight_set, scale_arg):
        return total_loss(weight_set, scale_arg, token_ids, seq_lengths, valid_mask, deal_order)
    loss_value, pull_back = jax.vjp(loss_of, masters, log_scale)
    grad_set, grad_scale = pull_back(jnp.ones_like(loss_value))
    grad_embed, grad_qkv, grad_attn, grad_gate_up, grad_down, grad_head, grad_norm = grad_set
    wide_rate = RATE_SCALE / D ** 0.5
    embed_step, embed_row_new, embed_col_new, embed_rms = factored(grad_embed[None], embed_rows[None], embed_head_cols[0:1], RATE_SCALE)
    head_step, head_row_new, head_col_new, head_rms = factored(grad_head[None], head_rows[None], embed_head_cols[1:2], wide_rate)
    qkv_step, qkv_row_new, qkv_col_new, qkv_rms = factored(grad_qkv, layer_rows[:, 0], layer_cols[:, :3 * D], wide_rate)
    attn_step, attn_row_new, attn_col_new, attn_rms = factored(grad_attn, layer_rows[:, 1], layer_cols[:, 3 * D:4 * D], RATE_SCALE / (D // 8) ** 0.5)
    gate_step, gate_row_new, gate_col_new, gate_rms = factored(grad_gate_up, layer_rows[:, 2], layer_cols[:, 4 * D:4 * D + 2 * FF], wide_rate)
    down_step, down_row_new, down_col_new, down_rms = factored(grad_down, ffn_out_rows, layer_cols[:, 4 * D + 2 * FF:], RATE_SCALE / FF ** 0.5)
    norm_step, norm_state_new = unfactored(grad_norm, norm_state)
    scale_step, scale_state_new = unfactored(grad_scale, scale_state)
    rms_all = jnp.concatenate([embed_rms, head_rms, qkv_rms, attn_rms, gate_rms, down_rms])
    return (loss_value, embed_master + embed_step[0], attn_in + qkv_step, attn_out + attn_step, ffn_in + gate_step, ffn_out + down_step, head_master + head_step[0], norm_master + norm_step, log_scale + scale_step, embed_row_new[0], head_row_new[0], jnp.stack([qkv_row_new, attn_row_new, gate_row_new], axis=1), down_row_new, jnp.concatenate([qkv_col_new, attn_col_new, gate_col_new, down_col_new], axis=1), embed_col_new[0], head_col_new[0], norm_state_new, scale_state_new, rms_all)
```

```python
import functools

import jax
import jax.numpy as jnp
from jax import lax
from jax.experimental import pallas as pl
from jax.experimental.pallas import tpu as pltpu
from jax.sharding import PartitionSpec as P

D = 512
HEADS = 8
HEAD_DIM = 64
FF = 2048
VOCAB = 30528
LAYERS = 2


NORM_EPS = 1e-06
UNIT_EPS = 1e-06
STATE_EPS = 1e-30
DECAY_RATE = 0.5
CLIP_LEVEL = 0.05
RATE_SCALE = 10.0
NORM_RATE = 0.1


def layer_norm(values, gain_vec, shift_vec):
    center = values - jnp.mean(values, axis=-1, keepdims=True)
    spread = jnp.mean(center * center, axis=-1, keepdims=True)
    return center * lax.rsqrt(spread + NORM_EPS) * gain_vec + shift_vec


def geglu(joined):
    half_width = joined.shape[-1] // 2
    return jax.nn.gelu(joined[:, :half_width]) * joined[:, half_width:]


def alibi_slopes(head_count):
    return 2.0 ** (-8.0 * (jnp.arange(head_count).astype(jnp.float32) + 1.0) / head_count)


def normalize(vectors):
    return vectors * lax.rsqrt(jnp.sum(vectors * vectors, axis=-1, keepdims=True) + UNIT_EPS)


def contrast(unit_all, scale_arg, deal_order):
    pair_count = deal_order.shape[0] // 2
    queries = jnp.take(unit_all, deal_order[:pair_count], axis=0)
    documents = jnp.take(unit_all, deal_order[pair_count:], axis=0)
    logits = jnp.exp(scale_arg[0]) * jnp.matmul(
        queries, documents.T, precision=lax.Precision.HIGHEST
    )
    by_row = jax.nn.logsumexp(logits, axis=1)
    by_column = jax.nn.logsumexp(logits, axis=0)
    return jnp.sum(0.5 * (by_row + by_column) - jnp.diagonal(logits))


def unfactored(grad_full, state):
    state_new = DECAY_RATE * state + (1.0 - DECAY_RATE) * (grad_full * grad_full + STATE_EPS)
    return (-NORM_RATE * grad_full * lax.rsqrt(state_new), state_new)


def block_scores(query_rows, key_all, seg_rows, segment, head_count):
    row_count = query_rows.shape[0]
    raw_scores = jnp.einsum("thc,shc->hts", query_rows, key_all, preferred_element_type=jnp.float32)
    row_pos = jnp.arange(row_count, dtype=jnp.int32)
    col_pos = jnp.arange(key_all.shape[0], dtype=jnp.int32)
    distance = jnp.abs(row_pos[:, None] - col_pos[None, :]).astype(jnp.float32)
    scores = (
        raw_scores * HEAD_DIM ** (-0.5) + -alibi_slopes(head_count)[:, None, None] * distance[None]
    )
    same_seq = seg_rows[:, None] == segment[None, :]
    return jnp.where(same_seq[None], scores, -jnp.inf)


def split_qkv(qkv_low, head_count):
    tokens = qkv_low.shape[0]
    split_heads = qkv_low.reshape(tokens, 3, head_count, qkv_low.shape[1] // (3 * head_count))
    return (split_heads[:, 0], split_heads[:, 1], split_heads[:, 2])


def attend(qkv_low, segment, head_count):
    model_width = qkv_low.shape[1] // 3
    query_all, key_all, value_all = split_qkv(qkv_low, head_count)
    scores = block_scores(query_all, key_all, segment, segment, head_count)
    row_max = jnp.max(scores, axis=-1, keepdims=True)
    exponent = jnp.exp(scores - row_max)
    row_total = jnp.sum(exponent, axis=-1, keepdims=True)
    prob_low = (exponent / row_total).astype(jnp.bfloat16)
    mixed_list = jnp.einsum(
        "hts,shc->thc", prob_low, value_all, preferred_element_type=jnp.float32
    ).reshape(-1, model_width)
    lse_list = row_max[..., 0] + jnp.log(row_total[..., 0])
    return (mixed_list, lse_list)


def attend_back(qkv_low, segment, head_count, lse_all, grad_mixed):
    tokens = qkv_low.shape[0]
    query_all, key_all, value_all = split_qkv(qkv_low, head_count)
    grad_out = grad_mixed.reshape(tokens, head_count, -1)
    block_rows = min(tokens, 512)
    scores = block_scores(query_all, key_all, segment, segment, head_count)
    prob_full = jnp.exp(scores - lse_all[:, 0:block_rows, None])
    grad_value = jnp.einsum(
        "hts,thc->shc", prob_full.astype(jnp.bfloat16), grad_out, preferred_element_type=jnp.float32
    )
    grad_prob = jnp.einsum("thc,shc->hts", grad_out, value_all, preferred_element_type=jnp.float32)
    inner = jnp.sum(prob_full * grad_prob, axis=-1, keepdims=True)
    grad_raw = (prob_full * (grad_prob - inner) * HEAD_DIM ** (-0.5)).astype(jnp.bfloat16)
    query_list = jnp.einsum("hts,shc->thc", grad_raw, key_all, preferred_element_type=jnp.float32)
    grad_key = jnp.einsum("hts,thc->shc", grad_raw, query_all, preferred_element_type=jnp.float32)
    return (
        jnp.stack([query_list, grad_key, grad_value], axis=1)
        .reshape(tokens, -1)
        .astype(jnp.bfloat16)
    )


def shards(
    token_ids,
    seq_lengths,
    valid_mask,
    deal_order,
    log_scale,
    embed_master,
    attn_in,
    attn_out,
    ffn_in,
    ffn_out,
    head_master,
    norm_master,
    embed_rows,
    head_rows,
    layer_rows,
    ffn_out_rows,
    layer_cols,
    embed_head_cols,
    norm_state,
    scale_state,
):
    tokens = token_ids.shape[0]
    model_width = embed_master.shape[1]
    seq_count = seq_lengths.shape[1]
    head_count = HEADS
    position = jnp.arange(tokens, dtype=jnp.int32)
    bounds = jnp.cumsum(seq_lengths[0])
    segment = jnp.sum((position[:, None] >= bounds[None, :]).astype(jnp.int32), axis=1)
    piece_rows = lax.all_gather(embed_master.astype(jnp.bfloat16), "dp", axis=0, tiled=True)
    local_idx = token_ids
    inside = (local_idx >= 0) & (local_idx < piece_rows.shape[0])
    picked = jnp.take(piece_rows, jnp.clip(local_idx, 0, piece_rows.shape[0] - 1), axis=0).astype(
        jnp.float32
    )
    stream = jnp.where(inside[:, None], picked, 0.0)
    w_qkv, w_attn, w_gate_up, w_down, w_head, norm_low = (
        lax.all_gather(attn_in.astype(jnp.bfloat16), "dp", axis=1, tiled=True),
        lax.all_gather(attn_out.astype(jnp.bfloat16), "dp", axis=1, tiled=True),
        lax.all_gather(ffn_in.astype(jnp.bfloat16), "dp", axis=1, tiled=True),
        lax.all_gather(ffn_out.astype(jnp.bfloat16), "dp", axis=1, tiled=True),
        lax.all_gather(head_master.astype(jnp.bfloat16), "dp", axis=0, tiled=True),
        lax.all_gather(norm_master.astype(jnp.bfloat16), "dp", axis=2, tiled=True),
    )
    norms = norm_low.astype(jnp.float32)
    kept_list = []
    for layer_idx in range(LAYERS):
        stream_low = stream.astype(jnp.bfloat16)
        qkv_low = jnp.dot(stream_low, w_qkv[layer_idx], preferred_element_type=jnp.float32).astype(
            jnp.bfloat16
        )
        mixed_heads, lse_all = attend(qkv_low, segment, head_count)
        mixed_low = mixed_heads.astype(jnp.bfloat16)
        resid_one = stream + jnp.dot(
            mixed_low, w_attn[layer_idx], preferred_element_type=jnp.float32
        )
        normed = layer_norm(resid_one, norms[2 * layer_idx, 0], norms[2 * layer_idx, 1])
        normed_low = normed.astype(jnp.bfloat16)
        joined = jnp.dot(normed_low, w_gate_up[layer_idx], preferred_element_type=jnp.float32)
        hidden_low = geglu(joined).astype(jnp.bfloat16)
        resid_two = normed + jnp.dot(
            hidden_low, w_down[layer_idx], preferred_element_type=jnp.float32
        )
        kept_list.append(
            (
                stream_low,
                qkv_low,
                lse_all,
                mixed_low,
                resid_one,
                normed_low,
                joined,
                hidden_low,
                resid_two,
            )
        )
        stream = layer_norm(resid_two, norms[2 * layer_idx + 1, 0], norms[2 * layer_idx + 1, 1])
    final = layer_norm(stream, norms[2 * LAYERS, 0], norms[2 * LAYERS, 1])
    member = (
        (segment[None, :] == jnp.arange(seq_count, dtype=jnp.int32)[:, None])
        & (valid_mask[None, :] > 0)
    ).astype(jnp.float32)
    counts = jnp.maximum(jnp.sum(member, axis=1), 1.0)
    pooled = jnp.matmul(member, final, precision=lax.Precision.HIGHEST) / counts[:, None]
    pooled_low = pooled.astype(jnp.bfloat16)
    head_out = jnp.dot(pooled_low, w_head, preferred_element_type=jnp.float32)
    unit_vecs, unit_back = jax.vjp(normalize, head_out)
    unit_every = lax.all_gather(unit_vecs, ("dp", "group"), axis=0, tiled=True)
    loss_value, loss_back = jax.vjp(
        lambda unit_all, scale_arg: contrast(unit_all, scale_arg, deal_order), unit_every, log_scale
    )
    grad_units, grad_scale = loss_back(jnp.ones_like(loss_value))
    own_rows = lax.dynamic_slice_in_dim(
        grad_units, lax.axis_index(("dp", "group")) * seq_count, seq_count, 0
    )
    grad_head_out = unit_back(own_rows)[0].astype(jnp.bfloat16)
    grad_head = jnp.dot(pooled_low.T, grad_head_out, preferred_element_type=jnp.float32)
    grad_pooled = jnp.dot(grad_head_out, w_head.T, preferred_element_type=jnp.float32)
    grad_final = jnp.matmul(
        member.T, grad_pooled / counts[:, None], precision=lax.Precision.HIGHEST
    )
    final_back = jax.vjp(layer_norm, stream, norms[2 * LAYERS, 0], norms[2 * LAYERS, 1])[1]
    grad_stream, gain_last, shift_last = final_back(grad_final)
    norm_grads = [None] * (2 * LAYERS + 1)
    norm_grads[2 * LAYERS] = jnp.stack([gain_last, shift_last])
    qkv_grads = [None] * LAYERS
    attn_grads = [None] * LAYERS
    gate_grads = [None] * LAYERS
    down_grads = [None] * LAYERS
    for layer_idx in reversed(range(LAYERS)):
        (
            stream_low,
            qkv_low,
            lse_all,
            mixed_low,
            resid_one,
            normed_low,
            joined,
            hidden_low,
            resid_two,
        ) = kept_list[layer_idx]
        norm_two_back = jax.vjp(
            layer_norm, resid_two, norms[2 * layer_idx + 1, 0], norms[2 * layer_idx + 1, 1]
        )[1]
        grad_two, gain_two, shift_two = norm_two_back(grad_stream)
        norm_grads[2 * layer_idx + 1] = jnp.stack([gain_two, shift_two])
        grad_branch = grad_two.astype(jnp.bfloat16)
        down_grads[layer_idx] = jnp.dot(
            hidden_low.T, grad_branch, preferred_element_type=jnp.float32
        )
        grad_hidden = jnp.dot(grad_branch, w_down[layer_idx].T, preferred_element_type=jnp.float32)
        grad_joined = jax.vjp(geglu, joined)[1](grad_hidden)[0].astype(jnp.bfloat16)
        gate_grads[layer_idx] = jnp.dot(
            normed_low.T, grad_joined, preferred_element_type=jnp.float32
        )
        grad_normed = grad_two + jnp.dot(
            grad_joined, w_gate_up[layer_idx].T, preferred_element_type=jnp.float32
        )
        norm_one_back = jax.vjp(
            layer_norm, resid_one, norms[2 * layer_idx, 0], norms[2 * layer_idx, 1]
        )[1]
        grad_one, gain_one, shift_one = norm_one_back(grad_normed)
        norm_grads[2 * layer_idx] = jnp.stack([gain_one, shift_one])
        grad_attended = grad_one.astype(jnp.bfloat16)
        attn_grads[layer_idx] = jnp.dot(
            mixed_low.T, grad_attended, preferred_element_type=jnp.float32
        )
        grad_mixed = jnp.dot(
            grad_attended, w_attn[layer_idx].T, preferred_element_type=jnp.float32
        ).astype(jnp.bfloat16)
        grad_qkv_low = attend_back(qkv_low, segment, head_count, lse_all, grad_mixed)
        qkv_grads[layer_idx] = jnp.dot(
            stream_low.T, grad_qkv_low, preferred_element_type=jnp.float32
        )
        grad_stream = grad_one + jnp.dot(
            grad_qkv_low, w_qkv[layer_idx].T, preferred_element_type=jnp.float32
        )
    row_count = embed_master.shape[0] * lax.axis_size("dp")
    local_idx = token_ids
    inside = (local_idx >= 0) & (local_idx < row_count)
    slot_idx = jnp.where(inside, local_idx, row_count)
    embed_grad = lax.psum_scatter(
        jnp.zeros((row_count, model_width), jnp.float32).at[slot_idx].add(grad_stream, mode="drop"),
        "dp",
        scatter_dimension=0,
        tiled=True,
    )
    grad_qkv = jnp.stack(qkv_grads)
    grad_attn = jnp.stack(attn_grads)
    grad_gate_up = jnp.stack(gate_grads)
    grad_down = jnp.stack(down_grads)
    grad_norm = jnp.stack(norm_grads)
    owned = (
        lax.psum_scatter(grad_qkv, "dp", scatter_dimension=1, tiled=True),
        lax.psum_scatter(grad_attn, "dp", scatter_dimension=1, tiled=True),
        lax.psum_scatter(grad_gate_up, "dp", scatter_dimension=1, tiled=True),
        lax.psum_scatter(grad_down, "dp", scatter_dimension=1, tiled=True),
        lax.psum_scatter(grad_head, "dp", scatter_dimension=0, tiled=True),
        lax.psum_scatter(grad_norm, "dp", scatter_dimension=2, tiled=True),
    )
    shard_qkv, shard_attn, shard_gate_up, shard_down, shard_head, shard_norm, shard_embed = (
        lax.psum((owned[0], owned[1], owned[2], owned[3], owned[4], owned[5], embed_grad), "group")
    )
    grad_list = [
        shard_embed[None],
        shard_head[None],
        shard_qkv,
        shard_attn,
        shard_gate_up,
        shard_down,
    ]
    master_list = [embed_master[None], head_master[None], attn_in, attn_out, ffn_in, ffn_out]
    state_list = [
        embed_rows[None],
        head_rows[None],
        layer_rows[:, 0],
        layer_rows[:, 1],
        layer_rows[:, 2],
        ffn_out_rows,
    ]
    col_list = [
        embed_head_cols[0:1],
        embed_head_cols[1:2],
        layer_cols[:, : 3 * D],
        layer_cols[:, 3 * D : 4 * D],
        layer_cols[:, 4 * D : 4 * D + 2 * FF],
        layer_cols[:, 4 * D + 2 * FF :],
    ]
    total_rows = [VOCAB, D, D, D, D, FF]
    wide_rate = RATE_SCALE / D**0.5
    rates = [
        RATE_SCALE,
        wide_rate,
        wide_rate,
        RATE_SCALE / (D // 8) ** 0.5,
        wide_rate,
        RATE_SCALE / FF**0.5,
    ]
    square_list = [grad_part * grad_part for grad_part in grad_list]
    rows_new = [
        DECAY_RATE * state_list[entry_idx]
        + (1.0 - DECAY_RATE) * (jnp.mean(square_list[entry_idx], axis=-1) + STATE_EPS)
        for entry_idx in range(6)
    ]
    col_parts = jnp.concatenate(
        [jnp.sum(square_part, axis=1).reshape(-1) for square_part in square_list]
    )
    row_parts = jnp.concatenate([jnp.sum(row_part, axis=-1) for row_part in rows_new])
    col_sum, row_sum = lax.psum((col_parts, row_parts), "dp")
    row_means = []
    lead_start = 0
    for entry_idx in range(6):
        lead_count = grad_list[entry_idx].shape[0]
        row_means.append(row_sum[lead_start : lead_start + lead_count] / total_rows[entry_idx])
        lead_start = lead_start + lead_count
    cols_new = []
    steps_all = []
    col_start = 0
    for entry_idx in range(6):
        lead_count = grad_list[entry_idx].shape[0]
        col_width = grad_list[entry_idx].shape[2]
        col_full = col_sum[col_start : col_start + lead_count * col_width].reshape(
            lead_count, col_width
        )
        col_state_new = DECAY_RATE * col_list[entry_idx] + (1.0 - DECAY_RATE) * (
            col_full / total_rows[entry_idx] + STATE_EPS
        )
        cols_new.append(col_state_new)
        steps_all.append(
            grad_list[entry_idx]
            * lax.rsqrt(
                rows_new[entry_idx][:, :, None]
                * col_state_new[:, None, :]
                / row_means[entry_idx][:, None, None]
            )
        )
        col_start = col_start + lead_count * col_width
    step_squares = []
    step_parts = jnp.concatenate(
        [jnp.sum(step_dir * step_dir, axis=(1, 2)) for step_dir in steps_all]
    )
    step_sum = lax.psum(step_parts, "dp")
    lead_start = 0
    for entry_idx in range(6):
        lead_count = grad_list[entry_idx].shape[0]
        step_squares.append(step_sum[lead_start : lead_start + lead_count])
        lead_start = lead_start + lead_count
    new_weights = []
    rms_list = []
    for entry_idx in range(6):
        cell_count = total_rows[entry_idx] * grad_list[entry_idx].shape[2]
        step_rms = jnp.sqrt(step_squares[entry_idx] / cell_count)
        rms_list.append(step_rms)
        delta = (
            -rates[entry_idx]
            * steps_all[entry_idx]
            / jnp.maximum(1.0, step_rms / CLIP_LEVEL)[:, None, None]
        )
        new_weights.append(master_list[entry_idx] + delta)
    norm_delta, norm_second = unfactored(shard_norm, norm_state)
    scale_delta, scale_state_new = unfactored(grad_scale, scale_state)
    return (
        loss_value,
        new_weights[0][0],
        new_weights[2],
        new_weights[3],
        new_weights[4],
        new_weights[5],
        new_weights[1][0],
        norm_master + norm_delta,
        log_scale + scale_delta,
        rows_new[0][0],
        rows_new[1][0],
        jnp.stack([rows_new[2], rows_new[3], rows_new[4]], axis=1),
        rows_new[5],
        jnp.concatenate([cols_new[2], cols_new[3], cols_new[4], cols_new[5]], axis=1),
        cols_new[0][0],
        cols_new[1][0],
        norm_second,
        scale_state_new,
        jnp.concatenate(rms_list),
    )


MESH = pl.DeviceIdType.MESH
BF=jnp.bfloat16

def place():
    dp = lax.axis_index("dp"); g = lax.axis_index("group")
    return dp // 2, dp % 2, g // 2, g % 2

def dev(z, x, y, c):
    return (z * 2 + x, y * 2 + c)

def entry_barrier(peers):
    bar = pltpu.get_barrier_semaphore()
    for p in peers:
        pl.semaphore_signal(bar, inc=1, device_id=p, device_id_type=MESH)
    pl.semaphore_wait(bar, len(peers))

def mult(v, m=16):
    return pl.multiple_of(v, m)

def gather_kernel(chunks, w_ref, rows_ref, ag_ref, got_ref, zs, zr, xs, xr, ys, yr, cs, cr, ls, es, er):
    z, x, y, c = place()
    me = z * 2 + x
    ep = [(lax.rem(me + k, 8), y * 2 + c) for k in range(8)]
    zp = [dev((z + k) % 4, x, y, c) for k in range(4)]
    xp, yp, cp = dev(z, 1 - x, y, c), dev(z, x, 1 - y, c), dev(z, x, y, 1 - c)
    entry_barrier(ep[1:] + [yp, cp])
    Q = len(chunks)
    hs = [mult(b + c * h + y * nb) for b, h, nb in chunks]
    nh = [h - nb for b, h, nb in chunks]
    bs = [mult(b + c * h + y * (h - nb)) for b, h, nb in chunks]
    nbs = [nb for b, h, nb in chunks]
    cb = [mult(b + c * h) for b, h, nb in chunks]
    nc = [h for b, h, nb in chunks]
    def rc(src, dst, s, r, d):
        return pltpu.make_async_remote_copy(src, dst, s, r, device_id=d, device_id_type=MESH)
    def shard(k, f):
        return ((z + 4 - k) % 4) * 2 + (x if f == 0 else 1 - x)
    own = pltpu.make_async_copy(w_ref, ag_ref.at[me], ls.at[0])
    own.start()
    kept = pltpu.make_async_copy(rows_ref.at[me], got_ref.at[me], ls.at[1])
    kept.start()
    ec = [rc(rows_ref.at[ep[k][0]], got_ref.at[me], es.at[k], er.at[k], ep[k]) for k in range(1, 8)]
    for copy in ec:
        copy.start()
    zc = {}; xc = {}; yc = {}; cc = {}
    for q in range(Q):
        for k in range(1, 4):
            zc[q, k] = rc(w_ref.at[pl.ds(hs[q], nh[q])], ag_ref.at[me, pl.ds(hs[q], nh[q])], zs.at[q, k], zr.at[q, k], zp[k])
        for k in range(4):
            src = w_ref.at[pl.ds(hs[q], nh[q])] if k == 0 else ag_ref.at[shard(k, 0), pl.ds(hs[q], nh[q])]
            xc[q, k] = rc(src, ag_ref.at[shard(k, 0), pl.ds(hs[q], nh[q])], xs.at[q, k], xr.at[q, k], xp)
        for k in range(4):
            for f in range(2):
                if k == 0 and f == 0: continue
                s = shard(k, f)
                yc[q, k, f] = rc(ag_ref.at[s, pl.ds(bs[q], nbs[q])], ag_ref.at[s, pl.ds(bs[q], nbs[q])], ys.at[q, 2 * k + f], yr.at[q, 2 * k + f], yp)
                cc[q, k, f] = rc(ag_ref.at[s, pl.ds(cb[q], nc[q])], ag_ref.at[s, pl.ds(cb[q], nc[q])], cs.at[q, 2 * k + f], cr.at[q, 2 * k + f], cp)
    def s0(q):
        for k in (2, 1, 3):
            zc[q, k].start()
        xc[q, 0].start()
    def s1(q):
        for k in (1, 3, 2):
            zc[q, k].wait_recv()
            xc[q, k].start()
            yc[q, k, 0].start()
    def s2(q):
        for k in (0, 1, 3, 2):
            xc[q, k].wait_recv()
            yc[q, k, 1].start()
    def s3(q):
        for k, f in ((1, 0), (3, 0), (2, 0), (0, 1), (1, 1), (3, 1), (2, 1)):
            yc[q, k, f].wait_recv()
            cc[q, k, f].start()
    st = [s0, s1, s2, s3]
    for t in range(Q + 3):
        for i in reversed(range(4)):
            q = t - i
            if 0 <= q < Q:
                st[i](q)
    for q in range(Q):
        for k in range(4):
            for f in range(2):
                if k or f: cc[q, k, f].wait_recv()
    for d in (zc, xc, cc) + (yc,):
        for v in d.values(): v.wait_send()
    for copy in ec:
        copy.wait()
    own.wait()
    kept.wait()

def gather_weights(w, rows, chunks, cid=1):
    Q = len(chunks)
    D = pltpu.SemaphoreType.DMA
    return pl.pallas_call(
        functools.partial(gather_kernel, chunks),
        out_shape=(jax.ShapeDtypeStruct((8,) + w.shape, w.dtype), jax.ShapeDtypeStruct(rows.shape, rows.dtype)),
        in_specs=[pl.BlockSpec(memory_space=pl.ANY)] * 2, out_specs=[pl.BlockSpec(memory_space=pl.ANY)] * 2,
        scratch_shapes=[D((Q, 4)), D((Q, 4)), D((Q, 4)), D((Q, 4)), D((Q, 8)), D((Q, 8)), D((Q, 8)), D((Q, 8)), D((2,)), D((8,)), D((8,))],
        compiler_params=pltpu.CompilerParams(collective_id=cid, has_side_effects=True),
    )(w, rows)

def spread_kernel(v_ref, o_ref, ss, rs, ls):
    lin = lax.axis_index("dp") * 4 + lax.axis_index("group")
    peers = [lax.rem(lin + k, 32) for k in range(32)]
    peers = [(p // 4, p % 4) for p in peers]
    entry_barrier(peers[1:])
    copies = [pltpu.make_async_remote_copy(v_ref, o_ref.at[lin], ss.at[k], rs.at[k], device_id=peers[k], device_id_type=MESH) for k in range(1, 32)]
    for copy in copies:
        copy.start()
    own = pltpu.make_async_copy(v_ref, o_ref.at[lin], ls)
    own.start()
    for copy in copies:
        copy.wait()
    own.wait()

def spread(v, cid):
    D = pltpu.SemaphoreType.DMA
    return pl.pallas_call(
        spread_kernel,
        out_shape=jax.ShapeDtypeStruct((32,) + v.shape, v.dtype),
        in_specs=[pl.BlockSpec(memory_space=pltpu.VMEM)], out_specs=pl.BlockSpec(memory_space=pltpu.VMEM),
        scratch_shapes=[D((32,)), D((32,)), D],
        compiler_params=pltpu.CompilerParams(collective_id=cid, has_side_effects=True),
    )(v)

def scatter_kernel(chunks, g_ref, e_ref, out_ref, t_ref, acc, b1, b2, b3, b4, b5, fin,
                   cs, cr, ys, yr, xs, xr, zs, zr, as_, ar, fs, fr, ls, os_, es, er, el):
    z, x, y, c = place()
    me = z * 2 + x
    g = y * 2 + c
    ep = [(lax.rem(me + k, 8), g) for k in range(8)]
    zp = [dev((z + k) % 4, x, y, c) for k in range(4)]
    xp, yp, cp = dev(z, 1 - x, y, c), dev(z, x, 1 - y, c), dev(z, x, y, 1 - c)
    entry_barrier(ep[1:] + [yp, cp])
    Q = len(chunks)
    lo = []; o = 0; lb = []; ob = 0; lh = []; oh = 0; la = []; oa = 0
    for b, h, nb in chunks:
        lo.append(o); o += h
        lb.append(ob); ob += nb
        lh.append(oh); oh += h - nb
        la.append(oa); oa += h - 2 * nb
    nh = [h - nb for b, h, nb in chunks]
    nbs = [nb for b, h, nb in chunks]
    na = [h - 2 * nb for b, h, nb in chunks]
    hs = [mult(lo[q] + y * nbs[q]) for q in range(Q)]
    mb = [mult(lo[q] + y * nh[q]) for q in range(Q)]
    ob_ = [mult(lo[q] + (1 - y) * nh[q]) for q in range(Q)]
    aa = [lo[q] + nbs[q] for q in range(Q)]
    def rc(src, dst, s, r, d):
        return pltpu.make_async_remote_copy(src, dst, s, r, device_id=d, device_id_type=MESH)
    def add(dst, src, n, blk=16):
        def body(i, _):
            a = mult(i * blk)
            d = dst(a, blk); s = src(a, blk)
            d[...] = (d[...].astype(jnp.float32) + s[...].astype(jnp.float32)).astype(BF)
            return _
        lax.fori_loop(0, n // blk, body, 0)
    order = []
    for k in (2, 1, 3, 0):
        for f in (1, 0):
            order.append((k, f))
    def owner(k, f):
        return ((z + k) % 4) * 2 + (x if f == 0 else 1 - x)
    C1 = {}; Y = {}; X = {}; Z = {}; A = {}; F = {}; L = {}; O = {}; BX = {}
    for q, (b, h, nb) in enumerate(chunks):
        for i, (k, f) in enumerate(order):
            s = owner(k, f)
            L[q, i] = pltpu.make_async_copy(g_ref.at[s, pl.ds(mult(b + c * h), h)], acc.at[s, pl.ds(lo[q], h)], ls.at[q, i])
            C1[q, i] = rc(g_ref.at[s, pl.ds(mult(b + (1 - c) * h), h)], b1.at[s, pl.ds(lo[q], h)], cs.at[q, i], cr.at[q, i], cp)
            Y[q, i] = rc(acc.at[s, pl.ds(ob_[q], nb)], b2.at[s, pl.ds(lb[q], nb)], ys.at[q, i], yr.at[q, i], yp)
        for k in range(4):
            X[q, k] = rc(acc.at[owner(k, 1), pl.ds(hs[q], nh[q])], b3.at[k, pl.ds(lh[q], nh[q])], xs.at[q, k], xr.at[q, k], xp)
            if k:
                Z[q, k] = rc(acc.at[owner(k, 0), pl.ds(hs[q], nh[q])], b4.at[k - 1, pl.ds(lh[q], nh[q])], zs.at[q, k], zr.at[q, k], zp[k])
        A[q] = rc(fin.at[pl.ds(aa[q], na[q])], b5.at[pl.ds(la[q], na[q])], as_.at[q, 0], ar.at[q, 0], yp)
        BX[q] = rc(fin.at[pl.ds(mb[q], nb)], fin.at[pl.ds(mb[q], nb)], as_.at[q, 1], ar.at[q, 1], yp)
        F[q] = rc(fin.at[pl.ds(lo[q], h)], out_ref.at[pl.ds(mult(b + c * h), h)], fs.at[q], fr.at[q], cp)
        O[q] = pltpu.make_async_copy(fin.at[pl.ds(lo[q], h)], out_ref.at[pl.ds(mult(b + c * h), h)], os_.at[q])
    g2 = (1 - y) * 2 + c
    kept = pltpu.make_async_copy(e_ref.at[me], t_ref.at[g, me], el)
    E = [rc(e_ref.at[ep[k][0]], t_ref.at[g, me], es.at[k], er.at[k], ep[k]) for k in range(1, 8)]
    EY = rc(t_ref.at[g], t_ref.at[g], es.at[8], er.at[8], yp)
    EC = rc(t_ref.at[g], t_ref.at[g], es.at[9], er.at[9], cp)
    ED = rc(t_ref.at[g2], t_ref.at[g2], es.at[10], er.at[10], cp)
    def e0():
        kept.start()
        for v in E: v.start()
    def e1():
        kept.wait()
        for v in E: v.wait_recv()
        EY.start(); EC.start()
    def e2():
        EY.wait_recv()
        ED.start()
    def e3():
        EC.wait_recv(); ED.wait_recv()
        for v in E + [EY, EC, ED]: v.wait_send()
    ev = {0: e0, 3: e1, 5: e2}
    def s0(q):
        for i in range(8):
            L[q, i].start(); C1[q, i].start()
    def s1(q):
        h = chunks[q][1]
        for i, (k, f) in enumerate(order):
            s = owner(k, f)
            L[q, i].wait(); C1[q, i].wait_recv()
            add(lambda a, n: acc.at[s, pl.ds(lo[q] + a, n)], lambda a, n: b1.at[s, pl.ds(lo[q] + a, n)], h)
            Y[q, i].start()
    def s2(q):
        for i, (k, f) in enumerate(order):
            s = owner(k, f)
            if nbs[q]:
                Y[q, i].wait_recv()
                add(lambda a, n: acc.at[s, pl.ds(mb[q] + a, n)], lambda a, n: b2.at[s, pl.ds(lb[q] + a, n)], nbs[q])
            if f == 1:
                X[q, k].start()
    def s3(q):
        for k in (2, 1, 3, 0):
            s = owner(k, 0)
            X[q, k].wait_recv()
            add(lambda a, n: acc.at[s, pl.ds(hs[q] + a, n)], lambda a, n: b3.at[k, pl.ds(lh[q] + a, n)], nh[q])
            if k: Z[q, k].start()
    def s4(q):
        for k in range(1, 4):
            Z[q, k].wait_recv()
        def body(i, _):
            a = mult(i * 16)
            t = acc[me, pl.ds(hs[q] + a, 16)].astype(jnp.float32)
            for k in range(3):
                t += b4[k, pl.ds(lh[q] + a, 16)].astype(jnp.float32)
            fin[pl.ds(hs[q] + a, 16)] = t.astype(BF)
            return _
        lax.fori_loop(0, nh[q] // 16, body, 0)
        A[q].start()
        BX[q].start()
    def s5(q):
        A[q].wait_recv()
        A[q].wait_send()
        add(lambda a, n: fin.at[pl.ds(aa[q] + a, n)], lambda a, n: b5.at[pl.ds(la[q] + a, n)], na[q])
        BX[q].wait_recv()
        F[q].start(); O[q].start()
    st = [s0, s1, s2, s3, s4, s5]
    for t in range(Q + 5):
        if t in ev: ev[t]()
        for i in reversed(range(6)):
            q = t - i
            if 0 <= q < Q:
                st[i](q)
    for q in range(Q):
        F[q].wait(); O[q].wait()
        BX[q].wait_send()
    for d in (C1, Y, X, Z):
        for v in d.values(): v.wait_send()
    e3()

def scatter_grads(g, e, chunks, cid=2):
    Q = len(chunks)
    D = pltpu.SemaphoreType.DMA
    H = sum(h for _, h, _ in chunks); NB = sum(nb for _, _, nb in chunks); NH = H - NB
    V = lambda *s: pltpu.VMEM(s, BF)
    return pl.pallas_call(
        functools.partial(scatter_kernel, chunks),
        out_shape=(jax.ShapeDtypeStruct(g.shape[1:], g.dtype), jax.ShapeDtypeStruct((4,) + e.shape, e.dtype)),
        in_specs=[pl.BlockSpec(memory_space=pl.ANY)] * 2, out_specs=[pl.BlockSpec(memory_space=pl.ANY)] * 2,
        scratch_shapes=[V(8, H, 512), V(8, H, 512), V(8, NB, 512), V(4, NH, 512), V(3, NH, 512), V(H - 2 * NB, 512), V(H, 512),
            D((Q, 8)), D((Q, 8)), D((Q, 8)), D((Q, 8)), D((Q, 4)), D((Q, 4)), D((Q, 4)), D((Q, 4)), D((Q, 2)), D((Q, 2)), D((Q,)), D((Q,)), D((Q, 8)), D((Q,)),
            D((11,)), D((11,)), D],
        compiler_params=pltpu.CompilerParams(collective_id=cid, has_side_effects=True, vmem_limit_bytes=60 * 2**20),
    )(g, e)

def plan(rows, count, share):
    units = rows // 32
    chunks = []
    base = 0
    for i in range(count):
        size = units // count + (1 if i < units % count else 0)
        chunks.append((base, 16 * size, 16 * int(round(size * share))))
        base += 32 * size
    return chunks


SLOTS = 96
PART = 1024
HEAD_AT = 2 * PART
NORM_AT = HEAD_AT + 64
PACKED = NORM_AT + 32


def slot_plan(token_ids, shard_rows):
    tokens = token_ids.shape[0]
    owner = token_ids // shard_rows
    local = token_ids - owner * shard_rows
    index = jnp.arange(tokens, dtype=jnp.int32)
    same_id = token_ids[:, None] == token_ids[None, :]
    first = jnp.min(jnp.where(same_id, index[None, :], tokens), axis=1)
    leads = first == index
    same_owner = owner[:, None] == owner[None, :]
    slot = jnp.sum(
        (same_owner & leads[None, :] & (index[None, :] < first[:, None])).astype(jnp.int32), axis=1
    )
    key = jnp.where(slot < SLOTS, owner * SLOTS + slot, 8 * SLOTS)
    wanted = jnp.max(
        jnp.where(
            key[:, None] == jnp.arange(8 * SLOTS, dtype=jnp.int32)[None, :], local[:, None], -1
        ),
        axis=0,
    )
    return key, wanted, jnp.max(slot)


def column_blocks(rows):
    lead, count, width = rows.shape
    return (
        rows.reshape(lead, count, width // D, D).transpose(0, 2, 1, 3).reshape(lead, -1, D)
    )


def pack_weights(attn_in, attn_out, ffn_in, ffn_out, head_master, norm_master):
    layers = jnp.concatenate(
        [column_blocks(attn_in), attn_out, column_blocks(ffn_in), ffn_out], axis=1
    ).astype(jnp.bfloat16)
    norm_rows = jnp.pad(
        norm_master.reshape(10, -1).astype(jnp.bfloat16), ((0, 22), (0, D - norm_master.shape[2]))
    )
    return jnp.concatenate(
        [layers.reshape(-1, D), head_master.astype(jnp.bfloat16), norm_rows], axis=0
    )


def whole_columns(part, blocks):
    return (
        part.reshape(8, blocks, -1, D).transpose(0, 2, 1, 3).reshape(-1, blocks * D)
    )


def shard_columns(part, blocks):
    return part.reshape(blocks, -1, D).transpose(1, 0, 2).reshape(-1, blocks * D)


def owned_columns(grad):
    rows, width = grad.shape
    return (
        grad.reshape(8, rows // 8, width // D, D).transpose(0, 2, 1, 3).reshape(8, -1, D)
    )


def place_kernel(slot_ref, rows_ref, out_ref):
    start = pl.program_id(0) * out_ref.shape[0]
    rows = lax.broadcasted_iota(jnp.int32, (out_ref.shape[0], slot_ref.shape[1]), 0) + start
    picks = jnp.where(rows == slot_ref[...], 1.0, 0.0).astype(jnp.bfloat16)
    out_ref[...] = jnp.dot(picks, rows_ref[...], preferred_element_type=jnp.float32)


def place_rows(slots, rows, row_count):
    tile = row_count // 9
    return pl.pallas_call(
        place_kernel,
        grid=(9,),
        in_specs=[
            pl.BlockSpec((1, slots.shape[1]), lambda i: (0, 0)),
            pl.BlockSpec(rows.shape, lambda i: (0, 0)),
        ],
        out_specs=pl.BlockSpec((tile, D), lambda i: (i, 0)),
        out_shape=jax.ShapeDtypeStruct((row_count, D), jnp.float32),
        compiler_params=pltpu.CompilerParams(vmem_limit_bytes=48 * 2**20),
    )(slots, rows)


def fast_shards(
    token_ids,
    seq_lengths,
    valid_mask,
    deal_order,
    log_scale,
    embed_master,
    attn_in,
    attn_out,
    ffn_in,
    ffn_out,
    head_master,
    norm_master,
    embed_rows,
    head_rows,
    layer_rows,
    ffn_out_rows,
    layer_cols,
    embed_head_cols,
    norm_state,
    scale_state,
):
    tokens = token_ids.shape[0]
    seq_count = seq_lengths.shape[1]
    head_count = HEADS
    shard_rows = embed_master.shape[0]
    my_dp = lax.axis_index("dp")
    my_group = lax.axis_index("group")
    position = jnp.arange(tokens, dtype=jnp.int32)
    bounds = jnp.cumsum(seq_lengths[0])
    segment = jnp.sum((position[:, None] >= bounds[None, :]).astype(jnp.int32), axis=1)

    key, wanted, most = slot_plan(token_ids, shard_rows)
    request = jnp.concatenate(
        [wanted.reshape(-1, 128), jnp.broadcast_to(most, (2, 128))], axis=0
    ).astype(jnp.int32)
    requests = spread(request, 0)
    crowded = jnp.max(requests[:, 6]) >= SLOTS
    asked = requests[:, :6].reshape(32, 8, SLOTS)
    asked_here = lax.dynamic_index_in_dim(asked, my_dp, 1, keepdims=False)
    group_asks = asked_here.reshape(8, 4, SLOTS)
    to_send = lax.dynamic_index_in_dim(group_asks, my_group, 1, keepdims=False)
    sent_rows = jnp.take(
        embed_master, jnp.clip(to_send.reshape(-1), 0, shard_rows - 1), axis=0
    ).astype(jnp.bfloat16)
    packed = pack_weights(attn_in, attn_out, ffn_in, ffn_out, head_master, norm_master)
    weights, got_rows = gather_weights(
        packed, sent_rows.reshape(8, SLOTS, D), plan(PACKED, 4, 0.36)
    )

    def dense_rows():
        table = lax.all_gather(embed_master.astype(jnp.bfloat16), "dp", axis=0, tiled=True)
        return jnp.take(table, token_ids, axis=0)

    def slot_rows():
        return jnp.take(got_rows.reshape(-1, D), jnp.minimum(key, 8 * SLOTS - 1), axis=0)

    stream = lax.cond(crowded, dense_rows, slot_rows).astype(jnp.float32)
    w_qkv = [whole_columns(weights[:, l * PART : l * PART + 192], 3) for l in range(LAYERS)]
    w_attn = [weights[:, l * PART + 192 : l * PART + 256].reshape(D, D) for l in range(LAYERS)]
    w_gate_up = [whole_columns(weights[:, l * PART + 256 : l * PART + 768], 8) for l in range(LAYERS)]
    w_down = [weights[:, l * PART + 768 : l * PART + 1024].reshape(FF, D) for l in range(LAYERS)]
    w_head = weights[:, HEAD_AT : HEAD_AT + 64].reshape(D, D)
    norms = (
        weights[:, NORM_AT : NORM_AT + 10, :64]
        .transpose(1, 0, 2)
        .reshape(5, 2, D)
        .astype(jnp.float32)
    )
    kept_list = []
    for layer_idx in range(LAYERS):
        stream_low = stream.astype(jnp.bfloat16)
        qkv_low = jnp.dot(stream_low, w_qkv[layer_idx], preferred_element_type=jnp.float32).astype(
            jnp.bfloat16
        )
        mixed_heads, lse_all = attend(qkv_low, segment, head_count)
        mixed_low = mixed_heads.astype(jnp.bfloat16)
        resid_one = stream + jnp.dot(
            mixed_low, w_attn[layer_idx], preferred_element_type=jnp.float32
        )
        normed = layer_norm(resid_one, norms[2 * layer_idx, 0], norms[2 * layer_idx, 1])
        normed_low = normed.astype(jnp.bfloat16)
        joined = jnp.dot(normed_low, w_gate_up[layer_idx], preferred_element_type=jnp.float32)
        hidden_low = geglu(joined).astype(jnp.bfloat16)
        resid_two = normed + jnp.dot(
            hidden_low, w_down[layer_idx], preferred_element_type=jnp.float32
        )
        kept_list.append(
            (
                stream_low,
                qkv_low,
                lse_all,
                mixed_low,
                resid_one,
                normed_low,
                joined,
                hidden_low,
                resid_two,
            )
        )
        stream = layer_norm(resid_two, norms[2 * layer_idx + 1, 0], norms[2 * layer_idx + 1, 1])
    final = layer_norm(stream, norms[2 * LAYERS, 0], norms[2 * LAYERS, 1])
    member = (
        (segment[None, :] == jnp.arange(seq_count, dtype=jnp.int32)[:, None])
        & (valid_mask[None, :] > 0)
    ).astype(jnp.float32)
    counts = jnp.maximum(jnp.sum(member, axis=1), 1.0)
    pooled = jnp.matmul(member, final, precision=lax.Precision.HIGHEST) / counts[:, None]
    pooled_low = pooled.astype(jnp.bfloat16)
    head_out = jnp.dot(pooled_low, w_head, preferred_element_type=jnp.float32)
    unit_vecs, unit_back = jax.vjp(normalize, head_out)
    unit_every = spread(unit_vecs, 3).reshape(-1, D)
    loss_value, loss_back = jax.vjp(
        lambda unit_all, scale_arg: contrast(unit_all, scale_arg, deal_order), unit_every, log_scale
    )
    grad_units, grad_scale = loss_back(jnp.ones_like(loss_value))
    own_rows = lax.dynamic_slice_in_dim(
        grad_units, lax.axis_index(("dp", "group")) * seq_count, seq_count, 0
    )
    grad_head_out = unit_back(own_rows)[0].astype(jnp.bfloat16)
    grad_head = jnp.dot(pooled_low.T, grad_head_out, preferred_element_type=jnp.float32)
    grad_pooled = jnp.dot(grad_head_out, w_head.T, preferred_element_type=jnp.float32)
    grad_final = jnp.matmul(
        member.T, grad_pooled / counts[:, None], precision=lax.Precision.HIGHEST
    )
    final_back = jax.vjp(layer_norm, stream, norms[2 * LAYERS, 0], norms[2 * LAYERS, 1])[1]
    grad_stream, gain_last, shift_last = final_back(grad_final)
    norm_grads = [None] * (2 * LAYERS + 1)
    norm_grads[2 * LAYERS] = jnp.stack([gain_last, shift_last])
    packed_grads = [None] * LAYERS
    for layer_idx in reversed(range(LAYERS)):
        (
            stream_low,
            qkv_low,
            lse_all,
            mixed_low,
            resid_one,
            normed_low,
            joined,
            hidden_low,
            resid_two,
        ) = kept_list[layer_idx]
        norm_two_back = jax.vjp(
            layer_norm, resid_two, norms[2 * layer_idx + 1, 0], norms[2 * layer_idx + 1, 1]
        )[1]
        grad_two, gain_two, shift_two = norm_two_back(grad_stream)
        norm_grads[2 * layer_idx + 1] = jnp.stack([gain_two, shift_two])
        grad_branch = grad_two.astype(jnp.bfloat16)
        down_grad = jnp.dot(hidden_low.T, grad_branch, preferred_element_type=jnp.float32)
        grad_hidden = jnp.dot(grad_branch, w_down[layer_idx].T, preferred_element_type=jnp.float32)
        grad_joined = jax.vjp(geglu, joined)[1](grad_hidden)[0].astype(jnp.bfloat16)
        gate_grad = jnp.dot(normed_low.T, grad_joined, preferred_element_type=jnp.float32)
        grad_normed = grad_two + jnp.dot(
            grad_joined, w_gate_up[layer_idx].T, preferred_element_type=jnp.float32
        )
        norm_one_back = jax.vjp(
            layer_norm, resid_one, norms[2 * layer_idx, 0], norms[2 * layer_idx, 1]
        )[1]
        grad_one, gain_one, shift_one = norm_one_back(grad_normed)
        norm_grads[2 * layer_idx] = jnp.stack([gain_one, shift_one])
        grad_attended = grad_one.astype(jnp.bfloat16)
        attn_grad = jnp.dot(mixed_low.T, grad_attended, preferred_element_type=jnp.float32)
        grad_mixed = jnp.dot(
            grad_attended, w_attn[layer_idx].T, preferred_element_type=jnp.float32
        ).astype(jnp.bfloat16)
        grad_qkv_low = attend_back(qkv_low, segment, head_count, lse_all, grad_mixed)
        qkv_grad = jnp.dot(stream_low.T, grad_qkv_low, preferred_element_type=jnp.float32)
        grad_stream = grad_one + jnp.dot(
            grad_qkv_low, w_qkv[layer_idx].T, preferred_element_type=jnp.float32
        )
        packed_grads[layer_idx] = jnp.concatenate(
            [
                owned_columns(qkv_grad),
                owned_columns(attn_grad),
                owned_columns(gate_grad),
                down_grad.reshape(8, -1, D),
            ],
            axis=1,
        ).astype(jnp.bfloat16)
    head_part = owned_columns(grad_head).astype(jnp.bfloat16)
    all_grads = jnp.concatenate(
        packed_grads + [head_part, jnp.zeros((8, PACKED - NORM_AT, D), jnp.bfloat16)], axis=1
    )
    slot_grads = jnp.dot(
        (jnp.arange(8 * SLOTS, dtype=jnp.int32)[:, None] == key[None, :]).astype(jnp.bfloat16),
        grad_stream.astype(jnp.bfloat16),
        preferred_element_type=jnp.float32,
    ).astype(jnp.bfloat16)
    shard_grads, table_rows = scatter_grads(
        all_grads, slot_grads.reshape(8, SLOTS, D), plan(PACKED, 4, 0.29)
    )
    table_slots = asked_here.reshape(8, 4, SLOTS).transpose(1, 0, 2).reshape(1, -1)

    def dense_grad():
        total = jnp.zeros((shard_rows * 8, D), jnp.float32).at[token_ids].add(grad_stream)
        return lax.psum(
            lax.psum_scatter(total, "dp", scatter_dimension=0, tiled=True), "group"
        )

    def slot_grad():
        return place_rows(table_slots, table_rows.reshape(-1, D), shard_rows)

    shard_embed = lax.cond(crowded, dense_grad, slot_grad)
    shard_full = shard_grads.astype(jnp.float32)
    shard_layers = shard_full[:HEAD_AT].reshape(LAYERS, PART, D)
    shard_qkv = jnp.stack([shard_columns(shard_layers[l, :192], 3) for l in range(LAYERS)])
    shard_attn = shard_layers[:, 192:256]
    shard_gate_up = jnp.stack([shard_columns(shard_layers[l, 256:768], 8) for l in range(LAYERS)])
    shard_down = shard_layers[:, 768:]
    shard_head = shard_full[HEAD_AT : HEAD_AT + 64]
    grad_list = [
        shard_embed[None],
        shard_head[None],
        shard_qkv,
        shard_attn,
        shard_gate_up,
        shard_down,
    ]
    master_list = [embed_master[None], head_master[None], attn_in, attn_out, ffn_in, ffn_out]
    state_list = [
        embed_rows[None],
        head_rows[None],
        layer_rows[:, 0],
        layer_rows[:, 1],
        layer_rows[:, 2],
        ffn_out_rows,
    ]
    col_list = [
        embed_head_cols[0:1],
        embed_head_cols[1:2],
        layer_cols[:, : 3 * D],
        layer_cols[:, 3 * D : 4 * D],
        layer_cols[:, 4 * D : 4 * D + 2 * FF],
        layer_cols[:, 4 * D + 2 * FF :],
    ]
    total_rows = [VOCAB, D, D, D, D, FF]
    wide_rate = RATE_SCALE / D**0.5
    rates = [
        RATE_SCALE,
        wide_rate,
        wide_rate,
        RATE_SCALE / (D // 8) ** 0.5,
        wide_rate,
        RATE_SCALE / FF**0.5,
    ]
    square_list = [grad_part * grad_part for grad_part in grad_list]
    rows_new = [
        DECAY_RATE * state_list[i]
        + (1.0 - DECAY_RATE) * (jnp.mean(square_list[i], axis=-1) + STATE_EPS)
        for i in range(6)
    ]
    col_parts = jnp.concatenate([jnp.sum(part, axis=1).reshape(-1) for part in square_list])
    step_parts = jnp.concatenate(
        [
            jnp.sum(square_list[i] * (1.0 / rows_new[i])[:, :, None], axis=1).reshape(-1)
            for i in range(6)
        ]
    )
    row_parts = jnp.concatenate([jnp.sum(part, axis=-1) for part in rows_new])
    col_sum, step_sum, row_sum, norm_grad = lax.psum(
        (0.25 * col_parts, 0.25 * step_parts, 0.25 * row_parts, jnp.stack(norm_grads)),
        ("dp", "group"),
    )
    shard_norm = lax.dynamic_slice_in_dim(norm_grad, my_dp * 64, 64, 2)
    cols_new = []
    new_weights = []
    rms_list = []
    lead_start = 0
    col_start = 0
    for i in range(6):
        lead_count, _, col_width = grad_list[i].shape
        span = slice(col_start, col_start + lead_count * col_width)
        row_mean = row_sum[lead_start : lead_start + lead_count] / total_rows[i]
        col_state_new = DECAY_RATE * col_list[i] + (1.0 - DECAY_RATE) * (
            col_sum[span].reshape(lead_count, col_width) / total_rows[i] + STATE_EPS
        )
        cols_new.append(col_state_new)
        step_total = jnp.sum(
            step_sum[span].reshape(lead_count, col_width) * row_mean[:, None] / col_state_new,
            axis=1,
        )
        step_rms = jnp.sqrt(step_total / (total_rows[i] * col_width))
        rms_list.append(step_rms)
        row_factor = lax.rsqrt(rows_new[i] / row_mean[:, None]) * (
            -rates[i] / jnp.maximum(1.0, step_rms / CLIP_LEVEL)[:, None]
        )
        new_weights.append(
            master_list[i]
            + grad_list[i] * row_factor[:, :, None] * lax.rsqrt(col_state_new)[:, None, :]
        )
        lead_start = lead_start + lead_count
        col_start = col_start + lead_count * col_width
    norm_delta, norm_second = unfactored(shard_norm, norm_state)
    scale_delta, scale_state_new = unfactored(grad_scale, scale_state)
    return (
        loss_value,
        new_weights[0][0],
        new_weights[2],
        new_weights[3],
        new_weights[4],
        new_weights[5],
        new_weights[1][0],
        norm_master + norm_delta,
        log_scale + scale_delta,
        rows_new[0][0],
        rows_new[1][0],
        jnp.stack([rows_new[2], rows_new[3], rows_new[4]], axis=1),
        rows_new[5],
        jnp.concatenate([cols_new[2], cols_new[3], cols_new[4], cols_new[5]], axis=1),
        cols_new[0][0],
        cols_new[1][0],
        norm_second,
        scale_state_new,
        jnp.concatenate(rms_list),
    )


def solution(mesh):
    in_specs = (
        P(("dp", "group")),
        P(("dp", "group"), None),
        P(("dp", "group")),
        P(),
        P(),
        P("dp", None),
        P(None, "dp", None),
        P(None, "dp", None),
        P(None, "dp", None),
        P(None, "dp", None),
        P("dp", None),
        P(None, None, "dp"),
        P("dp"),
        P("dp"),
        P(None, None, "dp"),
        P(None, "dp"),
        P(),
        P(),
        P(None, None, "dp"),
        P(),
    )
    out_specs = (
        P(),
        P("dp", None),
        P(None, "dp", None),
        P(None, "dp", None),
        P(None, "dp", None),
        P(None, "dp", None),
        P("dp", None),
        P(None, None, "dp"),
        P(),
        P("dp"),
        P("dp"),
        P(None, None, "dp"),
        P(None, "dp"),
        P(),
        P(),
        P(),
        P(None, None, "dp"),
        P(),
        P(),
    )
    body = fast_shards if dict(mesh.shape) == {"dp": 8, "group": 4} else shards
    return jax.shard_map(body, mesh=mesh, in_specs=in_specs, out_specs=out_specs, check_vma=False)
```

```python
import functools

import jax
import jax.numpy as jnp
from jax import lax
from jax.experimental import pallas as pl
from jax.experimental.pallas import tpu as pltpu
from jax.sharding import PartitionSpec as P

D = 512
HEADS = 8
HEAD_DIM = 64
FF = 2048
VOCAB = 30528
LAYERS = 2


NORM_EPS = 1e-06
UNIT_EPS = 1e-06
STATE_EPS = 1e-30
DECAY_RATE = 0.5
CLIP_LEVEL = 0.05
RATE_SCALE = 10.0
NORM_RATE = 0.1


def layer_norm(values, gain_vec, shift_vec):
    center = values - jnp.mean(values, axis=-1, keepdims=True)
    spread = jnp.mean(center * center, axis=-1, keepdims=True)
    return center * lax.rsqrt(spread + NORM_EPS) * gain_vec + shift_vec


def geglu(joined):
    half_width = joined.shape[-1] // 2
    return jax.nn.gelu(joined[:, :half_width]) * joined[:, half_width:]


def alibi_slopes(head_count):
    return 2.0 ** (-8.0 * (jnp.arange(head_count).astype(jnp.float32) + 1.0) / head_count)


def normalize(vectors):
    return vectors * lax.rsqrt(jnp.sum(vectors * vectors, axis=-1, keepdims=True) + UNIT_EPS)


def contrast(unit_all, scale_arg, deal_order):
    pair_count = deal_order.shape[0] // 2
    queries = jnp.take(unit_all, deal_order[:pair_count], axis=0)
    documents = jnp.take(unit_all, deal_order[pair_count:], axis=0)
    logits = jnp.exp(scale_arg[0]) * jnp.matmul(
        queries, documents.T, precision=lax.Precision.HIGHEST
    )
    by_row = jax.nn.logsumexp(logits, axis=1)
    by_column = jax.nn.logsumexp(logits, axis=0)
    return jnp.sum(0.5 * (by_row + by_column) - jnp.diagonal(logits))


def unfactored(grad_full, state):
    state_new = DECAY_RATE * state + (1.0 - DECAY_RATE) * (grad_full * grad_full + STATE_EPS)
    return (-NORM_RATE * grad_full * lax.rsqrt(state_new), state_new)


def block_scores(query_rows, key_all, seg_rows, segment, head_count):
    row_count = query_rows.shape[0]
    raw_scores = jnp.einsum("thc,shc->hts", query_rows, key_all, preferred_element_type=jnp.float32)
    row_pos = jnp.arange(row_count, dtype=jnp.int32)
    col_pos = jnp.arange(key_all.shape[0], dtype=jnp.int32)
    distance = jnp.abs(row_pos[:, None] - col_pos[None, :]).astype(jnp.float32)
    scores = (
        raw_scores * HEAD_DIM ** (-0.5) + -alibi_slopes(head_count)[:, None, None] * distance[None]
    )
    same_seq = seg_rows[:, None] == segment[None, :]
    return jnp.where(same_seq[None], scores, -jnp.inf)


def split_qkv(qkv_low, head_count):
    tokens = qkv_low.shape[0]
    split_heads = qkv_low.reshape(tokens, 3, head_count, qkv_low.shape[1] // (3 * head_count))
    return (split_heads[:, 0], split_heads[:, 1], split_heads[:, 2])


def attend(qkv_low, segment, head_count):
    model_width = qkv_low.shape[1] // 3
    query_all, key_all, value_all = split_qkv(qkv_low, head_count)
    scores = block_scores(query_all, key_all, segment, segment, head_count)
    row_max = jnp.max(scores, axis=-1, keepdims=True)
    exponent = jnp.exp(scores - row_max)
    row_total = jnp.sum(exponent, axis=-1, keepdims=True)
    prob_low = (exponent / row_total).astype(jnp.bfloat16)
    mixed_list = jnp.einsum(
        "hts,shc->thc", prob_low, value_all, preferred_element_type=jnp.float32
    ).reshape(-1, model_width)
    lse_list = row_max[..., 0] + jnp.log(row_total[..., 0])
    return (mixed_list, lse_list)


def attend_back(qkv_low, segment, head_count, lse_all, grad_mixed):
    tokens = qkv_low.shape[0]
    query_all, key_all, value_all = split_qkv(qkv_low, head_count)
    grad_out = grad_mixed.reshape(tokens, head_count, -1)
    block_rows = min(tokens, 512)
    scores = block_scores(query_all, key_all, segment, segment, head_count)
    prob_full = jnp.exp(scores - lse_all[:, 0:block_rows, None])
    grad_value = jnp.einsum(
        "hts,thc->shc", prob_full.astype(jnp.bfloat16), grad_out, preferred_element_type=jnp.float32
    )
    grad_prob = jnp.einsum("thc,shc->hts", grad_out, value_all, preferred_element_type=jnp.float32)
    inner = jnp.sum(prob_full * grad_prob, axis=-1, keepdims=True)
    grad_raw = (prob_full * (grad_prob - inner) * HEAD_DIM ** (-0.5)).astype(jnp.bfloat16)
    query_list = jnp.einsum("hts,shc->thc", grad_raw, key_all, preferred_element_type=jnp.float32)
    grad_key = jnp.einsum("hts,thc->shc", grad_raw, query_all, preferred_element_type=jnp.float32)
    return (
        jnp.stack([query_list, grad_key, grad_value], axis=1)
        .reshape(tokens, -1)
        .astype(jnp.bfloat16)
    )


def shards(
    token_ids,
    seq_lengths,
    valid_mask,
    deal_order,
    log_scale,
    embed_master,
    attn_in,
    attn_out,
    ffn_in,
    ffn_out,
    head_master,
    norm_master,
    embed_rows,
    head_rows,
    layer_rows,
    ffn_out_rows,
    layer_cols,
    embed_head_cols,
    norm_state,
    scale_state,
):
    tokens = token_ids.shape[0]
    model_width = embed_master.shape[1]
    seq_count = seq_lengths.shape[1]
    head_count = HEADS
    position = jnp.arange(tokens, dtype=jnp.int32)
    bounds = jnp.cumsum(seq_lengths[0])
    segment = jnp.sum((position[:, None] >= bounds[None, :]).astype(jnp.int32), axis=1)
    piece_rows = lax.all_gather(embed_master.astype(jnp.bfloat16), "dp", axis=0, tiled=True)
    local_idx = token_ids
    inside = (local_idx >= 0) & (local_idx < piece_rows.shape[0])
    picked = jnp.take(piece_rows, jnp.clip(local_idx, 0, piece_rows.shape[0] - 1), axis=0).astype(
        jnp.float32
    )
    stream = jnp.where(inside[:, None], picked, 0.0)
    w_qkv, w_attn, w_gate_up, w_down, w_head, norm_low = (
        lax.all_gather(attn_in.astype(jnp.bfloat16), "dp", axis=1, tiled=True),
        lax.all_gather(attn_out.astype(jnp.bfloat16), "dp", axis=1, tiled=True),
        lax.all_gather(ffn_in.astype(jnp.bfloat16), "dp", axis=1, tiled=True),
        lax.all_gather(ffn_out.astype(jnp.bfloat16), "dp", axis=1, tiled=True),
        lax.all_gather(head_master.astype(jnp.bfloat16), "dp", axis=0, tiled=True),
        lax.all_gather(norm_master.astype(jnp.bfloat16), "dp", axis=2, tiled=True),
    )
    norms = norm_low.astype(jnp.float32)
    kept_list = []
    for layer_idx in range(LAYERS):
        stream_low = stream.astype(jnp.bfloat16)
        qkv_low = jnp.dot(stream_low, w_qkv[layer_idx], preferred_element_type=jnp.float32).astype(
            jnp.bfloat16
        )
        mixed_heads, lse_all = attend(qkv_low, segment, head_count)
        mixed_low = mixed_heads.astype(jnp.bfloat16)
        resid_one = stream + jnp.dot(
            mixed_low, w_attn[layer_idx], preferred_element_type=jnp.float32
        )
        normed = layer_norm(resid_one, norms[2 * layer_idx, 0], norms[2 * layer_idx, 1])
        normed_low = normed.astype(jnp.bfloat16)
        joined = jnp.dot(normed_low, w_gate_up[layer_idx], preferred_element_type=jnp.float32)
        hidden_low = geglu(joined).astype(jnp.bfloat16)
        resid_two = normed + jnp.dot(
            hidden_low, w_down[layer_idx], preferred_element_type=jnp.float32
        )
        kept_list.append(
            (
                stream_low,
                qkv_low,
                lse_all,
                mixed_low,
                resid_one,
                normed_low,
                joined,
                hidden_low,
                resid_two,
            )
        )
        stream = layer_norm(resid_two, norms[2 * layer_idx + 1, 0], norms[2 * layer_idx + 1, 1])
    final = layer_norm(stream, norms[2 * LAYERS, 0], norms[2 * LAYERS, 1])
    member = (
        (segment[None, :] == jnp.arange(seq_count, dtype=jnp.int32)[:, None])
        & (valid_mask[None, :] > 0)
    ).astype(jnp.float32)
    counts = jnp.maximum(jnp.sum(member, axis=1), 1.0)
    pooled = jnp.matmul(member, final, precision=lax.Precision.HIGHEST) / counts[:, None]
    pooled_low = pooled.astype(jnp.bfloat16)
    head_out = jnp.dot(pooled_low, w_head, preferred_element_type=jnp.float32)
    unit_vecs, unit_back = jax.vjp(normalize, head_out)
    unit_every = lax.all_gather(unit_vecs, ("dp", "group"), axis=0, tiled=True)
    loss_value, loss_back = jax.vjp(
        lambda unit_all, scale_arg: contrast(unit_all, scale_arg, deal_order), unit_every, log_scale
    )
    grad_units, grad_scale = loss_back(jnp.ones_like(loss_value))
    own_rows = lax.dynamic_slice_in_dim(
        grad_units, lax.axis_index(("dp", "group")) * seq_count, seq_count, 0
    )
    grad_head_out = unit_back(own_rows)[0].astype(jnp.bfloat16)
    grad_head = jnp.dot(pooled_low.T, grad_head_out, preferred_element_type=jnp.float32)
    grad_pooled = jnp.dot(grad_head_out, w_head.T, preferred_element_type=jnp.float32)
    grad_final = jnp.matmul(
        member.T, grad_pooled / counts[:, None], precision=lax.Precision.HIGHEST
    )
    final_back = jax.vjp(layer_norm, stream, norms[2 * LAYERS, 0], norms[2 * LAYERS, 1])[1]
    grad_stream, gain_last, shift_last = final_back(grad_final)
    norm_grads = [None] * (2 * LAYERS + 1)
    norm_grads[2 * LAYERS] = jnp.stack([gain_last, shift_last])
    qkv_grads = [None] * LAYERS
    attn_grads = [None] * LAYERS
    gate_grads = [None] * LAYERS
    down_grads = [None] * LAYERS
    for layer_idx in reversed(range(LAYERS)):
        (
            stream_low,
            qkv_low,
            lse_all,
            mixed_low,
            resid_one,
            normed_low,
            joined,
            hidden_low,
            resid_two,
        ) = kept_list[layer_idx]
        norm_two_back = jax.vjp(
            layer_norm, resid_two, norms[2 * layer_idx + 1, 0], norms[2 * layer_idx + 1, 1]
        )[1]
        grad_two, gain_two, shift_two = norm_two_back(grad_stream)
        norm_grads[2 * layer_idx + 1] = jnp.stack([gain_two, shift_two])
        grad_branch = grad_two.astype(jnp.bfloat16)
        down_grads[layer_idx] = jnp.dot(
            hidden_low.T, grad_branch, preferred_element_type=jnp.float32
        )
        grad_hidden = jnp.dot(grad_branch, w_down[layer_idx].T, preferred_element_type=jnp.float32)
        grad_joined = jax.vjp(geglu, joined)[1](grad_hidden)[0].astype(jnp.bfloat16)
        gate_grads[layer_idx] = jnp.dot(
            normed_low.T, grad_joined, preferred_element_type=jnp.float32
        )
        grad_normed = grad_two + jnp.dot(
            grad_joined, w_gate_up[layer_idx].T, preferred_element_type=jnp.float32
        )
        norm_one_back = jax.vjp(
            layer_norm, resid_one, norms[2 * layer_idx, 0], norms[2 * layer_idx, 1]
        )[1]
        grad_one, gain_one, shift_one = norm_one_back(grad_normed)
        norm_grads[2 * layer_idx] = jnp.stack([gain_one, shift_one])
        grad_attended = grad_one.astype(jnp.bfloat16)
        attn_grads[layer_idx] = jnp.dot(
            mixed_low.T, grad_attended, preferred_element_type=jnp.float32
        )
        grad_mixed = jnp.dot(
            grad_attended, w_attn[layer_idx].T, preferred_element_type=jnp.float32
        ).astype(jnp.bfloat16)
        grad_qkv_low = attend_back(qkv_low, segment, head_count, lse_all, grad_mixed)
        qkv_grads[layer_idx] = jnp.dot(
            stream_low.T, grad_qkv_low, preferred_element_type=jnp.float32
        )
        grad_stream = grad_one + jnp.dot(
            grad_qkv_low, w_qkv[layer_idx].T, preferred_element_type=jnp.float32
        )
    row_count = embed_master.shape[0] * lax.axis_size("dp")
    local_idx = token_ids
    inside = (local_idx >= 0) & (local_idx < row_count)
    slot_idx = jnp.where(inside, local_idx, row_count)
    embed_grad = lax.psum_scatter(
        jnp.zeros((row_count, model_width), jnp.float32).at[slot_idx].add(grad_stream, mode="drop"),
        "dp",
        scatter_dimension=0,
        tiled=True,
    )
    grad_qkv = jnp.stack(qkv_grads)
    grad_attn = jnp.stack(attn_grads)
    grad_gate_up = jnp.stack(gate_grads)
    grad_down = jnp.stack(down_grads)
    grad_norm = jnp.stack(norm_grads)
    owned = (
        lax.psum_scatter(grad_qkv, "dp", scatter_dimension=1, tiled=True),
        lax.psum_scatter(grad_attn, "dp", scatter_dimension=1, tiled=True),
        lax.psum_scatter(grad_gate_up, "dp", scatter_dimension=1, tiled=True),
        lax.psum_scatter(grad_down, "dp", scatter_dimension=1, tiled=True),
        lax.psum_scatter(grad_head, "dp", scatter_dimension=0, tiled=True),
        lax.psum_scatter(grad_norm, "dp", scatter_dimension=2, tiled=True),
    )
    shard_qkv, shard_attn, shard_gate_up, shard_down, shard_head, shard_norm, shard_embed = (
        lax.psum((owned[0], owned[1], owned[2], owned[3], owned[4], owned[5], embed_grad), "group")
    )
    grad_list = [
        shard_embed[None],
        shard_head[None],
        shard_qkv,
        shard_attn,
        shard_gate_up,
        shard_down,
    ]
    master_list = [embed_master[None], head_master[None], attn_in, attn_out, ffn_in, ffn_out]
    state_list = [
        embed_rows[None],
        head_rows[None],
        layer_rows[:, 0],
        layer_rows[:, 1],
        layer_rows[:, 2],
        ffn_out_rows,
    ]
    col_list = [
        embed_head_cols[0:1],
        embed_head_cols[1:2],
        layer_cols[:, : 3 * D],
        layer_cols[:, 3 * D : 4 * D],
        layer_cols[:, 4 * D : 4 * D + 2 * FF],
        layer_cols[:, 4 * D + 2 * FF :],
    ]
    total_rows = [VOCAB, D, D, D, D, FF]
    wide_rate = RATE_SCALE / D**0.5
    rates = [
        RATE_SCALE,
        wide_rate,
        wide_rate,
        RATE_SCALE / (D // 8) ** 0.5,
        wide_rate,
        RATE_SCALE / FF**0.5,
    ]
    square_list = [grad_part * grad_part for grad_part in grad_list]
    rows_new = [
        DECAY_RATE * state_list[entry_idx]
        + (1.0 - DECAY_RATE) * (jnp.mean(square_list[entry_idx], axis=-1) + STATE_EPS)
        for entry_idx in range(6)
    ]
    col_parts = jnp.concatenate(
        [jnp.sum(square_part, axis=1).reshape(-1) for square_part in square_list]
    )
    row_parts = jnp.concatenate([jnp.sum(row_part, axis=-1) for row_part in rows_new])
    col_sum, row_sum = lax.psum((col_parts, row_parts), "dp")
    row_means = []
    lead_start = 0
    for entry_idx in range(6):
        lead_count = grad_list[entry_idx].shape[0]
        row_means.append(row_sum[lead_start : lead_start + lead_count] / total_rows[entry_idx])
        lead_start = lead_start + lead_count
    cols_new = []
    steps_all = []
    col_start = 0
    for entry_idx in range(6):
        lead_count = grad_list[entry_idx].shape[0]
        col_width = grad_list[entry_idx].shape[2]
        col_full = col_sum[col_start : col_start + lead_count * col_width].reshape(
            lead_count, col_width
        )
        col_state_new = DECAY_RATE * col_list[entry_idx] + (1.0 - DECAY_RATE) * (
            col_full / total_rows[entry_idx] + STATE_EPS
        )
        cols_new.append(col_state_new)
        steps_all.append(
            grad_list[entry_idx]
            * lax.rsqrt(
                rows_new[entry_idx][:, :, None]
                * col_state_new[:, None, :]
                / row_means[entry_idx][:, None, None]
            )
        )
        col_start = col_start + lead_count * col_width
    step_squares = []
    step_parts = jnp.concatenate(
        [jnp.sum(step_dir * step_dir, axis=(1, 2)) for step_dir in steps_all]
    )
    step_sum = lax.psum(step_parts, "dp")
    lead_start = 0
    for entry_idx in range(6):
        lead_count = grad_list[entry_idx].shape[0]
        step_squares.append(step_sum[lead_start : lead_start + lead_count])
        lead_start = lead_start + lead_count
    new_weights = []
    rms_list = []
    for entry_idx in range(6):
        cell_count = total_rows[entry_idx] * grad_list[entry_idx].shape[2]
        step_rms = jnp.sqrt(step_squares[entry_idx] / cell_count)
        rms_list.append(step_rms)
        delta = (
            -rates[entry_idx]
            * steps_all[entry_idx]
            / jnp.maximum(1.0, step_rms / CLIP_LEVEL)[:, None, None]
        )
        new_weights.append(master_list[entry_idx] + delta)
    norm_delta, norm_second = unfactored(shard_norm, norm_state)
    scale_delta, scale_state_new = unfactored(grad_scale, scale_state)
    return (
        loss_value,
        new_weights[0][0],
        new_weights[2],
        new_weights[3],
        new_weights[4],
        new_weights[5],
        new_weights[1][0],
        norm_master + norm_delta,
        log_scale + scale_delta,
        rows_new[0][0],
        rows_new[1][0],
        jnp.stack([rows_new[2], rows_new[3], rows_new[4]], axis=1),
        rows_new[5],
        jnp.concatenate([cols_new[2], cols_new[3], cols_new[4], cols_new[5]], axis=1),
        cols_new[0][0],
        cols_new[1][0],
        norm_second,
        scale_state_new,
        jnp.concatenate(rms_list),
    )


MESH = pl.DeviceIdType.MESH
BF=jnp.bfloat16

def place():
    dp = lax.axis_index("dp"); g = lax.axis_index("group")
    return dp // 2, dp % 2, g // 2, g % 2

def dev(z, x, y, c):
    return (z * 2 + x, y * 2 + c)

def entry_barrier(peers):
    bar = pltpu.get_barrier_semaphore()
    for p in peers:
        pl.semaphore_signal(bar, inc=1, device_id=p, device_id_type=MESH)
    pl.semaphore_wait(bar, len(peers))

def mult(v, m=16):
    return pl.multiple_of(v, m)

def gather_kernel(chunks, w_ref, rows_ref, ag_ref, got_ref, zs, zr, xs, xr, ys, yr, cs, cr, ls, es, er):
    z, x, y, c = place()
    me = z * 2 + x
    ep = [(lax.rem(me + k, 8), y * 2 + c) for k in range(8)]
    zp = [dev((z + k) % 4, x, y, c) for k in range(4)]
    xp, yp, cp = dev(z, 1 - x, y, c), dev(z, x, 1 - y, c), dev(z, x, y, 1 - c)
    entry_barrier(ep[1:] + [yp, cp])
    Q = len(chunks)
    hs = [mult(b + c * h + y * nb) for b, h, nb in chunks]
    nh = [h - nb for b, h, nb in chunks]
    bs = [mult(b + c * h + y * (h - nb)) for b, h, nb in chunks]
    nbs = [nb for b, h, nb in chunks]
    cb = [mult(b + c * h) for b, h, nb in chunks]
    nc = [h for b, h, nb in chunks]
    def rc(src, dst, s, r, d):
        return pltpu.make_async_remote_copy(src, dst, s, r, device_id=d, device_id_type=MESH)
    def shard(k, f):
        return ((z + 4 - k) % 4) * 2 + (x if f == 0 else 1 - x)
    own = pltpu.make_async_copy(w_ref, ag_ref.at[me], ls.at[0])
    own.start()
    kept = pltpu.make_async_copy(rows_ref.at[me], got_ref.at[me], ls.at[1])
    kept.start()
    ec = [rc(rows_ref.at[ep[k][0]], got_ref.at[me], es.at[k], er.at[k], ep[k]) for k in range(1, 8)]
    for copy in ec:
        copy.start()
    zc = {}; xc = {}; yc = {}; cc = {}
    for q in range(Q):
        for k in range(1, 4):
            zc[q, k] = rc(w_ref.at[pl.ds(hs[q], nh[q])], ag_ref.at[me, pl.ds(hs[q], nh[q])], zs.at[q, k], zr.at[q, k], zp[k])
        for k in range(4):
            src = w_ref.at[pl.ds(hs[q], nh[q])] if k == 0 else ag_ref.at[shard(k, 0), pl.ds(hs[q], nh[q])]
            xc[q, k] = rc(src, ag_ref.at[shard(k, 0), pl.ds(hs[q], nh[q])], xs.at[q, k], xr.at[q, k], xp)
        for k in range(4):
            for f in range(2):
                if k == 0 and f == 0: continue
                s = shard(k, f)
                yc[q, k, f] = rc(ag_ref.at[s, pl.ds(bs[q], nbs[q])], ag_ref.at[s, pl.ds(bs[q], nbs[q])], ys.at[q, 2 * k + f], yr.at[q, 2 * k + f], yp)
                cc[q, k, f] = rc(ag_ref.at[s, pl.ds(cb[q], nc[q])], ag_ref.at[s, pl.ds(cb[q], nc[q])], cs.at[q, 2 * k + f], cr.at[q, 2 * k + f], cp)
    def s0(q):
        for k in (2, 1, 3):
            zc[q, k].start()
        xc[q, 0].start()
    def s1(q):
        for k in (1, 3, 2):
            zc[q, k].wait_recv()
            xc[q, k].start()
            yc[q, k, 0].start()
    def s2(q):
        for k in (0, 1, 3, 2):
            xc[q, k].wait_recv()
            yc[q, k, 1].start()
    def s3(q):
        for k, f in ((1, 0), (3, 0), (2, 0), (0, 1), (1, 1), (3, 1), (2, 1)):
            yc[q, k, f].wait_recv()
            cc[q, k, f].start()
    st = [s0, s1, s2, s3]
    for t in range(Q + 3):
        for i in reversed(range(4)):
            q = t - i
            if 0 <= q < Q:
                st[i](q)
    for q in range(Q):
        for k in range(4):
            for f in range(2):
                if k or f: cc[q, k, f].wait_recv()
    for d in (zc, xc, cc) + (yc,):
        for v in d.values(): v.wait_send()
    for copy in ec:
        copy.wait()
    own.wait()
    kept.wait()

def gather_weights(w, rows, chunks, cid=1):
    Q = len(chunks)
    D = pltpu.SemaphoreType.DMA
    return pl.pallas_call(
        functools.partial(gather_kernel, chunks),
        out_shape=(jax.ShapeDtypeStruct((8,) + w.shape, w.dtype), jax.ShapeDtypeStruct(rows.shape, rows.dtype)),
        in_specs=[pl.BlockSpec(memory_space=pl.ANY)] * 2, out_specs=[pl.BlockSpec(memory_space=pl.ANY)] * 2,
        scratch_shapes=[D((Q, 4)), D((Q, 4)), D((Q, 4)), D((Q, 4)), D((Q, 8)), D((Q, 8)), D((Q, 8)), D((Q, 8)), D((2,)), D((8,)), D((8,))],
        compiler_params=pltpu.CompilerParams(collective_id=cid, has_side_effects=True),
    )(w, rows)

def spread_kernel(v_ref, o_ref, ss, rs, ls):
    lin = lax.axis_index("dp") * 4 + lax.axis_index("group")
    peers = [lax.rem(lin + k, 32) for k in range(32)]
    peers = [(p // 4, p % 4) for p in peers]
    entry_barrier(peers[1:])
    copies = [pltpu.make_async_remote_copy(v_ref, o_ref.at[lin], ss.at[k], rs.at[k], device_id=peers[k], device_id_type=MESH) for k in range(1, 32)]
    for copy in copies:
        copy.start()
    own = pltpu.make_async_copy(v_ref, o_ref.at[lin], ls)
    own.start()
    for copy in copies:
        copy.wait()
    own.wait()

def spread(v, cid):
    D = pltpu.SemaphoreType.DMA
    return pl.pallas_call(
        spread_kernel,
        out_shape=jax.ShapeDtypeStruct((32,) + v.shape, v.dtype),
        in_specs=[pl.BlockSpec(memory_space=pltpu.VMEM)], out_specs=pl.BlockSpec(memory_space=pltpu.VMEM),
        scratch_shapes=[D((32,)), D((32,)), D],
        compiler_params=pltpu.CompilerParams(collective_id=cid, has_side_effects=True),
    )(v)

def scatter_kernel(chunks, g_ref, e_ref, out_ref, t_ref, acc, b1, b2, b3, b4, b5, fin,
                   cs, cr, ys, yr, xs, xr, zs, zr, as_, ar, fs, fr, ls, os_, es, er, el):
    z, x, y, c = place()
    me = z * 2 + x
    g = y * 2 + c
    ep = [(lax.rem(me + k, 8), g) for k in range(8)]
    zp = [dev((z + k) % 4, x, y, c) for k in range(4)]
    xp, yp, cp = dev(z, 1 - x, y, c), dev(z, x, 1 - y, c), dev(z, x, y, 1 - c)
    entry_barrier(ep[1:] + [yp, cp])
    Q = len(chunks)
    lo = []; o = 0; lb = []; ob = 0; lh = []; oh = 0; la = []; oa = 0
    for b, h, nb in chunks:
        lo.append(o); o += h
        lb.append(ob); ob += nb
        lh.append(oh); oh += h - nb
        la.append(oa); oa += h - 2 * nb
    nh = [h - nb for b, h, nb in chunks]
    nbs = [nb for b, h, nb in chunks]
    na = [h - 2 * nb for b, h, nb in chunks]
    hs = [mult(lo[q] + y * nbs[q]) for q in range(Q)]
    mb = [mult(lo[q] + y * nh[q]) for q in range(Q)]
    ob_ = [mult(lo[q] + (1 - y) * nh[q]) for q in range(Q)]
    aa = [lo[q] + nbs[q] for q in range(Q)]
    def rc(src, dst, s, r, d):
        return pltpu.make_async_remote_copy(src, dst, s, r, device_id=d, device_id_type=MESH)
    def add(dst, src, n, blk=16):
        def body(i, _):
            a = mult(i * blk)
            d = dst(a, blk); s = src(a, blk)
            d[...] = (d[...].astype(jnp.float32) + s[...].astype(jnp.float32)).astype(BF)
            return _
        lax.fori_loop(0, n // blk, body, 0)
    order = []
    for k in (2, 1, 3, 0):
        for f in (1, 0):
            order.append((k, f))
    def owner(k, f):
        return ((z + k) % 4) * 2 + (x if f == 0 else 1 - x)
    C1 = {}; Y = {}; X = {}; Z = {}; A = {}; F = {}; L = {}; O = {}; BX = {}
    for q, (b, h, nb) in enumerate(chunks):
        for i, (k, f) in enumerate(order):
            s = owner(k, f)
            L[q, i] = pltpu.make_async_copy(g_ref.at[s, pl.ds(mult(b + c * h), h)], acc.at[s, pl.ds(lo[q], h)], ls.at[q, i])
            C1[q, i] = rc(g_ref.at[s, pl.ds(mult(b + (1 - c) * h), h)], b1.at[s, pl.ds(lo[q], h)], cs.at[q, i], cr.at[q, i], cp)
            Y[q, i] = rc(acc.at[s, pl.ds(ob_[q], nb)], b2.at[s, pl.ds(lb[q], nb)], ys.at[q, i], yr.at[q, i], yp)
        for k in range(4):
            X[q, k] = rc(acc.at[owner(k, 1), pl.ds(hs[q], nh[q])], b3.at[k, pl.ds(lh[q], nh[q])], xs.at[q, k], xr.at[q, k], xp)
            if k:
                Z[q, k] = rc(acc.at[owner(k, 0), pl.ds(hs[q], nh[q])], b4.at[k - 1, pl.ds(lh[q], nh[q])], zs.at[q, k], zr.at[q, k], zp[k])
        A[q] = rc(fin.at[pl.ds(aa[q], na[q])], b5.at[pl.ds(la[q], na[q])], as_.at[q, 0], ar.at[q, 0], yp)
        BX[q] = rc(fin.at[pl.ds(mb[q], nb)], fin.at[pl.ds(mb[q], nb)], as_.at[q, 1], ar.at[q, 1], yp)
        F[q] = rc(fin.at[pl.ds(lo[q], h)], out_ref.at[pl.ds(mult(b + c * h), h)], fs.at[q], fr.at[q], cp)
        O[q] = pltpu.make_async_copy(fin.at[pl.ds(lo[q], h)], out_ref.at[pl.ds(mult(b + c * h), h)], os_.at[q])
    g2 = (1 - y) * 2 + c
    kept = pltpu.make_async_copy(e_ref.at[me], t_ref.at[g, me], el)
    E = [rc(e_ref.at[ep[k][0]], t_ref.at[g, me], es.at[k], er.at[k], ep[k]) for k in range(1, 8)]
    EY = rc(t_ref.at[g], t_ref.at[g], es.at[8], er.at[8], yp)
    EC = rc(t_ref.at[g], t_ref.at[g], es.at[9], er.at[9], cp)
    ED = rc(t_ref.at[g2], t_ref.at[g2], es.at[10], er.at[10], cp)
    def e0():
        kept.start()
        for v in E: v.start()
    def e1():
        kept.wait()
        for v in E: v.wait_recv()
        EY.start(); EC.start()
    def e2():
        EY.wait_recv()
        ED.start()
    def e3():
        EC.wait_recv(); ED.wait_recv()
        for v in E + [EY, EC, ED]: v.wait_send()
    ev = {0: e0, 3: e1, 5: e2}
    def s0(q):
        for i in range(8):
            L[q, i].start(); C1[q, i].start()
    def s1(q):
        h = chunks[q][1]
        for i, (k, f) in enumerate(order):
            s = owner(k, f)
            L[q, i].wait(); C1[q, i].wait_recv()
            add(lambda a, n: acc.at[s, pl.ds(lo[q] + a, n)], lambda a, n: b1.at[s, pl.ds(lo[q] + a, n)], h)
            Y[q, i].start()
    def s2(q):
        for i, (k, f) in enumerate(order):
            s = owner(k, f)
            if nbs[q]:
                Y[q, i].wait_recv()
                add(lambda a, n: acc.at[s, pl.ds(mb[q] + a, n)], lambda a, n: b2.at[s, pl.ds(lb[q] + a, n)], nbs[q])
            if f == 1:
                X[q, k].start()
    def s3(q):
        for k in (2, 1, 3, 0):
            s = owner(k, 0)
            X[q, k].wait_recv()
            add(lambda a, n: acc.at[s, pl.ds(hs[q] + a, n)], lambda a, n: b3.at[k, pl.ds(lh[q] + a, n)], nh[q])
            if k: Z[q, k].start()
    def s4(q):
        for k in range(1, 4):
            Z[q, k].wait_recv()
        def body(i, _):
            a = mult(i * 16)
            t = acc[me, pl.ds(hs[q] + a, 16)].astype(jnp.float32)
            for k in range(3):
                t += b4[k, pl.ds(lh[q] + a, 16)].astype(jnp.float32)
            fin[pl.ds(hs[q] + a, 16)] = t.astype(BF)
            return _
        lax.fori_loop(0, nh[q] // 16, body, 0)
        A[q].start()
        BX[q].start()
    def s5(q):
        A[q].wait_recv()
        A[q].wait_send()
        add(lambda a, n: fin.at[pl.ds(aa[q] + a, n)], lambda a, n: b5.at[pl.ds(la[q] + a, n)], na[q])
        BX[q].wait_recv()
        F[q].start(); O[q].start()
    st = [s0, s1, s2, s3, s4, s5]
    for t in range(Q + 5):
        if t in ev: ev[t]()
        for i in reversed(range(6)):
            q = t - i
            if 0 <= q < Q:
                st[i](q)
    for q in range(Q):
        F[q].wait(); O[q].wait()
        BX[q].wait_send()
    for d in (C1, Y, X, Z):
        for v in d.values(): v.wait_send()
    e3()

def scatter_grads(g, e, chunks, cid=2):
    Q = len(chunks)
    D = pltpu.SemaphoreType.DMA
    H = sum(h for _, h, _ in chunks); NB = sum(nb for _, _, nb in chunks); NH = H - NB
    V = lambda *s: pltpu.VMEM(s, BF)
    return pl.pallas_call(
        functools.partial(scatter_kernel, chunks),
        out_shape=(jax.ShapeDtypeStruct(g.shape[1:], g.dtype), jax.ShapeDtypeStruct((4,) + e.shape, e.dtype)),
        in_specs=[pl.BlockSpec(memory_space=pl.ANY)] * 2, out_specs=[pl.BlockSpec(memory_space=pl.ANY)] * 2,
        scratch_shapes=[V(8, H, 512), V(8, H, 512), V(8, NB, 512), V(4, NH, 512), V(3, NH, 512), V(H - 2 * NB, 512), V(H, 512),
            D((Q, 8)), D((Q, 8)), D((Q, 8)), D((Q, 8)), D((Q, 4)), D((Q, 4)), D((Q, 4)), D((Q, 4)), D((Q, 2)), D((Q, 2)), D((Q,)), D((Q,)), D((Q, 8)), D((Q,)),
            D((11,)), D((11,)), D],
        compiler_params=pltpu.CompilerParams(collective_id=cid, has_side_effects=True, vmem_limit_bytes=60 * 2**20),
    )(g, e)

def plan(rows, count, share):
    units = rows // 32
    chunks = []
    base = 0
    for i in range(count):
        size = units // count + (1 if i < units % count else 0)
        chunks.append((base, 16 * size, 16 * int(round(size * share))))
        base += 32 * size
    return chunks


SLOTS = 96
PART = 1024
HEAD_AT = 2 * PART
NORM_AT = HEAD_AT + 64
PACKED = NORM_AT + 32


def slot_plan(token_ids, shard_rows):
    tokens = token_ids.shape[0]
    owner = token_ids // shard_rows
    local = token_ids - owner * shard_rows
    index = jnp.arange(tokens, dtype=jnp.int32)
    same_id = token_ids[:, None] == token_ids[None, :]
    first = jnp.min(jnp.where(same_id, index[None, :], tokens), axis=1)
    leads = first == index
    same_owner = owner[:, None] == owner[None, :]
    slot = jnp.sum(
        (same_owner & leads[None, :] & (index[None, :] < first[:, None])).astype(jnp.int32), axis=1
    )
    key = jnp.where(slot < SLOTS, owner * SLOTS + slot, 8 * SLOTS)
    wanted = jnp.max(
        jnp.where(
            key[:, None] == jnp.arange(8 * SLOTS, dtype=jnp.int32)[None, :], local[:, None], -1
        ),
        axis=0,
    )
    return key, wanted, jnp.max(slot)


def column_blocks(rows):
    lead, count, width = rows.shape
    return (
        rows.reshape(lead, count, width // D, D).transpose(0, 2, 1, 3).reshape(lead, -1, D)
    )


def pack_weights(attn_in, attn_out, ffn_in, ffn_out, head_master, norm_master):
    layers = jnp.concatenate(
        [column_blocks(attn_in), attn_out, column_blocks(ffn_in), ffn_out], axis=1
    ).astype(jnp.bfloat16)
    norm_rows = jnp.pad(
        norm_master.reshape(10, -1).astype(jnp.bfloat16), ((0, 22), (0, D - norm_master.shape[2]))
    )
    return jnp.concatenate(
        [layers.reshape(-1, D), head_master.astype(jnp.bfloat16), norm_rows], axis=0
    )


def whole_columns(part, blocks):
    return (
        part.reshape(8, blocks, -1, D).transpose(0, 2, 1, 3).reshape(-1, blocks * D)
    )


def shard_columns(part, blocks):
    return part.reshape(blocks, -1, D).transpose(1, 0, 2).reshape(-1, blocks * D)


def owned_columns(grad):
    rows, width = grad.shape
    return (
        grad.reshape(8, rows // 8, width // D, D).transpose(0, 2, 1, 3).reshape(8, -1, D)
    )


def place_kernel(slot_ref, rows_ref, out_ref):
    start = pl.program_id(0) * out_ref.shape[0]
    rows = lax.broadcasted_iota(jnp.int32, (out_ref.shape[0], slot_ref.shape[1]), 0) + start
    picks = jnp.where(rows == slot_ref[...], 1.0, 0.0).astype(jnp.bfloat16)
    out_ref[...] = jnp.dot(picks, rows_ref[...], preferred_element_type=jnp.float32)


def place_rows(slots, rows, row_count):
    tile = row_count // 9
    return pl.pallas_call(
        place_kernel,
        grid=(9,),
        in_specs=[
            pl.BlockSpec((1, slots.shape[1]), lambda i: (0, 0)),
            pl.BlockSpec(rows.shape, lambda i: (0, 0)),
        ],
        out_specs=pl.BlockSpec((tile, D), lambda i: (i, 0)),
        out_shape=jax.ShapeDtypeStruct((row_count, D), jnp.float32),
        compiler_params=pltpu.CompilerParams(vmem_limit_bytes=48 * 2**20),
    )(slots, rows)


def dot_nn(left, right):
    return lax.dot_general(left, right, (((1,), (0,)), ((), ())), preferred_element_type=jnp.float32)


def dot_nt(left, right):
    return lax.dot_general(left, right, (((1,), (1,)), ((), ())), preferred_element_type=jnp.float32)


def dot_tn(left, right):
    return lax.dot_general(left, right, (((0,), (0,)), ((), ())), preferred_element_type=jnp.float32)


def exact_dot(left, right, dims=((1,), (0,))):
    return lax.dot_general(
        left, right, (dims, ((), ())), precision=lax.Precision.HIGHEST, preferred_element_type=jnp.float32
    )


GELU_SCALE = (2.0 / 3.141592653589793) ** 0.5
GELU_CUBE = 0.044715
TILE = 256


def norm_parts(values):
    center = values - jnp.mean(values, axis=-1, keepdims=True)
    inverse = lax.rsqrt(jnp.mean(center * center, axis=-1, keepdims=True) + NORM_EPS)
    return center * inverse, inverse


def norm_back(scaled, inverse, grad_out, gain):
    grad_scaled = grad_out * gain
    mean_grad = jnp.mean(grad_scaled, axis=-1, keepdims=True)
    mean_both = jnp.mean(grad_scaled * scaled, axis=-1, keepdims=True)
    return inverse * (grad_scaled - mean_grad - scaled * mean_both)


def gelu_parts(value):
    bend = jnp.tanh(GELU_SCALE * (value + GELU_CUBE * value * value * value))
    half = 0.5 * (1.0 + bend)
    slope = half + 0.5 * value * (1.0 - bend * bend) * GELU_SCALE * (1.0 + 3.0 * GELU_CUBE * value * value)
    return value * half, slope


def block(w_ref, start):
    return w_ref[:, start : start + 64, :].reshape(D, D)


def down_block(w_ref, j):
    return w_ref[2 * j : 2 * j + 2, 768:1024, :].reshape(D, D)


def fill_distance(far, seg_col_ref, seg_row_ref):
    tokens = far.shape[0]
    def body(i, carry):
        start = pl.multiple_of(i * 64, 64)
        rows = lax.broadcasted_iota(jnp.int32, (64, tokens), 0) + start
        cols = lax.broadcasted_iota(jnp.int32, (64, tokens), 1)
        gap = jnp.abs(rows - cols).astype(jnp.float32)
        same = seg_col_ref[pl.ds(start, 64), :] == seg_row_ref[...]
        far[pl.ds(start, 64), :] = jnp.where(same, gap, jnp.inf)
        return carry
    lax.fori_loop(0, tokens // 64, body, 0)


def forward_kernel(
    first_ref, seg_col_ref, seg_row_ref, valid_ref, w_ref, head_ref, norm_ref,
    low_ref, qkv_ref, lse_ref, mix_ref, one_ref, two_ref, unit_ref, pool_ref, zed_ref,
    x_s, far, acc,
):
    layer = pl.program_id(0)
    tokens = x_s.shape[0]
    tiles = tokens // TILE

    @pl.when(layer == 0)
    def _():
        x_s[...] = first_ref[...].astype(jnp.float32)
        fill_distance(far, seg_col_ref, seg_row_ref)

    def project(i, carry):
        rows = pl.ds(pl.multiple_of(i * TILE, TILE), TILE)
        low = x_s[rows, :].astype(jnp.bfloat16)
        low_ref[0, rows, :] = low
        for j in range(3):
            qkv_ref[0, rows, j * D : (j + 1) * D] = dot_nn(low, block(w_ref, j * 64)).astype(jnp.bfloat16)
        return carry

    lax.fori_loop(0, tiles, project, 0)
    for head in range(HEADS):
        lanes = slice(head * HEAD_DIM, (head + 1) * HEAD_DIM)
        keys = qkv_ref[0, :, D + head * HEAD_DIM : D + (head + 1) * HEAD_DIM]
        vals_t = qkv_ref[0, :, 2 * D + head * HEAD_DIM : 2 * D + (head + 1) * HEAD_DIM].T
        slope = 2.0 ** (-8.0 * (head + 1) / HEADS)
        for i in range(tiles):
            cols = slice(i * TILE, (i + 1) * TILE)
            scores = dot_nt(keys, qkv_ref[0, cols, lanes]) * HEAD_DIM**-0.5 - slope * far[:, cols]
            top = jnp.max(scores, axis=0, keepdims=True)
            raised = jnp.exp(scores - top)
            total = jnp.sum(raised, axis=0, keepdims=True)
            lse_ref[0, head, :, cols] = top + jnp.log(total)
            prob = (raised * (1.0 / total)).astype(jnp.bfloat16)
            mix_ref[0, lanes, cols] = dot_nn(vals_t, prob).astype(jnp.bfloat16)

    acc[...] = dot_tn(mix_ref[0], block(w_ref, 192))

    def feed(i, carry):
        rows = pl.ds(pl.multiple_of(i * TILE, TILE), TILE)
        resid = x_s[rows, :] + acc[rows, :]
        one_ref[0, rows, :] = resid
        at = 4 * layer
        scaled, _ = norm_parts(resid)
        hidden = scaled * norm_ref[pl.ds(at, 1), :] + norm_ref[pl.ds(at + 1, 1), :]
        low = hidden.astype(jnp.bfloat16)
        total = hidden
        for j in range(4):
            gate = dot_nn(low, block(w_ref, 256 + j * 64))
            up = dot_nn(low, block(w_ref, 512 + j * 64))
            bend = jnp.tanh(GELU_SCALE * (gate + GELU_CUBE * gate * gate * gate))
            mid = (0.5 * gate * (1.0 + bend) * up).astype(jnp.bfloat16)
            total = total + dot_nn(mid, down_block(w_ref, j))
        two_ref[0, rows, :] = total
        scaled, _ = norm_parts(total)
        x_s[rows, :] = scaled * norm_ref[pl.ds(at + 2, 1), :] + norm_ref[pl.ds(at + 3, 1), :]
        return carry

    lax.fori_loop(0, tiles, feed, 0)

    @pl.when(layer == LAYERS - 1)
    def _():
        scaled, _ = norm_parts(x_s[...])
        final = scaled * norm_ref[8:9, :] + norm_ref[9:10, :]
        member = members(seg_row_ref, valid_ref)
        counts = jnp.maximum(jnp.sum(member, axis=1, keepdims=True), 1.0)
        pooled = (exact_dot(member, final) / counts).astype(jnp.bfloat16)
        pool_ref[...] = pooled
        zed = dot_nn(pooled, head_ref[...].reshape(D, D))
        zed_ref[...] = zed
        unit = zed * lax.rsqrt(jnp.sum(zed * zed, axis=-1, keepdims=True) + UNIT_EPS)
        for s in range(4):
            for part in range(4):
                unit_ref[4 * s + part : 4 * s + part + 1, :] = unit[s : s + 1, part * 128 : (part + 1) * 128]


def members(seg_row_ref, valid_ref):
    tokens = seg_row_ref.shape[1]
    slot = lax.broadcasted_iota(jnp.int32, (8, tokens), 0)
    return jnp.where((seg_row_ref[...] == slot) & (valid_ref[...] > 0), 1.0, 0.0)


def whole(shape):
    return pl.BlockSpec(shape, lambda i: (0,) * len(shape))


def run_forward(first, seg_col, seg_row, valid, weights, norms):
    tokens = first.shape[0]
    low = jnp.bfloat16
    layered = lambda *s: pl.BlockSpec((1,) + s, lambda i: (i,) + (0,) * len(s))
    return pl.pallas_call(
        forward_kernel,
        grid=(LAYERS,),
        in_specs=[
            whole((tokens, D)), whole((tokens, 1)), whole((1, tokens)), whole((1, tokens)),
            pl.BlockSpec((8, PART, D), lambda i: (0, i, 0)),
            pl.BlockSpec((8, 64, D), lambda i: (0, HEAD_AT // 64, 0)),
            whole(norms.shape),
        ],
        out_specs=[
            layered(tokens, D), layered(tokens, 3 * D), layered(HEADS, 1, tokens), layered(D, tokens),
            layered(tokens, D), layered(tokens, D), whole((16, 128)), whole((8, D)), whole((8, D)),
        ],
        out_shape=[
            jax.ShapeDtypeStruct((LAYERS, tokens, D), low),
            jax.ShapeDtypeStruct((LAYERS, tokens, 3 * D), low),
            jax.ShapeDtypeStruct((LAYERS, HEADS, 1, tokens), jnp.float32),
            jax.ShapeDtypeStruct((LAYERS, D, tokens), low),
            jax.ShapeDtypeStruct((LAYERS, tokens, D), jnp.float32),
            jax.ShapeDtypeStruct((LAYERS, tokens, D), jnp.float32),
            jax.ShapeDtypeStruct((16, 128), jnp.float32),
            jax.ShapeDtypeStruct((8, D), low),
            jax.ShapeDtypeStruct((8, D), jnp.float32),
        ],
        scratch_shapes=[
            pltpu.VMEM((tokens, D), jnp.float32), pltpu.VMEM((tokens, tokens), jnp.float32),
            pltpu.VMEM((tokens, D), jnp.float32),
        ],
        compiler_params=pltpu.CompilerParams(vmem_limit_bytes=60 * 2**20),
    )(first, seg_col, seg_row, valid, weights, weights, norms)


def contrast_kernel(unit_ref, deal_col_ref, deal_row_ref, scale_ref, loss_ref, own_ref, slope_ref, every, ss, rs, ls):
    lin = lax.axis_index("dp") * 4 + lax.axis_index("group")
    peers = [lax.rem(lin + k, 32) for k in range(32)]
    peers = [(p // 4, p % 4) for p in peers]
    entry_barrier(peers[1:])
    copies = [
        pltpu.make_async_remote_copy(
            unit_ref, every.at[lin], ss.at[k], rs.at[k], device_id=peers[k], device_id_type=MESH
        )
        for k in range(1, 32)
    ]
    for copy in copies:
        copy.start()
    own = pltpu.make_async_copy(unit_ref, every.at[lin], ls)
    own.start()
    for copy in copies:
        copy.wait()
    own.wait()
    units = every[...].reshape(512, 128)
    place_at = lax.broadcasted_iota(jnp.int32, (128, 512), 1)
    sorted_units = jnp.concatenate(
        [
            exact_dot(jnp.where(deal_col_ref[...] * 4 + part == place_at, 1.0, 0.0), units)
            for part in range(4)
        ],
        axis=1,
    )
    queries, documents = sorted_units[:64], sorted_units[64:]
    scale = jnp.exp(scale_ref[...])
    logits = scale * exact_dot(queries, documents, ((1,), (1,)))
    row_top = jnp.max(logits, axis=1, keepdims=True)
    row_lse = row_top + jnp.log(jnp.sum(jnp.exp(logits - row_top), axis=1, keepdims=True))
    col_top = jnp.max(logits, axis=0, keepdims=True)
    col_lse = col_top + jnp.log(jnp.sum(jnp.exp(logits - col_top), axis=0, keepdims=True))
    diagonal = jnp.where(
        lax.broadcasted_iota(jnp.int32, (64, 64), 0) == lax.broadcasted_iota(jnp.int32, (64, 64), 1), 1.0, 0.0
    )
    on_diagonal = jnp.sum(logits * diagonal, axis=1, keepdims=True)
    col_sum = jnp.sum(col_lse, axis=1, keepdims=True)
    row_sum = jnp.sum(row_lse, axis=0, keepdims=True)
    loss_ref[...] = 0.5 * (row_sum + col_sum) - jnp.sum(on_diagonal, axis=0, keepdims=True)
    grad_logits = 0.5 * (jnp.exp(logits - row_lse) + jnp.exp(logits - col_lse)) - diagonal
    slope = jnp.sum(grad_logits * logits, axis=1, keepdims=True)
    slope_ref[...] = jnp.sum(slope, axis=0, keepdims=True)
    grad_raw = scale * grad_logits
    grad_queries = exact_dot(grad_raw, documents)
    grad_documents = exact_dot(grad_raw, queries, ((0,), (0,)))
    mine = lax.broadcasted_iota(jnp.int32, (8, 128), 0)
    picks = jnp.where((deal_row_ref[...] == mine + lin * 4) & (mine < 4), 1.0, 0.0)
    own_ref[...] = exact_dot(picks, jnp.concatenate([grad_queries, grad_documents], axis=0))


def run_contrast(unit, deal_order, log_scale, cid):
    sems = pltpu.SemaphoreType.DMA
    one = jax.ShapeDtypeStruct((1, 1), jnp.float32)
    return pl.pallas_call(
        contrast_kernel,
        out_shape=[one, jax.ShapeDtypeStruct((8, D), jnp.float32), one],
        in_specs=[pl.BlockSpec(memory_space=pltpu.VMEM)] * 4,
        out_specs=[pl.BlockSpec(memory_space=pltpu.VMEM)] * 3,
        scratch_shapes=[pltpu.VMEM((32, 16, 128), jnp.float32), sems((32,)), sems((32,)), sems],
        compiler_params=pltpu.CompilerParams(collective_id=cid, has_side_effects=True),
    )(unit, deal_order.reshape(128, 1), deal_order.reshape(1, 128), log_scale.reshape(1, 1))


def backward_kernel(
    own_ref, zed_ref, pool_ref, seg_col_ref, seg_row_ref, valid_ref, w_ref, head_ref, norm_ref,
    low_ref, qkv_ref, lse_ref, mix_ref, one_ref, two_ref, last_ref,
    grad_ref, norm_out_ref, first_ref,
    dx, far, acc, two_s, low_s, mid_s, ups, gates, back,
):
    step = pl.program_id(0)
    tokens = dx.shape[0]
    tiles = tokens // TILE
    low_type = jnp.bfloat16

    @pl.when(step == 0)
    def _():
        fill_distance(far, seg_col_ref, seg_row_ref)
        zed = zed_ref[...]
        square = jnp.sum(zed * zed, axis=-1, keepdims=True) + UNIT_EPS
        inverse = lax.rsqrt(square)
        own = own_ref[...]
        inner = jnp.sum(own * zed, axis=-1, keepdims=True)
        grad_zed = (inverse * (own - zed * (inner / square))).astype(low_type)
        head = head_ref[...].reshape(D, D)
        grad_head = dot_tn(pool_ref[...], grad_zed)
        grad_ref[:, 0:64, :] = grad_head.reshape(8, 64, D).astype(low_type)
        grad_ref[:, 64:96, :] = jnp.zeros((8, 32, D), low_type)
        member = members(seg_row_ref, valid_ref)
        counts = jnp.maximum(jnp.sum(member, axis=1, keepdims=True), 1.0)
        grad_pooled = dot_nt(grad_zed, head) / counts
        grad_final = exact_dot(member, grad_pooled, ((0,), (0,)))
        gain_last = norm_ref[6:7, :]
        stream_scaled, _ = norm_parts(last_ref[0])
        stream = stream_scaled * gain_last + norm_ref[7:8, :]
        scaled, inverse = norm_parts(stream)
        norm_out_ref[0, 0:1, :] = jnp.sum(grad_final * scaled, axis=0, keepdims=True)
        norm_out_ref[0, 1:2, :] = jnp.sum(grad_final, axis=0, keepdims=True)
        dx[...] = norm_back(scaled, inverse, grad_final, norm_ref[8:9, :])

    @pl.when(step > 0)
    def _():
        at = 4 * (LAYERS - step)
        norm_out_ref[0] = jnp.zeros((8, D), jnp.float32)

        def enter(i, carry):
            rows = pl.ds(pl.multiple_of(i * TILE, TILE), TILE)
            scaled, inverse = norm_parts(two_ref[0, rows, :])
            grad = dx[rows, :]
            norm_out_ref[0, 2:3, :] += jnp.sum(grad * scaled, axis=0, keepdims=True)
            norm_out_ref[0, 3:4, :] += jnp.sum(grad, axis=0, keepdims=True)
            grad = norm_back(scaled, inverse, grad, norm_ref[pl.ds(at + 2, 1), :])
            acc[rows, :] = grad
            two_s[rows, :] = grad.astype(low_type)
            scaled, _ = norm_parts(one_ref[0, rows, :])
            hidden = scaled * norm_ref[pl.ds(at, 1), :] + norm_ref[pl.ds(at + 1, 1), :]
            low_s[rows, :] = hidden.astype(low_type)
            return carry

        lax.fori_loop(0, tiles, enter, 0)
        for j in range(4):
            def feed(i, carry):
                rows = pl.ds(pl.multiple_of(i * TILE, TILE), TILE)
                low = low_s[rows, :]
                gate = dot_nn(low, block(w_ref, 256 + j * 64))
                up = dot_nn(low, block(w_ref, 512 + j * 64))
                grad_mid = dot_nt(two_s[rows, :], down_block(w_ref, j))
                value, slope = gelu_parts(gate)
                mid_s[rows, :] = (value * up).astype(low_type)
                grad_gate = (grad_mid * up * slope).astype(low_type)
                grad_up = (grad_mid * value).astype(low_type)
                gates[rows, :] = grad_gate
                ups[rows, :] = grad_up
                acc[rows, :] += dot_nt(grad_gate, block(w_ref, 256 + j * 64)) + dot_nt(
                    grad_up, block(w_ref, 512 + j * 64)
                )
                return carry

            lax.fori_loop(0, tiles, feed, 0)
            grad_ref[2 * j : 2 * j + 2, 768:1024, :] = (
                dot_tn(mid_s[...], two_s[...]).reshape(2, 256, D).astype(low_type)
            )
            grad_ref[:, 256 + j * 64 : 320 + j * 64, :] = (
                dot_tn(low_s[...], gates[...]).reshape(8, 64, D).astype(low_type)
            )
            grad_ref[:, 512 + j * 64 : 576 + j * 64, :] = (
                dot_tn(low_s[...], ups[...]).reshape(8, 64, D).astype(low_type)
            )

        def middle(i, carry):
            rows = pl.ds(pl.multiple_of(i * TILE, TILE), TILE)
            scaled, inverse = norm_parts(one_ref[0, rows, :])
            grad = acc[rows, :]
            norm_out_ref[0, 0:1, :] += jnp.sum(grad * scaled, axis=0, keepdims=True)
            norm_out_ref[0, 1:2, :] += jnp.sum(grad, axis=0, keepdims=True)
            grad = norm_back(scaled, inverse, grad, norm_ref[pl.ds(at, 1), :])
            dx[rows, :] = grad
            low = grad.astype(low_type)
            two_s[rows, :] = low
            mid_s[rows, :] = dot_nt(low, block(w_ref, 192)).astype(low_type)
            return carry

        lax.fori_loop(0, tiles, middle, 0)
        grad_ref[:, 192:256, :] = dot_nn(mix_ref[0], two_s[...]).reshape(8, 64, D).astype(low_type)
        for head in range(HEADS):
            lanes = slice(head * HEAD_DIM, (head + 1) * HEAD_DIM)
            key_lanes = slice(D + head * HEAD_DIM, D + (head + 1) * HEAD_DIM)
            val_lanes = slice(2 * D + head * HEAD_DIM, 2 * D + (head + 1) * HEAD_DIM)
            keys = qkv_ref[0, :, key_lanes]
            keys_t = keys.T
            vals = qkv_ref[0, :, val_lanes]
            slope = 2.0 ** (-8.0 * (head + 1) / HEADS)
            grad_vals = None
            grad_keys = None
            for i in range(tiles):
                cols = slice(i * TILE, (i + 1) * TILE)
                query = qkv_ref[0, cols, lanes]
                grad_mix = mid_s[cols, lanes]
                scores = dot_nt(keys, query) * HEAD_DIM**-0.5 - slope * far[:, cols]
                prob = jnp.exp(scores - lse_ref[0, head, :, cols])
                grad_prob = dot_nt(vals, grad_mix)
                inner = jnp.sum(prob * grad_prob, axis=0, keepdims=True)
                grad_raw = (prob * (grad_prob - inner) * HEAD_DIM**-0.5).astype(low_type)
                back[cols, lanes] = dot_nn(keys_t, grad_raw).T.astype(low_type)
                value_part = dot_nn(prob.astype(low_type), grad_mix)
                key_part = dot_nn(grad_raw, query)
                grad_vals = value_part if grad_vals is None else grad_vals + value_part
                grad_keys = key_part if grad_keys is None else grad_keys + key_part
            back[:, key_lanes] = grad_keys.astype(low_type)
            back[:, val_lanes] = grad_vals.astype(low_type)

        def leave(i, carry):
            rows = pl.ds(pl.multiple_of(i * TILE, TILE), TILE)
            total = dx[rows, :]
            for j in range(3):
                total = total + dot_nt(back[rows, j * D : (j + 1) * D], block(w_ref, j * 64))
            dx[rows, :] = total
            return carry

        lax.fori_loop(0, tiles, leave, 0)
        for j in range(3):
            grad_ref[:, j * 64 : (j + 1) * 64, :] = (
                dot_tn(low_ref[0], back[:, j * D : (j + 1) * D]).reshape(8, 64, D).astype(low_type)
            )

        @pl.when(step == LAYERS)
        def _():
            first_ref[...] = dx[...].astype(low_type)


def run_backward(own, zed, pool, seg_col, seg_row, valid, weights, norms, saved):
    low_x, qkv, lse, mix, one, two = saved
    tokens = low_x.shape[1]
    low = jnp.bfloat16
    pick = lambda i: jnp.minimum(LAYERS - i, LAYERS - 1)
    layered = lambda *s: pl.BlockSpec((1,) + s, lambda i: (pick(i),) + (0,) * len(s))
    return pl.pallas_call(
        backward_kernel,
        grid=(LAYERS + 1,),
        in_specs=[
            whole((8, D)), whole((8, D)), whole((8, D)), whole((tokens, 1)), whole((1, tokens)), whole((1, tokens)),
            pl.BlockSpec((8, PART, D), lambda i: (0, pick(i), 0)),
            pl.BlockSpec((8, 64, D), lambda i: (0, HEAD_AT // 64, 0)),
            whole(norms.shape),
            layered(tokens, D), layered(tokens, 3 * D), layered(HEADS, 1, tokens), layered(D, tokens),
            layered(tokens, D), layered(tokens, D),
            pl.BlockSpec((1, tokens, D), lambda i: (LAYERS - 1, 0, 0)),
        ],
        out_specs=[
            pl.BlockSpec((8, PART, D), lambda i: (0, LAYERS - i, 0)),
            pl.BlockSpec((1, 8, D), lambda i: (LAYERS - i, 0, 0)),
            whole((tokens, D)),
        ],
        out_shape=[
            jax.ShapeDtypeStruct((8, PACKED, D), low),
            jax.ShapeDtypeStruct((LAYERS + 1, 8, D), jnp.float32),
            jax.ShapeDtypeStruct((tokens, D), low),
        ],
        scratch_shapes=[
            pltpu.VMEM((tokens, D), jnp.float32), pltpu.VMEM((tokens, tokens), jnp.float32),
            pltpu.VMEM((tokens, D), jnp.float32), pltpu.VMEM((tokens, D), low), pltpu.VMEM((tokens, D), low),
            pltpu.VMEM((tokens, D), low), pltpu.VMEM((tokens, D), low), pltpu.VMEM((tokens, D), low),
            pltpu.VMEM((tokens, 3 * D), low),
        ],
        compiler_params=pltpu.CompilerParams(vmem_limit_bytes=62 * 2**20),
    )(own, zed, pool, seg_col, seg_row, valid, weights, weights, norms, low_x, qkv, lse, mix, one, two, two)


def total_kernel(v_ref, o_ref, got, mine, ss, rs, ts, us, ls):
    lin = lax.axis_index("dp") * 4 + lax.axis_index("group")
    to = [lax.rem(lin + k, 32) for k in range(32)]
    peers = [(p // 4, p % 4) for p in to]
    entry_barrier(peers[1:])
    first = [
        pltpu.make_async_remote_copy(
            v_ref.at[to[k]], got.at[k], ss.at[k], rs.at[k], device_id=peers[k], device_id_type=MESH
        )
        for k in range(1, 32)
    ]
    for copy in first:
        copy.start()
    own = pltpu.make_async_copy(v_ref.at[lin], got.at[0], ls.at[0])
    own.start()
    for copy in first:
        copy.wait()
    own.wait()
    mine[...] = jnp.sum(got[...], axis=0)
    second = [
        pltpu.make_async_remote_copy(
            mine, o_ref.at[lin], ts.at[k], us.at[k], device_id=peers[k], device_id_type=MESH
        )
        for k in range(1, 32)
    ]
    for copy in second:
        copy.start()
    own = pltpu.make_async_copy(mine, o_ref.at[lin], ls.at[1])
    own.start()
    for copy in second:
        copy.wait()
    own.wait()


def total(v, cid):
    sems = pltpu.SemaphoreType.DMA
    return pl.pallas_call(
        total_kernel,
        out_shape=jax.ShapeDtypeStruct(v.shape, v.dtype),
        in_specs=[pl.BlockSpec(memory_space=pltpu.VMEM)], out_specs=pl.BlockSpec(memory_space=pltpu.VMEM),
        scratch_shapes=[
            pltpu.VMEM(v.shape, v.dtype), pltpu.VMEM(v.shape[1:], v.dtype),
            sems((32,)), sems((32,)), sems((32,)), sems((32,)), sems((2,)),
        ],
        compiler_params=pltpu.CompilerParams(collective_id=cid, has_side_effects=True),
    )(v)


def fast_shards(
    token_ids,
    seq_lengths,
    valid_mask,
    deal_order,
    log_scale,
    embed_master,
    attn_in,
    attn_out,
    ffn_in,
    ffn_out,
    head_master,
    norm_master,
    embed_rows,
    head_rows,
    layer_rows,
    ffn_out_rows,
    layer_cols,
    embed_head_cols,
    norm_state,
    scale_state,
):
    tokens = token_ids.shape[0]
    seq_count = seq_lengths.shape[1]
    head_count = HEADS
    shard_rows = embed_master.shape[0]
    my_dp = lax.axis_index("dp")
    my_group = lax.axis_index("group")
    position = jnp.arange(tokens, dtype=jnp.int32)
    bounds = jnp.cumsum(seq_lengths[0])
    segment = jnp.sum((position[:, None] >= bounds[None, :]).astype(jnp.int32), axis=1)

    key, wanted, most = slot_plan(token_ids, shard_rows)
    request = jnp.concatenate(
        [wanted.reshape(-1, 128), jnp.broadcast_to(most, (2, 128))], axis=0
    ).astype(jnp.int32)
    requests = spread(request, 0)
    crowded = jnp.max(requests[:, 6]) >= SLOTS
    asked = requests[:, :6].reshape(32, 8, SLOTS)
    asked_here = lax.dynamic_index_in_dim(asked, my_dp, 1, keepdims=False)
    group_asks = asked_here.reshape(8, 4, SLOTS)
    to_send = lax.dynamic_index_in_dim(group_asks, my_group, 1, keepdims=False)
    sent_rows = jnp.take(
        embed_master, jnp.clip(to_send.reshape(-1), 0, shard_rows - 1), axis=0
    ).astype(jnp.bfloat16)
    packed = pack_weights(attn_in, attn_out, ffn_in, ffn_out, head_master, norm_master)
    weights, got_rows = gather_weights(
        packed, sent_rows.reshape(8, SLOTS, D), plan(PACKED, 4, 0.36)
    )

    def dense_rows():
        table = lax.all_gather(embed_master.astype(jnp.bfloat16), "dp", axis=0, tiled=True)
        return jnp.take(table, token_ids, axis=0)

    def slot_rows():
        return jnp.take(got_rows.reshape(-1, D), jnp.minimum(key, 8 * SLOTS - 1), axis=0)

    stream = lax.cond(crowded, dense_rows, slot_rows)
    norms = jnp.pad(
        weights[:, NORM_AT : NORM_AT + 10, :64].transpose(1, 0, 2).reshape(10, D).astype(jnp.float32),
        ((0, 6), (0, 0)),
    )
    seg_col, seg_row = segment.reshape(-1, 1), segment.reshape(1, -1)
    valid_row = valid_mask.reshape(1, -1)
    *saved, unit_parts, pooled_low, head_out = run_forward(
        stream, seg_col, seg_row, valid_row, weights, norms
    )
    loss_value, own_rows, grad_scale = run_contrast(unit_parts, deal_order, log_scale, 3)
    loss_value, grad_scale = loss_value[0, 0], grad_scale[0]
    all_grads, norm_parts_out, grad_first = run_backward(
        own_rows, head_out, pooled_low, seg_col, seg_row, valid_row, weights, norms, saved
    )
    norm_grads = jnp.concatenate(
        [norm_parts_out[:LAYERS, :4].reshape(-1, D), norm_parts_out[LAYERS, :2]], axis=0
    )
    slot_grads = jnp.dot(
        (jnp.arange(8 * SLOTS, dtype=jnp.int32)[:, None] == key[None, :]).astype(jnp.bfloat16),
        grad_first,
        preferred_element_type=jnp.float32,
    ).astype(jnp.bfloat16)
    shard_grads, table_rows = scatter_grads(
        all_grads, slot_grads.reshape(8, SLOTS, D), plan(PACKED, 4, 0.29)
    )
    table_slots = asked_here.reshape(8, 4, SLOTS).transpose(1, 0, 2).reshape(1, -1)

    def dense_grad():
        total = jnp.zeros((shard_rows * 8, D), jnp.float32).at[token_ids].add(grad_first.astype(jnp.float32))
        return lax.psum(
            lax.psum_scatter(total, "dp", scatter_dimension=0, tiled=True), "group"
        )

    def slot_grad():
        return place_rows(table_slots, table_rows.reshape(-1, D), shard_rows)

    shard_embed = lax.cond(crowded, dense_grad, slot_grad)
    shard_full = shard_grads.astype(jnp.float32)
    shard_layers = shard_full[:HEAD_AT].reshape(LAYERS, PART, D)
    shard_qkv = jnp.stack([shard_columns(shard_layers[l, :192], 3) for l in range(LAYERS)])
    shard_attn = shard_layers[:, 192:256]
    shard_gate_up = jnp.stack([shard_columns(shard_layers[l, 256:768], 8) for l in range(LAYERS)])
    shard_down = shard_layers[:, 768:]
    shard_head = shard_full[HEAD_AT : HEAD_AT + 64]
    grad_list = [
        shard_embed[None],
        shard_head[None],
        shard_qkv,
        shard_attn,
        shard_gate_up,
        shard_down,
    ]
    master_list = [embed_master[None], head_master[None], attn_in, attn_out, ffn_in, ffn_out]
    state_list = [
        embed_rows[None],
        head_rows[None],
        layer_rows[:, 0],
        layer_rows[:, 1],
        layer_rows[:, 2],
        ffn_out_rows,
    ]
    col_list = [
        embed_head_cols[0:1],
        embed_head_cols[1:2],
        layer_cols[:, : 3 * D],
        layer_cols[:, 3 * D : 4 * D],
        layer_cols[:, 4 * D : 4 * D + 2 * FF],
        layer_cols[:, 4 * D + 2 * FF :],
    ]
    total_rows = [VOCAB, D, D, D, D, FF]
    wide_rate = RATE_SCALE / D**0.5
    rates = [
        RATE_SCALE,
        wide_rate,
        wide_rate,
        RATE_SCALE / (D // 8) ** 0.5,
        wide_rate,
        RATE_SCALE / FF**0.5,
    ]
    square_list = [grad_part * grad_part for grad_part in grad_list]
    rows_new = [
        DECAY_RATE * state_list[i]
        + (1.0 - DECAY_RATE) * (jnp.mean(square_list[i], axis=-1) + STATE_EPS)
        for i in range(6)
    ]
    col_parts = jnp.concatenate([jnp.sum(part, axis=1).reshape(-1) for part in square_list])
    step_parts = jnp.concatenate(
        [
            jnp.sum(square_list[i] * (1.0 / rows_new[i])[:, :, None], axis=1).reshape(-1)
            for i in range(6)
        ]
    )
    row_parts = jnp.concatenate([jnp.sum(part, axis=-1) for part in rows_new])
    width = col_parts.shape[0]
    pieces = jnp.concatenate([0.25 * col_parts, 0.25 * step_parts, 0.25 * row_parts, norm_grads.reshape(-1)])
    size = pieces.shape[0]
    pieces = jnp.pad(pieces, (0, 32 * 1152 - size)).reshape(32, 9, 128)
    sums = total(pieces, 4).reshape(-1)
    col_sum, step_sum, row_sum = sums[:width], sums[width : 2 * width], sums[2 * width : 2 * width + 10]
    norm_grad = sums[2 * width + 10 : size].reshape(2 * LAYERS + 1, 2, D)
    shard_norm = lax.dynamic_slice_in_dim(norm_grad, my_dp * 64, 64, 2)
    cols_new = []
    new_weights = []
    rms_list = []
    lead_start = 0
    col_start = 0
    for i in range(6):
        lead_count, _, col_width = grad_list[i].shape
        span = slice(col_start, col_start + lead_count * col_width)
        row_mean = row_sum[lead_start : lead_start + lead_count] / total_rows[i]
        col_state_new = DECAY_RATE * col_list[i] + (1.0 - DECAY_RATE) * (
            col_sum[span].reshape(lead_count, col_width) / total_rows[i] + STATE_EPS
        )
        cols_new.append(col_state_new)
        step_total = jnp.sum(
            step_sum[span].reshape(lead_count, col_width) * row_mean[:, None] / col_state_new,
            axis=1,
        )
        step_rms = jnp.sqrt(step_total / (total_rows[i] * col_width))
        rms_list.append(step_rms)
        row_factor = lax.rsqrt(rows_new[i] / row_mean[:, None]) * (
            -rates[i] / jnp.maximum(1.0, step_rms / CLIP_LEVEL)[:, None]
        )
        new_weights.append(
            master_list[i]
            + grad_list[i] * row_factor[:, :, None] * lax.rsqrt(col_state_new)[:, None, :]
        )
        lead_start = lead_start + lead_count
        col_start = col_start + lead_count * col_width
    norm_delta, norm_second = unfactored(shard_norm, norm_state)
    scale_delta, scale_state_new = unfactored(grad_scale, scale_state)
    return (
        loss_value,
        new_weights[0][0],
        new_weights[2],
        new_weights[3],
        new_weights[4],
        new_weights[5],
        new_weights[1][0],
        norm_master + norm_delta,
        log_scale + scale_delta,
        rows_new[0][0],
        rows_new[1][0],
        jnp.stack([rows_new[2], rows_new[3], rows_new[4]], axis=1),
        rows_new[5],
        jnp.concatenate([cols_new[2], cols_new[3], cols_new[4], cols_new[5]], axis=1),
        cols_new[0][0],
        cols_new[1][0],
        norm_second,
        scale_state_new,
        jnp.concatenate(rms_list),
    )


def solution(mesh):
    in_specs = (
        P(("dp", "group")),
        P(("dp", "group"), None),
        P(("dp", "group")),
        P(),
        P(),
        P("dp", None),
        P(None, "dp", None),
        P(None, "dp", None),
        P(None, "dp", None),
        P(None, "dp", None),
        P("dp", None),
        P(None, None, "dp"),
        P("dp"),
        P("dp"),
        P(None, None, "dp"),
        P(None, "dp"),
        P(),
        P(),
        P(None, None, "dp"),
        P(),
    )
    out_specs = (
        P(),
        P("dp", None),
        P(None, "dp", None),
        P(None, "dp", None),
        P(None, "dp", None),
        P(None, "dp", None),
        P("dp", None),
        P(None, None, "dp"),
        P(),
        P("dp"),
        P("dp"),
        P(None, None, "dp"),
        P(None, "dp"),
        P(),
        P(),
        P(),
        P(None, None, "dp"),
        P(),
        P(),
    )
    body = fast_shards if dict(mesh.shape) == {"dp": 8, "group": 4} else shards
    return jax.shard_map(body, mesh=mesh, in_specs=in_specs, out_specs=out_specs, check_vma=False)
```

```python
import functools

import jax
import jax.numpy as jnp
from jax import lax
from jax.experimental import pallas as pl
from jax.experimental.pallas import tpu as pltpu
from jax.sharding import PartitionSpec as P

D = 512
HEADS = 8
HEAD_DIM = 64
FF = 2048
VOCAB = 30528
LAYERS = 2


NORM_EPS = 1e-06
UNIT_EPS = 1e-06
STATE_EPS = 1e-30
DECAY_RATE = 0.5
CLIP_LEVEL = 0.05
RATE_SCALE = 10.0
NORM_RATE = 0.1


def layer_norm(values, gain_vec, shift_vec):
    center = values - jnp.mean(values, axis=-1, keepdims=True)
    spread = jnp.mean(center * center, axis=-1, keepdims=True)
    return center * lax.rsqrt(spread + NORM_EPS) * gain_vec + shift_vec


def geglu(joined):
    half_width = joined.shape[-1] // 2
    return jax.nn.gelu(joined[:, :half_width]) * joined[:, half_width:]


def alibi_slopes(head_count):
    return 2.0 ** (-8.0 * (jnp.arange(head_count).astype(jnp.float32) + 1.0) / head_count)


def normalize(vectors):
    return vectors * lax.rsqrt(jnp.sum(vectors * vectors, axis=-1, keepdims=True) + UNIT_EPS)


def contrast(unit_all, scale_arg, deal_order):
    pair_count = deal_order.shape[0] // 2
    queries = jnp.take(unit_all, deal_order[:pair_count], axis=0)
    documents = jnp.take(unit_all, deal_order[pair_count:], axis=0)
    logits = jnp.exp(scale_arg[0]) * jnp.matmul(
        queries, documents.T, precision=lax.Precision.HIGHEST
    )
    by_row = jax.nn.logsumexp(logits, axis=1)
    by_column = jax.nn.logsumexp(logits, axis=0)
    return jnp.sum(0.5 * (by_row + by_column) - jnp.diagonal(logits))


def unfactored(grad_full, state):
    state_new = DECAY_RATE * state + (1.0 - DECAY_RATE) * (grad_full * grad_full + STATE_EPS)
    return (-NORM_RATE * grad_full * lax.rsqrt(state_new), state_new)


def block_scores(query_rows, key_all, seg_rows, segment, head_count):
    row_count = query_rows.shape[0]
    raw_scores = jnp.einsum("thc,shc->hts", query_rows, key_all, preferred_element_type=jnp.float32)
    row_pos = jnp.arange(row_count, dtype=jnp.int32)
    col_pos = jnp.arange(key_all.shape[0], dtype=jnp.int32)
    distance = jnp.abs(row_pos[:, None] - col_pos[None, :]).astype(jnp.float32)
    scores = (
        raw_scores * HEAD_DIM ** (-0.5) + -alibi_slopes(head_count)[:, None, None] * distance[None]
    )
    same_seq = seg_rows[:, None] == segment[None, :]
    return jnp.where(same_seq[None], scores, -jnp.inf)


def split_qkv(qkv_low, head_count):
    tokens = qkv_low.shape[0]
    split_heads = qkv_low.reshape(tokens, 3, head_count, qkv_low.shape[1] // (3 * head_count))
    return (split_heads[:, 0], split_heads[:, 1], split_heads[:, 2])


def attend(qkv_low, segment, head_count):
    model_width = qkv_low.shape[1] // 3
    query_all, key_all, value_all = split_qkv(qkv_low, head_count)
    scores = block_scores(query_all, key_all, segment, segment, head_count)
    row_max = jnp.max(scores, axis=-1, keepdims=True)
    exponent = jnp.exp(scores - row_max)
    row_total = jnp.sum(exponent, axis=-1, keepdims=True)
    prob_low = (exponent / row_total).astype(jnp.bfloat16)
    mixed_list = jnp.einsum(
        "hts,shc->thc", prob_low, value_all, preferred_element_type=jnp.float32
    ).reshape(-1, model_width)
    lse_list = row_max[..., 0] + jnp.log(row_total[..., 0])
    return (mixed_list, lse_list)


def attend_back(qkv_low, segment, head_count, lse_all, grad_mixed):
    tokens = qkv_low.shape[0]
    query_all, key_all, value_all = split_qkv(qkv_low, head_count)
    grad_out = grad_mixed.reshape(tokens, head_count, -1)
    block_rows = min(tokens, 512)
    scores = block_scores(query_all, key_all, segment, segment, head_count)
    prob_full = jnp.exp(scores - lse_all[:, 0:block_rows, None])
    grad_value = jnp.einsum(
        "hts,thc->shc", prob_full.astype(jnp.bfloat16), grad_out, preferred_element_type=jnp.float32
    )
    grad_prob = jnp.einsum("thc,shc->hts", grad_out, value_all, preferred_element_type=jnp.float32)
    inner = jnp.sum(prob_full * grad_prob, axis=-1, keepdims=True)
    grad_raw = (prob_full * (grad_prob - inner) * HEAD_DIM ** (-0.5)).astype(jnp.bfloat16)
    query_list = jnp.einsum("hts,shc->thc", grad_raw, key_all, preferred_element_type=jnp.float32)
    grad_key = jnp.einsum("hts,thc->shc", grad_raw, query_all, preferred_element_type=jnp.float32)
    return (
        jnp.stack([query_list, grad_key, grad_value], axis=1)
        .reshape(tokens, -1)
        .astype(jnp.bfloat16)
    )


def shards(
    token_ids,
    seq_lengths,
    valid_mask,
    deal_order,
    log_scale,
    embed_master,
    attn_in,
    attn_out,
    ffn_in,
    ffn_out,
    head_master,
    norm_master,
    embed_rows,
    head_rows,
    layer_rows,
    ffn_out_rows,
    layer_cols,
    embed_head_cols,
    norm_state,
    scale_state,
):
    tokens = token_ids.shape[0]
    model_width = embed_master.shape[1]
    seq_count = seq_lengths.shape[1]
    head_count = HEADS
    position = jnp.arange(tokens, dtype=jnp.int32)
    bounds = jnp.cumsum(seq_lengths[0])
    segment = jnp.sum((position[:, None] >= bounds[None, :]).astype(jnp.int32), axis=1)
    piece_rows = lax.all_gather(embed_master.astype(jnp.bfloat16), "dp", axis=0, tiled=True)
    local_idx = token_ids
    inside = (local_idx >= 0) & (local_idx < piece_rows.shape[0])
    picked = jnp.take(piece_rows, jnp.clip(local_idx, 0, piece_rows.shape[0] - 1), axis=0).astype(
        jnp.float32
    )
    stream = jnp.where(inside[:, None], picked, 0.0)
    w_qkv, w_attn, w_gate_up, w_down, w_head, norm_low = (
        lax.all_gather(attn_in.astype(jnp.bfloat16), "dp", axis=1, tiled=True),
        lax.all_gather(attn_out.astype(jnp.bfloat16), "dp", axis=1, tiled=True),
        lax.all_gather(ffn_in.astype(jnp.bfloat16), "dp", axis=1, tiled=True),
        lax.all_gather(ffn_out.astype(jnp.bfloat16), "dp", axis=1, tiled=True),
        lax.all_gather(head_master.astype(jnp.bfloat16), "dp", axis=0, tiled=True),
        lax.all_gather(norm_master.astype(jnp.bfloat16), "dp", axis=2, tiled=True),
    )
    norms = norm_low.astype(jnp.float32)
    kept_list = []
    for layer_idx in range(LAYERS):
        stream_low = stream.astype(jnp.bfloat16)
        qkv_low = jnp.dot(stream_low, w_qkv[layer_idx], preferred_element_type=jnp.float32).astype(
            jnp.bfloat16
        )
        mixed_heads, lse_all = attend(qkv_low, segment, head_count)
        mixed_low = mixed_heads.astype(jnp.bfloat16)
        resid_one = stream + jnp.dot(
            mixed_low, w_attn[layer_idx], preferred_element_type=jnp.float32
        )
        normed = layer_norm(resid_one, norms[2 * layer_idx, 0], norms[2 * layer_idx, 1])
        normed_low = normed.astype(jnp.bfloat16)
        joined = jnp.dot(normed_low, w_gate_up[layer_idx], preferred_element_type=jnp.float32)
        hidden_low = geglu(joined).astype(jnp.bfloat16)
        resid_two = normed + jnp.dot(
            hidden_low, w_down[layer_idx], preferred_element_type=jnp.float32
        )
        kept_list.append(
            (
                stream_low,
                qkv_low,
                lse_all,
                mixed_low,
                resid_one,
                normed_low,
                joined,
                hidden_low,
                resid_two,
            )
        )
        stream = layer_norm(resid_two, norms[2 * layer_idx + 1, 0], norms[2 * layer_idx + 1, 1])
    final = layer_norm(stream, norms[2 * LAYERS, 0], norms[2 * LAYERS, 1])
    member = (
        (segment[None, :] == jnp.arange(seq_count, dtype=jnp.int32)[:, None])
        & (valid_mask[None, :] > 0)
    ).astype(jnp.float32)
    counts = jnp.maximum(jnp.sum(member, axis=1), 1.0)
    pooled = jnp.matmul(member, final, precision=lax.Precision.HIGHEST) / counts[:, None]
    pooled_low = pooled.astype(jnp.bfloat16)
    head_out = jnp.dot(pooled_low, w_head, preferred_element_type=jnp.float32)
    unit_vecs, unit_back = jax.vjp(normalize, head_out)
    unit_every = lax.all_gather(unit_vecs, ("dp", "group"), axis=0, tiled=True)
    loss_value, loss_back = jax.vjp(
        lambda unit_all, scale_arg: contrast(unit_all, scale_arg, deal_order), unit_every, log_scale
    )
    grad_units, grad_scale = loss_back(jnp.ones_like(loss_value))
    own_rows = lax.dynamic_slice_in_dim(
        grad_units, lax.axis_index(("dp", "group")) * seq_count, seq_count, 0
    )
    grad_head_out = unit_back(own_rows)[0].astype(jnp.bfloat16)
    grad_head = jnp.dot(pooled_low.T, grad_head_out, preferred_element_type=jnp.float32)
    grad_pooled = jnp.dot(grad_head_out, w_head.T, preferred_element_type=jnp.float32)
    grad_final = jnp.matmul(
        member.T, grad_pooled / counts[:, None], precision=lax.Precision.HIGHEST
    )
    final_back = jax.vjp(layer_norm, stream, norms[2 * LAYERS, 0], norms[2 * LAYERS, 1])[1]
    grad_stream, gain_last, shift_last = final_back(grad_final)
    norm_grads = [None] * (2 * LAYERS + 1)
    norm_grads[2 * LAYERS] = jnp.stack([gain_last, shift_last])
    qkv_grads = [None] * LAYERS
    attn_grads = [None] * LAYERS
    gate_grads = [None] * LAYERS
    down_grads = [None] * LAYERS
    for layer_idx in reversed(range(LAYERS)):
        (
            stream_low,
            qkv_low,
            lse_all,
            mixed_low,
            resid_one,
            normed_low,
            joined,
            hidden_low,
            resid_two,
        ) = kept_list[layer_idx]
        norm_two_back = jax.vjp(
            layer_norm, resid_two, norms[2 * layer_idx + 1, 0], norms[2 * layer_idx + 1, 1]
        )[1]
        grad_two, gain_two, shift_two = norm_two_back(grad_stream)
        norm_grads[2 * layer_idx + 1] = jnp.stack([gain_two, shift_two])
        grad_branch = grad_two.astype(jnp.bfloat16)
        down_grads[layer_idx] = jnp.dot(
            hidden_low.T, grad_branch, preferred_element_type=jnp.float32
        )
        grad_hidden = jnp.dot(grad_branch, w_down[layer_idx].T, preferred_element_type=jnp.float32)
        grad_joined = jax.vjp(geglu, joined)[1](grad_hidden)[0].astype(jnp.bfloat16)
        gate_grads[layer_idx] = jnp.dot(
            normed_low.T, grad_joined, preferred_element_type=jnp.float32
        )
        grad_normed = grad_two + jnp.dot(
            grad_joined, w_gate_up[layer_idx].T, preferred_element_type=jnp.float32
        )
        norm_one_back = jax.vjp(
            layer_norm, resid_one, norms[2 * layer_idx, 0], norms[2 * layer_idx, 1]
        )[1]
        grad_one, gain_one, shift_one = norm_one_back(grad_normed)
        norm_grads[2 * layer_idx] = jnp.stack([gain_one, shift_one])
        grad_attended = grad_one.astype(jnp.bfloat16)
        attn_grads[layer_idx] = jnp.dot(
            mixed_low.T, grad_attended, preferred_element_type=jnp.float32
        )
        grad_mixed = jnp.dot(
            grad_attended, w_attn[layer_idx].T, preferred_element_type=jnp.float32
        ).astype(jnp.bfloat16)
        grad_qkv_low = attend_back(qkv_low, segment, head_count, lse_all, grad_mixed)
        qkv_grads[layer_idx] = jnp.dot(
            stream_low.T, grad_qkv_low, preferred_element_type=jnp.float32
        )
        grad_stream = grad_one + jnp.dot(
            grad_qkv_low, w_qkv[layer_idx].T, preferred_element_type=jnp.float32
        )
    row_count = embed_master.shape[0] * lax.axis_size("dp")
    local_idx = token_ids
    inside = (local_idx >= 0) & (local_idx < row_count)
    slot_idx = jnp.where(inside, local_idx, row_count)
    embed_grad = lax.psum_scatter(
        jnp.zeros((row_count, model_width), jnp.float32).at[slot_idx].add(grad_stream, mode="drop"),
        "dp",
        scatter_dimension=0,
        tiled=True,
    )
    grad_qkv = jnp.stack(qkv_grads)
    grad_attn = jnp.stack(attn_grads)
    grad_gate_up = jnp.stack(gate_grads)
    grad_down = jnp.stack(down_grads)
    grad_norm = jnp.stack(norm_grads)
    owned = (
        lax.psum_scatter(grad_qkv, "dp", scatter_dimension=1, tiled=True),
        lax.psum_scatter(grad_attn, "dp", scatter_dimension=1, tiled=True),
        lax.psum_scatter(grad_gate_up, "dp", scatter_dimension=1, tiled=True),
        lax.psum_scatter(grad_down, "dp", scatter_dimension=1, tiled=True),
        lax.psum_scatter(grad_head, "dp", scatter_dimension=0, tiled=True),
        lax.psum_scatter(grad_norm, "dp", scatter_dimension=2, tiled=True),
    )
    shard_qkv, shard_attn, shard_gate_up, shard_down, shard_head, shard_norm, shard_embed = (
        lax.psum((owned[0], owned[1], owned[2], owned[3], owned[4], owned[5], embed_grad), "group")
    )
    grad_list = [
        shard_embed[None],
        shard_head[None],
        shard_qkv,
        shard_attn,
        shard_gate_up,
        shard_down,
    ]
    master_list = [embed_master[None], head_master[None], attn_in, attn_out, ffn_in, ffn_out]
    state_list = [
        embed_rows[None],
        head_rows[None],
        layer_rows[:, 0],
        layer_rows[:, 1],
        layer_rows[:, 2],
        ffn_out_rows,
    ]
    col_list = [
        embed_head_cols[0:1],
        embed_head_cols[1:2],
        layer_cols[:, : 3 * D],
        layer_cols[:, 3 * D : 4 * D],
        layer_cols[:, 4 * D : 4 * D + 2 * FF],
        layer_cols[:, 4 * D + 2 * FF :],
    ]
    total_rows = [VOCAB, D, D, D, D, FF]
    wide_rate = RATE_SCALE / D**0.5
    rates = [
        RATE_SCALE,
        wide_rate,
        wide_rate,
        RATE_SCALE / (D // 8) ** 0.5,
        wide_rate,
        RATE_SCALE / FF**0.5,
    ]
    square_list = [grad_part * grad_part for grad_part in grad_list]
    rows_new = [
        DECAY_RATE * state_list[entry_idx]
        + (1.0 - DECAY_RATE) * (jnp.mean(square_list[entry_idx], axis=-1) + STATE_EPS)
        for entry_idx in range(6)
    ]
    col_parts = jnp.concatenate(
        [jnp.sum(square_part, axis=1).reshape(-1) for square_part in square_list]
    )
    row_parts = jnp.concatenate([jnp.sum(row_part, axis=-1) for row_part in rows_new])
    col_sum, row_sum = lax.psum((col_parts, row_parts), "dp")
    row_means = []
    lead_start = 0
    for entry_idx in range(6):
        lead_count = grad_list[entry_idx].shape[0]
        row_means.append(row_sum[lead_start : lead_start + lead_count] / total_rows[entry_idx])
        lead_start = lead_start + lead_count
    cols_new = []
    steps_all = []
    col_start = 0
    for entry_idx in range(6):
        lead_count = grad_list[entry_idx].shape[0]
        col_width = grad_list[entry_idx].shape[2]
        col_full = col_sum[col_start : col_start + lead_count * col_width].reshape(
            lead_count, col_width
        )
        col_state_new = DECAY_RATE * col_list[entry_idx] + (1.0 - DECAY_RATE) * (
            col_full / total_rows[entry_idx] + STATE_EPS
        )
        cols_new.append(col_state_new)
        steps_all.append(
            grad_list[entry_idx]
            * lax.rsqrt(
                rows_new[entry_idx][:, :, None]
                * col_state_new[:, None, :]
                / row_means[entry_idx][:, None, None]
            )
        )
        col_start = col_start + lead_count * col_width
    step_squares = []
    step_parts = jnp.concatenate(
        [jnp.sum(step_dir * step_dir, axis=(1, 2)) for step_dir in steps_all]
    )
    step_sum = lax.psum(step_parts, "dp")
    lead_start = 0
    for entry_idx in range(6):
        lead_count = grad_list[entry_idx].shape[0]
        step_squares.append(step_sum[lead_start : lead_start + lead_count])
        lead_start = lead_start + lead_count
    new_weights = []
    rms_list = []
    for entry_idx in range(6):
        cell_count = total_rows[entry_idx] * grad_list[entry_idx].shape[2]
        step_rms = jnp.sqrt(step_squares[entry_idx] / cell_count)
        rms_list.append(step_rms)
        delta = (
            -rates[entry_idx]
            * steps_all[entry_idx]
            / jnp.maximum(1.0, step_rms / CLIP_LEVEL)[:, None, None]
        )
        new_weights.append(master_list[entry_idx] + delta)
    norm_delta, norm_second = unfactored(shard_norm, norm_state)
    scale_delta, scale_state_new = unfactored(grad_scale, scale_state)
    return (
        loss_value,
        new_weights[0][0],
        new_weights[2],
        new_weights[3],
        new_weights[4],
        new_weights[5],
        new_weights[1][0],
        norm_master + norm_delta,
        log_scale + scale_delta,
        rows_new[0][0],
        rows_new[1][0],
        jnp.stack([rows_new[2], rows_new[3], rows_new[4]], axis=1),
        rows_new[5],
        jnp.concatenate([cols_new[2], cols_new[3], cols_new[4], cols_new[5]], axis=1),
        cols_new[0][0],
        cols_new[1][0],
        norm_second,
        scale_state_new,
        jnp.concatenate(rms_list),
    )


SLOTS = 96
PART = 1024
HEAD_AT = 2 * PART
NORM_AT = HEAD_AT + 64
PACKED = NORM_AT + 32


MESH = pl.DeviceIdType.MESH
BF=jnp.bfloat16

def place():
    dp = lax.axis_index("dp"); g = lax.axis_index("group")
    return dp // 2, dp % 2, g // 2, g % 2

def dev(z, x, y, c):
    return (z * 2 + x, y * 2 + c)

def entry_barrier(peers):
    bar = pltpu.get_barrier_semaphore()
    for p in peers:
        pl.semaphore_signal(bar, inc=1, device_id=p, device_id_type=MESH)
    pl.semaphore_wait(bar, len(peers))

def mult(v, m=16):
    return pl.multiple_of(v, m)

def gather_kernel(chunks, w_ref, ask_ref, table_ref, ag_ref, got_ref, asks_ref, table, picked, rows_s,
                  zs, zr, xs, xr, ys, yr, cs, cr, ls, es, er, qs, qr):
    z, x, y, c = place()
    me = z * 2 + x
    g = y * 2 + c
    g2 = (1 - y) * 2 + c
    ep = [(lax.rem(me + k, 8), g) for k in range(8)]
    zp = [dev((z + k) % 4, x, y, c) for k in range(4)]
    xp, yp, cp = dev(z, 1 - x, y, c), dev(z, x, 1 - y, c), dev(z, x, y, 1 - c)
    entry_barrier(ep[1:] + [yp, cp])
    Q = len(chunks)
    hs = [mult(b + c * h + y * nb) for b, h, nb in chunks]
    nh = [h - nb for b, h, nb in chunks]
    bs = [mult(b + c * h + y * (h - nb)) for b, h, nb in chunks]
    nbs = [nb for b, h, nb in chunks]
    cb = [mult(b + c * h) for b, h, nb in chunks]
    nc = [h for b, h, nb in chunks]
    def rc(src, dst, s, r, d):
        return pltpu.make_async_remote_copy(src, dst, s, r, device_id=d, device_id_type=MESH)
    def shard(k, f):
        return ((z + 4 - k) % 4) * 2 + (x if f == 0 else 1 - x)
    qc = [rc(ask_ref.at[ep[k][0]], asks_ref.at[g, me], qs.at[k], qr.at[k], ep[k]) for k in range(1, 8)]
    for copy in qc:
        copy.start()
    mine = pltpu.make_async_copy(ask_ref.at[me], asks_ref.at[g, me], ls.at[0])
    mine.start()
    near = pltpu.make_async_copy(table_ref, table.at[pl.ds(0, table_ref.shape[0])], ls.at[1])
    near.start()
    qy = rc(asks_ref.at[g], asks_ref.at[g], qs.at[8], qr.at[8], yp)
    qcc = rc(asks_ref.at[g], asks_ref.at[g], qs.at[9], qr.at[9], cp)
    qd = rc(asks_ref.at[g2], asks_ref.at[g2], qs.at[10], qr.at[10], cp)
    own = pltpu.make_async_copy(w_ref, ag_ref.at[me], ls.at[2])
    own.start()
    kept = pltpu.make_async_copy(rows_s.at[me], got_ref.at[me], ls.at[3])
    ec = [rc(rows_s.at[ep[k][0]], got_ref.at[me], es.at[k], er.at[k], ep[k]) for k in range(1, 8)]
    def pick_rows():
        mine.wait()
        for copy in qc:
            copy.wait_recv()
        qy.start()
        qcc.start()
        wanted = asks_ref[pl.ds(g, 1)].reshape(8, 128).astype(jnp.float32).T
        near.wait()
        depth = table.shape[0] // 5
        table[pl.ds(table_ref.shape[0], table.shape[0] - table_ref.shape[0]), :] = jnp.zeros(
            (table.shape[0] - table_ref.shape[0], 512), jnp.float32
        )
        picked[...] = jnp.zeros(picked.shape, jnp.float32)
        ramp = lax.broadcasted_iota(jnp.int32, (SLOTS, depth), 1).astype(jnp.float32)
        def body(i, carry):
            start = pl.multiple_of(i * depth, depth)
            low = table[pl.ds(start, depth), :].astype(BF)
            shifted = ramp + (i * depth).astype(jnp.float32)
            for r in range(8):
                hot = jnp.where(wanted[:SLOTS, r : r + 1] == shifted, 1.0, 0.0).astype(BF)
                picked[r] += jnp.dot(hot, low, preferred_element_type=jnp.float32)
            return carry
        lax.fori_loop(0, 5, body, 0)
        rows_s[...] = picked[...].astype(BF)
        kept.start()
        for copy in ec:
            copy.start()
    zc = {}; xc = {}; yc = {}; cc = {}
    for q in range(Q):
        for k in range(1, 4):
            zc[q, k] = rc(w_ref.at[pl.ds(hs[q], nh[q])], ag_ref.at[me, pl.ds(hs[q], nh[q])], zs.at[q, k], zr.at[q, k], zp[k])
        for k in range(4):
            src = w_ref.at[pl.ds(hs[q], nh[q])] if k == 0 else ag_ref.at[shard(k, 0), pl.ds(hs[q], nh[q])]
            xc[q, k] = rc(src, ag_ref.at[shard(k, 0), pl.ds(hs[q], nh[q])], xs.at[q, k], xr.at[q, k], xp)
        for k in range(4):
            for f in range(2):
                if k == 0 and f == 0: continue
                s = shard(k, f)
                yc[q, k, f] = rc(ag_ref.at[s, pl.ds(bs[q], nbs[q])], ag_ref.at[s, pl.ds(bs[q], nbs[q])], ys.at[q, 2 * k + f], yr.at[q, 2 * k + f], yp)
                cc[q, k, f] = rc(ag_ref.at[s, pl.ds(cb[q], nc[q])], ag_ref.at[s, pl.ds(cb[q], nc[q])], cs.at[q, 2 * k + f], cr.at[q, 2 * k + f], cp)
    def s0(q):
        for k in (2, 1, 3):
            zc[q, k].start()
        xc[q, 0].start()
    def s1(q):
        for k in (1, 3, 2):
            zc[q, k].wait_recv()
            xc[q, k].start()
            yc[q, k, 0].start()
    def s2(q):
        for k in (0, 1, 3, 2):
            xc[q, k].wait_recv()
            yc[q, k, 1].start()
    def s3(q):
        for k, f in ((1, 0), (3, 0), (2, 0), (0, 1), (1, 1), (3, 1), (2, 1)):
            yc[q, k, f].wait_recv()
            cc[q, k, f].start()
    st = [s0, s1, s2, s3]
    for t in range(Q + 3):
        for i in reversed(range(4)):
            q = t - i
            if 0 <= q < Q:
                st[i](q)
        if t == 0:
            pick_rows()
        if t == 2:
            qy.wait_recv()
            qd.start()
    for q in range(Q):
        for k in range(4):
            for f in range(2):
                if k or f: cc[q, k, f].wait_recv()
    for d in (zc, xc, cc) + (yc,):
        for v in d.values(): v.wait_send()
    for copy in ec:
        copy.wait()
    qcc.wait_recv()
    qd.wait_recv()
    for copy in qc + [qy, qcc, qd]:
        copy.wait_send()
    own.wait()
    kept.wait()

def gather_weights(w, asks, table, chunks, cid):
    Q = len(chunks)
    D = pltpu.SemaphoreType.DMA
    anywhere = pl.BlockSpec(memory_space=pl.ANY)
    near = pl.BlockSpec(memory_space=pltpu.VMEM)
    padded = -(-table.shape[0] // 640) * 640
    return pl.pallas_call(
        functools.partial(gather_kernel, chunks),
        out_shape=(jax.ShapeDtypeStruct((8,) + w.shape, w.dtype), jax.ShapeDtypeStruct((8, SLOTS, 512), BF), jax.ShapeDtypeStruct((4,) + asks.shape, asks.dtype)),
        in_specs=[anywhere, near, anywhere], out_specs=[anywhere, anywhere, near],
        scratch_shapes=[pltpu.VMEM((padded, 512), jnp.float32), pltpu.VMEM((8, SLOTS, 512), jnp.float32), pltpu.VMEM((8, SLOTS, 512), BF),
            D((Q, 4)), D((Q, 4)), D((Q, 4)), D((Q, 4)), D((Q, 8)), D((Q, 8)), D((Q, 8)), D((Q, 8)), D((4,)), D((8,)), D((8,)), D((11,)), D((11,))],
        compiler_params=pltpu.CompilerParams(collective_id=cid, has_side_effects=True, vmem_limit_bytes=48 * 2**20),
    )(w, asks, table)

def scatter_kernel(chunks, g_ref, e_ref, n_ref, out_ref, t_ref, n_out, nbuf, acc, b1, b2, b3, b4, b5, fin,
                   cs, cr, ys, yr, xs, xr, zs, zr, as_, ar, fs, fr, ls, os_, es, er, el, ns, nr):
    z, x, y, c = place()
    me = z * 2 + x
    g = y * 2 + c
    ep = [(lax.rem(me + k, 8), g) for k in range(8)]
    zp = [dev((z + k) % 4, x, y, c) for k in range(4)]
    xp, yp, cp = dev(z, 1 - x, y, c), dev(z, x, 1 - y, c), dev(z, x, y, 1 - c)
    entry_barrier(ep[1:] + [yp, cp])
    Q = len(chunks)
    lo = []; o = 0; lb = []; ob = 0; lh = []; oh = 0; la = []; oa = 0
    for b, h, nb in chunks:
        lo.append(o); o += h
        lb.append(ob); ob += nb
        lh.append(oh); oh += h - nb
        la.append(oa); oa += h - 2 * nb
    nh = [h - nb for b, h, nb in chunks]
    nbs = [nb for b, h, nb in chunks]
    na = [h - 2 * nb for b, h, nb in chunks]
    hs = [mult(lo[q] + y * nbs[q]) for q in range(Q)]
    mb = [mult(lo[q] + y * nh[q]) for q in range(Q)]
    ob_ = [mult(lo[q] + (1 - y) * nh[q]) for q in range(Q)]
    aa = [lo[q] + nbs[q] for q in range(Q)]
    def rc(src, dst, s, r, d):
        return pltpu.make_async_remote_copy(src, dst, s, r, device_id=d, device_id_type=MESH)
    def add(dst, src, n, blk=16):
        def body(i, _):
            a = mult(i * blk)
            d = dst(a, blk); s = src(a, blk)
            d[...] = (d[...].astype(jnp.float32) + s[...].astype(jnp.float32)).astype(BF)
            return _
        lax.fori_loop(0, n // blk, body, 0)
    order = []
    for k in (2, 1, 3, 0):
        for f in (1, 0):
            order.append((k, f))
    def owner(k, f):
        return ((z + k) % 4) * 2 + (x if f == 0 else 1 - x)
    C1 = {}; Y = {}; X = {}; Z = {}; A = {}; F = {}; L = {}; O = {}; BX = {}
    for q, (b, h, nb) in enumerate(chunks):
        for i, (k, f) in enumerate(order):
            s = owner(k, f)
            L[q, i] = pltpu.make_async_copy(g_ref.at[s, pl.ds(mult(b + c * h), h)], acc.at[s, pl.ds(lo[q], h)], ls.at[q, i])
            C1[q, i] = rc(g_ref.at[s, pl.ds(mult(b + (1 - c) * h), h)], b1.at[s, pl.ds(lo[q], h)], cs.at[q, i], cr.at[q, i], cp)
            Y[q, i] = rc(acc.at[s, pl.ds(ob_[q], nb)], b2.at[s, pl.ds(lb[q], nb)], ys.at[q, i], yr.at[q, i], yp)
        for k in range(4):
            X[q, k] = rc(acc.at[owner(k, 1), pl.ds(hs[q], nh[q])], b3.at[k, pl.ds(lh[q], nh[q])], xs.at[q, k], xr.at[q, k], xp)
            if k:
                Z[q, k] = rc(acc.at[owner(k, 0), pl.ds(hs[q], nh[q])], b4.at[k - 1, pl.ds(lh[q], nh[q])], zs.at[q, k], zr.at[q, k], zp[k])
        A[q] = rc(fin.at[pl.ds(aa[q], na[q])], b5.at[pl.ds(la[q], na[q])], as_.at[q, 0], ar.at[q, 0], yp)
        BX[q] = rc(fin.at[pl.ds(mb[q], nb)], fin.at[pl.ds(mb[q], nb)], as_.at[q, 1], ar.at[q, 1], yp)
        F[q] = rc(fin.at[pl.ds(lo[q], h)], out_ref.at[pl.ds(mult(b + c * h), h)], fs.at[q], fr.at[q], cp)
        O[q] = pltpu.make_async_copy(fin.at[pl.ds(lo[q], h)], out_ref.at[pl.ds(mult(b + c * h), h)], os_.at[q])
    g2 = (1 - y) * 2 + c
    kept = pltpu.make_async_copy(e_ref.at[me], t_ref.at[g, me], el)
    E = [rc(e_ref.at[ep[k][0]], t_ref.at[g, me], es.at[k], er.at[k], ep[k]) for k in range(1, 8)]
    EY = rc(t_ref.at[g], t_ref.at[g], es.at[8], er.at[8], yp)
    EC = rc(t_ref.at[g], t_ref.at[g], es.at[9], er.at[9], cp)
    ED = rc(t_ref.at[g2], t_ref.at[g2], es.at[10], er.at[10], cp)
    NC = rc(n_ref, nbuf.at[0], ns.at[0], nr.at[0], cp)
    NY = rc(nbuf.at[1], nbuf.at[2], ns.at[1], nr.at[1], yp)
    def e0():
        NC.start()
        kept.start()
        for v in E: v.start()
    def e1():
        NC.wait_recv()
        nbuf[1] = nbuf[0] + n_ref[...]
        NY.start()
        kept.wait()
        for v in E: v.wait_recv()
        EY.start(); EC.start()
    def e2():
        NY.wait_recv()
        n_out[...] = nbuf[1] + nbuf[2]
        EY.wait_recv()
        ED.start()
    def e3():
        EC.wait_recv(); ED.wait_recv()
        for v in E + [EY, EC, ED, NC, NY]: v.wait_send()
    ev = {0: e0, 3: e1, 5: e2}
    def s0(q):
        for i in range(8):
            L[q, i].start(); C1[q, i].start()
    def s1(q):
        h = chunks[q][1]
        for i, (k, f) in enumerate(order):
            s = owner(k, f)
            L[q, i].wait(); C1[q, i].wait_recv()
            add(lambda a, n: acc.at[s, pl.ds(lo[q] + a, n)], lambda a, n: b1.at[s, pl.ds(lo[q] + a, n)], h)
            Y[q, i].start()
    def s2(q):
        for i, (k, f) in enumerate(order):
            s = owner(k, f)
            if nbs[q]:
                Y[q, i].wait_recv()
                add(lambda a, n: acc.at[s, pl.ds(mb[q] + a, n)], lambda a, n: b2.at[s, pl.ds(lb[q] + a, n)], nbs[q])
            if f == 1:
                X[q, k].start()
    def s3(q):
        for k in (2, 1, 3, 0):
            s = owner(k, 0)
            X[q, k].wait_recv()
            add(lambda a, n: acc.at[s, pl.ds(hs[q] + a, n)], lambda a, n: b3.at[k, pl.ds(lh[q] + a, n)], nh[q])
            if k: Z[q, k].start()
    def s4(q):
        for k in range(1, 4):
            Z[q, k].wait_recv()
        def body(i, _):
            a = mult(i * 16)
            t = acc[me, pl.ds(hs[q] + a, 16)].astype(jnp.float32)
            for k in range(3):
                t += b4[k, pl.ds(lh[q] + a, 16)].astype(jnp.float32)
            fin[pl.ds(hs[q] + a, 16)] = t.astype(BF)
            return _
        lax.fori_loop(0, nh[q] // 16, body, 0)
        A[q].start()
        BX[q].start()
    def s5(q):
        A[q].wait_recv()
        A[q].wait_send()
        add(lambda a, n: fin.at[pl.ds(aa[q] + a, n)], lambda a, n: b5.at[pl.ds(la[q] + a, n)], na[q])
        BX[q].wait_recv()
        F[q].start(); O[q].start()
    st = [s0, s1, s2, s3, s4, s5]
    for t in range(Q + 5):
        if t in ev: ev[t]()
        for i in reversed(range(6)):
            q = t - i
            if 0 <= q < Q:
                st[i](q)
    for q in range(Q):
        F[q].wait(); O[q].wait()
        BX[q].wait_send()
    for d in (C1, Y, X, Z):
        for v in d.values(): v.wait_send()
    e3()

def scatter_grads(g, e, n, chunks, cid):
    Q = len(chunks)
    D = pltpu.SemaphoreType.DMA
    H = sum(h for _, h, _ in chunks); NB = sum(nb for _, _, nb in chunks); NH = H - NB
    V = lambda *s: pltpu.VMEM(s, BF)
    anywhere = pl.BlockSpec(memory_space=pl.ANY)
    near = pl.BlockSpec(memory_space=pltpu.VMEM)
    return pl.pallas_call(
        functools.partial(scatter_kernel, chunks),
        out_shape=(jax.ShapeDtypeStruct(g.shape[1:], g.dtype), jax.ShapeDtypeStruct((4,) + e.shape, e.dtype), jax.ShapeDtypeStruct(n.shape, n.dtype)),
        in_specs=[anywhere, anywhere, near], out_specs=[anywhere, anywhere, near],
        scratch_shapes=[pltpu.VMEM((3,) + n.shape, n.dtype), V(8, H, 512), V(8, H, 512), V(8, NB, 512), V(4, NH, 512), V(3, NH, 512), V(H - 2 * NB, 512), V(H, 512),
            D((Q, 8)), D((Q, 8)), D((Q, 8)), D((Q, 8)), D((Q, 4)), D((Q, 4)), D((Q, 4)), D((Q, 4)), D((Q, 2)), D((Q, 2)), D((Q,)), D((Q,)), D((Q, 8)), D((Q,)),
            D((11,)), D((11,)), D, D((2,)), D((2,))],
        compiler_params=pltpu.CompilerParams(collective_id=cid, has_side_effects=True, vmem_limit_bytes=60 * 2**20),
    )(g, e, n)

def plan(rows, count, share):
    units = rows // 32
    chunks = []
    base = 0
    for i in range(count):
        size = units // count + (1 if i < units % count else 0)
        chunks.append((base, 16 * size, 16 * int(round(size * share))))
        base += 32 * size
    return chunks


def slot_plan(token_ids, shard_rows):
    tokens = token_ids.shape[0]
    owner = token_ids // shard_rows
    local = token_ids - owner * shard_rows
    index = jnp.arange(tokens, dtype=jnp.int32)
    same_id = token_ids[:, None] == token_ids[None, :]
    first = jnp.min(jnp.where(same_id, index[None, :], tokens), axis=1)
    leads = first == index
    same_owner = owner[:, None] == owner[None, :]
    slot = jnp.sum(
        (same_owner & leads[None, :] & (index[None, :] < first[:, None])).astype(jnp.int32), axis=1
    )
    key = jnp.where(slot < SLOTS, owner * SLOTS + slot, 8 * SLOTS)
    wanted = jnp.max(
        jnp.where(
            key[:, None] == jnp.arange(8 * SLOTS, dtype=jnp.int32)[None, :], local[:, None], -1
        ),
        axis=0,
    )
    return key, wanted, jnp.max(slot)


def column_blocks(rows):
    lead, count, width = rows.shape
    return (
        rows.reshape(lead, count, width // D, D).transpose(0, 2, 1, 3).reshape(lead, -1, D)
    )


def pack_weights(attn_in, attn_out, ffn_in, ffn_out, head_master, norm_master):
    layers = jnp.concatenate(
        [column_blocks(attn_in), attn_out, column_blocks(ffn_in), ffn_out], axis=1
    ).astype(jnp.bfloat16)
    norm_rows = jnp.pad(
        norm_master.reshape(10, -1).astype(jnp.bfloat16), ((0, 22), (0, D - norm_master.shape[2]))
    )
    return jnp.concatenate(
        [layers.reshape(-1, D), head_master.astype(jnp.bfloat16), norm_rows], axis=0
    )


def dot_nn(left, right):
    return lax.dot_general(left, right, (((1,), (0,)), ((), ())), preferred_element_type=jnp.float32)


def dot_nt(left, right):
    return lax.dot_general(left, right, (((1,), (1,)), ((), ())), preferred_element_type=jnp.float32)


def dot_tn(left, right):
    return lax.dot_general(left, right, (((0,), (0,)), ((), ())), preferred_element_type=jnp.float32)


def exact_dot(left, right, dims=((1,), (0,))):
    return lax.dot_general(
        left, right, (dims, ((), ())), precision=lax.Precision.HIGHEST, preferred_element_type=jnp.float32
    )


GELU_SCALE = (2.0 / 3.141592653589793) ** 0.5
GELU_CUBE = 0.044715
TILE = 256


def norm_parts(values):
    center = values - jnp.mean(values, axis=-1, keepdims=True)
    inverse = lax.rsqrt(jnp.mean(center * center, axis=-1, keepdims=True) + NORM_EPS)
    return center * inverse, inverse


def norm_back(scaled, inverse, grad_out, gain):
    grad_scaled = grad_out * gain
    mean_grad = jnp.mean(grad_scaled, axis=-1, keepdims=True)
    mean_both = jnp.mean(grad_scaled * scaled, axis=-1, keepdims=True)
    return inverse * (grad_scaled - mean_grad - scaled * mean_both)


def gelu_parts(value):
    bend = jnp.tanh(GELU_SCALE * (value + GELU_CUBE * value * value * value))
    half = 0.5 * (1.0 + bend)
    slope = half + 0.5 * value * (1.0 - bend * bend) * GELU_SCALE * (1.0 + 3.0 * GELU_CUBE * value * value)
    return value * half, slope


def block(w_ref, start):
    return w_ref[:, start : start + 64, :].reshape(D, D)


def down_block(w_ref, j):
    return w_ref[2 * j : 2 * j + 2, 768:1024, :].reshape(D, D)


def fill_distance(far, seg_col_ref, seg_row_ref):
    tokens = far.shape[0]
    def body(i, carry):
        start = pl.multiple_of(i * 64, 64)
        rows = lax.broadcasted_iota(jnp.int32, (64, tokens), 0) + start
        cols = lax.broadcasted_iota(jnp.int32, (64, tokens), 1)
        gap = jnp.abs(rows - cols).astype(jnp.float32)
        same = seg_col_ref[pl.ds(start, 64), :] == seg_row_ref[...]
        far[pl.ds(start, 64), :] = jnp.where(same, gap, jnp.inf)
        return carry
    lax.fori_loop(0, tokens // 64, body, 0)


def forward_kernel(
    first_ref, seg_col_ref, seg_row_ref, valid_ref, w_ref, head_ref, norm_ref,
    low_ref, qkv_ref, lse_ref, mix_ref, one_ref, two_ref, unit_ref, pool_ref, zed_ref,
    x_s, far, acc,
):
    layer = pl.program_id(0)
    tokens = x_s.shape[0]
    tiles = tokens // TILE

    @pl.when(layer == 0)
    def _():
        x_s[...] = first_ref[...].astype(jnp.float32)
        fill_distance(far, seg_col_ref, seg_row_ref)

    def project(i, carry):
        rows = pl.ds(pl.multiple_of(i * TILE, TILE), TILE)
        low = x_s[rows, :].astype(jnp.bfloat16)
        low_ref[0, rows, :] = low
        for j in range(3):
            qkv_ref[0, rows, j * D : (j + 1) * D] = dot_nn(low, block(w_ref, j * 64)).astype(jnp.bfloat16)
        return carry

    lax.fori_loop(0, tiles, project, 0)
    for head in range(HEADS):
        lanes = slice(head * HEAD_DIM, (head + 1) * HEAD_DIM)
        keys = qkv_ref[0, :, D + head * HEAD_DIM : D + (head + 1) * HEAD_DIM]
        vals_t = qkv_ref[0, :, 2 * D + head * HEAD_DIM : 2 * D + (head + 1) * HEAD_DIM].T
        slope = 2.0 ** (-8.0 * (head + 1) / HEADS)
        for i in range(tiles):
            cols = slice(i * TILE, (i + 1) * TILE)
            scores = dot_nt(keys, qkv_ref[0, cols, lanes]) * HEAD_DIM**-0.5 - slope * far[:, cols]
            top = jnp.max(scores, axis=0, keepdims=True)
            raised = jnp.exp(scores - top)
            total = jnp.sum(raised, axis=0, keepdims=True)
            lse_ref[0, head, :, cols] = top + jnp.log(total)
            prob = (raised * (1.0 / total)).astype(jnp.bfloat16)
            mix_ref[0, lanes, cols] = dot_nn(vals_t, prob).astype(jnp.bfloat16)

    acc[...] = dot_tn(mix_ref[0], block(w_ref, 192))

    def feed(i, carry):
        rows = pl.ds(pl.multiple_of(i * TILE, TILE), TILE)
        resid = x_s[rows, :] + acc[rows, :]
        one_ref[0, rows, :] = resid
        at = 4 * layer
        scaled, _ = norm_parts(resid)
        hidden = scaled * norm_ref[pl.ds(at, 1), :] + norm_ref[pl.ds(at + 1, 1), :]
        low = hidden.astype(jnp.bfloat16)
        total = hidden
        for j in range(4):
            gate = dot_nn(low, block(w_ref, 256 + j * 64))
            up = dot_nn(low, block(w_ref, 512 + j * 64))
            bend = jnp.tanh(GELU_SCALE * (gate + GELU_CUBE * gate * gate * gate))
            mid = (0.5 * gate * (1.0 + bend) * up).astype(jnp.bfloat16)
            total = total + dot_nn(mid, down_block(w_ref, j))
        two_ref[0, rows, :] = total
        scaled, _ = norm_parts(total)
        x_s[rows, :] = scaled * norm_ref[pl.ds(at + 2, 1), :] + norm_ref[pl.ds(at + 3, 1), :]
        return carry

    lax.fori_loop(0, tiles, feed, 0)

    @pl.when(layer == LAYERS - 1)
    def _():
        scaled, _ = norm_parts(x_s[...])
        final = scaled * norm_ref[8:9, :] + norm_ref[9:10, :]
        member = members(seg_row_ref, valid_ref)
        counts = jnp.maximum(jnp.sum(member, axis=1, keepdims=True), 1.0)
        pooled = (exact_dot(member, final) / counts).astype(jnp.bfloat16)
        pool_ref[...] = pooled
        zed = dot_nn(pooled, head_ref[...].reshape(D, D))
        zed_ref[...] = zed
        unit = zed * lax.rsqrt(jnp.sum(zed * zed, axis=-1, keepdims=True) + UNIT_EPS)
        for s in range(4):
            for part in range(4):
                unit_ref[4 * s + part : 4 * s + part + 1, :] = unit[s : s + 1, part * 128 : (part + 1) * 128]


def members(seg_row_ref, valid_ref):
    tokens = seg_row_ref.shape[1]
    slot = lax.broadcasted_iota(jnp.int32, (8, tokens), 0)
    return jnp.where((seg_row_ref[...] == slot) & (valid_ref[...] > 0), 1.0, 0.0)


def whole(shape):
    return pl.BlockSpec(shape, lambda i: (0,) * len(shape))


def run_forward(first, seg_col, seg_row, valid, weights, norms):
    tokens = first.shape[0]
    low = jnp.bfloat16
    layered = lambda *s: pl.BlockSpec((1,) + s, lambda i: (i,) + (0,) * len(s))
    return pl.pallas_call(
        forward_kernel,
        grid=(LAYERS,),
        in_specs=[
            whole((tokens, D)), whole((tokens, 1)), whole((1, tokens)), whole((1, tokens)),
            pl.BlockSpec((8, PART, D), lambda i: (0, i, 0)),
            pl.BlockSpec((8, 64, D), lambda i: (0, HEAD_AT // 64, 0)),
            whole(norms.shape),
        ],
        out_specs=[
            layered(tokens, D), layered(tokens, 3 * D), layered(HEADS, 1, tokens), layered(D, tokens),
            layered(tokens, D), layered(tokens, D), whole((16, 128)), whole((8, D)), whole((8, D)),
        ],
        out_shape=[
            jax.ShapeDtypeStruct((LAYERS, tokens, D), low),
            jax.ShapeDtypeStruct((LAYERS, tokens, 3 * D), low),
            jax.ShapeDtypeStruct((LAYERS, HEADS, 1, tokens), jnp.float32),
            jax.ShapeDtypeStruct((LAYERS, D, tokens), low),
            jax.ShapeDtypeStruct((LAYERS, tokens, D), jnp.float32),
            jax.ShapeDtypeStruct((LAYERS, tokens, D), jnp.float32),
            jax.ShapeDtypeStruct((16, 128), jnp.float32),
            jax.ShapeDtypeStruct((8, D), low),
            jax.ShapeDtypeStruct((8, D), jnp.float32),
        ],
        scratch_shapes=[
            pltpu.VMEM((tokens, D), jnp.float32), pltpu.VMEM((tokens, tokens), jnp.float32),
            pltpu.VMEM((tokens, D), jnp.float32),
        ],
        compiler_params=pltpu.CompilerParams(vmem_limit_bytes=60 * 2**20),
    )(first, seg_col, seg_row, valid, weights, weights, norms)


def contrast_kernel(unit_ref, deal_col_ref, deal_row_ref, scale_ref, loss_ref, own_ref, slope_ref, every, ss, rs, ls):
    lin = lax.axis_index("dp") * 4 + lax.axis_index("group")
    peers = [lax.rem(lin + k, 32) for k in range(32)]
    peers = [(p // 4, p % 4) for p in peers]
    entry_barrier(peers[1:])
    copies = [
        pltpu.make_async_remote_copy(
            unit_ref, every.at[lin], ss.at[k], rs.at[k], device_id=peers[k], device_id_type=MESH
        )
        for k in range(1, 32)
    ]
    for copy in copies:
        copy.start()
    own = pltpu.make_async_copy(unit_ref, every.at[lin], ls)
    own.start()
    for copy in copies:
        copy.wait()
    own.wait()
    units = every[...].reshape(512, 128)
    place_at = lax.broadcasted_iota(jnp.int32, (128, 512), 1)
    sorted_units = jnp.concatenate(
        [
            exact_dot(jnp.where(deal_col_ref[...] * 4 + part == place_at, 1.0, 0.0), units)
            for part in range(4)
        ],
        axis=1,
    )
    queries, documents = sorted_units[:64], sorted_units[64:]
    scale = jnp.exp(scale_ref[...])
    logits = scale * exact_dot(queries, documents, ((1,), (1,)))
    row_top = jnp.max(logits, axis=1, keepdims=True)
    row_lse = row_top + jnp.log(jnp.sum(jnp.exp(logits - row_top), axis=1, keepdims=True))
    col_top = jnp.max(logits, axis=0, keepdims=True)
    col_lse = col_top + jnp.log(jnp.sum(jnp.exp(logits - col_top), axis=0, keepdims=True))
    diagonal = jnp.where(
        lax.broadcasted_iota(jnp.int32, (64, 64), 0) == lax.broadcasted_iota(jnp.int32, (64, 64), 1), 1.0, 0.0
    )
    on_diagonal = jnp.sum(logits * diagonal, axis=1, keepdims=True)
    col_sum = jnp.sum(col_lse, axis=1, keepdims=True)
    row_sum = jnp.sum(row_lse, axis=0, keepdims=True)
    loss_ref[...] = 0.5 * (row_sum + col_sum) - jnp.sum(on_diagonal, axis=0, keepdims=True)
    grad_logits = 0.5 * (jnp.exp(logits - row_lse) + jnp.exp(logits - col_lse)) - diagonal
    slope = jnp.sum(grad_logits * logits, axis=1, keepdims=True)
    slope_ref[...] = jnp.sum(slope, axis=0, keepdims=True)
    grad_raw = scale * grad_logits
    grad_queries = exact_dot(grad_raw, documents)
    grad_documents = exact_dot(grad_raw, queries, ((0,), (0,)))
    mine = lax.broadcasted_iota(jnp.int32, (8, 128), 0)
    picks = jnp.where((deal_row_ref[...] == mine + lin * 4) & (mine < 4), 1.0, 0.0)
    own_ref[...] = exact_dot(picks, jnp.concatenate([grad_queries, grad_documents], axis=0))


def run_contrast(unit, deal_order, log_scale, cid):
    sems = pltpu.SemaphoreType.DMA
    one = jax.ShapeDtypeStruct((1, 1), jnp.float32)
    return pl.pallas_call(
        contrast_kernel,
        out_shape=[one, jax.ShapeDtypeStruct((8, D), jnp.float32), one],
        in_specs=[pl.BlockSpec(memory_space=pltpu.VMEM)] * 4,
        out_specs=[pl.BlockSpec(memory_space=pltpu.VMEM)] * 3,
        scratch_shapes=[pltpu.VMEM((32, 16, 128), jnp.float32), sems((32,)), sems((32,)), sems],
        compiler_params=pltpu.CompilerParams(collective_id=cid, has_side_effects=True),
    )(unit, deal_order.reshape(128, 1), deal_order.reshape(1, 128), log_scale.reshape(1, 1))


def backward_kernel(
    own_ref, zed_ref, pool_ref, seg_col_ref, seg_row_ref, valid_ref, w_ref, head_ref, norm_ref,
    low_ref, qkv_ref, lse_ref, mix_ref, one_ref, two_ref, last_ref,
    grad_ref, norm_out_ref, first_ref,
    dx, far, acc, two_s, low_s, mid_s, ups, gates, back,
):
    step = pl.program_id(0)
    tokens = dx.shape[0]
    tiles = tokens // TILE
    low_type = jnp.bfloat16

    @pl.when(step == 0)
    def _():
        fill_distance(far, seg_col_ref, seg_row_ref)
        zed = zed_ref[...]
        square = jnp.sum(zed * zed, axis=-1, keepdims=True) + UNIT_EPS
        inverse = lax.rsqrt(square)
        own = own_ref[...]
        inner = jnp.sum(own * zed, axis=-1, keepdims=True)
        grad_zed = (inverse * (own - zed * (inner / square))).astype(low_type)
        head = head_ref[...].reshape(D, D)
        grad_head = dot_tn(pool_ref[...], grad_zed)
        grad_ref[:, 0:64, :] = grad_head.reshape(8, 64, D).astype(low_type)
        grad_ref[:, 64:96, :] = jnp.zeros((8, 32, D), low_type)
        member = members(seg_row_ref, valid_ref)
        counts = jnp.maximum(jnp.sum(member, axis=1, keepdims=True), 1.0)
        grad_pooled = dot_nt(grad_zed, head) / counts
        grad_final = exact_dot(member, grad_pooled, ((0,), (0,)))
        gain_last = norm_ref[6:7, :]
        stream_scaled, _ = norm_parts(last_ref[0])
        stream = stream_scaled * gain_last + norm_ref[7:8, :]
        scaled, inverse = norm_parts(stream)
        norm_out_ref[0, 0:1, :] = jnp.sum(grad_final * scaled, axis=0, keepdims=True)
        norm_out_ref[0, 1:2, :] = jnp.sum(grad_final, axis=0, keepdims=True)
        dx[...] = norm_back(scaled, inverse, grad_final, norm_ref[8:9, :])

    @pl.when(step > 0)
    def _():
        at = 4 * (LAYERS - step)
        norm_out_ref[0] = jnp.zeros((8, D), jnp.float32)

        def enter(i, carry):
            rows = pl.ds(pl.multiple_of(i * TILE, TILE), TILE)
            scaled, inverse = norm_parts(two_ref[0, rows, :])
            grad = dx[rows, :]
            norm_out_ref[0, 2:3, :] += jnp.sum(grad * scaled, axis=0, keepdims=True)
            norm_out_ref[0, 3:4, :] += jnp.sum(grad, axis=0, keepdims=True)
            grad = norm_back(scaled, inverse, grad, norm_ref[pl.ds(at + 2, 1), :])
            acc[rows, :] = grad
            two_s[rows, :] = grad.astype(low_type)
            scaled, _ = norm_parts(one_ref[0, rows, :])
            hidden = scaled * norm_ref[pl.ds(at, 1), :] + norm_ref[pl.ds(at + 1, 1), :]
            low_s[rows, :] = hidden.astype(low_type)
            return carry

        lax.fori_loop(0, tiles, enter, 0)
        for j in range(4):
            def feed(i, carry):
                rows = pl.ds(pl.multiple_of(i * TILE, TILE), TILE)
                low = low_s[rows, :]
                gate = dot_nn(low, block(w_ref, 256 + j * 64))
                up = dot_nn(low, block(w_ref, 512 + j * 64))
                grad_mid = dot_nt(two_s[rows, :], down_block(w_ref, j))
                value, slope = gelu_parts(gate)
                mid_s[rows, :] = (value * up).astype(low_type)
                grad_gate = (grad_mid * up * slope).astype(low_type)
                grad_up = (grad_mid * value).astype(low_type)
                gates[rows, :] = grad_gate
                ups[rows, :] = grad_up
                acc[rows, :] += dot_nt(grad_gate, block(w_ref, 256 + j * 64)) + dot_nt(
                    grad_up, block(w_ref, 512 + j * 64)
                )
                return carry

            lax.fori_loop(0, tiles, feed, 0)
            grad_ref[2 * j : 2 * j + 2, 768:1024, :] = (
                dot_tn(mid_s[...], two_s[...]).reshape(2, 256, D).astype(low_type)
            )
            grad_ref[:, 256 + j * 64 : 320 + j * 64, :] = (
                dot_tn(low_s[...], gates[...]).reshape(8, 64, D).astype(low_type)
            )
            grad_ref[:, 512 + j * 64 : 576 + j * 64, :] = (
                dot_tn(low_s[...], ups[...]).reshape(8, 64, D).astype(low_type)
            )

        def middle(i, carry):
            rows = pl.ds(pl.multiple_of(i * TILE, TILE), TILE)
            scaled, inverse = norm_parts(one_ref[0, rows, :])
            grad = acc[rows, :]
            norm_out_ref[0, 0:1, :] += jnp.sum(grad * scaled, axis=0, keepdims=True)
            norm_out_ref[0, 1:2, :] += jnp.sum(grad, axis=0, keepdims=True)
            grad = norm_back(scaled, inverse, grad, norm_ref[pl.ds(at, 1), :])
            dx[rows, :] = grad
            low = grad.astype(low_type)
            two_s[rows, :] = low
            mid_s[rows, :] = dot_nt(low, block(w_ref, 192)).astype(low_type)
            return carry

        lax.fori_loop(0, tiles, middle, 0)
        grad_ref[:, 192:256, :] = dot_nn(mix_ref[0], two_s[...]).reshape(8, 64, D).astype(low_type)
        for head in range(HEADS):
            lanes = slice(head * HEAD_DIM, (head + 1) * HEAD_DIM)
            key_lanes = slice(D + head * HEAD_DIM, D + (head + 1) * HEAD_DIM)
            val_lanes = slice(2 * D + head * HEAD_DIM, 2 * D + (head + 1) * HEAD_DIM)
            keys = qkv_ref[0, :, key_lanes]
            keys_t = keys.T
            vals = qkv_ref[0, :, val_lanes]
            slope = 2.0 ** (-8.0 * (head + 1) / HEADS)
            grad_vals = None
            grad_keys = None
            for i in range(tiles):
                cols = slice(i * TILE, (i + 1) * TILE)
                query = qkv_ref[0, cols, lanes]
                grad_mix = mid_s[cols, lanes]
                scores = dot_nt(keys, query) * HEAD_DIM**-0.5 - slope * far[:, cols]
                prob = jnp.exp(scores - lse_ref[0, head, :, cols])
                grad_prob = dot_nt(vals, grad_mix)
                inner = jnp.sum(prob * grad_prob, axis=0, keepdims=True)
                grad_raw = (prob * (grad_prob - inner) * HEAD_DIM**-0.5).astype(low_type)
                back[cols, lanes] = dot_nn(keys_t, grad_raw).T.astype(low_type)
                value_part = dot_nn(prob.astype(low_type), grad_mix)
                key_part = dot_nn(grad_raw, query)
                grad_vals = value_part if grad_vals is None else grad_vals + value_part
                grad_keys = key_part if grad_keys is None else grad_keys + key_part
            back[:, key_lanes] = grad_keys.astype(low_type)
            back[:, val_lanes] = grad_vals.astype(low_type)

        def leave(i, carry):
            rows = pl.ds(pl.multiple_of(i * TILE, TILE), TILE)
            total = dx[rows, :]
            for j in range(3):
                total = total + dot_nt(back[rows, j * D : (j + 1) * D], block(w_ref, j * 64))
            dx[rows, :] = total
            return carry

        lax.fori_loop(0, tiles, leave, 0)
        for j in range(3):
            grad_ref[:, j * 64 : (j + 1) * 64, :] = (
                dot_tn(low_ref[0], back[:, j * D : (j + 1) * D]).reshape(8, 64, D).astype(low_type)
            )

        @pl.when(step == LAYERS)
        def _():
            first_ref[...] = dx[...].astype(low_type)


def run_backward(own, zed, pool, seg_col, seg_row, valid, weights, norms, saved):
    low_x, qkv, lse, mix, one, two = saved
    tokens = low_x.shape[1]
    low = jnp.bfloat16
    pick = lambda i: jnp.minimum(LAYERS - i, LAYERS - 1)
    layered = lambda *s: pl.BlockSpec((1,) + s, lambda i: (pick(i),) + (0,) * len(s))
    return pl.pallas_call(
        backward_kernel,
        grid=(LAYERS + 1,),
        in_specs=[
            whole((8, D)), whole((8, D)), whole((8, D)), whole((tokens, 1)), whole((1, tokens)), whole((1, tokens)),
            pl.BlockSpec((8, PART, D), lambda i: (0, pick(i), 0)),
            pl.BlockSpec((8, 64, D), lambda i: (0, HEAD_AT // 64, 0)),
            whole(norms.shape),
            layered(tokens, D), layered(tokens, 3 * D), layered(HEADS, 1, tokens), layered(D, tokens),
            layered(tokens, D), layered(tokens, D),
            pl.BlockSpec((1, tokens, D), lambda i: (LAYERS - 1, 0, 0)),
        ],
        out_specs=[
            pl.BlockSpec((8, PART, D), lambda i: (0, LAYERS - i, 0)),
            pl.BlockSpec((1, 8, D), lambda i: (LAYERS - i, 0, 0)),
            whole((tokens, D)),
        ],
        out_shape=[
            jax.ShapeDtypeStruct((8, PACKED, D), low),
            jax.ShapeDtypeStruct((LAYERS + 1, 8, D), jnp.float32),
            jax.ShapeDtypeStruct((tokens, D), low),
        ],
        scratch_shapes=[
            pltpu.VMEM((tokens, D), jnp.float32), pltpu.VMEM((tokens, tokens), jnp.float32),
            pltpu.VMEM((tokens, D), jnp.float32), pltpu.VMEM((tokens, D), low), pltpu.VMEM((tokens, D), low),
            pltpu.VMEM((tokens, D), low), pltpu.VMEM((tokens, D), low), pltpu.VMEM((tokens, D), low),
            pltpu.VMEM((tokens, 3 * D), low),
        ],
        compiler_params=pltpu.CompilerParams(vmem_limit_bytes=62 * 2**20),
    )(own, zed, pool, seg_col, seg_row, valid, weights, weights, norms, low_x, qkv, lse, mix, one, two, two)


def total_kernel(v_ref, o_ref, got, mine, ss, rs, ts, us, ls):
    me = lax.axis_index("dp")
    g = lax.axis_index("group")
    lin = me * 4 + g
    to = [lax.rem(lin + k, 32) for k in range(32)]
    peers = [(p // 4, p % 4) for p in to]
    owners = [(lax.rem(me + k, 8), g) for k in range(8)]
    entry_barrier(peers[1:])
    first = [
        pltpu.make_async_remote_copy(
            v_ref.at[owners[k][0] * 4 + g], got.at[k], ss.at[k], rs.at[k], device_id=owners[k], device_id_type=MESH
        )
        for k in range(1, 8)
    ]
    for copy in first:
        copy.start()
    own = pltpu.make_async_copy(v_ref.at[lin], got.at[0], ls.at[0])
    own.start()
    for copy in first:
        copy.wait()
    own.wait()
    mine[...] = jnp.sum(got[...], axis=0)
    second = [
        pltpu.make_async_remote_copy(
            mine, o_ref.at[lin], ts.at[k], us.at[k], device_id=peers[k], device_id_type=MESH
        )
        for k in range(1, 32)
    ]
    for copy in second:
        copy.start()
    own = pltpu.make_async_copy(mine, o_ref.at[lin], ls.at[1])
    own.start()
    for copy in second:
        copy.wait()
    own.wait()


def total(v, cid):
    sems = pltpu.SemaphoreType.DMA
    return pl.pallas_call(
        total_kernel,
        out_shape=jax.ShapeDtypeStruct(v.shape, v.dtype),
        in_specs=[pl.BlockSpec(memory_space=pltpu.VMEM)], out_specs=pl.BlockSpec(memory_space=pltpu.VMEM),
        scratch_shapes=[
            pltpu.VMEM((8,) + v.shape[1:], v.dtype), pltpu.VMEM(v.shape[1:], v.dtype),
            sems((8,)), sems((8,)), sems((32,)), sems((32,)), sems((2,)),
        ],
        compiler_params=pltpu.CompilerParams(collective_id=cid, has_side_effects=True),
    )(v)


BLOCKS = 28
STEP_AT = 28
SUM_AT = 56
NORM_ROW = 57
ROW_TILE = 512
RATES = (
    RATE_SCALE, RATE_SCALE / D**0.5, RATE_SCALE / D**0.5, RATE_SCALE / (D // 8) ** 0.5,
    RATE_SCALE / D**0.5, RATE_SCALE / FF**0.5,
)


def matrices(layer):
    at = layer * PART
    first = 2 + 13 * layer
    return (
        (2, at, 64, 3, first), (3, at + 192, 64, 1, first + 3),
        (4, at + 256, 64, 8, first + 4), (5, at + 768, 256, 1, first + 12),
    )


def turn(row):
    return jnp.broadcast_to(row, (8, row.shape[1])).T[:, 0:1]


def lane_pick(value, lane):
    return jnp.where(lax.broadcasted_iota(jnp.int32, (1, D), 1) == lane, value, 0.0)


def stats_kernel(dense, row_count, *refs):
    if dense:
        full_ref, grads_ref, norm_ref, table_row_ref, rows_ref, down_ref, *outs = refs
    else:
        slot_ref, slot_rows_ref, grads_ref, norm_ref, table_row_ref, rows_ref, down_ref, *outs = refs
    table_ref, table_row_out, stat_ref, rows_out, down_out = outs
    step = pl.program_id(0)

    def put(at, value):
        stat_ref[at // 3, at % 3 : at % 3 + 1, :] = value

    def add(at, value):
        stat_ref[at // 3, at % 3 : at % 3 + 1, :] += value

    @pl.when(step == 0)
    def _():
        stat_ref[...] = jnp.zeros(stat_ref.shape, jnp.float32)
        for row in range(10):
            put(NORM_ROW + row, norm_ref[row // 4, row % 4 : row % 4 + 1, :])
        sums = jnp.zeros((1, D), jnp.float32)
        rows_out[...] = jnp.zeros(rows_out.shape, jnp.float32)

        def part(first, count, blocks, block_at, old):
            squares = [
                grads_ref[first + j * count : first + (j + 1) * count, :].astype(jnp.float32) ** 2 for j in range(blocks)
            ]
            mean = jnp.sum(functools.reduce(jnp.add, squares), axis=-1, keepdims=True) / (blocks * D)
            new = DECAY_RATE * old + (1.0 - DECAY_RATE) * (mean + STATE_EPS)
            inverse = 1.0 / new
            for j in range(blocks):
                put(block_at + j, jnp.sum(squares[j], axis=0, keepdims=True))
                put(STEP_AT + block_at + j, jnp.sum(squares[j] * inverse, axis=0, keepdims=True))
            return new, jnp.sum(new, axis=0, keepdims=True)

        new, count = part(HEAD_AT, 64, 1, 1, rows_ref[:, 6:7])
        rows_out[:, 6:7] = new
        sums += lane_pick(count, 1)
        for layer in range(LAYERS):
            for name, first, rows, blocks, block_at in matrices(layer):
                if name == 5:
                    new, count = part(first, rows, blocks, block_at, down_ref[:, layer : layer + 1])
                    down_out[:, layer : layer + 1] = new
                else:
                    lane = 3 * layer + name - 2
                    new, count = part(first, rows, blocks, block_at, rows_ref[:, lane : lane + 1])
                    rows_out[:, lane : lane + 1] = new
                sums += lane_pick(count, 2 * name - 2 + layer)
        put(SUM_AT, sums)

    index = lax.broadcasted_iota(jnp.int32, (ROW_TILE, 1), 0) + step * ROW_TILE
    if dense:
        grad = jnp.where(index < row_count, full_ref[...], 0.0)
    else:
        picks = jnp.where(index == slot_ref[...], 1.0, 0.0).astype(jnp.bfloat16)
        grad = jnp.dot(picks, slot_rows_ref[...], preferred_element_type=jnp.float32)
    low = grad.astype(jnp.bfloat16)
    table_ref[...] = low
    squares = low.astype(jnp.float32) ** 2
    mean = jnp.mean(squares, axis=-1, keepdims=True)
    mean_row = jnp.broadcast_to(mean, (ROW_TILE, 128)).T[0:1, :]
    new = DECAY_RATE * table_row_ref[...] + (1.0 - DECAY_RATE) * (mean_row + STATE_EPS)
    real = lax.broadcasted_iota(jnp.int32, (1, ROW_TILE), 1) + step * ROW_TILE < row_count
    new = jnp.where(real, new, 1.0)
    table_row_out[...] = new
    add(0, jnp.sum(squares, axis=0, keepdims=True))
    add(STEP_AT, jnp.sum(squares * (1.0 / turn(new)), axis=0, keepdims=True))
    add(SUM_AT, lane_pick(jnp.sum(jnp.where(real, new, 0.0), axis=1, keepdims=True), 0))


def run_stats(dense, heads, grads, norm, table_row, rows, down):
    row_count = table_row.shape[1]
    tile = pl.BlockSpec((ROW_TILE, D), lambda i: (i, 0))
    lane = pl.BlockSpec((1, ROW_TILE), lambda i: (0, i))
    head_specs = [tile] if dense else [whole(v.shape) for v in heads]
    stat = (32, 3, D)
    return pl.pallas_call(
        functools.partial(stats_kernel, dense, row_count),
        grid=(-(-row_count // ROW_TILE),),
        in_specs=head_specs + [whole(grads.shape), whole(norm.shape), lane, whole(rows.shape), whole(down.shape)],
        out_specs=[tile, lane, whole(stat), whole(rows.shape), whole(down.shape)],
        out_shape=[
            jax.ShapeDtypeStruct((row_count, D), jnp.bfloat16), jax.ShapeDtypeStruct(table_row.shape, jnp.float32),
            jax.ShapeDtypeStruct(stat, jnp.float32), jax.ShapeDtypeStruct(rows.shape, jnp.float32),
            jax.ShapeDtypeStruct(down.shape, jnp.float32),
        ],
        compiler_params=pltpu.CompilerParams(vmem_limit_bytes=48 * 2**20),
    )(*heads, grads, norm, table_row, rows, down)


def update_kernel(
    totals, stat_ref, table_ref, embed_ref, table_row_ref, grads_ref, rows_ref, down_ref, top_cols_ref, cols_ref,
    in_ref, mix_ref, gate_ref, low_ref, head_ref,
    embed_out, table_cols_out, head_cols_out, cols_out, in_out, mix_out, gate_out, low_out, head_out, rms_out, factors,
):
    step = pl.program_id(0)

    def stat(at):
        return stat_ref[at // 3, at % 3 : at % 3 + 1, :]

    def mean_of(lane, name):
        return jnp.sum(jnp.where(lax.broadcasted_iota(jnp.int32, (1, D), 1) == lane, stat(SUM_AT), 0.0), axis=1, keepdims=True) / totals[name]

    def columns(block_at, blocks, old, lane, name):
        row_mean = mean_of(lane, name)
        news = []
        steps = 0.0
        for j in range(blocks):
            new = DECAY_RATE * old(j) + (1.0 - DECAY_RATE) * (stat(block_at + j) / totals[name] + STATE_EPS)
            news.append(new)
            steps += jnp.sum(row_mean * stat(STEP_AT + block_at + j) / new, axis=1, keepdims=True)
        rms = jnp.sqrt(steps / (totals[name] * blocks * D))
        scale = -RATES[name] / jnp.maximum(1.0, rms / CLIP_LEVEL)
        return news, row_mean, rms, scale

    @pl.when(step == 0)
    def _():
        news, row_mean, rms, scale = columns(0, 1, lambda j: top_cols_ref[0:1, :], 0, 0)
        table_cols_out[...] = news[0]
        factors[0:1, :] = lax.rsqrt(news[0])
        factors[1:2, :] = jnp.broadcast_to(row_mean, (1, D))
        factors[2:3, :] = jnp.broadcast_to(scale, (1, D))
        all_rms = lane_pick(rms, 0)
        news, row_mean, rms, scale = columns(1, 1, lambda j: top_cols_ref[1:2, :], 1, 1)
        head_cols_out[...] = news[0]
        all_rms += lane_pick(rms, 1)
        row = lax.rsqrt(rows_ref[:, 6:7] / row_mean) * scale
        head_out[...] = head_ref[...] + grads_ref[HEAD_AT : HEAD_AT + 64, :].astype(jnp.float32) * row * lax.rsqrt(news[0])
        for layer in range(LAYERS):
            for name, first, rows, blocks, block_at in matrices(layer):
                col_at = (block_at - 2 - 13 * layer) * D
                old = lambda j: cols_ref[layer : layer + 1, col_at + j * D : col_at + (j + 1) * D]
                news, row_mean, rms, scale = columns(block_at, blocks, old, 2 * name - 2 + layer, name)
                all_rms += lane_pick(rms, 2 * name - 2 + layer)
                lane = 3 * layer + name - 2
                state = down_ref[:, layer : layer + 1] if name == 5 else rows_ref[:, lane : lane + 1]
                row = lax.rsqrt(state / row_mean) * scale
                source, target = ((in_ref, in_out), (mix_ref, mix_out), (gate_ref, gate_out), (low_ref, low_out))[name - 2]
                for j in range(blocks):
                    cols_out[layer : layer + 1, col_at + j * D : col_at + (j + 1) * D] = news[j]
                    span = slice(j * D, (j + 1) * D)
                    grad = grads_ref[first + j * rows : first + (j + 1) * rows, :].astype(jnp.float32)
                    target[layer, :, span] = source[layer, :, span] + grad * row * lax.rsqrt(news[j])
        rms_out[...] = all_rms

    row = lax.rsqrt(turn(table_row_ref[...] / factors[1:2, :ROW_TILE])) * factors[2:3, 0:1]
    embed_out[...] = embed_ref[...] + table_ref[...].astype(jnp.float32) * row * factors[0:1, :]


def run_update(totals, stat, table, embed, table_row, grads, rows, down, top_cols, cols, others):
    row_count = embed.shape[0]
    tile = pl.BlockSpec((ROW_TILE, D), lambda i: (i, 0))
    lane = pl.BlockSpec((1, ROW_TILE), lambda i: (0, i))
    shape = lambda v: jax.ShapeDtypeStruct(v.shape, jnp.float32)
    one = jax.ShapeDtypeStruct((1, D), jnp.float32)
    outs = [shape(embed), one, one, shape(cols)] + [shape(v) for v in others] + [one]
    return pl.pallas_call(
        functools.partial(update_kernel, totals),
        grid=(-(-row_count // ROW_TILE),),
        in_specs=[whole(stat.shape), tile, tile, lane]
        + [whole(v.shape) for v in (grads, rows, down, top_cols, cols)]
        + [whole(v.shape) for v in others],
        out_specs=[tile] + [whole(v.shape) for v in outs[1:]],
        out_shape=outs,
        scratch_shapes=[pltpu.VMEM((8, D), jnp.float32)],
        compiler_params=pltpu.CompilerParams(vmem_limit_bytes=48 * 2**20),
    )(stat, table, embed, table_row, grads, rows, down, top_cols, cols, *others)


def fast_shards(
    token_ids,
    seq_lengths,
    valid_mask,
    deal_order,
    log_scale,
    embed_master,
    attn_in,
    attn_out,
    ffn_in,
    ffn_out,
    head_master,
    norm_master,
    embed_rows,
    head_rows,
    layer_rows,
    ffn_out_rows,
    layer_cols,
    embed_head_cols,
    norm_state,
    scale_state,
):
    tokens = token_ids.shape[0]
    shard_rows = embed_master.shape[0]
    my_dp = lax.axis_index("dp")
    position = jnp.arange(tokens, dtype=jnp.int32)
    bounds = jnp.cumsum(seq_lengths[0])
    segment = jnp.sum((position[:, None] >= bounds[None, :]).astype(jnp.int32), axis=1)

    key, wanted, most = slot_plan(token_ids, shard_rows)
    asks = jnp.concatenate(
        [wanted.reshape(8, 1, SLOTS), jnp.broadcast_to(most, (8, 1, 128 - SLOTS))], axis=2
    ).astype(jnp.int32)
    packed = pack_weights(attn_in, attn_out, ffn_in, ffn_out, head_master, norm_master)
    weights, got_rows, asked = gather_weights(packed, asks, embed_master, plan(PACKED, 4, 0.36), 0)
    crowded = jnp.max(asked[:, :, 0, SLOTS:]) >= SLOTS

    def dense_rows():
        table = lax.all_gather(embed_master.astype(jnp.bfloat16), "dp", axis=0, tiled=True)
        return jnp.take(table, token_ids, axis=0)

    def slot_rows():
        return jnp.take(got_rows.reshape(-1, D), jnp.minimum(key, 8 * SLOTS - 1), axis=0)

    stream = lax.cond(crowded, dense_rows, slot_rows)
    norms = jnp.pad(
        weights[:, NORM_AT : NORM_AT + 10, :64].transpose(1, 0, 2).reshape(10, D).astype(jnp.float32),
        ((0, 6), (0, 0)),
    )
    seg_col, seg_row = segment.reshape(-1, 1), segment.reshape(1, -1)
    valid_row = valid_mask.reshape(1, -1)
    *saved, unit_parts, pooled_low, head_out = run_forward(
        stream, seg_col, seg_row, valid_row, weights, norms
    )
    loss_value, own_rows, grad_scale = run_contrast(unit_parts, deal_order, log_scale, 1)
    loss_value, grad_scale = loss_value[0, 0], grad_scale[0]
    all_grads, norm_parts_out, grad_first = run_backward(
        own_rows, head_out, pooled_low, seg_col, seg_row, valid_row, weights, norms, saved
    )
    slot_grads = jnp.dot(
        (jnp.arange(8 * SLOTS, dtype=jnp.int32)[:, None] == key[None, :]).astype(jnp.bfloat16),
        grad_first,
        preferred_element_type=jnp.float32,
    ).astype(jnp.bfloat16)
    shard_grads, table_rows, norm_sum = scatter_grads(
        all_grads, slot_grads.reshape(8, SLOTS, D), norm_parts_out, plan(PACKED, 4, 0.29), 2
    )
    table_slots = asked[:, :, 0, :SLOTS].reshape(1, -1)
    table_row = embed_rows.reshape(1, -1)
    row_state = jnp.pad(
        jnp.concatenate([layer_rows.reshape(6, -1), head_rows.reshape(1, -1)], axis=0), ((0, 1), (0, 0))
    ).T
    shared = (shard_grads, norm_sum, table_row, row_state, ffn_out_rows.T)

    def dense_stats():
        full = jnp.zeros((shard_rows * 8, D), jnp.float32).at[token_ids].add(
            grad_first.astype(jnp.float32)
        )
        full = lax.psum_scatter(full, "dp", scatter_dimension=0, tiled=True)
        return run_stats(True, (lax.psum(full, "group"),), *shared)

    def slot_stats():
        return run_stats(False, (table_slots, table_rows.reshape(-1, D)), *shared)

    table_grad, table_row_new, stats, rows_new, down_new = lax.cond(
        crowded, dense_stats, slot_stats
    )
    sums = total(stats, 3)
    totals = (VOCAB, D, D, D, D, FF)
    (
        new_embed, new_table_cols, new_head_cols, new_cols, new_in, new_mix, new_gate, new_low, new_head, rms_row,
    ) = run_update(
        totals, sums, table_grad, embed_master, table_row_new, shard_grads, rows_new, down_new,
        embed_head_cols, layer_cols, (attn_in, attn_out, ffn_in, ffn_out, head_master),
    )
    norm_grad = sums.reshape(-1, D)[NORM_ROW : NORM_ROW + 10].reshape(2 * LAYERS + 1, 2, D)
    shard_norm = lax.dynamic_slice_in_dim(norm_grad, my_dp * norm_state.shape[2], norm_state.shape[2], 2)
    norm_delta, norm_second = unfactored(shard_norm, norm_state)
    scale_delta, scale_state_new = unfactored(grad_scale, scale_state)
    state_new = rows_new.T
    return (
        loss_value,
        new_embed,
        new_in,
        new_mix,
        new_gate,
        new_low,
        new_head,
        norm_master + norm_delta,
        log_scale + scale_delta,
        table_row_new[0],
        state_new[6],
        state_new[:6].reshape(layer_rows.shape),
        down_new.T,
        new_cols,
        new_table_cols[0],
        new_head_cols[0],
        norm_second,
        scale_state_new,
        rms_row[0, :10],
    )


def solution(mesh):
    in_specs = (
        P(("dp", "group")),
        P(("dp", "group"), None),
        P(("dp", "group")),
        P(),
        P(),
        P("dp", None),
        P(None, "dp", None),
        P(None, "dp", None),
        P(None, "dp", None),
        P(None, "dp", None),
        P("dp", None),
        P(None, None, "dp"),
        P("dp"),
        P("dp"),
        P(None, None, "dp"),
        P(None, "dp"),
        P(),
        P(),
        P(None, None, "dp"),
        P(),
    )
    out_specs = (
        P(),
        P("dp", None),
        P(None, "dp", None),
        P(None, "dp", None),
        P(None, "dp", None),
        P(None, "dp", None),
        P("dp", None),
        P(None, None, "dp"),
        P(),
        P("dp"),
        P("dp"),
        P(None, None, "dp"),
        P(None, "dp"),
        P(),
        P(),
        P(),
        P(None, None, "dp"),
        P(),
        P(),
    )
    body = fast_shards if dict(mesh.shape) == {"dp": 8, "group": 4} else shards
    return jax.shard_map(body, mesh=mesh, in_specs=in_specs, out_specs=out_specs, check_vma=False)
```

```python
import functools

import jax
import jax.numpy as jnp
from jax import lax
from jax.experimental import pallas as pl
from jax.experimental.pallas import tpu as pltpu
from jax.sharding import PartitionSpec as P

D = 512
HEADS = 8
HEAD_DIM = 64
FF = 2048
VOCAB = 30528
LAYERS = 2


NORM_EPS = 1e-06
UNIT_EPS = 1e-06
STATE_EPS = 1e-30
DECAY_RATE = 0.5
CLIP_LEVEL = 0.05
RATE_SCALE = 10.0
NORM_RATE = 0.1


def layer_norm(values, gain_vec, shift_vec):
    center = values - jnp.mean(values, axis=-1, keepdims=True)
    spread = jnp.mean(center * center, axis=-1, keepdims=True)
    return center * lax.rsqrt(spread + NORM_EPS) * gain_vec + shift_vec


def geglu(joined):
    half_width = joined.shape[-1] // 2
    return jax.nn.gelu(joined[:, :half_width]) * joined[:, half_width:]


def alibi_slopes(head_count):
    return 2.0 ** (-8.0 * (jnp.arange(head_count).astype(jnp.float32) + 1.0) / head_count)


def normalize(vectors):
    return vectors * lax.rsqrt(jnp.sum(vectors * vectors, axis=-1, keepdims=True) + UNIT_EPS)


def contrast(unit_all, scale_arg, deal_order):
    pair_count = deal_order.shape[0] // 2
    queries = jnp.take(unit_all, deal_order[:pair_count], axis=0)
    documents = jnp.take(unit_all, deal_order[pair_count:], axis=0)
    logits = jnp.exp(scale_arg[0]) * jnp.matmul(
        queries, documents.T, precision=lax.Precision.HIGHEST
    )
    by_row = jax.nn.logsumexp(logits, axis=1)
    by_column = jax.nn.logsumexp(logits, axis=0)
    return jnp.sum(0.5 * (by_row + by_column) - jnp.diagonal(logits))


def unfactored(grad_full, state):
    state_new = DECAY_RATE * state + (1.0 - DECAY_RATE) * (grad_full * grad_full + STATE_EPS)
    return (-NORM_RATE * grad_full * lax.rsqrt(state_new), state_new)


def block_scores(query_rows, key_all, seg_rows, segment, head_count):
    row_count = query_rows.shape[0]
    raw_scores = jnp.einsum("thc,shc->hts", query_rows, key_all, preferred_element_type=jnp.float32)
    row_pos = jnp.arange(row_count, dtype=jnp.int32)
    col_pos = jnp.arange(key_all.shape[0], dtype=jnp.int32)
    distance = jnp.abs(row_pos[:, None] - col_pos[None, :]).astype(jnp.float32)
    scores = (
        raw_scores * HEAD_DIM ** (-0.5) + -alibi_slopes(head_count)[:, None, None] * distance[None]
    )
    same_seq = seg_rows[:, None] == segment[None, :]
    return jnp.where(same_seq[None], scores, -jnp.inf)


def split_qkv(qkv_low, head_count):
    tokens = qkv_low.shape[0]
    split_heads = qkv_low.reshape(tokens, 3, head_count, qkv_low.shape[1] // (3 * head_count))
    return (split_heads[:, 0], split_heads[:, 1], split_heads[:, 2])


def attend(qkv_low, segment, head_count):
    model_width = qkv_low.shape[1] // 3
    query_all, key_all, value_all = split_qkv(qkv_low, head_count)
    scores = block_scores(query_all, key_all, segment, segment, head_count)
    row_max = jnp.max(scores, axis=-1, keepdims=True)
    exponent = jnp.exp(scores - row_max)
    row_total = jnp.sum(exponent, axis=-1, keepdims=True)
    prob_low = (exponent / row_total).astype(jnp.bfloat16)
    mixed_list = jnp.einsum(
        "hts,shc->thc", prob_low, value_all, preferred_element_type=jnp.float32
    ).reshape(-1, model_width)
    lse_list = row_max[..., 0] + jnp.log(row_total[..., 0])
    return (mixed_list, lse_list)


def attend_back(qkv_low, segment, head_count, lse_all, grad_mixed):
    tokens = qkv_low.shape[0]
    query_all, key_all, value_all = split_qkv(qkv_low, head_count)
    grad_out = grad_mixed.reshape(tokens, head_count, -1)
    block_rows = min(tokens, 512)
    scores = block_scores(query_all, key_all, segment, segment, head_count)
    prob_full = jnp.exp(scores - lse_all[:, 0:block_rows, None])
    grad_value = jnp.einsum(
        "hts,thc->shc", prob_full.astype(jnp.bfloat16), grad_out, preferred_element_type=jnp.float32
    )
    grad_prob = jnp.einsum("thc,shc->hts", grad_out, value_all, preferred_element_type=jnp.float32)
    inner = jnp.sum(prob_full * grad_prob, axis=-1, keepdims=True)
    grad_raw = (prob_full * (grad_prob - inner) * HEAD_DIM ** (-0.5)).astype(jnp.bfloat16)
    query_list = jnp.einsum("hts,shc->thc", grad_raw, key_all, preferred_element_type=jnp.float32)
    grad_key = jnp.einsum("hts,thc->shc", grad_raw, query_all, preferred_element_type=jnp.float32)
    return (
        jnp.stack([query_list, grad_key, grad_value], axis=1)
        .reshape(tokens, -1)
        .astype(jnp.bfloat16)
    )


def shards(
    token_ids,
    seq_lengths,
    valid_mask,
    deal_order,
    log_scale,
    embed_master,
    attn_in,
    attn_out,
    ffn_in,
    ffn_out,
    head_master,
    norm_master,
    embed_rows,
    head_rows,
    layer_rows,
    ffn_out_rows,
    layer_cols,
    embed_head_cols,
    norm_state,
    scale_state,
):
    tokens = token_ids.shape[0]
    model_width = embed_master.shape[1]
    seq_count = seq_lengths.shape[1]
    head_count = HEADS
    position = jnp.arange(tokens, dtype=jnp.int32)
    bounds = jnp.cumsum(seq_lengths[0])
    segment = jnp.sum((position[:, None] >= bounds[None, :]).astype(jnp.int32), axis=1)
    piece_rows = lax.all_gather(embed_master.astype(jnp.bfloat16), "dp", axis=0, tiled=True)
    local_idx = token_ids
    inside = (local_idx >= 0) & (local_idx < piece_rows.shape[0])
    picked = jnp.take(piece_rows, jnp.clip(local_idx, 0, piece_rows.shape[0] - 1), axis=0).astype(
        jnp.float32
    )
    stream = jnp.where(inside[:, None], picked, 0.0)
    w_qkv, w_attn, w_gate_up, w_down, w_head, norm_low = (
        lax.all_gather(attn_in.astype(jnp.bfloat16), "dp", axis=1, tiled=True),
        lax.all_gather(attn_out.astype(jnp.bfloat16), "dp", axis=1, tiled=True),
        lax.all_gather(ffn_in.astype(jnp.bfloat16), "dp", axis=1, tiled=True),
        lax.all_gather(ffn_out.astype(jnp.bfloat16), "dp", axis=1, tiled=True),
        lax.all_gather(head_master.astype(jnp.bfloat16), "dp", axis=0, tiled=True),
        lax.all_gather(norm_master.astype(jnp.bfloat16), "dp", axis=2, tiled=True),
    )
    norms = norm_low.astype(jnp.float32)
    kept_list = []
    for layer_idx in range(LAYERS):
        stream_low = stream.astype(jnp.bfloat16)
        qkv_low = jnp.dot(stream_low, w_qkv[layer_idx], preferred_element_type=jnp.float32).astype(
            jnp.bfloat16
        )
        mixed_heads, lse_all = attend(qkv_low, segment, head_count)
        mixed_low = mixed_heads.astype(jnp.bfloat16)
        resid_one = stream + jnp.dot(
            mixed_low, w_attn[layer_idx], preferred_element_type=jnp.float32
        )
        normed = layer_norm(resid_one, norms[2 * layer_idx, 0], norms[2 * layer_idx, 1])
        normed_low = normed.astype(jnp.bfloat16)
        joined = jnp.dot(normed_low, w_gate_up[layer_idx], preferred_element_type=jnp.float32)
        hidden_low = geglu(joined).astype(jnp.bfloat16)
        resid_two = normed + jnp.dot(
            hidden_low, w_down[layer_idx], preferred_element_type=jnp.float32
        )
        kept_list.append(
            (
                stream_low,
                qkv_low,
                lse_all,
                mixed_low,
                resid_one,
                normed_low,
                joined,
                hidden_low,
                resid_two,
            )
        )
        stream = layer_norm(resid_two, norms[2 * layer_idx + 1, 0], norms[2 * layer_idx + 1, 1])
    final = layer_norm(stream, norms[2 * LAYERS, 0], norms[2 * LAYERS, 1])
    member = (
        (segment[None, :] == jnp.arange(seq_count, dtype=jnp.int32)[:, None])
        & (valid_mask[None, :] > 0)
    ).astype(jnp.float32)
    counts = jnp.maximum(jnp.sum(member, axis=1), 1.0)
    pooled = jnp.matmul(member, final, precision=lax.Precision.HIGHEST) / counts[:, None]
    pooled_low = pooled.astype(jnp.bfloat16)
    head_out = jnp.dot(pooled_low, w_head, preferred_element_type=jnp.float32)
    unit_vecs, unit_back = jax.vjp(normalize, head_out)
    unit_every = lax.all_gather(unit_vecs, ("dp", "group"), axis=0, tiled=True)
    loss_value, loss_back = jax.vjp(
        lambda unit_all, scale_arg: contrast(unit_all, scale_arg, deal_order), unit_every, log_scale
    )
    grad_units, grad_scale = loss_back(jnp.ones_like(loss_value))
    own_rows = lax.dynamic_slice_in_dim(
        grad_units, lax.axis_index(("dp", "group")) * seq_count, seq_count, 0
    )
    grad_head_out = unit_back(own_rows)[0].astype(jnp.bfloat16)
    grad_head = jnp.dot(pooled_low.T, grad_head_out, preferred_element_type=jnp.float32)
    grad_pooled = jnp.dot(grad_head_out, w_head.T, preferred_element_type=jnp.float32)
    grad_final = jnp.matmul(
        member.T, grad_pooled / counts[:, None], precision=lax.Precision.HIGHEST
    )
    final_back = jax.vjp(layer_norm, stream, norms[2 * LAYERS, 0], norms[2 * LAYERS, 1])[1]
    grad_stream, gain_last, shift_last = final_back(grad_final)
    norm_grads = [None] * (2 * LAYERS + 1)
    norm_grads[2 * LAYERS] = jnp.stack([gain_last, shift_last])
    qkv_grads = [None] * LAYERS
    attn_grads = [None] * LAYERS
    gate_grads = [None] * LAYERS
    down_grads = [None] * LAYERS
    for layer_idx in reversed(range(LAYERS)):
        (
            stream_low,
            qkv_low,
            lse_all,
            mixed_low,
            resid_one,
            normed_low,
            joined,
            hidden_low,
            resid_two,
        ) = kept_list[layer_idx]
        norm_two_back = jax.vjp(
            layer_norm, resid_two, norms[2 * layer_idx + 1, 0], norms[2 * layer_idx + 1, 1]
        )[1]
        grad_two, gain_two, shift_two = norm_two_back(grad_stream)
        norm_grads[2 * layer_idx + 1] = jnp.stack([gain_two, shift_two])
        grad_branch = grad_two.astype(jnp.bfloat16)
        down_grads[layer_idx] = jnp.dot(
            hidden_low.T, grad_branch, preferred_element_type=jnp.float32
        )
        grad_hidden = jnp.dot(grad_branch, w_down[layer_idx].T, preferred_element_type=jnp.float32)
        grad_joined = jax.vjp(geglu, joined)[1](grad_hidden)[0].astype(jnp.bfloat16)
        gate_grads[layer_idx] = jnp.dot(
            normed_low.T, grad_joined, preferred_element_type=jnp.float32
        )
        grad_normed = grad_two + jnp.dot(
            grad_joined, w_gate_up[layer_idx].T, preferred_element_type=jnp.float32
        )
        norm_one_back = jax.vjp(
            layer_norm, resid_one, norms[2 * layer_idx, 0], norms[2 * layer_idx, 1]
        )[1]
        grad_one, gain_one, shift_one = norm_one_back(grad_normed)
        norm_grads[2 * layer_idx] = jnp.stack([gain_one, shift_one])
        grad_attended = grad_one.astype(jnp.bfloat16)
        attn_grads[layer_idx] = jnp.dot(
            mixed_low.T, grad_attended, preferred_element_type=jnp.float32
        )
        grad_mixed = jnp.dot(
            grad_attended, w_attn[layer_idx].T, preferred_element_type=jnp.float32
        ).astype(jnp.bfloat16)
        grad_qkv_low = attend_back(qkv_low, segment, head_count, lse_all, grad_mixed)
        qkv_grads[layer_idx] = jnp.dot(
            stream_low.T, grad_qkv_low, preferred_element_type=jnp.float32
        )
        grad_stream = grad_one + jnp.dot(
            grad_qkv_low, w_qkv[layer_idx].T, preferred_element_type=jnp.float32
        )
    row_count = embed_master.shape[0] * lax.axis_size("dp")
    local_idx = token_ids
    inside = (local_idx >= 0) & (local_idx < row_count)
    slot_idx = jnp.where(inside, local_idx, row_count)
    embed_grad = lax.psum_scatter(
        jnp.zeros((row_count, model_width), jnp.float32).at[slot_idx].add(grad_stream, mode="drop"),
        "dp",
        scatter_dimension=0,
        tiled=True,
    )
    grad_qkv = jnp.stack(qkv_grads)
    grad_attn = jnp.stack(attn_grads)
    grad_gate_up = jnp.stack(gate_grads)
    grad_down = jnp.stack(down_grads)
    grad_norm = jnp.stack(norm_grads)
    owned = (
        lax.psum_scatter(grad_qkv, "dp", scatter_dimension=1, tiled=True),
        lax.psum_scatter(grad_attn, "dp", scatter_dimension=1, tiled=True),
        lax.psum_scatter(grad_gate_up, "dp", scatter_dimension=1, tiled=True),
        lax.psum_scatter(grad_down, "dp", scatter_dimension=1, tiled=True),
        lax.psum_scatter(grad_head, "dp", scatter_dimension=0, tiled=True),
        lax.psum_scatter(grad_norm, "dp", scatter_dimension=2, tiled=True),
    )
    shard_qkv, shard_attn, shard_gate_up, shard_down, shard_head, shard_norm, shard_embed = (
        lax.psum((owned[0], owned[1], owned[2], owned[3], owned[4], owned[5], embed_grad), "group")
    )
    grad_list = [
        shard_embed[None],
        shard_head[None],
        shard_qkv,
        shard_attn,
        shard_gate_up,
        shard_down,
    ]
    master_list = [embed_master[None], head_master[None], attn_in, attn_out, ffn_in, ffn_out]
    state_list = [
        embed_rows[None],
        head_rows[None],
        layer_rows[:, 0],
        layer_rows[:, 1],
        layer_rows[:, 2],
        ffn_out_rows,
    ]
    col_list = [
        embed_head_cols[0:1],
        embed_head_cols[1:2],
        layer_cols[:, : 3 * D],
        layer_cols[:, 3 * D : 4 * D],
        layer_cols[:, 4 * D : 4 * D + 2 * FF],
        layer_cols[:, 4 * D + 2 * FF :],
    ]
    total_rows = [VOCAB, D, D, D, D, FF]
    wide_rate = RATE_SCALE / D**0.5
    rates = [
        RATE_SCALE,
        wide_rate,
        wide_rate,
        RATE_SCALE / (D // 8) ** 0.5,
        wide_rate,
        RATE_SCALE / FF**0.5,
    ]
    square_list = [grad_part * grad_part for grad_part in grad_list]
    rows_new = [
        DECAY_RATE * state_list[entry_idx]
        + (1.0 - DECAY_RATE) * (jnp.mean(square_list[entry_idx], axis=-1) + STATE_EPS)
        for entry_idx in range(6)
    ]
    col_parts = jnp.concatenate(
        [jnp.sum(square_part, axis=1).reshape(-1) for square_part in square_list]
    )
    row_parts = jnp.concatenate([jnp.sum(row_part, axis=-1) for row_part in rows_new])
    col_sum, row_sum = lax.psum((col_parts, row_parts), "dp")
    row_means = []
    lead_start = 0
    for entry_idx in range(6):
        lead_count = grad_list[entry_idx].shape[0]
        row_means.append(row_sum[lead_start : lead_start + lead_count] / total_rows[entry_idx])
        lead_start = lead_start + lead_count
    cols_new = []
    steps_all = []
    col_start = 0
    for entry_idx in range(6):
        lead_count = grad_list[entry_idx].shape[0]
        col_width = grad_list[entry_idx].shape[2]
        col_full = col_sum[col_start : col_start + lead_count * col_width].reshape(
            lead_count, col_width
        )
        col_state_new = DECAY_RATE * col_list[entry_idx] + (1.0 - DECAY_RATE) * (
            col_full / total_rows[entry_idx] + STATE_EPS
        )
        cols_new.append(col_state_new)
        steps_all.append(
            grad_list[entry_idx]
            * lax.rsqrt(
                rows_new[entry_idx][:, :, None]
                * col_state_new[:, None, :]
                / row_means[entry_idx][:, None, None]
            )
        )
        col_start = col_start + lead_count * col_width
    step_squares = []
    step_parts = jnp.concatenate(
        [jnp.sum(step_dir * step_dir, axis=(1, 2)) for step_dir in steps_all]
    )
    step_sum = lax.psum(step_parts, "dp")
    lead_start = 0
    for entry_idx in range(6):
        lead_count = grad_list[entry_idx].shape[0]
        step_squares.append(step_sum[lead_start : lead_start + lead_count])
        lead_start = lead_start + lead_count
    new_weights = []
    rms_list = []
    for entry_idx in range(6):
        cell_count = total_rows[entry_idx] * grad_list[entry_idx].shape[2]
        step_rms = jnp.sqrt(step_squares[entry_idx] / cell_count)
        rms_list.append(step_rms)
        delta = (
            -rates[entry_idx]
            * steps_all[entry_idx]
            / jnp.maximum(1.0, step_rms / CLIP_LEVEL)[:, None, None]
        )
        new_weights.append(master_list[entry_idx] + delta)
    norm_delta, norm_second = unfactored(shard_norm, norm_state)
    scale_delta, scale_state_new = unfactored(grad_scale, scale_state)
    return (
        loss_value,
        new_weights[0][0],
        new_weights[2],
        new_weights[3],
        new_weights[4],
        new_weights[5],
        new_weights[1][0],
        norm_master + norm_delta,
        log_scale + scale_delta,
        rows_new[0][0],
        rows_new[1][0],
        jnp.stack([rows_new[2], rows_new[3], rows_new[4]], axis=1),
        rows_new[5],
        jnp.concatenate([cols_new[2], cols_new[3], cols_new[4], cols_new[5]], axis=1),
        cols_new[0][0],
        cols_new[1][0],
        norm_second,
        scale_state_new,
        jnp.concatenate(rms_list),
    )


SLOTS = 80
PART = 1024
HEAD_AT = 2 * PART
NORM_AT = HEAD_AT + 64
PACKED = NORM_AT + 32


MESH = pl.DeviceIdType.MESH
BF=jnp.bfloat16

def place():
    dp = lax.axis_index("dp"); g = lax.axis_index("group")
    return dp // 2, dp % 2, g // 2, g % 2

def dev(z, x, y, c):
    return (z * 2 + x, y * 2 + c)

def entry_barrier(peers):
    bar = pltpu.get_barrier_semaphore()
    for p in peers:
        pl.semaphore_signal(bar, inc=1, device_id=p, device_id_type=MESH)
    pl.semaphore_wait(bar, len(peers))

def mult(v, m=16):
    return pl.multiple_of(v, m)

def gather_kernel(chunks, w_ref, ask_ref, table_ref, ag_ref, got_ref, asks_ref, table, picked, rows_s,
                  zs, zr, xs, xr, ys, yr, cs, cr, ls, es, er, qs, qr):
    z, x, y, c = place()
    me = z * 2 + x
    g = y * 2 + c
    g2 = (1 - y) * 2 + c
    ep = [(lax.rem(me + k, 8), g) for k in range(8)]
    zp = [dev((z + k) % 4, x, y, c) for k in range(4)]
    xp, yp, cp = dev(z, 1 - x, y, c), dev(z, x, 1 - y, c), dev(z, x, y, 1 - c)
    entry_barrier(ep[1:] + [yp, cp])
    Q = len(chunks)
    hs = [mult(b + c * h + y * nb) for b, h, nb in chunks]
    nh = [h - nb for b, h, nb in chunks]
    bs = [mult(b + c * h + y * (h - nb)) for b, h, nb in chunks]
    nbs = [nb for b, h, nb in chunks]
    cb = [mult(b + c * h) for b, h, nb in chunks]
    nc = [h for b, h, nb in chunks]
    def rc(src, dst, s, r, d):
        return pltpu.make_async_remote_copy(src, dst, s, r, device_id=d, device_id_type=MESH)
    def shard(k, f):
        return ((z + 4 - k) % 4) * 2 + (x if f == 0 else 1 - x)
    qc = [rc(ask_ref.at[ep[k][0]], asks_ref.at[g, me], qs.at[k], qr.at[k], ep[k]) for k in range(1, 8)]
    for copy in qc:
        copy.start()
    mine = pltpu.make_async_copy(ask_ref.at[me], asks_ref.at[g, me], ls.at[0])
    mine.start()
    near = pltpu.make_async_copy(table_ref, table.at[pl.ds(0, table_ref.shape[0])], ls.at[1])
    near.start()
    qy = rc(asks_ref.at[g], asks_ref.at[g], qs.at[8], qr.at[8], yp)
    qcc = rc(asks_ref.at[g], asks_ref.at[g], qs.at[9], qr.at[9], cp)
    qd = rc(asks_ref.at[g2], asks_ref.at[g2], qs.at[10], qr.at[10], cp)
    own = pltpu.make_async_copy(w_ref, ag_ref.at[me], ls.at[2])
    own.start()
    kept = pltpu.make_async_copy(rows_s.at[me], got_ref.at[me], ls.at[3])
    ec = [rc(rows_s.at[ep[k][0]], got_ref.at[me], es.at[k], er.at[k], ep[k]) for k in range(1, 8)]
    def pick_rows():
        mine.wait()
        for copy in qc:
            copy.wait_recv()
        qy.start()
        qcc.start()
        wanted = asks_ref[pl.ds(g, 1)].reshape(8, 128).astype(jnp.float32).T
        near.wait()
        depth = table.shape[0] // 5
        table[pl.ds(table_ref.shape[0], table.shape[0] - table_ref.shape[0]), :] = jnp.zeros(
            (table.shape[0] - table_ref.shape[0], 512), jnp.float32
        )
        picked[...] = jnp.zeros(picked.shape, jnp.float32)
        ramp = lax.broadcasted_iota(jnp.int32, (SLOTS, depth), 1).astype(jnp.float32)
        def body(i, carry):
            start = pl.multiple_of(i * depth, depth)
            low = table[pl.ds(start, depth), :].astype(BF)
            shifted = ramp + (i * depth).astype(jnp.float32)
            for r in range(8):
                hot = jnp.where(wanted[:SLOTS, r : r + 1] == shifted, 1.0, 0.0).astype(BF)
                picked[r] += jnp.dot(hot, low, preferred_element_type=jnp.float32)
            return carry
        lax.fori_loop(0, 5, body, 0)
        rows_s[...] = picked[...].astype(BF)
        kept.start()
        for copy in ec:
            copy.start()
    zc = {}; xc = {}; yc = {}; cc = {}
    for q in range(Q):
        for k in range(1, 4):
            zc[q, k] = rc(w_ref.at[pl.ds(hs[q], nh[q])], ag_ref.at[me, pl.ds(hs[q], nh[q])], zs.at[q, k], zr.at[q, k], zp[k])
        for k in range(4):
            src = w_ref.at[pl.ds(hs[q], nh[q])] if k == 0 else ag_ref.at[shard(k, 0), pl.ds(hs[q], nh[q])]
            xc[q, k] = rc(src, ag_ref.at[shard(k, 0), pl.ds(hs[q], nh[q])], xs.at[q, k], xr.at[q, k], xp)
        for k in range(4):
            for f in range(2):
                if k == 0 and f == 0: continue
                s = shard(k, f)
                yc[q, k, f] = rc(ag_ref.at[s, pl.ds(bs[q], nbs[q])], ag_ref.at[s, pl.ds(bs[q], nbs[q])], ys.at[q, 2 * k + f], yr.at[q, 2 * k + f], yp)
                cc[q, k, f] = rc(ag_ref.at[s, pl.ds(cb[q], nc[q])], ag_ref.at[s, pl.ds(cb[q], nc[q])], cs.at[q, 2 * k + f], cr.at[q, 2 * k + f], cp)
    def s0(q):
        for k in (2, 1, 3):
            zc[q, k].start()
        xc[q, 0].start()
    def s1(q):
        for k in (1, 3, 2):
            zc[q, k].wait_recv()
            xc[q, k].start()
            yc[q, k, 0].start()
    def s2(q):
        for k in (0, 1, 3, 2):
            xc[q, k].wait_recv()
            yc[q, k, 1].start()
    def s3(q):
        for k, f in ((1, 0), (3, 0), (2, 0), (0, 1), (1, 1), (3, 1), (2, 1)):
            yc[q, k, f].wait_recv()
            cc[q, k, f].start()
    st = [s0, s1, s2, s3]
    for t in range(Q + 3):
        for i in reversed(range(4)):
            q = t - i
            if 0 <= q < Q:
                st[i](q)
        if t == 0:
            pick_rows()
        if t == 2:
            qy.wait_recv()
            qd.start()
    for q in range(Q):
        for k in range(4):
            for f in range(2):
                if k or f: cc[q, k, f].wait_recv()
    for d in (zc, xc, cc) + (yc,):
        for v in d.values(): v.wait_send()
    for copy in ec:
        copy.wait()
    qcc.wait_recv()
    qd.wait_recv()
    for copy in qc + [qy, qcc, qd]:
        copy.wait_send()
    own.wait()
    kept.wait()

def gather_weights(w, asks, table, chunks, cid):
    Q = len(chunks)
    D = pltpu.SemaphoreType.DMA
    anywhere = pl.BlockSpec(memory_space=pl.ANY)
    near = pl.BlockSpec(memory_space=pltpu.VMEM)
    padded = -(-table.shape[0] // 640) * 640
    return pl.pallas_call(
        functools.partial(gather_kernel, chunks),
        out_shape=(jax.ShapeDtypeStruct((8,) + w.shape, w.dtype), jax.ShapeDtypeStruct((8, SLOTS, 512), BF), jax.ShapeDtypeStruct((4,) + asks.shape, asks.dtype)),
        in_specs=[anywhere, near, anywhere], out_specs=[anywhere, anywhere, near],
        scratch_shapes=[pltpu.VMEM((padded, 512), jnp.float32), pltpu.VMEM((8, SLOTS, 512), jnp.float32), pltpu.VMEM((8, SLOTS, 512), BF),
            D((Q, 4)), D((Q, 4)), D((Q, 4)), D((Q, 4)), D((Q, 8)), D((Q, 8)), D((Q, 8)), D((Q, 8)), D((4,)), D((8,)), D((8,)), D((11,)), D((11,))],
        compiler_params=pltpu.CompilerParams(collective_id=cid, has_side_effects=True, vmem_limit_bytes=48 * 2**20),
    )(w, asks, table)

def plan(rows, count, share):
    units = rows // 32
    chunks = []
    base = 0
    for i in range(count):
        size = units // count + (1 if i < units % count else 0)
        chunks.append((base, 16 * size, 16 * int(round(size * share))))
        base += 32 * size
    return chunks


def slot_plan(token_ids, shard_rows):
    tokens = token_ids.shape[0]
    owner = token_ids // shard_rows
    local = token_ids - owner * shard_rows
    index = jnp.arange(tokens, dtype=jnp.int32)
    same_id = token_ids[:, None] == token_ids[None, :]
    first = jnp.min(jnp.where(same_id, index[None, :], tokens), axis=1)
    leads = first == index
    same_owner = owner[:, None] == owner[None, :]
    slot = jnp.sum(
        (same_owner & leads[None, :] & (index[None, :] < first[:, None])).astype(jnp.int32), axis=1
    )
    key = jnp.where(slot < SLOTS, owner * SLOTS + slot, 8 * SLOTS)
    wanted = jnp.max(
        jnp.where(
            key[:, None] == jnp.arange(8 * SLOTS, dtype=jnp.int32)[None, :], local[:, None], -1
        ),
        axis=0,
    )
    return key, wanted, jnp.max(slot)


def column_blocks(rows):
    lead, count, width = rows.shape
    return (
        rows.reshape(lead, count, width // D, D).transpose(0, 2, 1, 3).reshape(lead, -1, D)
    )


def pack_weights(attn_in, attn_out, ffn_in, ffn_out, head_master, norm_master):
    layers = jnp.concatenate(
        [column_blocks(attn_in), attn_out, column_blocks(ffn_in), ffn_out], axis=1
    ).astype(jnp.bfloat16)
    norm_rows = jnp.pad(
        norm_master.reshape(10, -1).astype(jnp.bfloat16), ((0, 22), (0, D - norm_master.shape[2]))
    )
    return jnp.concatenate(
        [layers.reshape(-1, D), head_master.astype(jnp.bfloat16), norm_rows], axis=0
    )


def dot_nn(left, right):
    return lax.dot_general(left, right, (((1,), (0,)), ((), ())), preferred_element_type=jnp.float32)


def dot_nt(left, right):
    return lax.dot_general(left, right, (((1,), (1,)), ((), ())), preferred_element_type=jnp.float32)


def dot_tn(left, right):
    return lax.dot_general(left, right, (((0,), (0,)), ((), ())), preferred_element_type=jnp.float32)


def exact_dot(left, right, dims=((1,), (0,))):
    return lax.dot_general(
        left, right, (dims, ((), ())), precision=lax.Precision.HIGHEST, preferred_element_type=jnp.float32
    )


GELU_SCALE = (2.0 / 3.141592653589793) ** 0.5
GELU_CUBE = 0.044715
TILE = 256


def norm_parts(values):
    center = values - jnp.mean(values, axis=-1, keepdims=True)
    inverse = lax.rsqrt(jnp.mean(center * center, axis=-1, keepdims=True) + NORM_EPS)
    return center * inverse, inverse


def norm_back(scaled, inverse, grad_out, gain):
    grad_scaled = grad_out * gain
    mean_grad = jnp.mean(grad_scaled, axis=-1, keepdims=True)
    mean_both = jnp.mean(grad_scaled * scaled, axis=-1, keepdims=True)
    return inverse * (grad_scaled - mean_grad - scaled * mean_both)


def gelu_parts(value):
    bend = jnp.tanh(GELU_SCALE * (value + GELU_CUBE * value * value * value))
    half = 0.5 * (1.0 + bend)
    slope = half + 0.5 * value * (1.0 - bend * bend) * GELU_SCALE * (1.0 + 3.0 * GELU_CUBE * value * value)
    return value * half, slope


def block(w_ref, start):
    return w_ref[:, start : start + 64, :].reshape(D, D)


def down_block(w_ref, j):
    return w_ref[2 * j : 2 * j + 2, 768:1024, :].reshape(D, D)


def fill_distance(far, seg_col_ref, seg_row_ref):
    tokens = far.shape[0]
    def body(i, carry):
        start = pl.multiple_of(i * 64, 64)
        rows = lax.broadcasted_iota(jnp.int32, (64, tokens), 0) + start
        cols = lax.broadcasted_iota(jnp.int32, (64, tokens), 1)
        gap = jnp.abs(rows - cols).astype(jnp.float32)
        same = seg_col_ref[pl.ds(start, 64), :] == seg_row_ref[...]
        far[pl.ds(start, 64), :] = jnp.where(same, gap, jnp.inf)
        return carry
    lax.fori_loop(0, tokens // 64, body, 0)


def forward_kernel(
    first_ref, seg_col_ref, seg_row_ref, valid_ref, w_ref, head_ref, norm_ref,
    low_ref, qkv_ref, lse_ref, mix_ref, one_ref, two_ref, unit_ref, pool_ref, zed_ref,
    x_s, far, acc,
):
    layer = pl.program_id(0)
    tokens = x_s.shape[0]
    tiles = tokens // TILE

    @pl.when(layer == 0)
    def _():
        x_s[...] = first_ref[...].astype(jnp.float32)
        fill_distance(far, seg_col_ref, seg_row_ref)

    def project(i, carry):
        rows = pl.ds(pl.multiple_of(i * TILE, TILE), TILE)
        low = x_s[rows, :].astype(jnp.bfloat16)
        low_ref[0, rows, :] = low
        for j in range(3):
            qkv_ref[0, rows, j * D : (j + 1) * D] = dot_nn(low, block(w_ref, j * 64)).astype(jnp.bfloat16)
        return carry

    lax.fori_loop(0, tiles, project, 0)
    for head in range(HEADS):
        lanes = slice(head * HEAD_DIM, (head + 1) * HEAD_DIM)
        keys = qkv_ref[0, :, D + head * HEAD_DIM : D + (head + 1) * HEAD_DIM]
        vals_t = qkv_ref[0, :, 2 * D + head * HEAD_DIM : 2 * D + (head + 1) * HEAD_DIM].T
        slope = 2.0 ** (-8.0 * (head + 1) / HEADS)
        for i in range(tiles):
            cols = slice(i * TILE, (i + 1) * TILE)
            scores = dot_nt(keys, qkv_ref[0, cols, lanes]) * HEAD_DIM**-0.5 - slope * far[:, cols]
            top = jnp.max(scores, axis=0, keepdims=True)
            raised = jnp.exp(scores - top)
            total = jnp.sum(raised, axis=0, keepdims=True)
            lse_ref[0, head, :, cols] = top + jnp.log(total)
            prob = (raised * (1.0 / total)).astype(jnp.bfloat16)
            mix_ref[0, lanes, cols] = dot_nn(vals_t, prob).astype(jnp.bfloat16)

    acc[...] = dot_tn(mix_ref[0], block(w_ref, 192))

    def feed(i, carry):
        rows = pl.ds(pl.multiple_of(i * TILE, TILE), TILE)
        resid = x_s[rows, :] + acc[rows, :]
        one_ref[0, rows, :] = resid
        at = 4 * layer
        scaled, _ = norm_parts(resid)
        hidden = scaled * norm_ref[pl.ds(at, 1), :] + norm_ref[pl.ds(at + 1, 1), :]
        low = hidden.astype(jnp.bfloat16)
        total = hidden
        for j in range(4):
            gate = dot_nn(low, block(w_ref, 256 + j * 64))
            up = dot_nn(low, block(w_ref, 512 + j * 64))
            bend = jnp.tanh(GELU_SCALE * (gate + GELU_CUBE * gate * gate * gate))
            mid = (0.5 * gate * (1.0 + bend) * up).astype(jnp.bfloat16)
            total = total + dot_nn(mid, down_block(w_ref, j))
        two_ref[0, rows, :] = total
        scaled, _ = norm_parts(total)
        x_s[rows, :] = scaled * norm_ref[pl.ds(at + 2, 1), :] + norm_ref[pl.ds(at + 3, 1), :]
        return carry

    lax.fori_loop(0, tiles, feed, 0)

    @pl.when(layer == LAYERS - 1)
    def _():
        scaled, _ = norm_parts(x_s[...])
        final = scaled * norm_ref[8:9, :] + norm_ref[9:10, :]
        member = members(seg_row_ref, valid_ref)
        counts = jnp.maximum(jnp.sum(member, axis=1, keepdims=True), 1.0)
        pooled = (exact_dot(member, final) / counts).astype(jnp.bfloat16)
        pool_ref[...] = pooled
        zed = dot_nn(pooled, head_ref[...].reshape(D, D))
        zed_ref[...] = zed
        unit = zed * lax.rsqrt(jnp.sum(zed * zed, axis=-1, keepdims=True) + UNIT_EPS)
        for s in range(4):
            for part in range(4):
                unit_ref[4 * s + part : 4 * s + part + 1, :] = unit[s : s + 1, part * 128 : (part + 1) * 128]


def members(seg_row_ref, valid_ref):
    tokens = seg_row_ref.shape[1]
    slot = lax.broadcasted_iota(jnp.int32, (8, tokens), 0)
    return jnp.where((seg_row_ref[...] == slot) & (valid_ref[...] > 0), 1.0, 0.0)


def whole(shape):
    return pl.BlockSpec(shape, lambda i: (0,) * len(shape))


def run_forward(first, seg_col, seg_row, valid, weights, norms):
    tokens = first.shape[0]
    low = jnp.bfloat16
    layered = lambda *s: pl.BlockSpec((1,) + s, lambda i: (i,) + (0,) * len(s))
    return pl.pallas_call(
        forward_kernel,
        grid=(LAYERS,),
        in_specs=[
            whole((tokens, D)), whole((tokens, 1)), whole((1, tokens)), whole((1, tokens)),
            pl.BlockSpec((8, PART, D), lambda i: (0, i, 0)),
            pl.BlockSpec((8, 64, D), lambda i: (0, HEAD_AT // 64, 0)),
            whole(norms.shape),
        ],
        out_specs=[
            layered(tokens, D), layered(tokens, 3 * D), layered(HEADS, 1, tokens), layered(D, tokens),
            layered(tokens, D), layered(tokens, D), whole((16, 128)), whole((8, D)), whole((8, D)),
        ],
        out_shape=[
            jax.ShapeDtypeStruct((LAYERS, tokens, D), low),
            jax.ShapeDtypeStruct((LAYERS, tokens, 3 * D), low),
            jax.ShapeDtypeStruct((LAYERS, HEADS, 1, tokens), jnp.float32),
            jax.ShapeDtypeStruct((LAYERS, D, tokens), low),
            jax.ShapeDtypeStruct((LAYERS, tokens, D), jnp.float32),
            jax.ShapeDtypeStruct((LAYERS, tokens, D), jnp.float32),
            jax.ShapeDtypeStruct((16, 128), jnp.float32),
            jax.ShapeDtypeStruct((8, D), low),
            jax.ShapeDtypeStruct((8, D), jnp.float32),
        ],
        scratch_shapes=[
            pltpu.VMEM((tokens, D), jnp.float32), pltpu.VMEM((tokens, tokens), jnp.float32),
            pltpu.VMEM((tokens, D), jnp.float32),
        ],
        compiler_params=pltpu.CompilerParams(vmem_limit_bytes=60 * 2**20),
    )(first, seg_col, seg_row, valid, weights, weights, norms)


def contrast_kernel(unit_ref, deal_col_ref, deal_row_ref, scale_ref, loss_ref, own_ref, slope_ref, every, ss, rs, ls):
    lin = lax.axis_index("dp") * 4 + lax.axis_index("group")
    peers = [lax.rem(lin + k, 32) for k in range(32)]
    peers = [(p // 4, p % 4) for p in peers]
    entry_barrier(peers[1:])
    copies = [
        pltpu.make_async_remote_copy(
            unit_ref, every.at[lin], ss.at[k], rs.at[k], device_id=peers[k], device_id_type=MESH
        )
        for k in range(1, 32)
    ]
    for copy in copies:
        copy.start()
    own = pltpu.make_async_copy(unit_ref, every.at[lin], ls)
    own.start()
    for copy in copies:
        copy.wait()
    own.wait()
    units = every[...].reshape(512, 128)
    place_at = lax.broadcasted_iota(jnp.int32, (128, 512), 1)
    sorted_units = jnp.concatenate(
        [
            exact_dot(jnp.where(deal_col_ref[...] * 4 + part == place_at, 1.0, 0.0), units)
            for part in range(4)
        ],
        axis=1,
    )
    queries, documents = sorted_units[:64], sorted_units[64:]
    scale = jnp.exp(scale_ref[...])
    logits = scale * exact_dot(queries, documents, ((1,), (1,)))
    row_top = jnp.max(logits, axis=1, keepdims=True)
    row_lse = row_top + jnp.log(jnp.sum(jnp.exp(logits - row_top), axis=1, keepdims=True))
    col_top = jnp.max(logits, axis=0, keepdims=True)
    col_lse = col_top + jnp.log(jnp.sum(jnp.exp(logits - col_top), axis=0, keepdims=True))
    diagonal = jnp.where(
        lax.broadcasted_iota(jnp.int32, (64, 64), 0) == lax.broadcasted_iota(jnp.int32, (64, 64), 1), 1.0, 0.0
    )
    on_diagonal = jnp.sum(logits * diagonal, axis=1, keepdims=True)
    col_sum = jnp.sum(col_lse, axis=1, keepdims=True)
    row_sum = jnp.sum(row_lse, axis=0, keepdims=True)
    loss_ref[...] = 0.5 * (row_sum + col_sum) - jnp.sum(on_diagonal, axis=0, keepdims=True)
    grad_logits = 0.5 * (jnp.exp(logits - row_lse) + jnp.exp(logits - col_lse)) - diagonal
    slope = jnp.sum(grad_logits * logits, axis=1, keepdims=True)
    slope_ref[...] = jnp.sum(slope, axis=0, keepdims=True)
    grad_raw = scale * grad_logits
    grad_queries = exact_dot(grad_raw, documents)
    grad_documents = exact_dot(grad_raw, queries, ((0,), (0,)))
    mine = lax.broadcasted_iota(jnp.int32, (8, 128), 0)
    picks = jnp.where((deal_row_ref[...] == mine + lin * 4) & (mine < 4), 1.0, 0.0)
    own_ref[...] = exact_dot(picks, jnp.concatenate([grad_queries, grad_documents], axis=0))


def run_contrast(unit, deal_order, log_scale, cid):
    sems = pltpu.SemaphoreType.DMA
    one = jax.ShapeDtypeStruct((1, 1), jnp.float32)
    return pl.pallas_call(
        contrast_kernel,
        out_shape=[one, jax.ShapeDtypeStruct((8, D), jnp.float32), one],
        in_specs=[pl.BlockSpec(memory_space=pltpu.VMEM)] * 4,
        out_specs=[pl.BlockSpec(memory_space=pltpu.VMEM)] * 3,
        scratch_shapes=[pltpu.VMEM((32, 16, 128), jnp.float32), sems((32,)), sems((32,)), sems],
        compiler_params=pltpu.CompilerParams(collective_id=cid, has_side_effects=True),
    )(unit, deal_order.reshape(128, 1), deal_order.reshape(1, 128), log_scale.reshape(1, 1))


GRAD_ROWS = 2 * PART + 64
GRAD_LAYER = (0, PART + 64)
GRAD_HEAD = PART
PIECES = tuple(
    (stage, half, spare, at)
    for stage, half, spare, at in (
        (320, 128, 32, GRAD_LAYER[1] + 256), (576, 128, 48, GRAD_LAYER[1] + 512), (832, 128, 32, GRAD_LAYER[1] + 768),
        (0, 160, 48, GRAD_HEAD),
        (320, 128, 32, 256), (576, 128, 48, 512), (832, 128, 32, 768),
        (64, 128, 32, 0),
    )
)


def sum_stages(stage, out_ref, acc, b1, b2, b3, b4, b5, fin, sems, free):
    cs, cr, ys, yr, xs, xr, zs, zr, as_, ar, fs, fr, ls, os_ = sems
    z, x, y, c = place()
    me = z * 2 + x
    zp = [dev((z + k) % 4, x, y, c) for k in range(4)]
    xp, yp, cp = dev(z, 1 - x, y, c), dev(z, x, 1 - y, c), dev(z, x, y, 1 - c)

    def rc(src, dst, s, r, d):
        return pltpu.make_async_remote_copy(src, dst, s, r, device_id=d, device_id_type=MESH)

    def owner(k, f):
        return ((z + k) % 4) * 2 + (x if f == 0 else 1 - x)

    order = [(k, f) for k in (2, 1, 3, 0) for f in (1, 0)]
    lo, lb, lh, la, l1 = [0], [0], [0], [0], [0]
    for stage_at, half, spare, at in PIECES:
        lo.append(lo[-1] + half)
        lb.append(lb[-1] + spare)
        lh.append(lh[-1] + half - spare)
        la.append(la[-1] + half - 2 * spare)
        l1.append(l1[-1] + half)
    l1 = l1[:4] + l1[:4]

    def add(dst, src, count):
        def body(i, carry):
            at = mult(i * 32)
            into = dst(at)
            into[...] = (into[...].astype(jnp.float32) + src(at)[...].astype(jnp.float32)).astype(BF)
            return carry
        lax.fori_loop(0, count // 32, body, 0)
        if count % 32:
            into = dst(count - 16, 16)
            into[...] = (into[...].astype(jnp.float32) + src(count - 16, 16)[...].astype(jnp.float32)).astype(BF)

    class Piece:
        pass

    pieces = []
    for q, (stage_at, half, spare, at) in enumerate(PIECES):
        p = Piece()
        p.q, p.half, p.spare, p.main = q, half, spare, half - spare
        p.hs = mult(lo[q] + y * spare)
        p.mb = mult(lo[q] + y * p.main)
        p.ob = mult(lo[q] + (1 - y) * p.main)
        p.L, p.C, p.Y, p.X, p.Z = [], [], [], [], []
        for i, (k, f) in enumerate(order):
            s = owner(k, f)
            p.L.append(pltpu.make_async_copy(stage.at[s, pl.ds(mult(stage_at + c * half), half)], acc.at[s, pl.ds(lo[q], half)], ls.at[q, i]))
            p.C.append(rc(stage.at[s, pl.ds(mult(stage_at + (1 - c) * half), half)], b1.at[s, pl.ds(l1[q], half)], cs.at[q, i], cr.at[q, i], cp))
            p.Y.append(rc(acc.at[s, pl.ds(p.ob, spare)], b2.at[s, pl.ds(lb[q], spare)], ys.at[q, i], yr.at[q, i], yp))
        for k in range(4):
            p.X.append(rc(acc.at[owner(k, 1), pl.ds(p.hs, p.main)], b3.at[k, pl.ds(lh[q], p.main)], xs.at[q, k], xr.at[q, k], xp))
            p.Z.append(rc(acc.at[owner(k, 0), pl.ds(p.hs, p.main)], b4.at[k - 1, pl.ds(lh[q], p.main)], zs.at[q, k], zr.at[q, k], zp[k]) if k else None)
        p.aa, p.na = lo[q] + spare, half - 2 * spare
        p.A = rc(fin.at[pl.ds(p.aa, p.na)], b5.at[pl.ds(la[q], p.na)], as_.at[q, 0], ar.at[q, 0], yp)
        p.B = rc(fin.at[pl.ds(p.mb, spare)], fin.at[pl.ds(p.mb, spare)], as_.at[q, 1], ar.at[q, 1], yp)
        p.F = rc(fin.at[pl.ds(lo[q], half)], out_ref.at[pl.ds(mult(at + c * half), half)], fs.at[q], fr.at[q], cp)
        p.O = pltpu.make_async_copy(fin.at[pl.ds(lo[q], half)], out_ref.at[pl.ds(mult(at + c * half), half)], os_.at[q])
        pieces.append(p)

    def s0(q):
        p = pieces[q]
        if q >= 4:
            pl.semaphore_wait(free.at[q - 4], 1)
        for i in range(8):
            p.C[i].start()
            p.L[i].start()

    def s1(q):
        p = pieces[q]
        for i, (k, f) in enumerate(order):
            s = owner(k, f)
            p.L[i].wait()
            p.C[i].wait_recv()
            add(lambda a, n=32: acc.at[s, pl.ds(lo[q] + a, n)], lambda a, n=32: b1.at[s, pl.ds(l1[q] + a, n)], p.half)
            p.Y[i].start()
        if q < 4:
            pl.semaphore_signal(free.at[q], inc=1, device_id=cp, device_id_type=MESH)

    def s2(q):
        p = pieces[q]
        for i, (k, f) in enumerate(order):
            s = owner(k, f)
            p.Y[i].wait_recv()
            add(lambda a, n=32: acc.at[s, pl.ds(p.mb + a, n)], lambda a, n=32: b2.at[s, pl.ds(lb[q] + a, n)], p.spare)
            if f == 1:
                p.X[k].start()

    def s3(q):
        p = pieces[q]
        for k in (2, 1, 3, 0):
            s = owner(k, 0)
            p.X[k].wait_recv()
            add(lambda a, n=32: acc.at[s, pl.ds(p.hs + a, n)], lambda a, n=32: b3.at[k, pl.ds(lh[q] + a, n)], p.main)
            if k:
                p.Z[k].start()

    def s4(q):
        p = pieces[q]
        for k in range(1, 4):
            p.Z[k].wait_recv()
        def body(i, carry):
            at = mult(i * 16)
            total = acc[me, pl.ds(p.hs + at, 16)].astype(jnp.float32)
            for k in range(3):
                total += b4[k, pl.ds(lh[q] + at, 16)].astype(jnp.float32)
            fin[pl.ds(p.hs + at, 16)] = total.astype(BF)
            return carry
        lax.fori_loop(0, p.main // 16, body, 0)
        p.A.start()
        p.B.start()

    def s5(q):
        p = pieces[q]
        p.A.wait_recv()
        p.A.wait_send()
        add(lambda a, n=32: fin.at[pl.ds(p.aa + a, n)], lambda a, n=32: b5.at[pl.ds(la[q] + a, n)], p.na)
        p.B.wait_recv()
        p.F.start()
        p.O.start()

    def sent(q):
        for copy in pieces[q].C:
            copy.wait_send()

    def finish():
        for p in pieces:
            p.F.wait()
            p.O.wait()
            p.B.wait_send()
            for copy in p.Y + p.X + p.Z[1:]:
                copy.wait_send()

    return [s0, s1, s2, s3, s4, s5], sent, finish


def row_exchange(slots, t_ref, norm_ref, norm_out, nbuf, es, er, el, ns, nr):
    z, x, y, c = place()
    me = z * 2 + x
    g = y * 2 + c
    g2 = (1 - y) * 2 + c
    ep = [(lax.rem(me + k, 8), g) for k in range(8)]
    back = [lax.rem(me + 8 - k, 8) for k in range(8)]
    yp, cp = dev(z, x, 1 - y, c), dev(z, x, y, 1 - c)

    def rc(src, dst, s, r, d):
        return pltpu.make_async_remote_copy(src, dst, s, r, device_id=d, device_id_type=MESH)

    kept = pltpu.make_async_copy(slots.at[me], t_ref.at[g, me], el)
    E = [rc(slots.at[ep[k][0]], t_ref.at[g, me], es.at[0, k], er.at[0, k], ep[k]) for k in range(1, 8)]
    EY = [rc(t_ref.at[g, back[k]], t_ref.at[g, back[k]], es.at[1, k], er.at[1, k], yp) for k in range(8)]
    EC = [rc(t_ref.at[g, back[k]], t_ref.at[g, back[k]], es.at[2, k], er.at[2, k], cp) for k in range(8)]
    ED = [rc(t_ref.at[g2, back[k]], t_ref.at[g2, back[k]], es.at[3, k], er.at[3, k], cp) for k in range(8)]
    NC = rc(norm_ref, nbuf.at[0], ns.at[0], nr.at[0], cp)
    NY = rc(nbuf.at[1], nbuf.at[2], ns.at[1], nr.at[1], yp)

    def e0():
        kept.start()
        for copy in E:
            copy.start()
        NC.start()

    def e1():
        kept.wait()
        EY[0].start()
        EC[0].start()
        NC.wait_recv()
        nbuf[1] = nbuf[0] + norm_ref[...]
        NY.start()
        for k in range(1, 8):
            E[k - 1].wait_recv()
            EY[k].start()
            EC[k].start()

    def e2():
        for k in range(8):
            EY[k].wait_recv()
            ED[k].start()
        NY.wait_recv()
        norm_out[...] = nbuf[1] + nbuf[2]

    def e3():
        for copy in EC + ED:
            copy.wait_recv()
        for copy in E + EY + EC + ED + [NC, NY]:
            copy.wait_send()

    return [e0, e1, e2, e3]


def backward_kernel(
    own_ref, zed_ref, pool_ref, seg_col_ref, seg_row_ref, valid_ref, key_ref, norm_ref,
    w_ref, low_in, qkv_in, lse_in, mix_in, one_in, two_in,
    out_ref, t_ref, norm_out, first_ref,
    weights, head, low_ref, qkv_ref, lse_ref, mix_ref, one_ref, two_ref, stage,
    dx, far, acc, two_s, low_s, mid_s, ups, gates, back, norm_s, slots,
    total, b1, b2, b3, b4, b5, fin, nbuf,
    cs, cr, ys, yr, xs, xr, zs, zr, as_, ar, fs, fr, ls, os_, es, er, el, ns, nr, loads, free,
):
    tokens = dx.shape[0]
    tiles = tokens // TILE
    low_type = jnp.bfloat16
    z, x, y, c = place()
    me = z * 2 + x
    g = y * 2 + c
    peers = [(lax.rem(me + k, 8), g) for k in range(1, 8)] + [dev(z, x, 1 - y, c), dev(z, x, y, 1 - c)]
    barrier = pltpu.get_barrier_semaphore()
    for peer in peers:
        pl.semaphore_signal(barrier, inc=1, device_id=peer, device_id_type=MESH)
    stages, sent, finish = sum_stages(
        stage, out_ref, total, b1, b2, b3, b4, b5, fin, (cs, cr, ys, yr, xs, xr, zs, zr, as_, ar, fs, fr, ls, os_), free
    )
    rows_out = row_exchange(slots, t_ref, norm_s, norm_out, nbuf, es, er, el, ns, nr)

    def loading(layer):
        base = layer * PART
        copy = pltpu.make_async_copy
        return {
            "two": copy(two_in.at[layer], two_ref, loads.at[layer, 0]),
            "one": copy(one_in.at[layer], one_ref, loads.at[layer, 1]),
            "feed": copy(w_ref.at[:, pl.ds(base + 256, 768)], weights.at[:, pl.ds(256, 768)], loads.at[layer, 2]),
            "mix": copy(mix_in.at[layer], mix_ref, loads.at[layer, 3]),
            "qkv": copy(qkv_in.at[layer], qkv_ref, loads.at[layer, 4]),
            "lse": copy(lse_in.at[layer], lse_ref, loads.at[layer, 5]),
            "low": copy(low_in.at[layer], low_ref, loads.at[layer, 6]),
            "attend": copy(w_ref.at[:, pl.ds(base, 256)], weights.at[:, pl.ds(0, 256)], loads.at[layer, 7]),
        }

    load = [loading(layer) for layer in range(LAYERS)]
    head_load = pltpu.make_async_copy(w_ref.at[:, pl.ds(HEAD_AT, 64)], head, loads.at[0, 8])
    head_load.start()
    for copy in load[1].values():
        copy.start()

    def begin():
        fill_distance(far, seg_col_ref, seg_row_ref)
        head_load.wait()
        load[1]["two"].wait()
        zed = zed_ref[...]
        square = jnp.sum(zed * zed, axis=-1, keepdims=True) + UNIT_EPS
        inverse = lax.rsqrt(square)
        own = own_ref[...]
        inner = jnp.sum(own * zed, axis=-1, keepdims=True)
        grad_zed = (inverse * (own - zed * (inner / square))).astype(low_type)
        head_low = head[...].reshape(D, D)
        stage[:, 0:64, :] = dot_tn(pool_ref[...], grad_zed).reshape(8, 64, D).astype(low_type)
        member = members(seg_row_ref, valid_ref)
        counts = jnp.maximum(jnp.sum(member, axis=1, keepdims=True), 1.0)
        grad_pooled = dot_nt(grad_zed, head_low) / counts
        grad_final = exact_dot(member, grad_pooled, ((0,), (0,)))
        stream_scaled, _ = norm_parts(two_ref[...])
        stream = stream_scaled * norm_ref[6:7, :] + norm_ref[7:8, :]
        scaled, inverse = norm_parts(stream)
        norm_s[...] = jnp.zeros(norm_s.shape, jnp.float32)
        norm_s[2, 0:1, :] = jnp.sum(grad_final * scaled, axis=0, keepdims=True)
        norm_s[2, 1:2, :] = jnp.sum(grad_final, axis=0, keepdims=True)
        dx[...] = norm_back(scaled, inverse, grad_final, norm_ref[8:9, :])

    def enter(layer):
        at = 4 * layer
        if layer < LAYERS - 1:
            load[layer]["two"].wait()
        load[layer]["one"].wait()

        def body(i, carry):
            rows = pl.ds(pl.multiple_of(i * TILE, TILE), TILE)
            scaled, inverse = norm_parts(two_ref[rows, :])
            grad = dx[rows, :]
            norm_s[layer, 2:3, :] += jnp.sum(grad * scaled, axis=0, keepdims=True)
            norm_s[layer, 3:4, :] += jnp.sum(grad, axis=0, keepdims=True)
            grad = norm_back(scaled, inverse, grad, norm_ref[at + 2 : at + 3, :])
            acc[rows, :] = grad
            two_s[rows, :] = grad.astype(low_type)
            scaled, _ = norm_parts(one_ref[rows, :])
            hidden = scaled * norm_ref[at : at + 1, :] + norm_ref[at + 1 : at + 2, :]
            low_s[rows, :] = hidden.astype(low_type)
            return carry

        lax.fori_loop(0, tiles, body, 0)
        if layer > 0:
            load[layer - 1]["two"].start()
        load[layer]["feed"].wait()

    def feed(layer, j):
        def body(i, carry):
            rows = pl.ds(pl.multiple_of(i * TILE, TILE), TILE)
            low = low_s[rows, :]
            gate = dot_nn(low, block(weights, 256 + j * 64))
            up = dot_nn(low, block(weights, 512 + j * 64))
            grad_mid = dot_nt(two_s[rows, :], down_block(weights, j))
            value, slope = gelu_parts(gate)
            mid_s[rows, :] = (value * up).astype(low_type)
            grad_gate = (grad_mid * up * slope).astype(low_type)
            grad_up = (grad_mid * value).astype(low_type)
            gates[rows, :] = grad_gate
            ups[rows, :] = grad_up
            acc[rows, :] += dot_nt(grad_gate, block(weights, 256 + j * 64)) + dot_nt(
                grad_up, block(weights, 512 + j * 64)
            )
            return carry

        lax.fori_loop(0, tiles, body, 0)
        if layer < LAYERS - 1 and j == 0:
            for q in range(3):
                sent(q)
        stage[2 * j : 2 * j + 2, 832:1088, :] = dot_tn(mid_s[...], two_s[...]).reshape(2, 256, D).astype(low_type)
        stage[:, 320 + j * 64 : 384 + j * 64, :] = dot_tn(low_s[...], gates[...]).reshape(8, 64, D).astype(low_type)
        stage[:, 576 + j * 64 : 640 + j * 64, :] = dot_tn(low_s[...], ups[...]).reshape(8, 64, D).astype(low_type)

    def middle(layer):
        at = 4 * layer
        if layer > 0:
            load[layer - 1]["feed"].start()
        load[layer]["attend"].wait()
        load[layer]["mix"].wait()

        def body(i, carry):
            rows = pl.ds(pl.multiple_of(i * TILE, TILE), TILE)
            scaled, inverse = norm_parts(one_ref[rows, :])
            grad = acc[rows, :]
            norm_s[layer, 0:1, :] += jnp.sum(grad * scaled, axis=0, keepdims=True)
            norm_s[layer, 1:2, :] += jnp.sum(grad, axis=0, keepdims=True)
            grad = norm_back(scaled, inverse, grad, norm_ref[at : at + 1, :])
            dx[rows, :] = grad
            low = grad.astype(low_type)
            two_s[rows, :] = low
            mid_s[rows, :] = dot_nt(low, block(weights, 192)).astype(low_type)
            return carry

        lax.fori_loop(0, tiles, body, 0)
        if layer > 0:
            load[layer - 1]["one"].start()
        else:
            sent(3)
        stage[:, 256:320, :] = dot_nn(mix_ref[...], two_s[...]).reshape(8, 64, D).astype(low_type)
        load[layer]["qkv"].wait()
        load[layer]["lse"].wait()
        load[layer]["low"].wait()

    def attend_head(layer, head):
        lanes = slice(head * HEAD_DIM, (head + 1) * HEAD_DIM)
        key_lanes = slice(D + head * HEAD_DIM, D + (head + 1) * HEAD_DIM)
        val_lanes = slice(2 * D + head * HEAD_DIM, 2 * D + (head + 1) * HEAD_DIM)
        keys = qkv_ref[:, key_lanes]
        keys_t = keys.T
        vals = qkv_ref[:, val_lanes]
        slope = 2.0 ** (-8.0 * (head + 1) / HEADS)
        grad_vals = None
        grad_keys = None
        for i in range(tiles):
            cols = slice(i * TILE, (i + 1) * TILE)
            query = qkv_ref[cols, lanes]
            grad_mix = mid_s[cols, lanes]
            scores = dot_nt(keys, query) * HEAD_DIM**-0.5 - slope * far[:, cols]
            prob = jnp.exp(scores - lse_ref[head, :, cols])
            grad_prob = dot_nt(vals, grad_mix)
            inner = jnp.sum(prob * grad_prob, axis=0, keepdims=True)
            grad_raw = (prob * (grad_prob - inner) * HEAD_DIM**-0.5).astype(low_type)
            back[cols, lanes] = dot_nn(keys_t, grad_raw).T.astype(low_type)
            value_part = dot_nn(prob.astype(low_type), grad_mix)
            key_part = dot_nn(grad_raw, query)
            grad_vals = value_part if grad_vals is None else grad_vals + value_part
            grad_keys = key_part if grad_keys is None else grad_keys + key_part
        back[:, key_lanes] = grad_keys.astype(low_type)
        back[:, val_lanes] = grad_vals.astype(low_type)

    def leave(layer):
        def body(i, carry):
            rows = pl.ds(pl.multiple_of(i * TILE, TILE), TILE)
            grad = dx[rows, :]
            for j in range(3):
                grad = grad + dot_nt(back[rows, j * D : (j + 1) * D], block(weights, j * 64))
            dx[rows, :] = grad
            return carry

        lax.fori_loop(0, tiles, body, 0)
        for j in range(3):
            stage[:, 64 + j * 64 : 128 + j * 64, :] = (
                dot_tn(low_ref[...], back[:, j * D : (j + 1) * D]).reshape(8, 64, D).astype(low_type)
            )
        if layer > 0:
            for name in ("mix", "qkv", "lse", "low", "attend"):
                load[layer - 1][name].start()
        else:
            first_ref[...] = dx[...].astype(low_type)
            count = slots.shape[1]
            for d in range(8):
                hot = lax.broadcasted_iota(jnp.int32, (count, tokens), 0) + d * count == key_ref[...]
                slots[d] = dot_nn(jnp.where(hot, 1.0, 0.0).astype(low_type), first_ref[...]).astype(low_type)

    events = []
    clock = 0.0

    def do(cost, fn, *args):
        nonlocal clock
        events.append((clock, len(events), fn, args))
        clock += cost

    def wait_entry():
        pl.semaphore_wait(barrier, len(peers))

    ready = []
    do(3.0, begin)
    for layer in (1, 0):
        do(2.5, enter, layer)
        for j in range(4):
            do(4.7, feed, layer, j)
        if layer == 1:
            do(0.0, wait_entry)
        ready += [clock] * 3
        do(0.0, stages[0], len(ready) - 3)
        do(0.0, stages[0], len(ready) - 2)
        do(0.0, stages[0], len(ready) - 1)
        do(2.5, middle, layer)
        for head_index in range(HEADS):
            do(1.6, attend_head, layer, head_index)
        do(4.0, leave, layer)
        ready.append(clock)
        if layer == 0:
            do(0.0, rows_out[0])
        do(0.0, stages[0], len(ready) - 1)
    end = clock
    links = {"c": 0.0, "y": 0.0, "x": 0.0, "z": 0.0}
    for q in range(8):
        scale = PIECES[q][1] / 128.0
        now = ready[q]
        for number, link, cost in ((1, "c", 3.0), (2, "y", 8.0), (3, "x", 9.5), (4, "z", 9.5), (5, "y", 1.0)):
            now = max(now, links[link]) + cost * scale
            if number < 5:
                links[link] = now
            else:
                now += 3.0
            events.append((now, len(events), stages[number], (q,)))
    events.append((end + 8.0, len(events), rows_out[1], ()))
    events.append((end + 26.0, len(events), rows_out[2], ()))
    for _, _, fn, args in sorted(events, key=lambda event: event[:2]):
        fn(*args)
    finish()
    for q in range(4, 8):
        sent(q)
    rows_out[3]()


def run_backward(own, zed, pool, seg_col, seg_row, valid, key, weights, norms, saved, cid):
    low_x, qkv, lse, mix, one, two = saved
    tokens = low_x.shape[1]
    low = jnp.bfloat16
    full = jnp.float32
    vmem = lambda shape, kind=low: pltpu.VMEM(shape, kind)
    sems = lambda *shape: pltpu.SemaphoreType.DMA(shape)
    half = sum(p[1] for p in PIECES)
    spare = sum(p[2] for p in PIECES)
    near = pl.BlockSpec(memory_space=pltpu.VMEM)
    anywhere = pl.BlockSpec(memory_space=pl.ANY)
    norm_shape = (LAYERS + 1, 8, D)
    square = (tokens, D)
    return pl.pallas_call(
        backward_kernel,
        in_specs=[near] * 8 + [anywhere] * 7,
        out_specs=[anywhere, anywhere, near, near],
        out_shape=[
            jax.ShapeDtypeStruct((GRAD_ROWS, D), low),
            jax.ShapeDtypeStruct((4, 8, SLOTS, D), low),
            jax.ShapeDtypeStruct(norm_shape, full),
            jax.ShapeDtypeStruct(square, low),
        ],
        scratch_shapes=[
            vmem((8, PART, D)), vmem((8, 64, D)), vmem(square), vmem((tokens, 3 * D)), vmem((HEADS, 1, tokens), full),
            vmem((D, tokens)), vmem(square, full), vmem(square, full), vmem((8, PART + 64, D)),
            vmem(square, full), vmem((tokens, tokens), full), vmem(square, full), vmem(square), vmem(square),
            vmem(square), vmem(square), vmem(square), vmem((tokens, 3 * D)), vmem(norm_shape, full), vmem((8, SLOTS, D)),
            vmem((8, half, D)), vmem((8, sum(p[1] for p in PIECES[:4]), D)), vmem((8, spare, D)), vmem((4, half - spare, D)),
            vmem((3, half - spare, D)), vmem((half - 2 * spare, D)), vmem((half, D)), vmem((3,) + norm_shape, full),
            sems(8, 8), sems(8, 8), sems(8, 8), sems(8, 8), sems(8, 4), sems(8, 4), sems(8, 4), sems(8, 4),
            sems(8, 2), sems(8, 2), sems(8), sems(8), sems(8, 8), sems(8), sems(4, 8), sems(4, 8), pltpu.SemaphoreType.DMA,
            sems(2), sems(2), sems(2, 9), pltpu.SemaphoreType.REGULAR((4,)),
        ],
        compiler_params=pltpu.CompilerParams(collective_id=cid, has_side_effects=True, vmem_limit_bytes=63 * 2**20),
    )(own, zed, pool, seg_col, seg_row, valid, key, norms, weights, low_x, qkv, lse, mix, one, two)


def total_kernel(v_ref, o_ref, got, mine, ss, rs, ts, us, ls):
    me = lax.axis_index("dp")
    g = lax.axis_index("group")
    lin = me * 4 + g
    to = [lax.rem(lin + k, 32) for k in range(32)]
    peers = [(p // 4, p % 4) for p in to]
    owners = [(lax.rem(me + k, 8), g) for k in range(8)]
    entry_barrier(peers[1:])
    first = [
        pltpu.make_async_remote_copy(
            v_ref.at[owners[k][0] * 4 + g], got.at[k], ss.at[k], rs.at[k], device_id=owners[k], device_id_type=MESH
        )
        for k in range(1, 8)
    ]
    for copy in first:
        copy.start()
    own = pltpu.make_async_copy(v_ref.at[lin], got.at[0], ls.at[0])
    own.start()
    for copy in first:
        copy.wait()
    own.wait()
    mine[...] = jnp.sum(got[...], axis=0)
    second = [
        pltpu.make_async_remote_copy(
            mine, o_ref.at[lin], ts.at[k], us.at[k], device_id=peers[k], device_id_type=MESH
        )
        for k in range(1, 32)
    ]
    for copy in second:
        copy.start()
    own = pltpu.make_async_copy(mine, o_ref.at[lin], ls.at[1])
    own.start()
    for copy in second:
        copy.wait()
    own.wait()


def total(v, cid):
    sems = pltpu.SemaphoreType.DMA
    return pl.pallas_call(
        total_kernel,
        out_shape=jax.ShapeDtypeStruct(v.shape, v.dtype),
        in_specs=[pl.BlockSpec(memory_space=pltpu.VMEM)], out_specs=pl.BlockSpec(memory_space=pltpu.VMEM),
        scratch_shapes=[
            pltpu.VMEM((8,) + v.shape[1:], v.dtype), pltpu.VMEM(v.shape[1:], v.dtype),
            sems((8,)), sems((8,)), sems((32,)), sems((32,)), sems((2,)),
        ],
        compiler_params=pltpu.CompilerParams(collective_id=cid, has_side_effects=True),
    )(v)


BLOCKS = 28
STEP_AT = 28
SUM_AT = 56
NORM_ROW = 57
ROW_TILE = 512
RATES = (
    RATE_SCALE, RATE_SCALE / D**0.5, RATE_SCALE / D**0.5, RATE_SCALE / (D // 8) ** 0.5,
    RATE_SCALE / D**0.5, RATE_SCALE / FF**0.5,
)


def matrices(layer):
    at = GRAD_LAYER[layer]
    first = 2 + 13 * layer
    return (
        (2, at, 64, 3, first), (3, at + 192, 64, 1, first + 3),
        (4, at + 256, 64, 8, first + 4), (5, at + 768, 256, 1, first + 12),
    )


def turn(row):
    return jnp.broadcast_to(row, (8, row.shape[1])).T[:, 0:1]


def lane_pick(value, lane):
    return jnp.where(lax.broadcasted_iota(jnp.int32, (1, D), 1) == lane, value, 0.0)


def stats_kernel(dense, row_count, *refs):
    if dense:
        full_ref, grads_ref, norm_ref, table_row_ref, rows_ref, down_ref, *outs = refs
    else:
        slot_ref, slot_rows_ref, grads_ref, norm_ref, table_row_ref, rows_ref, down_ref, *outs = refs
    table_ref, table_row_out, stat_ref, rows_out, down_out = outs
    step = pl.program_id(0)

    def put(at, value):
        stat_ref[at // 3, at % 3 : at % 3 + 1, :] = value

    def add(at, value):
        stat_ref[at // 3, at % 3 : at % 3 + 1, :] += value

    @pl.when(step == 0)
    def _():
        stat_ref[...] = jnp.zeros(stat_ref.shape, jnp.float32)
        for row in range(10):
            put(NORM_ROW + row, norm_ref[row // 4, row % 4 : row % 4 + 1, :])
        sums = jnp.zeros((1, D), jnp.float32)
        rows_out[...] = jnp.zeros(rows_out.shape, jnp.float32)

        def part(first, count, blocks, block_at, old):
            squares = [
                grads_ref[first + j * count : first + (j + 1) * count, :].astype(jnp.float32) ** 2 for j in range(blocks)
            ]
            mean = jnp.sum(functools.reduce(jnp.add, squares), axis=-1, keepdims=True) / (blocks * D)
            new = DECAY_RATE * old + (1.0 - DECAY_RATE) * (mean + STATE_EPS)
            inverse = 1.0 / new
            for j in range(blocks):
                put(block_at + j, jnp.sum(squares[j], axis=0, keepdims=True))
                put(STEP_AT + block_at + j, jnp.sum(squares[j] * inverse, axis=0, keepdims=True))
            return new, jnp.sum(new, axis=0, keepdims=True)

        new, count = part(GRAD_HEAD, 64, 1, 1, rows_ref[:, 6:7])
        rows_out[:, 6:7] = new
        sums += lane_pick(count, 1)
        for layer in range(LAYERS):
            for name, first, rows, blocks, block_at in matrices(layer):
                if name == 5:
                    new, count = part(first, rows, blocks, block_at, down_ref[:, layer : layer + 1])
                    down_out[:, layer : layer + 1] = new
                else:
                    lane = 3 * layer + name - 2
                    new, count = part(first, rows, blocks, block_at, rows_ref[:, lane : lane + 1])
                    rows_out[:, lane : lane + 1] = new
                sums += lane_pick(count, 2 * name - 2 + layer)
        put(SUM_AT, sums)

    index = lax.broadcasted_iota(jnp.int32, (ROW_TILE, 1), 0) + step * ROW_TILE
    if dense:
        grad = jnp.where(index < row_count, full_ref[...], 0.0)
    else:
        picks = jnp.where(index == slot_ref[...], 1.0, 0.0).astype(jnp.bfloat16)
        grad = jnp.dot(picks, slot_rows_ref[...], preferred_element_type=jnp.float32)
    low = grad.astype(jnp.bfloat16)
    table_ref[...] = low
    squares = low.astype(jnp.float32) ** 2
    mean = jnp.mean(squares, axis=-1, keepdims=True)
    mean_row = jnp.broadcast_to(mean, (ROW_TILE, 128)).T[0:1, :]
    new = DECAY_RATE * table_row_ref[...] + (1.0 - DECAY_RATE) * (mean_row + STATE_EPS)
    real = lax.broadcasted_iota(jnp.int32, (1, ROW_TILE), 1) + step * ROW_TILE < row_count
    new = jnp.where(real, new, 1.0)
    table_row_out[...] = new
    add(0, jnp.sum(squares, axis=0, keepdims=True))
    add(STEP_AT, jnp.sum(squares * (1.0 / turn(new)), axis=0, keepdims=True))
    add(SUM_AT, lane_pick(jnp.sum(jnp.where(real, new, 0.0), axis=1, keepdims=True), 0))


def run_stats(dense, heads, grads, norm, table_row, rows, down):
    row_count = table_row.shape[1]
    tile = pl.BlockSpec((ROW_TILE, D), lambda i: (i, 0))
    lane = pl.BlockSpec((1, ROW_TILE), lambda i: (0, i))
    head_specs = [tile] if dense else [whole(v.shape) for v in heads]
    stat = (32, 3, D)
    return pl.pallas_call(
        functools.partial(stats_kernel, dense, row_count),
        grid=(-(-row_count // ROW_TILE),),
        in_specs=head_specs + [whole(grads.shape), whole(norm.shape), lane, whole(rows.shape), whole(down.shape)],
        out_specs=[tile, lane, whole(stat), whole(rows.shape), whole(down.shape)],
        out_shape=[
            jax.ShapeDtypeStruct((row_count, D), jnp.bfloat16), jax.ShapeDtypeStruct(table_row.shape, jnp.float32),
            jax.ShapeDtypeStruct(stat, jnp.float32), jax.ShapeDtypeStruct(rows.shape, jnp.float32),
            jax.ShapeDtypeStruct(down.shape, jnp.float32),
        ],
        compiler_params=pltpu.CompilerParams(vmem_limit_bytes=48 * 2**20),
    )(*heads, grads, norm, table_row, rows, down)


def update_kernel(
    totals, stat_ref, table_ref, embed_ref, table_row_ref, grads_ref, rows_ref, down_ref, top_cols_ref, cols_ref,
    in_ref, mix_ref, gate_ref, low_ref, head_ref,
    embed_out, table_cols_out, head_cols_out, cols_out, in_out, mix_out, gate_out, low_out, head_out, rms_out, factors,
):
    step = pl.program_id(0)

    def stat(at):
        return stat_ref[at // 3, at % 3 : at % 3 + 1, :]

    def mean_of(lane, name):
        return jnp.sum(jnp.where(lax.broadcasted_iota(jnp.int32, (1, D), 1) == lane, stat(SUM_AT), 0.0), axis=1, keepdims=True) / totals[name]

    def columns(block_at, blocks, old, lane, name):
        row_mean = mean_of(lane, name)
        news = []
        steps = 0.0
        for j in range(blocks):
            new = DECAY_RATE * old(j) + (1.0 - DECAY_RATE) * (stat(block_at + j) / totals[name] + STATE_EPS)
            news.append(new)
            steps += jnp.sum(row_mean * stat(STEP_AT + block_at + j) / new, axis=1, keepdims=True)
        rms = jnp.sqrt(steps / (totals[name] * blocks * D))
        scale = -RATES[name] / jnp.maximum(1.0, rms / CLIP_LEVEL)
        return news, row_mean, rms, scale

    @pl.when(step == 0)
    def _():
        news, row_mean, rms, scale = columns(0, 1, lambda j: top_cols_ref[0:1, :], 0, 0)
        table_cols_out[...] = news[0]
        factors[0:1, :] = lax.rsqrt(news[0])
        factors[1:2, :] = jnp.broadcast_to(row_mean, (1, D))
        factors[2:3, :] = jnp.broadcast_to(scale, (1, D))
        all_rms = lane_pick(rms, 0)
        news, row_mean, rms, scale = columns(1, 1, lambda j: top_cols_ref[1:2, :], 1, 1)
        head_cols_out[...] = news[0]
        all_rms += lane_pick(rms, 1)
        row = lax.rsqrt(rows_ref[:, 6:7] / row_mean) * scale
        head_out[...] = head_ref[...] + grads_ref[GRAD_HEAD : GRAD_HEAD + 64, :].astype(jnp.float32) * row * lax.rsqrt(news[0])
        for layer in range(LAYERS):
            for name, first, rows, blocks, block_at in matrices(layer):
                col_at = (block_at - 2 - 13 * layer) * D
                old = lambda j: cols_ref[layer : layer + 1, col_at + j * D : col_at + (j + 1) * D]
                news, row_mean, rms, scale = columns(block_at, blocks, old, 2 * name - 2 + layer, name)
                all_rms += lane_pick(rms, 2 * name - 2 + layer)
                lane = 3 * layer + name - 2
                state = down_ref[:, layer : layer + 1] if name == 5 else rows_ref[:, lane : lane + 1]
                row = lax.rsqrt(state / row_mean) * scale
                source, target = ((in_ref, in_out), (mix_ref, mix_out), (gate_ref, gate_out), (low_ref, low_out))[name - 2]
                for j in range(blocks):
                    cols_out[layer : layer + 1, col_at + j * D : col_at + (j + 1) * D] = news[j]
                    span = slice(j * D, (j + 1) * D)
                    grad = grads_ref[first + j * rows : first + (j + 1) * rows, :].astype(jnp.float32)
                    target[layer, :, span] = source[layer, :, span] + grad * row * lax.rsqrt(news[j])
        rms_out[...] = all_rms

    row = lax.rsqrt(turn(table_row_ref[...] / factors[1:2, :ROW_TILE])) * factors[2:3, 0:1]
    embed_out[...] = embed_ref[...] + table_ref[...].astype(jnp.float32) * row * factors[0:1, :]


def run_update(totals, stat, table, embed, table_row, grads, rows, down, top_cols, cols, others):
    row_count = embed.shape[0]
    tile = pl.BlockSpec((ROW_TILE, D), lambda i: (i, 0))
    lane = pl.BlockSpec((1, ROW_TILE), lambda i: (0, i))
    shape = lambda v: jax.ShapeDtypeStruct(v.shape, jnp.float32)
    one = jax.ShapeDtypeStruct((1, D), jnp.float32)
    outs = [shape(embed), one, one, shape(cols)] + [shape(v) for v in others] + [one]
    return pl.pallas_call(
        functools.partial(update_kernel, totals),
        grid=(-(-row_count // ROW_TILE),),
        in_specs=[whole(stat.shape), tile, tile, lane]
        + [whole(v.shape) for v in (grads, rows, down, top_cols, cols)]
        + [whole(v.shape) for v in others],
        out_specs=[tile] + [whole(v.shape) for v in outs[1:]],
        out_shape=outs,
        scratch_shapes=[pltpu.VMEM((8, D), jnp.float32)],
        compiler_params=pltpu.CompilerParams(vmem_limit_bytes=48 * 2**20),
    )(stat, table, embed, table_row, grads, rows, down, top_cols, cols, *others)


def fast_shards(
    token_ids,
    seq_lengths,
    valid_mask,
    deal_order,
    log_scale,
    embed_master,
    attn_in,
    attn_out,
    ffn_in,
    ffn_out,
    head_master,
    norm_master,
    embed_rows,
    head_rows,
    layer_rows,
    ffn_out_rows,
    layer_cols,
    embed_head_cols,
    norm_state,
    scale_state,
):
    tokens = token_ids.shape[0]
    shard_rows = embed_master.shape[0]
    my_dp = lax.axis_index("dp")
    position = jnp.arange(tokens, dtype=jnp.int32)
    bounds = jnp.cumsum(seq_lengths[0])
    segment = jnp.sum((position[:, None] >= bounds[None, :]).astype(jnp.int32), axis=1)

    key, wanted, most = slot_plan(token_ids, shard_rows)
    asks = jnp.concatenate(
        [wanted.reshape(8, 1, SLOTS), jnp.broadcast_to(most, (8, 1, 128 - SLOTS))], axis=2
    ).astype(jnp.int32)
    packed = pack_weights(attn_in, attn_out, ffn_in, ffn_out, head_master, norm_master)
    weights, got_rows, asked = gather_weights(packed, asks, embed_master, plan(PACKED, 4, 0.36), 0)
    crowded = jnp.max(asked[:, :, 0, SLOTS:]) >= SLOTS

    def dense_rows():
        table = lax.all_gather(embed_master.astype(jnp.bfloat16), "dp", axis=0, tiled=True)
        return jnp.take(table, token_ids, axis=0)

    def slot_rows():
        return jnp.take(got_rows.reshape(-1, D), jnp.minimum(key, 8 * SLOTS - 1), axis=0)

    stream = lax.cond(crowded, dense_rows, slot_rows)
    norms = jnp.pad(
        weights[:, NORM_AT : NORM_AT + 10, :64].transpose(1, 0, 2).reshape(10, D).astype(jnp.float32),
        ((0, 6), (0, 0)),
    )
    seg_col, seg_row = segment.reshape(-1, 1), segment.reshape(1, -1)
    valid_row = valid_mask.reshape(1, -1)
    *saved, unit_parts, pooled_low, head_out = run_forward(
        stream, seg_col, seg_row, valid_row, weights, norms
    )
    loss_value, own_rows, grad_scale = run_contrast(unit_parts, deal_order, log_scale, 1)
    loss_value, grad_scale = loss_value[0, 0], grad_scale[0]
    shard_grads, table_rows, norm_sum, grad_first = run_backward(
        own_rows, head_out, pooled_low, seg_col, seg_row, valid_row, key.reshape(1, -1), weights, norms, saved, 2
    )
    table_slots = asked[:, :, 0, :SLOTS].reshape(1, -1)
    table_row = embed_rows.reshape(1, -1)
    row_state = jnp.pad(
        jnp.concatenate([layer_rows.reshape(6, -1), head_rows.reshape(1, -1)], axis=0), ((0, 1), (0, 0))
    ).T
    shared = (shard_grads, norm_sum, table_row, row_state, ffn_out_rows.T)

    def dense_stats():
        full = jnp.zeros((shard_rows * 8, D), jnp.float32).at[token_ids].add(
            grad_first.astype(jnp.float32)
        )
        full = lax.psum_scatter(full, "dp", scatter_dimension=0, tiled=True)
        return run_stats(True, (lax.psum(full, "group"),), *shared)

    def slot_stats():
        return run_stats(False, (table_slots, table_rows.reshape(-1, D)), *shared)

    table_grad, table_row_new, stats, rows_new, down_new = lax.cond(
        crowded, dense_stats, slot_stats
    )
    sums = total(stats, 3)
    totals = (VOCAB, D, D, D, D, FF)
    (
        new_embed, new_table_cols, new_head_cols, new_cols, new_in, new_mix, new_gate, new_low, new_head, rms_row,
    ) = run_update(
        totals, sums, table_grad, embed_master, table_row_new, shard_grads, rows_new, down_new,
        embed_head_cols, layer_cols, (attn_in, attn_out, ffn_in, ffn_out, head_master),
    )
    norm_grad = sums.reshape(-1, D)[NORM_ROW : NORM_ROW + 10].reshape(2 * LAYERS + 1, 2, D)
    shard_norm = lax.dynamic_slice_in_dim(norm_grad, my_dp * norm_state.shape[2], norm_state.shape[2], 2)
    norm_delta, norm_second = unfactored(shard_norm, norm_state)
    scale_delta, scale_state_new = unfactored(grad_scale, scale_state)
    state_new = rows_new.T
    return (
        loss_value,
        new_embed,
        new_in,
        new_mix,
        new_gate,
        new_low,
        new_head,
        norm_master + norm_delta,
        log_scale + scale_delta,
        table_row_new[0],
        state_new[6],
        state_new[:6].reshape(layer_rows.shape),
        down_new.T,
        new_cols,
        new_table_cols[0],
        new_head_cols[0],
        norm_second,
        scale_state_new,
        rms_row[0, :10],
    )


def solution(mesh):
    in_specs = (
        P(("dp", "group")),
        P(("dp", "group"), None),
        P(("dp", "group")),
        P(),
        P(),
        P("dp", None),
        P(None, "dp", None),
        P(None, "dp", None),
        P(None, "dp", None),
        P(None, "dp", None),
        P("dp", None),
        P(None, None, "dp"),
        P("dp"),
        P("dp"),
        P(None, None, "dp"),
        P(None, "dp"),
        P(),
        P(),
        P(None, None, "dp"),
        P(),
    )
    out_specs = (
        P(),
        P("dp", None),
        P(None, "dp", None),
        P(None, "dp", None),
        P(None, "dp", None),
        P(None, "dp", None),
        P("dp", None),
        P(None, None, "dp"),
        P(),
        P("dp"),
        P("dp"),
        P(None, None, "dp"),
        P(None, "dp"),
        P(),
        P(),
        P(),
        P(None, None, "dp"),
        P(),
        P(),
    )
    body = fast_shards if dict(mesh.shape) == {"dp": 8, "group": 4} else shards
    return jax.shard_map(body, mesh=mesh, in_specs=in_specs, out_specs=out_specs, check_vma=False)
```

```python
import functools

import jax
import jax.numpy as jnp
from jax import lax
from jax.experimental import pallas as pl
from jax.experimental.pallas import tpu as pltpu
from jax.sharding import PartitionSpec as P

D = 512
HEADS = 8
HEAD_DIM = 64
FF = 2048
VOCAB = 30528
LAYERS = 2


NORM_EPS = 1e-06
UNIT_EPS = 1e-06
STATE_EPS = 1e-30
DECAY_RATE = 0.5
CLIP_LEVEL = 0.05
RATE_SCALE = 10.0
NORM_RATE = 0.1


def layer_norm(values, gain_vec, shift_vec):
    center = values - jnp.mean(values, axis=-1, keepdims=True)
    spread = jnp.mean(center * center, axis=-1, keepdims=True)
    return center * lax.rsqrt(spread + NORM_EPS) * gain_vec + shift_vec


def geglu(joined):
    half_width = joined.shape[-1] // 2
    return jax.nn.gelu(joined[:, :half_width]) * joined[:, half_width:]


def alibi_slopes(head_count):
    return 2.0 ** (-8.0 * (jnp.arange(head_count).astype(jnp.float32) + 1.0) / head_count)


def normalize(vectors):
    return vectors * lax.rsqrt(jnp.sum(vectors * vectors, axis=-1, keepdims=True) + UNIT_EPS)


def contrast(unit_all, scale_arg, deal_order):
    pair_count = deal_order.shape[0] // 2
    queries = jnp.take(unit_all, deal_order[:pair_count], axis=0)
    documents = jnp.take(unit_all, deal_order[pair_count:], axis=0)
    logits = jnp.exp(scale_arg[0]) * jnp.matmul(
        queries, documents.T, precision=lax.Precision.HIGHEST
    )
    by_row = jax.nn.logsumexp(logits, axis=1)
    by_column = jax.nn.logsumexp(logits, axis=0)
    return jnp.sum(0.5 * (by_row + by_column) - jnp.diagonal(logits))


def unfactored(grad_full, state):
    state_new = DECAY_RATE * state + (1.0 - DECAY_RATE) * (grad_full * grad_full + STATE_EPS)
    return (-NORM_RATE * grad_full * lax.rsqrt(state_new), state_new)


def block_scores(query_rows, key_all, seg_rows, segment, head_count):
    row_count = query_rows.shape[0]
    raw_scores = jnp.einsum("thc,shc->hts", query_rows, key_all, preferred_element_type=jnp.float32)
    row_pos = jnp.arange(row_count, dtype=jnp.int32)
    col_pos = jnp.arange(key_all.shape[0], dtype=jnp.int32)
    distance = jnp.abs(row_pos[:, None] - col_pos[None, :]).astype(jnp.float32)
    scores = (
        raw_scores * HEAD_DIM ** (-0.5) + -alibi_slopes(head_count)[:, None, None] * distance[None]
    )
    same_seq = seg_rows[:, None] == segment[None, :]
    return jnp.where(same_seq[None], scores, -jnp.inf)


def split_qkv(qkv_low, head_count):
    tokens = qkv_low.shape[0]
    split_heads = qkv_low.reshape(tokens, 3, head_count, qkv_low.shape[1] // (3 * head_count))
    return (split_heads[:, 0], split_heads[:, 1], split_heads[:, 2])


def attend(qkv_low, segment, head_count):
    model_width = qkv_low.shape[1] // 3
    query_all, key_all, value_all = split_qkv(qkv_low, head_count)
    scores = block_scores(query_all, key_all, segment, segment, head_count)
    row_max = jnp.max(scores, axis=-1, keepdims=True)
    exponent = jnp.exp(scores - row_max)
    row_total = jnp.sum(exponent, axis=-1, keepdims=True)
    prob_low = (exponent / row_total).astype(jnp.bfloat16)
    mixed_list = jnp.einsum(
        "hts,shc->thc", prob_low, value_all, preferred_element_type=jnp.float32
    ).reshape(-1, model_width)
    lse_list = row_max[..., 0] + jnp.log(row_total[..., 0])
    return (mixed_list, lse_list)


def attend_back(qkv_low, segment, head_count, lse_all, grad_mixed):
    tokens = qkv_low.shape[0]
    query_all, key_all, value_all = split_qkv(qkv_low, head_count)
    grad_out = grad_mixed.reshape(tokens, head_count, -1)
    block_rows = min(tokens, 512)
    scores = block_scores(query_all, key_all, segment, segment, head_count)
    prob_full = jnp.exp(scores - lse_all[:, 0:block_rows, None])
    grad_value = jnp.einsum(
        "hts,thc->shc", prob_full.astype(jnp.bfloat16), grad_out, preferred_element_type=jnp.float32
    )
    grad_prob = jnp.einsum("thc,shc->hts", grad_out, value_all, preferred_element_type=jnp.float32)
    inner = jnp.sum(prob_full * grad_prob, axis=-1, keepdims=True)
    grad_raw = (prob_full * (grad_prob - inner) * HEAD_DIM ** (-0.5)).astype(jnp.bfloat16)
    query_list = jnp.einsum("hts,shc->thc", grad_raw, key_all, preferred_element_type=jnp.float32)
    grad_key = jnp.einsum("hts,thc->shc", grad_raw, query_all, preferred_element_type=jnp.float32)
    return (
        jnp.stack([query_list, grad_key, grad_value], axis=1)
        .reshape(tokens, -1)
        .astype(jnp.bfloat16)
    )


def shards(
    token_ids,
    seq_lengths,
    valid_mask,
    deal_order,
    log_scale,
    embed_master,
    attn_in,
    attn_out,
    ffn_in,
    ffn_out,
    head_master,
    norm_master,
    embed_rows,
    head_rows,
    layer_rows,
    ffn_out_rows,
    layer_cols,
    embed_head_cols,
    norm_state,
    scale_state,
):
    tokens = token_ids.shape[0]
    model_width = embed_master.shape[1]
    seq_count = seq_lengths.shape[1]
    head_count = HEADS
    position = jnp.arange(tokens, dtype=jnp.int32)
    bounds = jnp.cumsum(seq_lengths[0])
    segment = jnp.sum((position[:, None] >= bounds[None, :]).astype(jnp.int32), axis=1)
    piece_rows = lax.all_gather(embed_master.astype(jnp.bfloat16), "dp", axis=0, tiled=True)
    local_idx = token_ids
    inside = (local_idx >= 0) & (local_idx < piece_rows.shape[0])
    picked = jnp.take(piece_rows, jnp.clip(local_idx, 0, piece_rows.shape[0] - 1), axis=0).astype(
        jnp.float32
    )
    stream = jnp.where(inside[:, None], picked, 0.0)
    w_qkv, w_attn, w_gate_up, w_down, w_head, norm_low = (
        lax.all_gather(attn_in.astype(jnp.bfloat16), "dp", axis=1, tiled=True),
        lax.all_gather(attn_out.astype(jnp.bfloat16), "dp", axis=1, tiled=True),
        lax.all_gather(ffn_in.astype(jnp.bfloat16), "dp", axis=1, tiled=True),
        lax.all_gather(ffn_out.astype(jnp.bfloat16), "dp", axis=1, tiled=True),
        lax.all_gather(head_master.astype(jnp.bfloat16), "dp", axis=0, tiled=True),
        lax.all_gather(norm_master.astype(jnp.bfloat16), "dp", axis=2, tiled=True),
    )
    norms = norm_low.astype(jnp.float32)
    kept_list = []
    for layer_idx in range(LAYERS):
        stream_low = stream.astype(jnp.bfloat16)
        qkv_low = jnp.dot(stream_low, w_qkv[layer_idx], preferred_element_type=jnp.float32).astype(
            jnp.bfloat16
        )
        mixed_heads, lse_all = attend(qkv_low, segment, head_count)
        mixed_low = mixed_heads.astype(jnp.bfloat16)
        resid_one = stream + jnp.dot(
            mixed_low, w_attn[layer_idx], preferred_element_type=jnp.float32
        )
        normed = layer_norm(resid_one, norms[2 * layer_idx, 0], norms[2 * layer_idx, 1])
        normed_low = normed.astype(jnp.bfloat16)
        joined = jnp.dot(normed_low, w_gate_up[layer_idx], preferred_element_type=jnp.float32)
        hidden_low = geglu(joined).astype(jnp.bfloat16)
        resid_two = normed + jnp.dot(
            hidden_low, w_down[layer_idx], preferred_element_type=jnp.float32
        )
        kept_list.append(
            (
                stream_low,
                qkv_low,
                lse_all,
                mixed_low,
                resid_one,
                normed_low,
                joined,
                hidden_low,
                resid_two,
            )
        )
        stream = layer_norm(resid_two, norms[2 * layer_idx + 1, 0], norms[2 * layer_idx + 1, 1])
    final = layer_norm(stream, norms[2 * LAYERS, 0], norms[2 * LAYERS, 1])
    member = (
        (segment[None, :] == jnp.arange(seq_count, dtype=jnp.int32)[:, None])
        & (valid_mask[None, :] > 0)
    ).astype(jnp.float32)
    counts = jnp.maximum(jnp.sum(member, axis=1), 1.0)
    pooled = jnp.matmul(member, final, precision=lax.Precision.HIGHEST) / counts[:, None]
    pooled_low = pooled.astype(jnp.bfloat16)
    head_out = jnp.dot(pooled_low, w_head, preferred_element_type=jnp.float32)
    unit_vecs, unit_back = jax.vjp(normalize, head_out)
    unit_every = lax.all_gather(unit_vecs, ("dp", "group"), axis=0, tiled=True)
    loss_value, loss_back = jax.vjp(
        lambda unit_all, scale_arg: contrast(unit_all, scale_arg, deal_order), unit_every, log_scale
    )
    grad_units, grad_scale = loss_back(jnp.ones_like(loss_value))
    own_rows = lax.dynamic_slice_in_dim(
        grad_units, lax.axis_index(("dp", "group")) * seq_count, seq_count, 0
    )
    grad_head_out = unit_back(own_rows)[0].astype(jnp.bfloat16)
    grad_head = jnp.dot(pooled_low.T, grad_head_out, preferred_element_type=jnp.float32)
    grad_pooled = jnp.dot(grad_head_out, w_head.T, preferred_element_type=jnp.float32)
    grad_final = jnp.matmul(
        member.T, grad_pooled / counts[:, None], precision=lax.Precision.HIGHEST
    )
    final_back = jax.vjp(layer_norm, stream, norms[2 * LAYERS, 0], norms[2 * LAYERS, 1])[1]
    grad_stream, gain_last, shift_last = final_back(grad_final)
    norm_grads = [None] * (2 * LAYERS + 1)
    norm_grads[2 * LAYERS] = jnp.stack([gain_last, shift_last])
    qkv_grads = [None] * LAYERS
    attn_grads = [None] * LAYERS
    gate_grads = [None] * LAYERS
    down_grads = [None] * LAYERS
    for layer_idx in reversed(range(LAYERS)):
        (
            stream_low,
            qkv_low,
            lse_all,
            mixed_low,
            resid_one,
            normed_low,
            joined,
            hidden_low,
            resid_two,
        ) = kept_list[layer_idx]
        norm_two_back = jax.vjp(
            layer_norm, resid_two, norms[2 * layer_idx + 1, 0], norms[2 * layer_idx + 1, 1]
        )[1]
        grad_two, gain_two, shift_two = norm_two_back(grad_stream)
        norm_grads[2 * layer_idx + 1] = jnp.stack([gain_two, shift_two])
        grad_branch = grad_two.astype(jnp.bfloat16)
        down_grads[layer_idx] = jnp.dot(
            hidden_low.T, grad_branch, preferred_element_type=jnp.float32
        )
        grad_hidden = jnp.dot(grad_branch, w_down[layer_idx].T, preferred_element_type=jnp.float32)
        grad_joined = jax.vjp(geglu, joined)[1](grad_hidden)[0].astype(jnp.bfloat16)
        gate_grads[layer_idx] = jnp.dot(
            normed_low.T, grad_joined, preferred_element_type=jnp.float32
        )
        grad_normed = grad_two + jnp.dot(
            grad_joined, w_gate_up[layer_idx].T, preferred_element_type=jnp.float32
        )
        norm_one_back = jax.vjp(
            layer_norm, resid_one, norms[2 * layer_idx, 0], norms[2 * layer_idx, 1]
        )[1]
        grad_one, gain_one, shift_one = norm_one_back(grad_normed)
        norm_grads[2 * layer_idx] = jnp.stack([gain_one, shift_one])
        grad_attended = grad_one.astype(jnp.bfloat16)
        attn_grads[layer_idx] = jnp.dot(
            mixed_low.T, grad_attended, preferred_element_type=jnp.float32
        )
        grad_mixed = jnp.dot(
            grad_attended, w_attn[layer_idx].T, preferred_element_type=jnp.float32
        ).astype(jnp.bfloat16)
        grad_qkv_low = attend_back(qkv_low, segment, head_count, lse_all, grad_mixed)
        qkv_grads[layer_idx] = jnp.dot(
            stream_low.T, grad_qkv_low, preferred_element_type=jnp.float32
        )
        grad_stream = grad_one + jnp.dot(
            grad_qkv_low, w_qkv[layer_idx].T, preferred_element_type=jnp.float32
        )
    row_count = embed_master.shape[0] * lax.axis_size("dp")
    local_idx = token_ids
    inside = (local_idx >= 0) & (local_idx < row_count)
    slot_idx = jnp.where(inside, local_idx, row_count)
    embed_grad = lax.psum_scatter(
        jnp.zeros((row_count, model_width), jnp.float32).at[slot_idx].add(grad_stream, mode="drop"),
        "dp",
        scatter_dimension=0,
        tiled=True,
    )
    grad_qkv = jnp.stack(qkv_grads)
    grad_attn = jnp.stack(attn_grads)
    grad_gate_up = jnp.stack(gate_grads)
    grad_down = jnp.stack(down_grads)
    grad_norm = jnp.stack(norm_grads)
    owned = (
        lax.psum_scatter(grad_qkv, "dp", scatter_dimension=1, tiled=True),
        lax.psum_scatter(grad_attn, "dp", scatter_dimension=1, tiled=True),
        lax.psum_scatter(grad_gate_up, "dp", scatter_dimension=1, tiled=True),
        lax.psum_scatter(grad_down, "dp", scatter_dimension=1, tiled=True),
        lax.psum_scatter(grad_head, "dp", scatter_dimension=0, tiled=True),
        lax.psum_scatter(grad_norm, "dp", scatter_dimension=2, tiled=True),
    )
    shard_qkv, shard_attn, shard_gate_up, shard_down, shard_head, shard_norm, shard_embed = (
        lax.psum((owned[0], owned[1], owned[2], owned[3], owned[4], owned[5], embed_grad), "group")
    )
    grad_list = [
        shard_embed[None],
        shard_head[None],
        shard_qkv,
        shard_attn,
        shard_gate_up,
        shard_down,
    ]
    master_list = [embed_master[None], head_master[None], attn_in, attn_out, ffn_in, ffn_out]
    state_list = [
        embed_rows[None],
        head_rows[None],
        layer_rows[:, 0],
        layer_rows[:, 1],
        layer_rows[:, 2],
        ffn_out_rows,
    ]
    col_list = [
        embed_head_cols[0:1],
        embed_head_cols[1:2],
        layer_cols[:, : 3 * D],
        layer_cols[:, 3 * D : 4 * D],
        layer_cols[:, 4 * D : 4 * D + 2 * FF],
        layer_cols[:, 4 * D + 2 * FF :],
    ]
    total_rows = [VOCAB, D, D, D, D, FF]
    wide_rate = RATE_SCALE / D**0.5
    rates = [
        RATE_SCALE,
        wide_rate,
        wide_rate,
        RATE_SCALE / (D // 8) ** 0.5,
        wide_rate,
        RATE_SCALE / FF**0.5,
    ]
    square_list = [grad_part * grad_part for grad_part in grad_list]
    rows_new = [
        DECAY_RATE * state_list[entry_idx]
        + (1.0 - DECAY_RATE) * (jnp.mean(square_list[entry_idx], axis=-1) + STATE_EPS)
        for entry_idx in range(6)
    ]
    col_parts = jnp.concatenate(
        [jnp.sum(square_part, axis=1).reshape(-1) for square_part in square_list]
    )
    row_parts = jnp.concatenate([jnp.sum(row_part, axis=-1) for row_part in rows_new])
    col_sum, row_sum = lax.psum((col_parts, row_parts), "dp")
    row_means = []
    lead_start = 0
    for entry_idx in range(6):
        lead_count = grad_list[entry_idx].shape[0]
        row_means.append(row_sum[lead_start : lead_start + lead_count] / total_rows[entry_idx])
        lead_start = lead_start + lead_count
    cols_new = []
    steps_all = []
    col_start = 0
    for entry_idx in range(6):
        lead_count = grad_list[entry_idx].shape[0]
        col_width = grad_list[entry_idx].shape[2]
        col_full = col_sum[col_start : col_start + lead_count * col_width].reshape(
            lead_count, col_width
        )
        col_state_new = DECAY_RATE * col_list[entry_idx] + (1.0 - DECAY_RATE) * (
            col_full / total_rows[entry_idx] + STATE_EPS
        )
        cols_new.append(col_state_new)
        steps_all.append(
            grad_list[entry_idx]
            * lax.rsqrt(
                rows_new[entry_idx][:, :, None]
                * col_state_new[:, None, :]
                / row_means[entry_idx][:, None, None]
            )
        )
        col_start = col_start + lead_count * col_width
    step_squares = []
    step_parts = jnp.concatenate(
        [jnp.sum(step_dir * step_dir, axis=(1, 2)) for step_dir in steps_all]
    )
    step_sum = lax.psum(step_parts, "dp")
    lead_start = 0
    for entry_idx in range(6):
        lead_count = grad_list[entry_idx].shape[0]
        step_squares.append(step_sum[lead_start : lead_start + lead_count])
        lead_start = lead_start + lead_count
    new_weights = []
    rms_list = []
    for entry_idx in range(6):
        cell_count = total_rows[entry_idx] * grad_list[entry_idx].shape[2]
        step_rms = jnp.sqrt(step_squares[entry_idx] / cell_count)
        rms_list.append(step_rms)
        delta = (
            -rates[entry_idx]
            * steps_all[entry_idx]
            / jnp.maximum(1.0, step_rms / CLIP_LEVEL)[:, None, None]
        )
        new_weights.append(master_list[entry_idx] + delta)
    norm_delta, norm_second = unfactored(shard_norm, norm_state)
    scale_delta, scale_state_new = unfactored(grad_scale, scale_state)
    return (
        loss_value,
        new_weights[0][0],
        new_weights[2],
        new_weights[3],
        new_weights[4],
        new_weights[5],
        new_weights[1][0],
        norm_master + norm_delta,
        log_scale + scale_delta,
        rows_new[0][0],
        rows_new[1][0],
        jnp.stack([rows_new[2], rows_new[3], rows_new[4]], axis=1),
        rows_new[5],
        jnp.concatenate([cols_new[2], cols_new[3], cols_new[4], cols_new[5]], axis=1),
        cols_new[0][0],
        cols_new[1][0],
        norm_second,
        scale_state_new,
        jnp.concatenate(rms_list),
    )


SLOTS = 80
PART = 1024


MESH = pl.DeviceIdType.MESH
BF=jnp.bfloat16

def place():
    dp = lax.axis_index("dp"); g = lax.axis_index("group")
    return dp // 2, dp % 2, g // 2, g % 2

def dev(z, x, y, c):
    return (z * 2 + x, y * 2 + c)

def entry_barrier(peers):
    bar = pltpu.get_barrier_semaphore()
    for p in peers:
        pl.semaphore_signal(bar, inc=1, device_id=p, device_id_type=MESH)
    pl.semaphore_wait(bar, len(peers))

def mult(v, m=16):
    return pl.multiple_of(v, m)


def slot_plan(token_ids, shard_rows):
    tokens = token_ids.shape[0]
    owner = token_ids // shard_rows
    local = token_ids - owner * shard_rows
    index = jnp.arange(tokens, dtype=jnp.int32)
    same_id = token_ids[:, None] == token_ids[None, :]
    first = jnp.min(jnp.where(same_id, index[None, :], tokens), axis=1)
    leads = first == index
    same_owner = owner[:, None] == owner[None, :]
    slot = jnp.sum(
        (same_owner & leads[None, :] & (index[None, :] < first[:, None])).astype(jnp.int32), axis=1
    )
    key = jnp.where(slot < SLOTS, owner * SLOTS + slot, 8 * SLOTS)
    wanted = jnp.max(
        jnp.where(
            key[:, None] == jnp.arange(8 * SLOTS, dtype=jnp.int32)[None, :], local[:, None], -1
        ),
        axis=0,
    )
    return key, wanted, jnp.max(slot)


def column_blocks(rows):
    lead, count, width = rows.shape
    return (
        rows.reshape(lead, count, width // D, D).transpose(0, 2, 1, 3).reshape(lead, -1, D)
    )


def pack_weights(attn_in, attn_out, ffn_in, ffn_out, head_master, norm_master):
    layers = jnp.concatenate(
        [column_blocks(attn_in), attn_out, column_blocks(ffn_in), ffn_out], axis=1
    ).astype(jnp.bfloat16)
    norm_rows = jnp.pad(
        norm_master.reshape(10, -1).astype(jnp.bfloat16), ((0, 22), (0, D - norm_master.shape[2]))
    )
    return jnp.concatenate(
        [norm_rows, layers.reshape(-1, D), head_master.astype(jnp.bfloat16)], axis=0
    )


def dot_nn(left, right):
    return lax.dot_general(left, right, (((1,), (0,)), ((), ())), preferred_element_type=jnp.float32)


def dot_nt(left, right):
    return lax.dot_general(left, right, (((1,), (1,)), ((), ())), preferred_element_type=jnp.float32)


def dot_tn(left, right):
    return lax.dot_general(left, right, (((0,), (0,)), ((), ())), preferred_element_type=jnp.float32)


def exact_dot(left, right, dims=((1,), (0,))):
    return lax.dot_general(
        left, right, (dims, ((), ())), precision=lax.Precision.HIGHEST, preferred_element_type=jnp.float32
    )


GELU_SCALE = (2.0 / 3.141592653589793) ** 0.5
GELU_CUBE = 0.044715
TILE = 256


def norm_parts(values):
    center = values - jnp.mean(values, axis=-1, keepdims=True)
    inverse = lax.rsqrt(jnp.mean(center * center, axis=-1, keepdims=True) + NORM_EPS)
    return center * inverse, inverse


def norm_back(scaled, inverse, grad_out, gain):
    grad_scaled = grad_out * gain
    mean_grad = jnp.mean(grad_scaled, axis=-1, keepdims=True)
    mean_both = jnp.mean(grad_scaled * scaled, axis=-1, keepdims=True)
    return inverse * (grad_scaled - mean_grad - scaled * mean_both)


def gelu_parts(value):
    bend = jnp.tanh(GELU_SCALE * (value + GELU_CUBE * value * value * value))
    half = 0.5 * (1.0 + bend)
    slope = half + 0.5 * value * (1.0 - bend * bend) * GELU_SCALE * (1.0 + 3.0 * GELU_CUBE * value * value)
    return value * half, slope


def block(w_ref, start):
    return w_ref[:, start : start + 64, :].reshape(D, D)


def down_block(w_ref, j):
    return w_ref[2 * j : 2 * j + 2, 768:1024, :].reshape(D, D)


def fill_distance(far, seg_col_ref, seg_row_ref):
    tokens = far.shape[0]
    def body(i, carry):
        start = pl.multiple_of(i * 64, 64)
        rows = lax.broadcasted_iota(jnp.int32, (64, tokens), 0) + start
        cols = lax.broadcasted_iota(jnp.int32, (64, tokens), 1)
        gap = jnp.abs(rows - cols).astype(jnp.float32)
        same = seg_col_ref[pl.ds(start, 64), :] == seg_row_ref[...]
        far[pl.ds(start, 64), :] = jnp.where(same, gap, jnp.inf)
        return carry
    lax.fori_loop(0, tokens // 64, body, 0)


def forward_kernel(
    first_ref, seg_col_ref, seg_row_ref, valid_ref, w_ref, head_ref, norm_ref,
    low_ref, qkv_ref, lse_ref, mix_ref, one_ref, two_ref, unit_ref, pool_ref, zed_ref,
    x_s, far, acc,
):
    layer = pl.program_id(0)
    tokens = x_s.shape[0]
    tiles = tokens // TILE

    @pl.when(layer == 0)
    def _():
        x_s[...] = first_ref[...].astype(jnp.float32)
        fill_distance(far, seg_col_ref, seg_row_ref)

    def project(i, carry):
        rows = pl.ds(pl.multiple_of(i * TILE, TILE), TILE)
        low = x_s[rows, :].astype(jnp.bfloat16)
        low_ref[0, rows, :] = low
        for j in range(3):
            qkv_ref[0, rows, j * D : (j + 1) * D] = dot_nn(low, block(w_ref, j * 64)).astype(jnp.bfloat16)
        return carry

    lax.fori_loop(0, tiles, project, 0)
    for head in range(HEADS):
        lanes = slice(head * HEAD_DIM, (head + 1) * HEAD_DIM)
        keys = qkv_ref[0, :, D + head * HEAD_DIM : D + (head + 1) * HEAD_DIM]
        vals_t = qkv_ref[0, :, 2 * D + head * HEAD_DIM : 2 * D + (head + 1) * HEAD_DIM].T
        slope = 2.0 ** (-8.0 * (head + 1) / HEADS)
        for i in range(tiles):
            cols = slice(i * TILE, (i + 1) * TILE)
            scores = dot_nt(keys, qkv_ref[0, cols, lanes]) * HEAD_DIM**-0.5 - slope * far[:, cols]
            top = jnp.max(scores, axis=0, keepdims=True)
            raised = jnp.exp(scores - top)
            total = jnp.sum(raised, axis=0, keepdims=True)
            lse_ref[0, head, :, cols] = top + jnp.log(total)
            prob = (raised * (1.0 / total)).astype(jnp.bfloat16)
            mix_ref[0, lanes, cols] = dot_nn(vals_t, prob).astype(jnp.bfloat16)

    acc[...] = dot_tn(mix_ref[0], block(w_ref, 192))

    def feed(i, carry):
        rows = pl.ds(pl.multiple_of(i * TILE, TILE), TILE)
        resid = x_s[rows, :] + acc[rows, :]
        one_ref[0, rows, :] = resid
        at = 4 * layer
        scaled, _ = norm_parts(resid)
        hidden = scaled * norm_ref[pl.ds(at, 1), :] + norm_ref[pl.ds(at + 1, 1), :]
        low = hidden.astype(jnp.bfloat16)
        total = hidden
        for j in range(4):
            gate = dot_nn(low, block(w_ref, 256 + j * 64))
            up = dot_nn(low, block(w_ref, 512 + j * 64))
            bend = jnp.tanh(GELU_SCALE * (gate + GELU_CUBE * gate * gate * gate))
            mid = (0.5 * gate * (1.0 + bend) * up).astype(jnp.bfloat16)
            total = total + dot_nn(mid, down_block(w_ref, j))
        two_ref[0, rows, :] = total
        scaled, _ = norm_parts(total)
        x_s[rows, :] = scaled * norm_ref[pl.ds(at + 2, 1), :] + norm_ref[pl.ds(at + 3, 1), :]
        return carry

    lax.fori_loop(0, tiles, feed, 0)

    @pl.when(layer == LAYERS - 1)
    def _():
        pool_units(x_s, norm_ref, seg_row_ref, valid_ref, head_ref, unit_ref, pool_ref, zed_ref)


def members(seg_row_ref, valid_ref):
    tokens = seg_row_ref.shape[1]
    slot = lax.broadcasted_iota(jnp.int32, (8, tokens), 0)
    return jnp.where((seg_row_ref[...] == slot) & (valid_ref[...] > 0), 1.0, 0.0)


def whole(shape):
    return pl.BlockSpec(shape, lambda i: (0,) * len(shape))


def run_forward(first, seg_col, seg_row, valid, weights, norms):
    tokens = first.shape[0]
    low = jnp.bfloat16
    layered = lambda *s: pl.BlockSpec((1,) + s, lambda i: (i,) + (0,) * len(s))
    return pl.pallas_call(
        forward_kernel,
        grid=(LAYERS,),
        in_specs=[
            whole((tokens, D)), whole((tokens, 1)), whole((1, tokens)), whole((1, tokens)),
            pl.BlockSpec((8, PART, D), lambda i: (0, i, 0)),
            pl.BlockSpec((8, 64, D), lambda i: (0, 2 * PART // 64, 0)),
            whole(norms.shape),
        ],
        out_specs=[
            layered(tokens, D), layered(tokens, 3 * D), layered(HEADS, 1, tokens), layered(D, tokens),
            layered(tokens, D), layered(tokens, D), whole((16, 128)), whole((8, D)), whole((8, D)),
        ],
        out_shape=[
            jax.ShapeDtypeStruct((LAYERS, tokens, D), low),
            jax.ShapeDtypeStruct((LAYERS, tokens, 3 * D), low),
            jax.ShapeDtypeStruct((LAYERS, HEADS, 1, tokens), jnp.float32),
            jax.ShapeDtypeStruct((LAYERS, D, tokens), low),
            jax.ShapeDtypeStruct((LAYERS, tokens, D), jnp.float32),
            jax.ShapeDtypeStruct((LAYERS, tokens, D), jnp.float32),
            jax.ShapeDtypeStruct((16, 128), jnp.float32),
            jax.ShapeDtypeStruct((8, D), low),
            jax.ShapeDtypeStruct((8, D), jnp.float32),
        ],
        scratch_shapes=[
            pltpu.VMEM((tokens, D), jnp.float32), pltpu.VMEM((tokens, tokens), jnp.float32),
            pltpu.VMEM((tokens, D), jnp.float32),
        ],
        compiler_params=pltpu.CompilerParams(vmem_limit_bytes=60 * 2**20),
    )(first, seg_col, seg_row, valid, weights, weights, norms)


PACK_LAYER = (32, 32 + PART)
PACK_HEAD = 32 + 2 * PART
PARCELS = (
    (0, 144, 64), (288, 128, 48), (544, 128, 48), (800, 128, 48),
    (1056, 128, 48), (1312, 128, 48), (1568, 128, 48), (1824, 160, 32),
)
GATHER_ORDER = (
    "ask", "s00", "s01", "s02", "s03", "set", "ans", "z00", "z10", "x03", "z20", "x13", "x23", "rel", "x33", "y000",
    "z30", "y100", "y031", "y131", "z01", "z11", "y200", "z21", "y231", "y300", "z31", "y331", "y010", "x00", "y210",
    "y110", "x10", "z02", "s04", "x20", "y001", "y310", "x01", "z12", "s05", "x11", "y101", "y020", "x30", "z22",
    "s06", "z40", "y011", "x21", "y201", "z32", "s07", "x31", "y301", "y111", "z50", "y120", "y400", "y220", "x02",
    "y211", "x43", "z41", "y311", "y320", "z60", "x12", "y500", "z42", "z51", "x53", "z70", "y021", "y431", "z52",
    "y410", "x40", "z61", "x22", "y600", "x63", "a0", "y121", "z62", "y420", "y510", "rows", "y531", "z71", "x50",
    "x32", "y700", "p0", "x73", "y401", "a1", "y520", "y221", "z72", "h00", "y610", "y631", "h01", "x60", "x41",
    "x42", "h02", "x51", "a2", "y620", "h03", "y321", "y501", "y710", "x70", "h04", "y731", "x52", "h05", "x61",
    "y720", "a3", "h06", "y601", "y411", "h07", "y421", "m0", "y511", "x62", "y701", "x71", "f00", "y521", "y611",
    "a4", "x72", "f01", "y621", "a5", "y711", "p1", "h10", "y721", "a6", "h11", "h12", "h13", "h14", "a7", "h15",
    "h16", "h17", "m1", "f10", "f11", "end",
)


def nearest(z):
    return (z + 1 - 2 * (z % 2), 2 - z // 2, 3 - 3 * (z // 2), z)


def gather_stages(w_ref, ag_ref, zs, zr, xs, xr, ys, yr, cs, cr):
    z, x, y, c = place()
    me = z * 2 + x
    inner = (z == 1) | (z == 2)
    pair = dev(z + 1 - 2 * (z % 2), x, y, c)
    across = dev(3 - z, x, y, c)
    outward = dev((3 * z + 1) % 4, x, y, c)
    xp, yp, cp = dev(z, 1 - x, y, c), dev(z, x, 1 - y, c), dev(z, x, y, 1 - c)
    near = nearest(z)

    def rc(src, dst, s, r, d):
        return pltpu.make_async_remote_copy(src, dst, s, r, device_id=d, device_id_type=MESH)

    def shard(n, f):
        return near[n] * 2 + (x if f == 0 else 1 - x)

    steps = {}
    always, within = [], []
    others = [(0, 0), (1, 0), (2, 0), (3, 1), (0, 1), (1, 1), (2, 1)]

    def parcel(q, base, half, spare):
        main = pl.ds(mult(base + c * half + y * spare), half - spare)
        extra = pl.ds(mult(base + c * half + y * (half - spare)), spare)
        every = pl.ds(mult(base + c * half), half)

        def at(n, f, rows):
            return ag_ref.at[shard(n, f), rows]

        own = w_ref.at[main]
        to_pair = rc(own, at(3, 0, main), zs.at[q, 0], zr.at[q, 0], pair)
        to_across = rc(own, at(3, 0, main), zs.at[q, 1], zr.at[q, 1], across)
        on = [
            rc(at(0, 0, main), at(0, 0, main), zs.at[q, 2], zr.at[q, 2], across),
            rc(at(1, 0, main), at(1, 0, main), zs.at[q, 3], zr.at[q, 1], outward),
            rc(at(2, 0, main), at(2, 0, main), zs.at[q, 4], zr.at[q, 2], outward),
        ]
        over = [rc(own if n == 3 else at(n, 0, main), at(n, 0, main), xs.at[q, n], xr.at[q, n], xp) for n in range(4)]
        planes, cores = {}, {}
        for n, f in others:
            planes[n, f] = rc(at(n, f, extra), at(n, f, extra), ys.at[q, 2 * n + f], yr.at[q, 2 * n + f], yp)
            cores[n, f] = rc(at(n, f, every), at(n, f, every), cs.at[q, 2 * n + f], cr.at[q, 2 * n + f], cp)
        always.extend([to_pair] + over + list(planes.values()) + list(cores.values()))
        within.extend([to_across] + on)
        landed = [rc(own, at(n, 0, main), zs.at[q, 0], zr.at[q, n], pair) for n in range(3)]

        def issue():
            pl.when(inner)(to_across.start)
            to_pair.start()
            over[3].start()

        def along(n):
            landed[n].wait_recv()
            pl.when(inner)(on[n].start)
            over[n].start()
            planes[n, 0].start()

        def sideways(n):
            over[n].wait_recv()
            planes[n, 1].start()

        def plane(n, f):
            planes[n, f].wait_recv()
            cores[n, f].start()

        def arrived():
            for copy in cores.values():
                copy.wait_recv()

        steps["s0%d" % q] = (issue,)
        for n in range(3):
            steps["z%d%d" % (q, n)] = (along, n)
        for n in range(4):
            steps["x%d%d" % (q, n)] = (sideways, n)
        for n, f in others:
            steps["y%d%d%d" % (q, n, f)] = (plane, n, f)
        steps["a%d" % q] = (arrived,)

    for q, spec in enumerate(PARCELS):
        parcel(q, *spec)

    def finish():
        for copy in always:
            copy.wait_send()

        @pl.when(inner)
        def _():
            for copy in within:
                copy.wait_send()

    return steps, finish


def request_stages(ask_ref, asks_ref, table_ref, table, picked, rows_s, got, sems, es, er, qs, qr):
    z, x, y, c = place()
    me = z * 2 + x
    g = y * 2 + c
    g2 = (1 - y) * 2 + c
    ep = [(lax.rem(me + k, 8), g) for k in range(8)]
    yp, cp = dev(z, x, 1 - y, c), dev(z, x, y, 1 - c)

    def rc(src, dst, s, r, d):
        return pltpu.make_async_remote_copy(src, dst, s, r, device_id=d, device_id_type=MESH)

    count = rows_s.shape[1]
    to_owner = [rc(ask_ref.at[ep[k][0]], asks_ref.at[g, me], qs.at[k], qr.at[k], ep[k]) for k in range(1, 8)]
    mine = pltpu.make_async_copy(ask_ref.at[me], asks_ref.at[g, me], sems.at[0])
    near = pltpu.make_async_copy(table_ref, table.at[pl.ds(0, table_ref.shape[0])], sems.at[1])
    to_plane = rc(asks_ref.at[g], asks_ref.at[g], qs.at[8], qr.at[8], yp)
    to_core = rc(asks_ref.at[g], asks_ref.at[g], qs.at[9], qr.at[9], cp)
    on_core = rc(asks_ref.at[g2], asks_ref.at[g2], qs.at[10], qr.at[10], cp)
    kept = pltpu.make_async_copy(rows_s.at[me], got.at[me], sems.at[2])
    answers = [rc(rows_s.at[ep[k][0]], got.at[me], es.at[k], er.at[k], ep[k]) for k in range(1, 8)]

    def load():
        near.start()

    def ask():
        for copy in to_owner:
            copy.start()
        mine.start()

    def answer():
        mine.wait()
        for copy in to_owner:
            copy.wait_recv()
        to_plane.start()
        to_core.start()
        wanted = asks_ref[pl.ds(g, 1)].reshape(8, 128).astype(jnp.float32).T
        near.wait()
        depth = table.shape[0] // 5
        rest = table.shape[0] - table_ref.shape[0]
        table[pl.ds(table_ref.shape[0], rest), :] = jnp.zeros((rest, D), jnp.float32)
        picked[...] = jnp.zeros(picked.shape, jnp.float32)
        ramp = lax.broadcasted_iota(jnp.int32, (count, depth), 1).astype(jnp.float32)

        def body(i, carry):
            low = table[pl.ds(pl.multiple_of(i * depth, depth), depth), :].astype(BF)
            shifted = ramp + (i * depth).astype(jnp.float32)
            for r in range(8):
                hot = jnp.where(wanted[:count, r : r + 1] == shifted, 1.0, 0.0).astype(BF)
                picked[r] += dot_nn(hot, low)
            return carry

        lax.fori_loop(0, 5, body, 0)
        rows_s[...] = picked[...].astype(BF)
        kept.start()
        for copy in answers:
            copy.start()

    def relay():
        to_plane.wait_recv()
        on_core.start()

    def take():
        kept.wait()
        for copy in answers:
            copy.wait_recv()

    def finish():
        to_core.wait_recv()
        on_core.wait_recv()
        for copy in answers + to_owner + [to_plane, to_core, on_core]:
            copy.wait_send()

    return load, ask, answer, relay, take, finish


def gather_forward_kernel(
    w_ref, ask_ref, table_ref, key_ref, seg_col_ref, seg_row_ref, valid_ref,
    ag_ref, asks_ref, low_out, qkv_out, lse_out, mix_out, one_out, two_out, unit_ref, pool_ref, zed_ref, norm_ref,
    table, picked, rows_s, got, weights, head, norm_low, low_s, qkv_s, lse_s, mix_s, one_s, two_s, x_s, far, acc,
    zs, zr, xs, xr, ys, yr, cs, cr, sems, es, er, qs, qr, loads, saves,
):
    z, x, y, c = place()
    me = z * 2 + x
    g = y * 2 + c
    tokens = x_s.shape[0]
    tiles = tokens // TILE
    peers = [(lax.rem(me + k, 8), g) for k in range(1, 8)] + [dev(z, x, 1 - y, c), dev(z, x, y, 1 - c)]
    barrier = pltpu.get_barrier_semaphore()
    for peer in peers:
        pl.semaphore_signal(barrier, inc=1, device_id=peer, device_id_type=MESH)
    steps, finish = gather_stages(w_ref, ag_ref, zs, zr, xs, xr, ys, yr, cs, cr)
    load, ask, answer, relay, take, ask_finish = request_stages(
        ask_ref, asks_ref, table_ref, table, picked, rows_s, got, sems, es, er, qs, qr
    )
    own = pltpu.make_async_copy(w_ref, ag_ref.at[me], sems.at[3])

    def loading(slot, rows, count, into):
        return pltpu.make_async_copy(ag_ref.at[:, pl.ds(rows, count)], into, loads.at[slot])

    fetch = {("norm", 0): loading(8, 0, 32, norm_low), ("head", 0): loading(9, PACK_HEAD, 64, head)}
    for layer in range(LAYERS):
        for part in range(4):
            fetch[layer, part] = loading(
                4 * layer + part, PACK_LAYER[layer] + 256 * part, 256, weights.at[layer, :, pl.ds(256 * part, 256)]
            )
    saving = {}
    for layer in range(LAYERS):
        for i, (source, target) in enumerate(
            ((low_s, low_out), (qkv_s, qkv_out), (lse_s, lse_out), (mix_s, mix_out), (one_s, one_out), (two_s, two_out))
        ):
            saving[layer, i] = pltpu.make_async_copy(source.at[layer], target.at[layer], saves.at[layer, i])

    def begin():
        load()
        own.start()

    def arrive(q):
        arrived[q]()
        if q == 0:
            own.wait()
            fetch["norm", 0].start()
        fetch[q // 4, q % 4].start()
        if q == 7:
            fetch["head", 0].start()

    def set_up():
        fill_distance(far, seg_col_ref, seg_row_ref)

    def first_rows():
        take()
        slots = lax.broadcasted_iota(jnp.int32, (tokens, got.shape[0] * got.shape[1]), 1)
        picks = jnp.where(slots == key_ref[...], 1.0, 0.0).astype(BF)
        x_s[...] = dot_nn(picks, got[...].reshape(-1, D))
        fetch["norm", 0].wait()
        norm_ref[...] = jnp.concatenate([norm_low[d, 0:16, 0:64].astype(jnp.float32) for d in range(8)], axis=1)

    def project(layer):
        fetch[layer, 0].wait()

        def body(i, carry):
            rows = pl.ds(pl.multiple_of(i * TILE, TILE), TILE)
            low = x_s[rows, :].astype(BF)
            low_s[layer, rows, :] = low
            for j in range(3):
                qkv_s[layer, rows, j * D : (j + 1) * D] = dot_nn(low, block(weights.at[layer], j * 64)).astype(BF)
            return carry

        lax.fori_loop(0, tiles, body, 0)
        saving[layer, 0].start()
        saving[layer, 1].start()

    def attend_head(layer, head):
        lanes = slice(head * HEAD_DIM, (head + 1) * HEAD_DIM)
        keys = qkv_s[layer, :, D + head * HEAD_DIM : D + (head + 1) * HEAD_DIM]
        vals_t = qkv_s[layer, :, 2 * D + head * HEAD_DIM : 2 * D + (head + 1) * HEAD_DIM].T
        slope = 2.0 ** (-8.0 * (head + 1) / HEADS)
        for i in range(tiles):
            cols = slice(i * TILE, (i + 1) * TILE)
            scores = dot_nt(keys, qkv_s[layer, cols, lanes]) * HEAD_DIM**-0.5 - slope * far[:, cols]
            top = jnp.max(scores, axis=0, keepdims=True)
            raised = jnp.exp(scores - top)
            total = jnp.sum(raised, axis=0, keepdims=True)
            lse_s[layer, head, :, cols] = top + jnp.log(total)
            prob = (raised * (1.0 / total)).astype(BF)
            mix_s[layer, lanes, cols] = dot_nn(vals_t, prob).astype(BF)

    def mix(layer):
        saving[layer, 2].start()
        saving[layer, 3].start()
        acc[...] = dot_tn(mix_s[layer], block(weights.at[layer], 192))

    def feed(layer, i):
        if i == 0:
            for part in (1, 2, 3):
                fetch[layer, part].wait()
        rows = pl.ds(i * TILE, TILE)
        resid = x_s[rows, :] + acc[rows, :]
        one_s[layer, rows, :] = resid
        at = 4 * layer
        scaled, _ = norm_parts(resid)
        hidden = scaled * norm_ref[at : at + 1, :] + norm_ref[at + 1 : at + 2, :]
        low = hidden.astype(BF)
        total = hidden
        for j in range(4):
            gate = dot_nn(low, block(weights.at[layer], 256 + j * 64))
            up = dot_nn(low, block(weights.at[layer], 512 + j * 64))
            bend = jnp.tanh(GELU_SCALE * (gate + GELU_CUBE * gate * gate * gate))
            mid = (0.5 * gate * (1.0 + bend) * up).astype(BF)
            total = total + dot_nn(mid, down_block(weights.at[layer], j))
        two_s[layer, rows, :] = total
        scaled, _ = norm_parts(total)
        x_s[rows, :] = scaled * norm_ref[at + 2 : at + 3, :] + norm_ref[at + 3 : at + 4, :]
        if i == tiles - 1:
            saving[layer, 4].start()
            saving[layer, 5].start()

    def end():
        fetch["head", 0].wait()
        pool_units(x_s, norm_ref, seg_row_ref, valid_ref, head, unit_ref, pool_ref, zed_ref)

    arrived = [steps["a%d" % q][0] for q in range(8)]
    for q in range(8):
        steps["a%d" % q] = (arrive, q)
    steps["ask"], steps["ans"], steps["rel"] = (ask,), (answer,), (relay,)
    steps["set"], steps["rows"], steps["end"] = (set_up,), (first_rows,), (end,)
    for layer in range(LAYERS):
        steps["p%d" % layer], steps["m%d" % layer] = (project, layer), (mix, layer)
        for head_index in range(HEADS):
            steps["h%d%d" % (layer, head_index)] = (attend_head, layer, head_index)
        for i in range(tiles):
            steps["f%d%d" % (layer, i)] = (feed, layer, i)
    begin()
    pl.semaphore_wait(barrier, len(peers))
    for name in GATHER_ORDER:
        fn, *rest = steps.pop(name)
        fn(*rest)
    assert not steps
    finish()
    ask_finish()
    for copy in saving.values():
        copy.wait()


def pool_units(x_s, norm_ref, seg_row_ref, valid_ref, head, unit_ref, pool_ref, zed_ref):
    scaled, _ = norm_parts(x_s[...])
    final = scaled * norm_ref[8:9, :] + norm_ref[9:10, :]
    member = members(seg_row_ref, valid_ref)
    counts = jnp.maximum(jnp.sum(member, axis=1, keepdims=True), 1.0)
    pooled = (exact_dot(member, final) / counts).astype(BF)
    pool_ref[...] = pooled
    zed = dot_nn(pooled, head[...].reshape(D, D))
    zed_ref[...] = zed
    unit = zed * lax.rsqrt(jnp.sum(zed * zed, axis=-1, keepdims=True) + UNIT_EPS)
    for s in range(4):
        for part in range(4):
            unit_ref[4 * s + part : 4 * s + part + 1, :] = unit[s : s + 1, part * 128 : (part + 1) * 128]


def run_gather_forward(packed, asks, embed, key_col, seg_col, seg_row, valid, cid):
    tokens = key_col.shape[0]
    low, full = jnp.bfloat16, jnp.float32
    near = pl.BlockSpec(memory_space=pltpu.VMEM)
    anywhere = pl.BlockSpec(memory_space=pl.ANY)
    shape = jax.ShapeDtypeStruct
    vmem = lambda dims, kind=low: pltpu.VMEM(dims, kind)
    sems = lambda *dims: pltpu.SemaphoreType.DMA(dims)
    padded = -(-embed.shape[0] // 640) * 640
    saved = [
        ((LAYERS, tokens, D), low), ((LAYERS, tokens, 3 * D), low), ((LAYERS, HEADS, 1, tokens), full),
        ((LAYERS, D, tokens), low), ((LAYERS, tokens, D), full), ((LAYERS, tokens, D), full),
    ]
    return pl.pallas_call(
        gather_forward_kernel,
        in_specs=[anywhere, near, anywhere, near, near, near, near],
        out_specs=[anywhere, near] + [anywhere] * 6 + [near] * 4,
        out_shape=[shape((8,) + packed.shape, low), shape((4,) + asks.shape, asks.dtype)]
        + [shape(*v) for v in saved]
        + [shape((16, 128), full), shape((8, D), low), shape((8, D), full), shape((16, D), full)],
        scratch_shapes=[
            vmem((padded, D), full), vmem((8, SLOTS, D), full), vmem((8, SLOTS, D)), vmem((8, SLOTS, D)),
            vmem((LAYERS, 8, PART, D)), vmem((8, 64, D)), vmem((8, 32, D)),
        ]
        + [vmem(*v) for v in saved]
        + [
            vmem((tokens, D), full), vmem((tokens, tokens), full), vmem((tokens, D), full),
            sems(8, 5), sems(8, 3), sems(8, 4), sems(8, 4), sems(8, 8), sems(8, 8), sems(8, 8), sems(8, 8),
            sems(4), sems(8), sems(8), sems(11), sems(11), sems(10), sems(2, 6),
        ],
        compiler_params=pltpu.CompilerParams(collective_id=cid, has_side_effects=True, vmem_limit_bytes=62 * 2**20),
    )(packed, asks, embed, key_col, seg_col, seg_row, valid)


def contrast_kernel(unit_ref, deal_col_ref, deal_row_ref, scale_ref, loss_ref, own_ref, slope_ref, every, ss, rs, ls):
    lin = lax.axis_index("dp") * 4 + lax.axis_index("group")
    peers = [lax.rem(lin + k, 32) for k in range(32)]
    peers = [(p // 4, p % 4) for p in peers]
    entry_barrier(peers[1:])
    copies = [
        pltpu.make_async_remote_copy(
            unit_ref, every.at[lin], ss.at[k], rs.at[k], device_id=peers[k], device_id_type=MESH
        )
        for k in range(1, 32)
    ]
    for copy in copies:
        copy.start()
    own = pltpu.make_async_copy(unit_ref, every.at[lin], ls)
    own.start()
    for copy in copies:
        copy.wait()
    own.wait()
    units = every[...].reshape(512, 128)
    place_at = lax.broadcasted_iota(jnp.int32, (128, 512), 1)
    sorted_units = jnp.concatenate(
        [
            exact_dot(jnp.where(deal_col_ref[...] * 4 + part == place_at, 1.0, 0.0), units)
            for part in range(4)
        ],
        axis=1,
    )
    queries, documents = sorted_units[:64], sorted_units[64:]
    scale = jnp.exp(scale_ref[...])
    logits = scale * exact_dot(queries, documents, ((1,), (1,)))
    row_top = jnp.max(logits, axis=1, keepdims=True)
    row_lse = row_top + jnp.log(jnp.sum(jnp.exp(logits - row_top), axis=1, keepdims=True))
    col_top = jnp.max(logits, axis=0, keepdims=True)
    col_lse = col_top + jnp.log(jnp.sum(jnp.exp(logits - col_top), axis=0, keepdims=True))
    diagonal = jnp.where(
        lax.broadcasted_iota(jnp.int32, (64, 64), 0) == lax.broadcasted_iota(jnp.int32, (64, 64), 1), 1.0, 0.0
    )
    on_diagonal = jnp.sum(logits * diagonal, axis=1, keepdims=True)
    col_sum = jnp.sum(col_lse, axis=1, keepdims=True)
    row_sum = jnp.sum(row_lse, axis=0, keepdims=True)
    loss_ref[...] = 0.5 * (row_sum + col_sum) - jnp.sum(on_diagonal, axis=0, keepdims=True)
    grad_logits = 0.5 * (jnp.exp(logits - row_lse) + jnp.exp(logits - col_lse)) - diagonal
    slope = jnp.sum(grad_logits * logits, axis=1, keepdims=True)
    slope_ref[...] = jnp.sum(slope, axis=0, keepdims=True)
    grad_raw = scale * grad_logits
    grad_queries = exact_dot(grad_raw, documents)
    grad_documents = exact_dot(grad_raw, queries, ((0,), (0,)))
    mine = lax.broadcasted_iota(jnp.int32, (8, 128), 0)
    picks = jnp.where((deal_row_ref[...] == mine + lin * 4) & (mine < 4), 1.0, 0.0)
    own_ref[...] = exact_dot(picks, jnp.concatenate([grad_queries, grad_documents], axis=0))


def run_contrast(unit, deal_order, log_scale, cid):
    sems = pltpu.SemaphoreType.DMA
    one = jax.ShapeDtypeStruct((1, 1), jnp.float32)
    return pl.pallas_call(
        contrast_kernel,
        out_shape=[one, jax.ShapeDtypeStruct((8, D), jnp.float32), one],
        in_specs=[pl.BlockSpec(memory_space=pltpu.VMEM)] * 4,
        out_specs=[pl.BlockSpec(memory_space=pltpu.VMEM)] * 3,
        scratch_shapes=[pltpu.VMEM((32, 16, 128), jnp.float32), sems((32,)), sems((32,)), sems],
        compiler_params=pltpu.CompilerParams(collective_id=cid, has_side_effects=True),
    )(unit, deal_order.reshape(128, 1), deal_order.reshape(1, 128), log_scale.reshape(1, 1))


GRAD_ROWS = 2 * PART + 64
GRAD_LAYER = (0, PART + 64)
GRAD_HEAD = PART
PIECES = tuple(
    (stage, half, spare, at)
    for stage, half, spare, at in (
        (320, 128, 32, GRAD_LAYER[1] + 256), (576, 128, 48, GRAD_LAYER[1] + 512), (832, 128, 32, GRAD_LAYER[1] + 768),
        (0, 160, 48, GRAD_HEAD),
        (320, 128, 32, 256), (576, 128, 48, 512), (832, 128, 32, 768),
        (64, 128, 32, 0),
    )
)


def sum_stages(stage, out_ref, acc, b1, b2, b3, b4, b5, fin, sems, free):
    cs, cr, ys, yr, xs, xr, zs, zr, as_, ar, fs, fr, ls, os_ = sems
    z, x, y, c = place()
    me = z * 2 + x
    zp = [dev((z + k) % 4, x, y, c) for k in range(4)]
    xp, yp, cp = dev(z, 1 - x, y, c), dev(z, x, 1 - y, c), dev(z, x, y, 1 - c)

    def rc(src, dst, s, r, d):
        return pltpu.make_async_remote_copy(src, dst, s, r, device_id=d, device_id_type=MESH)

    def owner(k, f):
        return ((z + k) % 4) * 2 + (x if f == 0 else 1 - x)

    order = [(k, f) for k in (2, 1, 3, 0) for f in (1, 0)]
    lo, lb, lh, la, l1 = [0], [0], [0], [0], [0]
    for stage_at, half, spare, at in PIECES:
        lo.append(lo[-1] + half)
        lb.append(lb[-1] + spare)
        lh.append(lh[-1] + half - spare)
        la.append(la[-1] + half - 2 * spare)
        l1.append(l1[-1] + half)
    l1 = l1[:4] + l1[:4]

    def add(dst, src, count):
        def body(i, carry):
            at = mult(i * 32)
            into = dst(at)
            into[...] = (into[...].astype(jnp.float32) + src(at)[...].astype(jnp.float32)).astype(BF)
            return carry
        lax.fori_loop(0, count // 32, body, 0)
        if count % 32:
            into = dst(count - 16, 16)
            into[...] = (into[...].astype(jnp.float32) + src(count - 16, 16)[...].astype(jnp.float32)).astype(BF)

    class Piece:
        pass

    pieces = []
    for q, (stage_at, half, spare, at) in enumerate(PIECES):
        p = Piece()
        p.q, p.half, p.spare, p.main = q, half, spare, half - spare
        p.hs = mult(lo[q] + y * spare)
        p.mb = mult(lo[q] + y * p.main)
        p.ob = mult(lo[q] + (1 - y) * p.main)
        p.L, p.C, p.Y, p.X, p.Z = [], [], [], [], []
        for i, (k, f) in enumerate(order):
            s = owner(k, f)
            p.L.append(pltpu.make_async_copy(stage.at[s, pl.ds(mult(stage_at + c * half), half)], acc.at[s, pl.ds(lo[q], half)], ls.at[q, i]))
            p.C.append(rc(stage.at[s, pl.ds(mult(stage_at + (1 - c) * half), half)], b1.at[s, pl.ds(l1[q], half)], cs.at[q, i], cr.at[q, i], cp))
            p.Y.append(rc(acc.at[s, pl.ds(p.ob, spare)], b2.at[s, pl.ds(lb[q], spare)], ys.at[q, i], yr.at[q, i], yp))
        for k in range(4):
            p.X.append(rc(acc.at[owner(k, 1), pl.ds(p.hs, p.main)], b3.at[k, pl.ds(lh[q], p.main)], xs.at[q, k], xr.at[q, k], xp))
            p.Z.append(rc(acc.at[owner(k, 0), pl.ds(p.hs, p.main)], b4.at[k - 1, pl.ds(lh[q], p.main)], zs.at[q, k], zr.at[q, k], zp[k]) if k else None)
        p.aa, p.na = lo[q] + spare, half - 2 * spare
        p.A = rc(fin.at[pl.ds(p.aa, p.na)], b5.at[pl.ds(la[q], p.na)], as_.at[q, 0], ar.at[q, 0], yp)
        p.B = rc(fin.at[pl.ds(p.mb, spare)], fin.at[pl.ds(p.mb, spare)], as_.at[q, 1], ar.at[q, 1], yp)
        p.F = rc(fin.at[pl.ds(lo[q], half)], out_ref.at[pl.ds(mult(at + c * half), half)], fs.at[q], fr.at[q], cp)
        p.O = pltpu.make_async_copy(fin.at[pl.ds(lo[q], half)], out_ref.at[pl.ds(mult(at + c * half), half)], os_.at[q])
        pieces.append(p)

    def s0(q):
        p = pieces[q]
        if q >= 4:
            pl.semaphore_wait(free.at[q - 4], 1)
        for i in range(8):
            p.C[i].start()
            p.L[i].start()

    def s1(q):
        p = pieces[q]
        for i, (k, f) in enumerate(order):
            s = owner(k, f)
            p.L[i].wait()
            p.C[i].wait_recv()
            add(lambda a, n=32: acc.at[s, pl.ds(lo[q] + a, n)], lambda a, n=32: b1.at[s, pl.ds(l1[q] + a, n)], p.half)
            p.Y[i].start()
        if q < 4:
            pl.semaphore_signal(free.at[q], inc=1, device_id=cp, device_id_type=MESH)

    def s2(q):
        p = pieces[q]
        for i, (k, f) in enumerate(order):
            s = owner(k, f)
            p.Y[i].wait_recv()
            add(lambda a, n=32: acc.at[s, pl.ds(p.mb + a, n)], lambda a, n=32: b2.at[s, pl.ds(lb[q] + a, n)], p.spare)
            if f == 1:
                p.X[k].start()

    def s3(q):
        p = pieces[q]
        for k in (2, 1, 3, 0):
            s = owner(k, 0)
            p.X[k].wait_recv()
            add(lambda a, n=32: acc.at[s, pl.ds(p.hs + a, n)], lambda a, n=32: b3.at[k, pl.ds(lh[q] + a, n)], p.main)
            if k:
                p.Z[k].start()

    def s4(q):
        p = pieces[q]
        for k in range(1, 4):
            p.Z[k].wait_recv()
        def body(i, carry):
            at = mult(i * 16)
            total = acc[me, pl.ds(p.hs + at, 16)].astype(jnp.float32)
            for k in range(3):
                total += b4[k, pl.ds(lh[q] + at, 16)].astype(jnp.float32)
            fin[pl.ds(p.hs + at, 16)] = total.astype(BF)
            return carry
        lax.fori_loop(0, p.main // 16, body, 0)
        p.A.start()
        p.B.start()

    def s5(q):
        p = pieces[q]
        p.A.wait_recv()
        p.A.wait_send()
        add(lambda a, n=32: fin.at[pl.ds(p.aa + a, n)], lambda a, n=32: b5.at[pl.ds(la[q] + a, n)], p.na)
        p.B.wait_recv()
        p.F.start()
        p.O.start()

    def sent(q):
        for copy in pieces[q].C:
            copy.wait_send()

    def finish():
        for p in pieces:
            p.F.wait()
            p.O.wait()
            p.B.wait_send()
            for copy in p.Y + p.X + p.Z[1:]:
                copy.wait_send()

    return [s0, s1, s2, s3, s4, s5], sent, finish


def row_exchange(slots, t_ref, norm_ref, norm_out, nbuf, es, er, el, ns, nr):
    z, x, y, c = place()
    me = z * 2 + x
    g = y * 2 + c
    g2 = (1 - y) * 2 + c
    ep = [(lax.rem(me + k, 8), g) for k in range(8)]
    back = [lax.rem(me + 8 - k, 8) for k in range(8)]
    yp, cp = dev(z, x, 1 - y, c), dev(z, x, y, 1 - c)

    def rc(src, dst, s, r, d):
        return pltpu.make_async_remote_copy(src, dst, s, r, device_id=d, device_id_type=MESH)

    kept = pltpu.make_async_copy(slots.at[me], t_ref.at[g, me], el)
    E = [rc(slots.at[ep[k][0]], t_ref.at[g, me], es.at[0, k], er.at[0, k], ep[k]) for k in range(1, 8)]
    EY = [rc(t_ref.at[g, back[k]], t_ref.at[g, back[k]], es.at[1, k], er.at[1, k], yp) for k in range(8)]
    EC = [rc(t_ref.at[g, back[k]], t_ref.at[g, back[k]], es.at[2, k], er.at[2, k], cp) for k in range(8)]
    ED = [rc(t_ref.at[g2, back[k]], t_ref.at[g2, back[k]], es.at[3, k], er.at[3, k], cp) for k in range(8)]
    NC = rc(norm_ref, nbuf.at[0], ns.at[0], nr.at[0], cp)
    NY = rc(nbuf.at[1], nbuf.at[2], ns.at[1], nr.at[1], yp)

    def e0():
        kept.start()
        for copy in E:
            copy.start()
        NC.start()

    def e1():
        kept.wait()
        EY[0].start()
        EC[0].start()
        NC.wait_recv()
        nbuf[1] = nbuf[0] + norm_ref[...]
        NY.start()
        for k in range(1, 8):
            E[k - 1].wait_recv()
            EY[k].start()
            EC[k].start()

    def e2():
        for k in range(8):
            EY[k].wait_recv()
            ED[k].start()
        NY.wait_recv()
        norm_out[...] = nbuf[1] + nbuf[2]

    def e3():
        for copy in EC + ED:
            copy.wait_recv()
        for copy in E + EY + EC + ED + [NC, NY]:
            copy.wait_send()

    return [e0, e1, e2, e3]


def backward_kernel(
    own_ref, zed_ref, pool_ref, seg_col_ref, seg_row_ref, valid_ref, key_ref, norm_ref,
    w_ref, low_in, qkv_in, lse_in, mix_in, one_in, two_in,
    out_ref, t_ref, norm_out, first_ref,
    weights, head, low_ref, qkv_ref, lse_ref, mix_ref, one_ref, two_ref, stage,
    dx, far, acc, two_s, low_s, mid_s, ups, gates, back, norm_s, slots,
    total, b1, b2, b3, b4, b5, fin, nbuf,
    cs, cr, ys, yr, xs, xr, zs, zr, as_, ar, fs, fr, ls, os_, es, er, el, ns, nr, loads, free,
):
    tokens = dx.shape[0]
    tiles = tokens // TILE
    low_type = jnp.bfloat16
    z, x, y, c = place()
    me = z * 2 + x
    g = y * 2 + c
    peers = [(lax.rem(me + k, 8), g) for k in range(1, 8)] + [dev(z, x, 1 - y, c), dev(z, x, y, 1 - c)]
    barrier = pltpu.get_barrier_semaphore()
    for peer in peers:
        pl.semaphore_signal(barrier, inc=1, device_id=peer, device_id_type=MESH)
    stages, sent, finish = sum_stages(
        stage, out_ref, total, b1, b2, b3, b4, b5, fin, (cs, cr, ys, yr, xs, xr, zs, zr, as_, ar, fs, fr, ls, os_), free
    )
    rows_out = row_exchange(slots, t_ref, norm_s, norm_out, nbuf, es, er, el, ns, nr)

    def loading(layer):
        base = PACK_LAYER[layer]
        copy = pltpu.make_async_copy
        return {
            "two": copy(two_in.at[layer], two_ref, loads.at[layer, 0]),
            "one": copy(one_in.at[layer], one_ref, loads.at[layer, 1]),
            "feed": copy(w_ref.at[:, pl.ds(base + 256, 768)], weights.at[:, pl.ds(256, 768)], loads.at[layer, 2]),
            "mix": copy(mix_in.at[layer], mix_ref, loads.at[layer, 3]),
            "qkv": copy(qkv_in.at[layer], qkv_ref, loads.at[layer, 4]),
            "lse": copy(lse_in.at[layer], lse_ref, loads.at[layer, 5]),
            "low": copy(low_in.at[layer], low_ref, loads.at[layer, 6]),
            "attend": copy(w_ref.at[:, pl.ds(base, 256)], weights.at[:, pl.ds(0, 256)], loads.at[layer, 7]),
        }

    load = [loading(layer) for layer in range(LAYERS)]
    head_load = pltpu.make_async_copy(w_ref.at[:, pl.ds(PACK_HEAD, 64)], head, loads.at[0, 8])
    head_load.start()
    for copy in load[1].values():
        copy.start()

    def begin():
        fill_distance(far, seg_col_ref, seg_row_ref)
        head_load.wait()
        load[1]["two"].wait()
        zed = zed_ref[...]
        square = jnp.sum(zed * zed, axis=-1, keepdims=True) + UNIT_EPS
        inverse = lax.rsqrt(square)
        own = own_ref[...]
        inner = jnp.sum(own * zed, axis=-1, keepdims=True)
        grad_zed = (inverse * (own - zed * (inner / square))).astype(low_type)
        head_low = head[...].reshape(D, D)
        stage[:, 0:64, :] = dot_tn(pool_ref[...], grad_zed).reshape(8, 64, D).astype(low_type)
        member = members(seg_row_ref, valid_ref)
        counts = jnp.maximum(jnp.sum(member, axis=1, keepdims=True), 1.0)
        grad_pooled = dot_nt(grad_zed, head_low) / counts
        grad_final = exact_dot(member, grad_pooled, ((0,), (0,)))
        stream_scaled, _ = norm_parts(two_ref[...])
        stream = stream_scaled * norm_ref[6:7, :] + norm_ref[7:8, :]
        scaled, inverse = norm_parts(stream)
        norm_s[...] = jnp.zeros(norm_s.shape, jnp.float32)
        norm_s[2, 0:1, :] = jnp.sum(grad_final * scaled, axis=0, keepdims=True)
        norm_s[2, 1:2, :] = jnp.sum(grad_final, axis=0, keepdims=True)
        dx[...] = norm_back(scaled, inverse, grad_final, norm_ref[8:9, :])

    def enter(layer):
        at = 4 * layer
        if layer < LAYERS - 1:
            load[layer]["two"].wait()
        load[layer]["one"].wait()

        def body(i, carry):
            rows = pl.ds(pl.multiple_of(i * TILE, TILE), TILE)
            scaled, inverse = norm_parts(two_ref[rows, :])
            grad = dx[rows, :]
            norm_s[layer, 2:3, :] += jnp.sum(grad * scaled, axis=0, keepdims=True)
            norm_s[layer, 3:4, :] += jnp.sum(grad, axis=0, keepdims=True)
            grad = norm_back(scaled, inverse, grad, norm_ref[at + 2 : at + 3, :])
            acc[rows, :] = grad
            two_s[rows, :] = grad.astype(low_type)
            scaled, _ = norm_parts(one_ref[rows, :])
            hidden = scaled * norm_ref[at : at + 1, :] + norm_ref[at + 1 : at + 2, :]
            low_s[rows, :] = hidden.astype(low_type)
            return carry

        lax.fori_loop(0, tiles, body, 0)
        if layer > 0:
            load[layer - 1]["two"].start()
        load[layer]["feed"].wait()

    def feed(layer, j):
        def body(i, carry):
            rows = pl.ds(pl.multiple_of(i * TILE, TILE), TILE)
            low = low_s[rows, :]
            gate = dot_nn(low, block(weights, 256 + j * 64))
            up = dot_nn(low, block(weights, 512 + j * 64))
            grad_mid = dot_nt(two_s[rows, :], down_block(weights, j))
            value, slope = gelu_parts(gate)
            mid_s[rows, :] = (value * up).astype(low_type)
            grad_gate = (grad_mid * up * slope).astype(low_type)
            grad_up = (grad_mid * value).astype(low_type)
            gates[rows, :] = grad_gate
            ups[rows, :] = grad_up
            acc[rows, :] += dot_nt(grad_gate, block(weights, 256 + j * 64)) + dot_nt(
                grad_up, block(weights, 512 + j * 64)
            )
            return carry

        lax.fori_loop(0, tiles, body, 0)
        if layer < LAYERS - 1 and j == 0:
            for q in range(3):
                sent(q)
        stage[2 * j : 2 * j + 2, 832:1088, :] = dot_tn(mid_s[...], two_s[...]).reshape(2, 256, D).astype(low_type)
        stage[:, 320 + j * 64 : 384 + j * 64, :] = dot_tn(low_s[...], gates[...]).reshape(8, 64, D).astype(low_type)
        stage[:, 576 + j * 64 : 640 + j * 64, :] = dot_tn(low_s[...], ups[...]).reshape(8, 64, D).astype(low_type)

    def middle(layer):
        at = 4 * layer
        if layer > 0:
            load[layer - 1]["feed"].start()
        load[layer]["attend"].wait()
        load[layer]["mix"].wait()

        def body(i, carry):
            rows = pl.ds(pl.multiple_of(i * TILE, TILE), TILE)
            scaled, inverse = norm_parts(one_ref[rows, :])
            grad = acc[rows, :]
            norm_s[layer, 0:1, :] += jnp.sum(grad * scaled, axis=0, keepdims=True)
            norm_s[layer, 1:2, :] += jnp.sum(grad, axis=0, keepdims=True)
            grad = norm_back(scaled, inverse, grad, norm_ref[at : at + 1, :])
            dx[rows, :] = grad
            low = grad.astype(low_type)
            two_s[rows, :] = low
            mid_s[rows, :] = dot_nt(low, block(weights, 192)).astype(low_type)
            return carry

        lax.fori_loop(0, tiles, body, 0)
        if layer > 0:
            load[layer - 1]["one"].start()
        else:
            sent(3)
        stage[:, 256:320, :] = dot_nn(mix_ref[...], two_s[...]).reshape(8, 64, D).astype(low_type)
        load[layer]["qkv"].wait()
        load[layer]["lse"].wait()
        load[layer]["low"].wait()

    def attend_head(layer, head):
        lanes = slice(head * HEAD_DIM, (head + 1) * HEAD_DIM)
        key_lanes = slice(D + head * HEAD_DIM, D + (head + 1) * HEAD_DIM)
        val_lanes = slice(2 * D + head * HEAD_DIM, 2 * D + (head + 1) * HEAD_DIM)
        keys = qkv_ref[:, key_lanes]
        keys_t = keys.T
        vals = qkv_ref[:, val_lanes]
        slope = 2.0 ** (-8.0 * (head + 1) / HEADS)
        grad_vals = None
        grad_keys = None
        for i in range(tiles):
            cols = slice(i * TILE, (i + 1) * TILE)
            query = qkv_ref[cols, lanes]
            grad_mix = mid_s[cols, lanes]
            scores = dot_nt(keys, query) * HEAD_DIM**-0.5 - slope * far[:, cols]
            prob = jnp.exp(scores - lse_ref[head, :, cols])
            grad_prob = dot_nt(vals, grad_mix)
            inner = jnp.sum(prob * grad_prob, axis=0, keepdims=True)
            grad_raw = (prob * (grad_prob - inner) * HEAD_DIM**-0.5).astype(low_type)
            back[cols, lanes] = dot_nn(keys_t, grad_raw).T.astype(low_type)
            value_part = dot_nn(prob.astype(low_type), grad_mix)
            key_part = dot_nn(grad_raw, query)
            grad_vals = value_part if grad_vals is None else grad_vals + value_part
            grad_keys = key_part if grad_keys is None else grad_keys + key_part
        back[:, key_lanes] = grad_keys.astype(low_type)
        back[:, val_lanes] = grad_vals.astype(low_type)

    def leave(layer):
        def body(i, carry):
            rows = pl.ds(pl.multiple_of(i * TILE, TILE), TILE)
            grad = dx[rows, :]
            for j in range(3):
                grad = grad + dot_nt(back[rows, j * D : (j + 1) * D], block(weights, j * 64))
            dx[rows, :] = grad
            return carry

        lax.fori_loop(0, tiles, body, 0)
        for j in range(3):
            stage[:, 64 + j * 64 : 128 + j * 64, :] = (
                dot_tn(low_ref[...], back[:, j * D : (j + 1) * D]).reshape(8, 64, D).astype(low_type)
            )
        if layer > 0:
            for name in ("mix", "qkv", "lse", "low", "attend"):
                load[layer - 1][name].start()
        else:
            first_ref[...] = dx[...].astype(low_type)
            count = slots.shape[1]
            for d in range(8):
                hot = lax.broadcasted_iota(jnp.int32, (count, tokens), 0) + d * count == key_ref[...]
                slots[d] = dot_nn(jnp.where(hot, 1.0, 0.0).astype(low_type), first_ref[...]).astype(low_type)

    events = []
    clock = 0.0

    def do(cost, fn, *args):
        nonlocal clock
        events.append((clock, len(events), fn, args))
        clock += cost

    def wait_entry():
        pl.semaphore_wait(barrier, len(peers))

    ready = []
    do(3.0, begin)
    for layer in (1, 0):
        do(2.5, enter, layer)
        for j in range(4):
            do(4.7, feed, layer, j)
        if layer == 1:
            do(0.0, wait_entry)
        ready += [clock] * 3
        do(0.0, stages[0], len(ready) - 3)
        do(0.0, stages[0], len(ready) - 2)
        do(0.0, stages[0], len(ready) - 1)
        do(2.5, middle, layer)
        for head_index in range(HEADS):
            do(1.6, attend_head, layer, head_index)
        do(4.0, leave, layer)
        ready.append(clock)
        if layer == 0:
            do(0.0, rows_out[0])
        do(0.0, stages[0], len(ready) - 1)
    end = clock
    links = {"c": 0.0, "y": 0.0, "x": 0.0, "z": 0.0}
    for q in range(8):
        scale = PIECES[q][1] / 128.0
        now = ready[q]
        for number, link, cost in ((1, "c", 3.0), (2, "y", 8.0), (3, "x", 9.5), (4, "z", 9.5), (5, "y", 1.0)):
            now = max(now, links[link]) + cost * scale
            if number < 5:
                links[link] = now
            else:
                now += 3.0
            events.append((now, len(events), stages[number], (q,)))
    events.append((end + 8.0, len(events), rows_out[1], ()))
    events.append((end + 26.0, len(events), rows_out[2], ()))
    for _, _, fn, args in sorted(events, key=lambda event: event[:2]):
        fn(*args)
    finish()
    for q in range(4, 8):
        sent(q)
    rows_out[3]()


def run_backward(own, zed, pool, seg_col, seg_row, valid, key, weights, norms, saved, cid):
    low_x, qkv, lse, mix, one, two = saved
    tokens = low_x.shape[1]
    low = jnp.bfloat16
    full = jnp.float32
    vmem = lambda shape, kind=low: pltpu.VMEM(shape, kind)
    sems = lambda *shape: pltpu.SemaphoreType.DMA(shape)
    half = sum(p[1] for p in PIECES)
    spare = sum(p[2] for p in PIECES)
    near = pl.BlockSpec(memory_space=pltpu.VMEM)
    anywhere = pl.BlockSpec(memory_space=pl.ANY)
    norm_shape = (LAYERS + 1, 8, D)
    square = (tokens, D)
    return pl.pallas_call(
        backward_kernel,
        in_specs=[near] * 8 + [anywhere] * 7,
        out_specs=[anywhere, anywhere, near, near],
        out_shape=[
            jax.ShapeDtypeStruct((GRAD_ROWS, D), low),
            jax.ShapeDtypeStruct((4, 8, SLOTS, D), low),
            jax.ShapeDtypeStruct(norm_shape, full),
            jax.ShapeDtypeStruct(square, low),
        ],
        scratch_shapes=[
            vmem((8, PART, D)), vmem((8, 64, D)), vmem(square), vmem((tokens, 3 * D)), vmem((HEADS, 1, tokens), full),
            vmem((D, tokens)), vmem(square, full), vmem(square, full), vmem((8, PART + 64, D)),
            vmem(square, full), vmem((tokens, tokens), full), vmem(square, full), vmem(square), vmem(square),
            vmem(square), vmem(square), vmem(square), vmem((tokens, 3 * D)), vmem(norm_shape, full), vmem((8, SLOTS, D)),
            vmem((8, half, D)), vmem((8, sum(p[1] for p in PIECES[:4]), D)), vmem((8, spare, D)), vmem((4, half - spare, D)),
            vmem((3, half - spare, D)), vmem((half - 2 * spare, D)), vmem((half, D)), vmem((3,) + norm_shape, full),
            sems(8, 8), sems(8, 8), sems(8, 8), sems(8, 8), sems(8, 4), sems(8, 4), sems(8, 4), sems(8, 4),
            sems(8, 2), sems(8, 2), sems(8), sems(8), sems(8, 8), sems(8), sems(4, 8), sems(4, 8), pltpu.SemaphoreType.DMA,
            sems(2), sems(2), sems(2, 9), pltpu.SemaphoreType.REGULAR((4,)),
        ],
        compiler_params=pltpu.CompilerParams(collective_id=cid, has_side_effects=True, vmem_limit_bytes=63 * 2**20),
    )(own, zed, pool, seg_col, seg_row, valid, key, norms, weights, low_x, qkv, lse, mix, one, two)


def total_kernel(v_ref, o_ref, got, mine, ss, rs, ts, us, ls):
    me = lax.axis_index("dp")
    g = lax.axis_index("group")
    lin = me * 4 + g
    to = [lax.rem(lin + k, 32) for k in range(32)]
    peers = [(p // 4, p % 4) for p in to]
    owners = [(lax.rem(me + k, 8), g) for k in range(8)]
    entry_barrier(peers[1:])
    first = [
        pltpu.make_async_remote_copy(
            v_ref.at[owners[k][0] * 4 + g], got.at[k], ss.at[k], rs.at[k], device_id=owners[k], device_id_type=MESH
        )
        for k in range(1, 8)
    ]
    for copy in first:
        copy.start()
    own = pltpu.make_async_copy(v_ref.at[lin], got.at[0], ls.at[0])
    own.start()
    for copy in first:
        copy.wait()
    own.wait()
    mine[...] = jnp.sum(got[...], axis=0)
    second = [
        pltpu.make_async_remote_copy(
            mine, o_ref.at[lin], ts.at[k], us.at[k], device_id=peers[k], device_id_type=MESH
        )
        for k in range(1, 32)
    ]
    for copy in second:
        copy.start()
    own = pltpu.make_async_copy(mine, o_ref.at[lin], ls.at[1])
    own.start()
    for copy in second:
        copy.wait()
    own.wait()


def total(v, cid):
    sems = pltpu.SemaphoreType.DMA
    return pl.pallas_call(
        total_kernel,
        out_shape=jax.ShapeDtypeStruct(v.shape, v.dtype),
        in_specs=[pl.BlockSpec(memory_space=pltpu.VMEM)], out_specs=pl.BlockSpec(memory_space=pltpu.VMEM),
        scratch_shapes=[
            pltpu.VMEM((8,) + v.shape[1:], v.dtype), pltpu.VMEM(v.shape[1:], v.dtype),
            sems((8,)), sems((8,)), sems((32,)), sems((32,)), sems((2,)),
        ],
        compiler_params=pltpu.CompilerParams(collective_id=cid, has_side_effects=True),
    )(v)


BLOCKS = 28
STEP_AT = 28
SUM_AT = 56
NORM_ROW = 57
ROW_TILE = 512
RATES = (
    RATE_SCALE, RATE_SCALE / D**0.5, RATE_SCALE / D**0.5, RATE_SCALE / (D // 8) ** 0.5,
    RATE_SCALE / D**0.5, RATE_SCALE / FF**0.5,
)


def matrices(layer):
    at = GRAD_LAYER[layer]
    first = 2 + 13 * layer
    return (
        (2, at, 64, 3, first), (3, at + 192, 64, 1, first + 3),
        (4, at + 256, 64, 8, first + 4), (5, at + 768, 256, 1, first + 12),
    )


def turn(row):
    return jnp.broadcast_to(row, (8, row.shape[1])).T[:, 0:1]


def lane_pick(value, lane):
    return jnp.where(lax.broadcasted_iota(jnp.int32, (1, D), 1) == lane, value, 0.0)


def stats_kernel(dense, row_count, *refs):
    if dense:
        full_ref, grads_ref, norm_ref, table_row_ref, rows_ref, down_ref, *outs = refs
    else:
        slot_ref, slot_rows_ref, grads_ref, norm_ref, table_row_ref, rows_ref, down_ref, *outs = refs
    table_ref, table_row_out, stat_ref, rows_out, down_out = outs
    step = pl.program_id(0)

    def put(at, value):
        stat_ref[at // 3, at % 3 : at % 3 + 1, :] = value

    def add(at, value):
        stat_ref[at // 3, at % 3 : at % 3 + 1, :] += value

    @pl.when(step == 0)
    def _():
        stat_ref[...] = jnp.zeros(stat_ref.shape, jnp.float32)
        for row in range(10):
            put(NORM_ROW + row, norm_ref[row // 4, row % 4 : row % 4 + 1, :])
        sums = jnp.zeros((1, D), jnp.float32)
        rows_out[...] = jnp.zeros(rows_out.shape, jnp.float32)

        def part(first, count, blocks, block_at, old):
            squares = [
                grads_ref[first + j * count : first + (j + 1) * count, :].astype(jnp.float32) ** 2 for j in range(blocks)
            ]
            mean = jnp.sum(functools.reduce(jnp.add, squares), axis=-1, keepdims=True) / (blocks * D)
            new = DECAY_RATE * old + (1.0 - DECAY_RATE) * (mean + STATE_EPS)
            inverse = 1.0 / new
            for j in range(blocks):
                put(block_at + j, jnp.sum(squares[j], axis=0, keepdims=True))
                put(STEP_AT + block_at + j, jnp.sum(squares[j] * inverse, axis=0, keepdims=True))
            return new, jnp.sum(new, axis=0, keepdims=True)

        new, count = part(GRAD_HEAD, 64, 1, 1, rows_ref[:, 6:7])
        rows_out[:, 6:7] = new
        sums += lane_pick(count, 1)
        for layer in range(LAYERS):
            for name, first, rows, blocks, block_at in matrices(layer):
                if name == 5:
                    new, count = part(first, rows, blocks, block_at, down_ref[:, layer : layer + 1])
                    down_out[:, layer : layer + 1] = new
                else:
                    lane = 3 * layer + name - 2
                    new, count = part(first, rows, blocks, block_at, rows_ref[:, lane : lane + 1])
                    rows_out[:, lane : lane + 1] = new
                sums += lane_pick(count, 2 * name - 2 + layer)
        put(SUM_AT, sums)

    index = lax.broadcasted_iota(jnp.int32, (ROW_TILE, 1), 0) + step * ROW_TILE
    if dense:
        grad = jnp.where(index < row_count, full_ref[...], 0.0)
    else:
        picks = jnp.where(index == slot_ref[...], 1.0, 0.0).astype(jnp.bfloat16)
        grad = jnp.dot(picks, slot_rows_ref[...], preferred_element_type=jnp.float32)
    low = grad.astype(jnp.bfloat16)
    table_ref[...] = low
    squares = low.astype(jnp.float32) ** 2
    mean = jnp.mean(squares, axis=-1, keepdims=True)
    mean_row = jnp.broadcast_to(mean, (ROW_TILE, 128)).T[0:1, :]
    new = DECAY_RATE * table_row_ref[...] + (1.0 - DECAY_RATE) * (mean_row + STATE_EPS)
    real = lax.broadcasted_iota(jnp.int32, (1, ROW_TILE), 1) + step * ROW_TILE < row_count
    new = jnp.where(real, new, 1.0)
    table_row_out[...] = new
    add(0, jnp.sum(squares, axis=0, keepdims=True))
    add(STEP_AT, jnp.sum(squares * (1.0 / turn(new)), axis=0, keepdims=True))
    add(SUM_AT, lane_pick(jnp.sum(jnp.where(real, new, 0.0), axis=1, keepdims=True), 0))


def run_stats(dense, heads, grads, norm, table_row, rows, down):
    row_count = table_row.shape[1]
    tile = pl.BlockSpec((ROW_TILE, D), lambda i: (i, 0))
    lane = pl.BlockSpec((1, ROW_TILE), lambda i: (0, i))
    head_specs = [tile] if dense else [whole(v.shape) for v in heads]
    stat = (32, 3, D)
    return pl.pallas_call(
        functools.partial(stats_kernel, dense, row_count),
        grid=(-(-row_count // ROW_TILE),),
        in_specs=head_specs + [whole(grads.shape), whole(norm.shape), lane, whole(rows.shape), whole(down.shape)],
        out_specs=[tile, lane, whole(stat), whole(rows.shape), whole(down.shape)],
        out_shape=[
            jax.ShapeDtypeStruct((row_count, D), jnp.bfloat16), jax.ShapeDtypeStruct(table_row.shape, jnp.float32),
            jax.ShapeDtypeStruct(stat, jnp.float32), jax.ShapeDtypeStruct(rows.shape, jnp.float32),
            jax.ShapeDtypeStruct(down.shape, jnp.float32),
        ],
        compiler_params=pltpu.CompilerParams(vmem_limit_bytes=48 * 2**20),
    )(*heads, grads, norm, table_row, rows, down)


def update_kernel(
    totals, stat_ref, table_ref, embed_ref, table_row_ref, grads_ref, rows_ref, down_ref, top_cols_ref, cols_ref,
    in_ref, mix_ref, gate_ref, low_ref, head_ref,
    embed_out, table_cols_out, head_cols_out, cols_out, in_out, mix_out, gate_out, low_out, head_out, rms_out, factors,
):
    step = pl.program_id(0)

    def stat(at):
        return stat_ref[at // 3, at % 3 : at % 3 + 1, :]

    def mean_of(lane, name):
        return jnp.sum(jnp.where(lax.broadcasted_iota(jnp.int32, (1, D), 1) == lane, stat(SUM_AT), 0.0), axis=1, keepdims=True) / totals[name]

    def columns(block_at, blocks, old, lane, name):
        row_mean = mean_of(lane, name)
        news = []
        steps = 0.0
        for j in range(blocks):
            new = DECAY_RATE * old(j) + (1.0 - DECAY_RATE) * (stat(block_at + j) / totals[name] + STATE_EPS)
            news.append(new)
            steps += jnp.sum(row_mean * stat(STEP_AT + block_at + j) / new, axis=1, keepdims=True)
        rms = jnp.sqrt(steps / (totals[name] * blocks * D))
        scale = -RATES[name] / jnp.maximum(1.0, rms / CLIP_LEVEL)
        return news, row_mean, rms, scale

    @pl.when(step == 0)
    def _():
        news, row_mean, rms, scale = columns(0, 1, lambda j: top_cols_ref[0:1, :], 0, 0)
        table_cols_out[...] = news[0]
        factors[0:1, :] = lax.rsqrt(news[0])
        factors[1:2, :] = jnp.broadcast_to(row_mean, (1, D))
        factors[2:3, :] = jnp.broadcast_to(scale, (1, D))
        all_rms = lane_pick(rms, 0)
        news, row_mean, rms, scale = columns(1, 1, lambda j: top_cols_ref[1:2, :], 1, 1)
        head_cols_out[...] = news[0]
        all_rms += lane_pick(rms, 1)
        row = lax.rsqrt(rows_ref[:, 6:7] / row_mean) * scale
        head_out[...] = head_ref[...] + grads_ref[GRAD_HEAD : GRAD_HEAD + 64, :].astype(jnp.float32) * row * lax.rsqrt(news[0])
        for layer in range(LAYERS):
            for name, first, rows, blocks, block_at in matrices(layer):
                col_at = (block_at - 2 - 13 * layer) * D
                old = lambda j: cols_ref[layer : layer + 1, col_at + j * D : col_at + (j + 1) * D]
                news, row_mean, rms, scale = columns(block_at, blocks, old, 2 * name - 2 + layer, name)
                all_rms += lane_pick(rms, 2 * name - 2 + layer)
                lane = 3 * layer + name - 2
                state = down_ref[:, layer : layer + 1] if name == 5 else rows_ref[:, lane : lane + 1]
                row = lax.rsqrt(state / row_mean) * scale
                source, target = ((in_ref, in_out), (mix_ref, mix_out), (gate_ref, gate_out), (low_ref, low_out))[name - 2]
                for j in range(blocks):
                    cols_out[layer : layer + 1, col_at + j * D : col_at + (j + 1) * D] = news[j]
                    span = slice(j * D, (j + 1) * D)
                    grad = grads_ref[first + j * rows : first + (j + 1) * rows, :].astype(jnp.float32)
                    target[layer, :, span] = source[layer, :, span] + grad * row * lax.rsqrt(news[j])
        rms_out[...] = all_rms

    row = lax.rsqrt(turn(table_row_ref[...] / factors[1:2, :ROW_TILE])) * factors[2:3, 0:1]
    embed_out[...] = embed_ref[...] + table_ref[...].astype(jnp.float32) * row * factors[0:1, :]


def run_update(totals, stat, table, embed, table_row, grads, rows, down, top_cols, cols, others):
    row_count = embed.shape[0]
    tile = pl.BlockSpec((ROW_TILE, D), lambda i: (i, 0))
    lane = pl.BlockSpec((1, ROW_TILE), lambda i: (0, i))
    shape = lambda v: jax.ShapeDtypeStruct(v.shape, jnp.float32)
    one = jax.ShapeDtypeStruct((1, D), jnp.float32)
    outs = [shape(embed), one, one, shape(cols)] + [shape(v) for v in others] + [one]
    return pl.pallas_call(
        functools.partial(update_kernel, totals),
        grid=(-(-row_count // ROW_TILE),),
        in_specs=[whole(stat.shape), tile, tile, lane]
        + [whole(v.shape) for v in (grads, rows, down, top_cols, cols)]
        + [whole(v.shape) for v in others],
        out_specs=[tile] + [whole(v.shape) for v in outs[1:]],
        out_shape=outs,
        scratch_shapes=[pltpu.VMEM((8, D), jnp.float32)],
        compiler_params=pltpu.CompilerParams(vmem_limit_bytes=48 * 2**20),
    )(stat, table, embed, table_row, grads, rows, down, top_cols, cols, *others)


def fast_shards(
    token_ids,
    seq_lengths,
    valid_mask,
    deal_order,
    log_scale,
    embed_master,
    attn_in,
    attn_out,
    ffn_in,
    ffn_out,
    head_master,
    norm_master,
    embed_rows,
    head_rows,
    layer_rows,
    ffn_out_rows,
    layer_cols,
    embed_head_cols,
    norm_state,
    scale_state,
):
    tokens = token_ids.shape[0]
    shard_rows = embed_master.shape[0]
    my_dp = lax.axis_index("dp")
    position = jnp.arange(tokens, dtype=jnp.int32)
    bounds = jnp.cumsum(seq_lengths[0])
    segment = jnp.sum((position[:, None] >= bounds[None, :]).astype(jnp.int32), axis=1)

    key, wanted, most = slot_plan(token_ids, shard_rows)
    asks = jnp.concatenate(
        [wanted.reshape(8, 1, SLOTS), jnp.broadcast_to(most, (8, 1, 128 - SLOTS))], axis=2
    ).astype(jnp.int32)
    packed = pack_weights(attn_in, attn_out, ffn_in, ffn_out, head_master, norm_master)
    seg_col, seg_row = segment.reshape(-1, 1), segment.reshape(1, -1)
    valid_row = valid_mask.reshape(1, -1)
    weights, asked, *saved, norms = run_gather_forward(
        packed, asks, embed_master, key.reshape(-1, 1), seg_col, seg_row, valid_row, 0
    )
    crowded = jnp.max(asked[:, :, 0, SLOTS:]) >= SLOTS

    def dense_forward(state):
        table = lax.all_gather(embed_master.astype(jnp.bfloat16), "dp", axis=0, tiled=True)
        first = jnp.take(table, token_ids, axis=0)
        return (False, *run_forward(first, seg_col, seg_row, valid_row, weights[:, 32:], norms))

    _, *saved, unit_parts, pooled_low, head_out = lax.while_loop(
        lambda state: state[0], dense_forward, (crowded, *saved)
    )
    loss_value, own_rows, grad_scale = run_contrast(unit_parts, deal_order, log_scale, 1)
    loss_value, grad_scale = loss_value[0, 0], grad_scale[0]
    shard_grads, table_rows, norm_sum, grad_first = run_backward(
        own_rows, head_out, pooled_low, seg_col, seg_row, valid_row, key.reshape(1, -1), weights, norms, saved, 2
    )
    table_slots = asked[:, :, 0, :SLOTS].reshape(1, -1)
    table_row = embed_rows.reshape(1, -1)
    row_state = jnp.pad(
        jnp.concatenate([layer_rows.reshape(6, -1), head_rows.reshape(1, -1)], axis=0), ((0, 1), (0, 0))
    ).T
    shared = (shard_grads, norm_sum, table_row, row_state, ffn_out_rows.T)

    def dense_stats():
        full = jnp.zeros((shard_rows * 8, D), jnp.float32).at[token_ids].add(
            grad_first.astype(jnp.float32)
        )
        full = lax.psum_scatter(full, "dp", scatter_dimension=0, tiled=True)
        return run_stats(True, (lax.psum(full, "group"),), *shared)

    def slot_stats():
        return run_stats(False, (table_slots, table_rows.reshape(-1, D)), *shared)

    table_grad, table_row_new, stats, rows_new, down_new = lax.cond(
        crowded, dense_stats, slot_stats
    )
    sums = total(stats, 3)
    totals = (VOCAB, D, D, D, D, FF)
    (
        new_embed, new_table_cols, new_head_cols, new_cols, new_in, new_mix, new_gate, new_low, new_head, rms_row,
    ) = run_update(
        totals, sums, table_grad, embed_master, table_row_new, shard_grads, rows_new, down_new,
        embed_head_cols, layer_cols, (attn_in, attn_out, ffn_in, ffn_out, head_master),
    )
    norm_grad = sums.reshape(-1, D)[NORM_ROW : NORM_ROW + 10].reshape(2 * LAYERS + 1, 2, D)
    shard_norm = lax.dynamic_slice_in_dim(norm_grad, my_dp * norm_state.shape[2], norm_state.shape[2], 2)
    norm_delta, norm_second = unfactored(shard_norm, norm_state)
    scale_delta, scale_state_new = unfactored(grad_scale, scale_state)
    state_new = rows_new.T
    return (
        loss_value,
        new_embed,
        new_in,
        new_mix,
        new_gate,
        new_low,
        new_head,
        norm_master + norm_delta,
        log_scale + scale_delta,
        table_row_new[0],
        state_new[6],
        state_new[:6].reshape(layer_rows.shape),
        down_new.T,
        new_cols,
        new_table_cols[0],
        new_head_cols[0],
        norm_second,
        scale_state_new,
        rms_row[0, :10],
    )


def solution(mesh):
    in_specs = (
        P(("dp", "group")),
        P(("dp", "group"), None),
        P(("dp", "group")),
        P(),
        P(),
        P("dp", None),
        P(None, "dp", None),
        P(None, "dp", None),
        P(None, "dp", None),
        P(None, "dp", None),
        P("dp", None),
        P(None, None, "dp"),
        P("dp"),
        P("dp"),
        P(None, None, "dp"),
        P(None, "dp"),
        P(),
        P(),
        P(None, None, "dp"),
        P(),
    )
    out_specs = (
        P(),
        P("dp", None),
        P(None, "dp", None),
        P(None, "dp", None),
        P(None, "dp", None),
        P(None, "dp", None),
        P("dp", None),
        P(None, None, "dp"),
        P(),
        P("dp"),
        P("dp"),
        P(None, None, "dp"),
        P(None, "dp"),
        P(),
        P(),
        P(),
        P(None, None, "dp"),
        P(),
        P(),
    )
    body = fast_shards if dict(mesh.shape) == {"dp": 8, "group": 4} else shards
    return jax.shard_map(body, mesh=mesh, in_specs=in_specs, out_specs=out_specs, check_vma=False)
```

```python
import functools

import jax
import jax.numpy as jnp
from jax import lax
from jax.experimental import pallas as pl
from jax.experimental.pallas import tpu as pltpu
from jax.sharding import PartitionSpec as P

D = 512
HEADS = 8
HEAD_DIM = 64
FF = 2048
VOCAB = 30528
LAYERS = 2


NORM_EPS = 1e-06
UNIT_EPS = 1e-06
STATE_EPS = 1e-30
DECAY_RATE = 0.5
CLIP_LEVEL = 0.05
RATE_SCALE = 10.0
NORM_RATE = 0.1


def layer_norm(values, gain_vec, shift_vec):
    center = values - jnp.mean(values, axis=-1, keepdims=True)
    spread = jnp.mean(center * center, axis=-1, keepdims=True)
    return center * lax.rsqrt(spread + NORM_EPS) * gain_vec + shift_vec


def geglu(joined):
    half_width = joined.shape[-1] // 2
    return jax.nn.gelu(joined[:, :half_width]) * joined[:, half_width:]


def alibi_slopes(head_count):
    return 2.0 ** (-8.0 * (jnp.arange(head_count).astype(jnp.float32) + 1.0) / head_count)


def normalize(vectors):
    return vectors * lax.rsqrt(jnp.sum(vectors * vectors, axis=-1, keepdims=True) + UNIT_EPS)


def contrast(unit_all, scale_arg, deal_order):
    pair_count = deal_order.shape[0] // 2
    queries = jnp.take(unit_all, deal_order[:pair_count], axis=0)
    documents = jnp.take(unit_all, deal_order[pair_count:], axis=0)
    logits = jnp.exp(scale_arg[0]) * jnp.matmul(
        queries, documents.T, precision=lax.Precision.HIGHEST
    )
    by_row = jax.nn.logsumexp(logits, axis=1)
    by_column = jax.nn.logsumexp(logits, axis=0)
    return jnp.sum(0.5 * (by_row + by_column) - jnp.diagonal(logits))


def unfactored(grad_full, state):
    state_new = DECAY_RATE * state + (1.0 - DECAY_RATE) * (grad_full * grad_full + STATE_EPS)
    return (-NORM_RATE * grad_full * lax.rsqrt(state_new), state_new)


def block_scores(query_rows, key_all, seg_rows, segment, head_count):
    row_count = query_rows.shape[0]
    raw_scores = jnp.einsum("thc,shc->hts", query_rows, key_all, preferred_element_type=jnp.float32)
    row_pos = jnp.arange(row_count, dtype=jnp.int32)
    col_pos = jnp.arange(key_all.shape[0], dtype=jnp.int32)
    distance = jnp.abs(row_pos[:, None] - col_pos[None, :]).astype(jnp.float32)
    scores = (
        raw_scores * HEAD_DIM ** (-0.5) + -alibi_slopes(head_count)[:, None, None] * distance[None]
    )
    same_seq = seg_rows[:, None] == segment[None, :]
    return jnp.where(same_seq[None], scores, -jnp.inf)


def split_qkv(qkv_low, head_count):
    tokens = qkv_low.shape[0]
    split_heads = qkv_low.reshape(tokens, 3, head_count, qkv_low.shape[1] // (3 * head_count))
    return (split_heads[:, 0], split_heads[:, 1], split_heads[:, 2])


def attend(qkv_low, segment, head_count):
    model_width = qkv_low.shape[1] // 3
    query_all, key_all, value_all = split_qkv(qkv_low, head_count)
    scores = block_scores(query_all, key_all, segment, segment, head_count)
    row_max = jnp.max(scores, axis=-1, keepdims=True)
    exponent = jnp.exp(scores - row_max)
    row_total = jnp.sum(exponent, axis=-1, keepdims=True)
    prob_low = (exponent / row_total).astype(jnp.bfloat16)
    mixed_list = jnp.einsum(
        "hts,shc->thc", prob_low, value_all, preferred_element_type=jnp.float32
    ).reshape(-1, model_width)
    lse_list = row_max[..., 0] + jnp.log(row_total[..., 0])
    return (mixed_list, lse_list)


def attend_back(qkv_low, segment, head_count, lse_all, grad_mixed):
    tokens = qkv_low.shape[0]
    query_all, key_all, value_all = split_qkv(qkv_low, head_count)
    grad_out = grad_mixed.reshape(tokens, head_count, -1)
    block_rows = min(tokens, 512)
    scores = block_scores(query_all, key_all, segment, segment, head_count)
    prob_full = jnp.exp(scores - lse_all[:, 0:block_rows, None])
    grad_value = jnp.einsum(
        "hts,thc->shc", prob_full.astype(jnp.bfloat16), grad_out, preferred_element_type=jnp.float32
    )
    grad_prob = jnp.einsum("thc,shc->hts", grad_out, value_all, preferred_element_type=jnp.float32)
    inner = jnp.sum(prob_full * grad_prob, axis=-1, keepdims=True)
    grad_raw = (prob_full * (grad_prob - inner) * HEAD_DIM ** (-0.5)).astype(jnp.bfloat16)
    query_list = jnp.einsum("hts,shc->thc", grad_raw, key_all, preferred_element_type=jnp.float32)
    grad_key = jnp.einsum("hts,thc->shc", grad_raw, query_all, preferred_element_type=jnp.float32)
    return (
        jnp.stack([query_list, grad_key, grad_value], axis=1)
        .reshape(tokens, -1)
        .astype(jnp.bfloat16)
    )


def shards(
    token_ids,
    seq_lengths,
    valid_mask,
    deal_order,
    log_scale,
    embed_master,
    attn_in,
    attn_out,
    ffn_in,
    ffn_out,
    head_master,
    norm_master,
    embed_rows,
    head_rows,
    layer_rows,
    ffn_out_rows,
    layer_cols,
    embed_head_cols,
    norm_state,
    scale_state,
):
    tokens = token_ids.shape[0]
    model_width = embed_master.shape[1]
    seq_count = seq_lengths.shape[1]
    head_count = HEADS
    position = jnp.arange(tokens, dtype=jnp.int32)
    bounds = jnp.cumsum(seq_lengths[0])
    segment = jnp.sum((position[:, None] >= bounds[None, :]).astype(jnp.int32), axis=1)
    piece_rows = lax.all_gather(embed_master.astype(jnp.bfloat16), "dp", axis=0, tiled=True)
    local_idx = token_ids
    inside = (local_idx >= 0) & (local_idx < piece_rows.shape[0])
    picked = jnp.take(piece_rows, jnp.clip(local_idx, 0, piece_rows.shape[0] - 1), axis=0).astype(
        jnp.float32
    )
    stream = jnp.where(inside[:, None], picked, 0.0)
    w_qkv, w_attn, w_gate_up, w_down, w_head, norm_low = (
        lax.all_gather(attn_in.astype(jnp.bfloat16), "dp", axis=1, tiled=True),
        lax.all_gather(attn_out.astype(jnp.bfloat16), "dp", axis=1, tiled=True),
        lax.all_gather(ffn_in.astype(jnp.bfloat16), "dp", axis=1, tiled=True),
        lax.all_gather(ffn_out.astype(jnp.bfloat16), "dp", axis=1, tiled=True),
        lax.all_gather(head_master.astype(jnp.bfloat16), "dp", axis=0, tiled=True),
        lax.all_gather(norm_master.astype(jnp.bfloat16), "dp", axis=2, tiled=True),
    )
    norms = norm_low.astype(jnp.float32)
    kept_list = []
    for layer_idx in range(LAYERS):
        stream_low = stream.astype(jnp.bfloat16)
        qkv_low = jnp.dot(stream_low, w_qkv[layer_idx], preferred_element_type=jnp.float32).astype(
            jnp.bfloat16
        )
        mixed_heads, lse_all = attend(qkv_low, segment, head_count)
        mixed_low = mixed_heads.astype(jnp.bfloat16)
        resid_one = stream + jnp.dot(
            mixed_low, w_attn[layer_idx], preferred_element_type=jnp.float32
        )
        normed = layer_norm(resid_one, norms[2 * layer_idx, 0], norms[2 * layer_idx, 1])
        normed_low = normed.astype(jnp.bfloat16)
        joined = jnp.dot(normed_low, w_gate_up[layer_idx], preferred_element_type=jnp.float32)
        hidden_low = geglu(joined).astype(jnp.bfloat16)
        resid_two = normed + jnp.dot(
            hidden_low, w_down[layer_idx], preferred_element_type=jnp.float32
        )
        kept_list.append(
            (
                stream_low,
                qkv_low,
                lse_all,
                mixed_low,
                resid_one,
                normed_low,
                joined,
                hidden_low,
                resid_two,
            )
        )
        stream = layer_norm(resid_two, norms[2 * layer_idx + 1, 0], norms[2 * layer_idx + 1, 1])
    final = layer_norm(stream, norms[2 * LAYERS, 0], norms[2 * LAYERS, 1])
    member = (
        (segment[None, :] == jnp.arange(seq_count, dtype=jnp.int32)[:, None])
        & (valid_mask[None, :] > 0)
    ).astype(jnp.float32)
    counts = jnp.maximum(jnp.sum(member, axis=1), 1.0)
    pooled = jnp.matmul(member, final, precision=lax.Precision.HIGHEST) / counts[:, None]
    pooled_low = pooled.astype(jnp.bfloat16)
    head_out = jnp.dot(pooled_low, w_head, preferred_element_type=jnp.float32)
    unit_vecs, unit_back = jax.vjp(normalize, head_out)
    unit_every = lax.all_gather(unit_vecs, ("dp", "group"), axis=0, tiled=True)
    loss_value, loss_back = jax.vjp(
        lambda unit_all, scale_arg: contrast(unit_all, scale_arg, deal_order), unit_every, log_scale
    )
    grad_units, grad_scale = loss_back(jnp.ones_like(loss_value))
    own_rows = lax.dynamic_slice_in_dim(
        grad_units, lax.axis_index(("dp", "group")) * seq_count, seq_count, 0
    )
    grad_head_out = unit_back(own_rows)[0].astype(jnp.bfloat16)
    grad_head = jnp.dot(pooled_low.T, grad_head_out, preferred_element_type=jnp.float32)
    grad_pooled = jnp.dot(grad_head_out, w_head.T, preferred_element_type=jnp.float32)
    grad_final = jnp.matmul(
        member.T, grad_pooled / counts[:, None], precision=lax.Precision.HIGHEST
    )
    final_back = jax.vjp(layer_norm, stream, norms[2 * LAYERS, 0], norms[2 * LAYERS, 1])[1]
    grad_stream, gain_last, shift_last = final_back(grad_final)
    norm_grads = [None] * (2 * LAYERS + 1)
    norm_grads[2 * LAYERS] = jnp.stack([gain_last, shift_last])
    qkv_grads = [None] * LAYERS
    attn_grads = [None] * LAYERS
    gate_grads = [None] * LAYERS
    down_grads = [None] * LAYERS
    for layer_idx in reversed(range(LAYERS)):
        (
            stream_low,
            qkv_low,
            lse_all,
            mixed_low,
            resid_one,
            normed_low,
            joined,
            hidden_low,
            resid_two,
        ) = kept_list[layer_idx]
        norm_two_back = jax.vjp(
            layer_norm, resid_two, norms[2 * layer_idx + 1, 0], norms[2 * layer_idx + 1, 1]
        )[1]
        grad_two, gain_two, shift_two = norm_two_back(grad_stream)
        norm_grads[2 * layer_idx + 1] = jnp.stack([gain_two, shift_two])
        grad_branch = grad_two.astype(jnp.bfloat16)
        down_grads[layer_idx] = jnp.dot(
            hidden_low.T, grad_branch, preferred_element_type=jnp.float32
        )
        grad_hidden = jnp.dot(grad_branch, w_down[layer_idx].T, preferred_element_type=jnp.float32)
        grad_joined = jax.vjp(geglu, joined)[1](grad_hidden)[0].astype(jnp.bfloat16)
        gate_grads[layer_idx] = jnp.dot(
            normed_low.T, grad_joined, preferred_element_type=jnp.float32
        )
        grad_normed = grad_two + jnp.dot(
            grad_joined, w_gate_up[layer_idx].T, preferred_element_type=jnp.float32
        )
        norm_one_back = jax.vjp(
            layer_norm, resid_one, norms[2 * layer_idx, 0], norms[2 * layer_idx, 1]
        )[1]
        grad_one, gain_one, shift_one = norm_one_back(grad_normed)
        norm_grads[2 * layer_idx] = jnp.stack([gain_one, shift_one])
        grad_attended = grad_one.astype(jnp.bfloat16)
        attn_grads[layer_idx] = jnp.dot(
            mixed_low.T, grad_attended, preferred_element_type=jnp.float32
        )
        grad_mixed = jnp.dot(
            grad_attended, w_attn[layer_idx].T, preferred_element_type=jnp.float32
        ).astype(jnp.bfloat16)
        grad_qkv_low = attend_back(qkv_low, segment, head_count, lse_all, grad_mixed)
        qkv_grads[layer_idx] = jnp.dot(
            stream_low.T, grad_qkv_low, preferred_element_type=jnp.float32
        )
        grad_stream = grad_one + jnp.dot(
            grad_qkv_low, w_qkv[layer_idx].T, preferred_element_type=jnp.float32
        )
    row_count = embed_master.shape[0] * lax.axis_size("dp")
    local_idx = token_ids
    inside = (local_idx >= 0) & (local_idx < row_count)
    slot_idx = jnp.where(inside, local_idx, row_count)
    embed_grad = lax.psum_scatter(
        jnp.zeros((row_count, model_width), jnp.float32).at[slot_idx].add(grad_stream, mode="drop"),
        "dp",
        scatter_dimension=0,
        tiled=True,
    )
    grad_qkv = jnp.stack(qkv_grads)
    grad_attn = jnp.stack(attn_grads)
    grad_gate_up = jnp.stack(gate_grads)
    grad_down = jnp.stack(down_grads)
    grad_norm = jnp.stack(norm_grads)
    owned = (
        lax.psum_scatter(grad_qkv, "dp", scatter_dimension=1, tiled=True),
        lax.psum_scatter(grad_attn, "dp", scatter_dimension=1, tiled=True),
        lax.psum_scatter(grad_gate_up, "dp", scatter_dimension=1, tiled=True),
        lax.psum_scatter(grad_down, "dp", scatter_dimension=1, tiled=True),
        lax.psum_scatter(grad_head, "dp", scatter_dimension=0, tiled=True),
        lax.psum_scatter(grad_norm, "dp", scatter_dimension=2, tiled=True),
    )
    shard_qkv, shard_attn, shard_gate_up, shard_down, shard_head, shard_norm, shard_embed = (
        lax.psum((owned[0], owned[1], owned[2], owned[3], owned[4], owned[5], embed_grad), "group")
    )
    grad_list = [
        shard_embed[None],
        shard_head[None],
        shard_qkv,
        shard_attn,
        shard_gate_up,
        shard_down,
    ]
    master_list = [embed_master[None], head_master[None], attn_in, attn_out, ffn_in, ffn_out]
    state_list = [
        embed_rows[None],
        head_rows[None],
        layer_rows[:, 0],
        layer_rows[:, 1],
        layer_rows[:, 2],
        ffn_out_rows,
    ]
    col_list = [
        embed_head_cols[0:1],
        embed_head_cols[1:2],
        layer_cols[:, : 3 * D],
        layer_cols[:, 3 * D : 4 * D],
        layer_cols[:, 4 * D : 4 * D + 2 * FF],
        layer_cols[:, 4 * D + 2 * FF :],
    ]
    total_rows = [VOCAB, D, D, D, D, FF]
    wide_rate = RATE_SCALE / D**0.5
    rates = [
        RATE_SCALE,
        wide_rate,
        wide_rate,
        RATE_SCALE / (D // 8) ** 0.5,
        wide_rate,
        RATE_SCALE / FF**0.5,
    ]
    square_list = [grad_part * grad_part for grad_part in grad_list]
    rows_new = [
        DECAY_RATE * state_list[entry_idx]
        + (1.0 - DECAY_RATE) * (jnp.mean(square_list[entry_idx], axis=-1) + STATE_EPS)
        for entry_idx in range(6)
    ]
    col_parts = jnp.concatenate(
        [jnp.sum(square_part, axis=1).reshape(-1) for square_part in square_list]
    )
    row_parts = jnp.concatenate([jnp.sum(row_part, axis=-1) for row_part in rows_new])
    col_sum, row_sum = lax.psum((col_parts, row_parts), "dp")
    row_means = []
    lead_start = 0
    for entry_idx in range(6):
        lead_count = grad_list[entry_idx].shape[0]
        row_means.append(row_sum[lead_start : lead_start + lead_count] / total_rows[entry_idx])
        lead_start = lead_start + lead_count
    cols_new = []
    steps_all = []
    col_start = 0
    for entry_idx in range(6):
        lead_count = grad_list[entry_idx].shape[0]
        col_width = grad_list[entry_idx].shape[2]
        col_full = col_sum[col_start : col_start + lead_count * col_width].reshape(
            lead_count, col_width
        )
        col_state_new = DECAY_RATE * col_list[entry_idx] + (1.0 - DECAY_RATE) * (
            col_full / total_rows[entry_idx] + STATE_EPS
        )
        cols_new.append(col_state_new)
        steps_all.append(
            grad_list[entry_idx]
            * lax.rsqrt(
                rows_new[entry_idx][:, :, None]
                * col_state_new[:, None, :]
                / row_means[entry_idx][:, None, None]
            )
        )
        col_start = col_start + lead_count * col_width
    step_squares = []
    step_parts = jnp.concatenate(
        [jnp.sum(step_dir * step_dir, axis=(1, 2)) for step_dir in steps_all]
    )
    step_sum = lax.psum(step_parts, "dp")
    lead_start = 0
    for entry_idx in range(6):
        lead_count = grad_list[entry_idx].shape[0]
        step_squares.append(step_sum[lead_start : lead_start + lead_count])
        lead_start = lead_start + lead_count
    new_weights = []
    rms_list = []
    for entry_idx in range(6):
        cell_count = total_rows[entry_idx] * grad_list[entry_idx].shape[2]
        step_rms = jnp.sqrt(step_squares[entry_idx] / cell_count)
        rms_list.append(step_rms)
        delta = (
            -rates[entry_idx]
            * steps_all[entry_idx]
            / jnp.maximum(1.0, step_rms / CLIP_LEVEL)[:, None, None]
        )
        new_weights.append(master_list[entry_idx] + delta)
    norm_delta, norm_second = unfactored(shard_norm, norm_state)
    scale_delta, scale_state_new = unfactored(grad_scale, scale_state)
    return (
        loss_value,
        new_weights[0][0],
        new_weights[2],
        new_weights[3],
        new_weights[4],
        new_weights[5],
        new_weights[1][0],
        norm_master + norm_delta,
        log_scale + scale_delta,
        rows_new[0][0],
        rows_new[1][0],
        jnp.stack([rows_new[2], rows_new[3], rows_new[4]], axis=1),
        rows_new[5],
        jnp.concatenate([cols_new[2], cols_new[3], cols_new[4], cols_new[5]], axis=1),
        cols_new[0][0],
        cols_new[1][0],
        norm_second,
        scale_state_new,
        jnp.concatenate(rms_list),
    )


SLOTS = 80
PART = 1024


MESH = pl.DeviceIdType.MESH
BF=jnp.bfloat16

def place():
    dp = lax.axis_index("dp"); g = lax.axis_index("group")
    return dp // 2, dp % 2, g // 2, g % 2

def dev(z, x, y, c):
    return (z * 2 + x, y * 2 + c)

def entry_barrier(peers):
    bar = pltpu.get_barrier_semaphore()
    for p in peers:
        pl.semaphore_signal(bar, inc=1, device_id=p, device_id_type=MESH)
    pl.semaphore_wait(bar, len(peers))

def mult(v, m=16):
    return pl.multiple_of(v, m)


def slot_plan(token_ids, shard_rows):
    tokens = token_ids.shape[0]
    owner = token_ids // shard_rows
    local = token_ids - owner * shard_rows
    index = jnp.arange(tokens, dtype=jnp.int32)
    same_id = token_ids[:, None] == token_ids[None, :]
    first = jnp.min(jnp.where(same_id, index[None, :], tokens), axis=1)
    leads = first == index
    same_owner = owner[:, None] == owner[None, :]
    slot = jnp.sum(
        (same_owner & leads[None, :] & (index[None, :] < first[:, None])).astype(jnp.int32), axis=1
    )
    key = jnp.where(slot < SLOTS, owner * SLOTS + slot, 8 * SLOTS)
    wanted = jnp.max(
        jnp.where(
            key[:, None] == jnp.arange(8 * SLOTS, dtype=jnp.int32)[None, :], local[:, None], -1
        ),
        axis=0,
    )
    return key, wanted, jnp.max(slot)


def column_blocks(rows):
    lead, count, width = rows.shape
    return (
        rows.reshape(lead, count, width // D, D).transpose(0, 2, 1, 3).reshape(lead, -1, D)
    )


def pack_weights(attn_in, attn_out, ffn_in, ffn_out, head_master, norm_master):
    layers = jnp.concatenate(
        [column_blocks(attn_in), attn_out, column_blocks(ffn_in), ffn_out], axis=1
    ).astype(jnp.bfloat16)
    norm_rows = jnp.pad(
        norm_master.reshape(10, -1).astype(jnp.bfloat16), ((0, 22), (0, D - norm_master.shape[2]))
    )
    return jnp.concatenate(
        [norm_rows, layers.reshape(-1, D), head_master.astype(jnp.bfloat16)], axis=0
    )


def dot_nn(left, right):
    return lax.dot_general(left, right, (((1,), (0,)), ((), ())), preferred_element_type=jnp.float32)


def dot_nt(left, right):
    return lax.dot_general(left, right, (((1,), (1,)), ((), ())), preferred_element_type=jnp.float32)


def dot_tn(left, right):
    return lax.dot_general(left, right, (((0,), (0,)), ((), ())), preferred_element_type=jnp.float32)


def exact_dot(left, right, dims=((1,), (0,))):
    return lax.dot_general(
        left, right, (dims, ((), ())), precision=lax.Precision.HIGHEST, preferred_element_type=jnp.float32
    )


def step_id(kind, first=0, second=0, third=0):
    return ord(kind) * 1000 + first * 100 + second * 10 + third


GELU_SCALE = (2.0 / 3.141592653589793) ** 0.5
GELU_CUBE = 0.044715
TILE = 256


def norm_parts(values):
    center = values - jnp.mean(values, axis=-1, keepdims=True)
    inverse = lax.rsqrt(jnp.mean(center * center, axis=-1, keepdims=True) + NORM_EPS)
    return center * inverse, inverse


def norm_back(scaled, inverse, grad_out, gain):
    grad_scaled = grad_out * gain
    mean_grad = jnp.mean(grad_scaled, axis=-1, keepdims=True)
    mean_both = jnp.mean(grad_scaled * scaled, axis=-1, keepdims=True)
    return inverse * (grad_scaled - mean_grad - scaled * mean_both)


def gelu_parts(value):
    bend = jnp.tanh(GELU_SCALE * (value + GELU_CUBE * value * value * value))
    half = 0.5 * (1.0 + bend)
    slope = half + 0.5 * value * (1.0 - bend * bend) * GELU_SCALE * (1.0 + 3.0 * GELU_CUBE * value * value)
    return value * half, slope


def block(w_ref, start):
    return w_ref[:, start : start + 64, :].reshape(D, D)


def down_block(w_ref, j):
    return w_ref[2 * j : 2 * j + 2, 768:1024, :].reshape(D, D)


def fill_distance(far, seg_col_ref, seg_row_ref):
    tokens = far.shape[0]
    def body(i, carry):
        start = pl.multiple_of(i * 64, 64)
        rows = lax.broadcasted_iota(jnp.int32, (64, tokens), 0) + start
        cols = lax.broadcasted_iota(jnp.int32, (64, tokens), 1)
        gap = jnp.abs(rows - cols).astype(jnp.float32)
        same = seg_col_ref[pl.ds(start, 64), :] == seg_row_ref[...]
        far[pl.ds(start, 64), :] = jnp.where(same, gap, jnp.inf)
        return carry
    lax.fori_loop(0, tokens // 64, body, 0)


def forward_kernel(
    first_ref, seg_col_ref, seg_row_ref, valid_ref, w_ref, head_ref, norm_ref,
    low_ref, qkv_ref, lse_ref, mix_ref, one_ref, two_ref, unit_ref, pool_ref, zed_ref,
    x_s, far, acc,
):
    layer = pl.program_id(0)
    tokens = x_s.shape[0]
    tiles = tokens // TILE

    @pl.when(layer == 0)
    def _():
        x_s[...] = first_ref[...].astype(jnp.float32)
        fill_distance(far, seg_col_ref, seg_row_ref)

    def project(i, carry):
        rows = pl.ds(pl.multiple_of(i * TILE, TILE), TILE)
        low = x_s[rows, :].astype(jnp.bfloat16)
        low_ref[0, rows, :] = low
        for j in range(3):
            qkv_ref[0, rows, j * D : (j + 1) * D] = dot_nn(low, block(w_ref, j * 64)).astype(jnp.bfloat16)
        return carry

    lax.fori_loop(0, tiles, project, 0)
    for head in range(HEADS):
        lanes = slice(head * HEAD_DIM, (head + 1) * HEAD_DIM)
        keys = qkv_ref[0, :, D + head * HEAD_DIM : D + (head + 1) * HEAD_DIM]
        vals_t = qkv_ref[0, :, 2 * D + head * HEAD_DIM : 2 * D + (head + 1) * HEAD_DIM].T
        slope = 2.0 ** (-8.0 * (head + 1) / HEADS)
        for i in range(tiles):
            cols = slice(i * TILE, (i + 1) * TILE)
            scores = dot_nt(keys, qkv_ref[0, cols, lanes]) * HEAD_DIM**-0.5 - slope * far[:, cols]
            top = jnp.max(scores, axis=0, keepdims=True)
            raised = jnp.exp(scores - top)
            total = jnp.sum(raised, axis=0, keepdims=True)
            lse_ref[0, head, :, cols] = top + jnp.log(total)
            prob = (raised * (1.0 / total)).astype(jnp.bfloat16)
            mix_ref[0, lanes, cols] = dot_nn(vals_t, prob).astype(jnp.bfloat16)

    acc[...] = dot_tn(mix_ref[0], block(w_ref, 192))

    def feed(i, carry):
        rows = pl.ds(pl.multiple_of(i * TILE, TILE), TILE)
        resid = x_s[rows, :] + acc[rows, :]
        one_ref[0, rows, :] = resid
        at = 4 * layer
        scaled, _ = norm_parts(resid)
        hidden = scaled * norm_ref[pl.ds(at, 1), :] + norm_ref[pl.ds(at + 1, 1), :]
        low = hidden.astype(jnp.bfloat16)
        total = hidden
        for j in range(4):
            gate = dot_nn(low, block(w_ref, 256 + j * 64))
            up = dot_nn(low, block(w_ref, 512 + j * 64))
            bend = jnp.tanh(GELU_SCALE * (gate + GELU_CUBE * gate * gate * gate))
            mid = (0.5 * gate * (1.0 + bend) * up).astype(jnp.bfloat16)
            total = total + dot_nn(mid, down_block(w_ref, j))
        two_ref[0, rows, :] = total
        scaled, _ = norm_parts(total)
        x_s[rows, :] = scaled * norm_ref[pl.ds(at + 2, 1), :] + norm_ref[pl.ds(at + 3, 1), :]
        return carry

    lax.fori_loop(0, tiles, feed, 0)

    @pl.when(layer == LAYERS - 1)
    def _():
        pool_units(x_s, norm_ref, seg_row_ref, valid_ref, head_ref, unit_ref, pool_ref, zed_ref)


def members(seg_row_ref, valid_ref):
    tokens = seg_row_ref.shape[1]
    slot = lax.broadcasted_iota(jnp.int32, (8, tokens), 0)
    return jnp.where((seg_row_ref[...] == slot) & (valid_ref[...] > 0), 1.0, 0.0)


def whole(shape):
    return pl.BlockSpec(shape, lambda i: (0,) * len(shape))


def run_forward(first, seg_col, seg_row, valid, weights, norms):
    tokens = first.shape[0]
    low = jnp.bfloat16
    layered = lambda *s: pl.BlockSpec((1,) + s, lambda i: (i,) + (0,) * len(s))
    return pl.pallas_call(
        forward_kernel,
        grid=(LAYERS,),
        in_specs=[
            whole((tokens, D)), whole((tokens, 1)), whole((1, tokens)), whole((1, tokens)),
            pl.BlockSpec((8, PART, D), lambda i: (0, i, 0)),
            pl.BlockSpec((8, 64, D), lambda i: (0, 2 * PART // 64, 0)),
            whole(norms.shape),
        ],
        out_specs=[
            layered(tokens, D), layered(tokens, 3 * D), layered(HEADS, 1, tokens), layered(D, tokens),
            layered(tokens, D), layered(tokens, D), whole((16, 128)), whole((8, D)), whole((8, D)),
        ],
        out_shape=[
            jax.ShapeDtypeStruct((LAYERS, tokens, D), low),
            jax.ShapeDtypeStruct((LAYERS, tokens, 3 * D), low),
            jax.ShapeDtypeStruct((LAYERS, HEADS, 1, tokens), jnp.float32),
            jax.ShapeDtypeStruct((LAYERS, D, tokens), low),
            jax.ShapeDtypeStruct((LAYERS, tokens, D), jnp.float32),
            jax.ShapeDtypeStruct((LAYERS, tokens, D), jnp.float32),
            jax.ShapeDtypeStruct((16, 128), jnp.float32),
            jax.ShapeDtypeStruct((8, D), low),
            jax.ShapeDtypeStruct((8, D), jnp.float32),
        ],
        scratch_shapes=[
            pltpu.VMEM((tokens, D), jnp.float32), pltpu.VMEM((tokens, tokens), jnp.float32),
            pltpu.VMEM((tokens, D), jnp.float32),
        ],
        compiler_params=pltpu.CompilerParams(vmem_limit_bytes=60 * 2**20),
    )(first, seg_col, seg_row, valid, weights, weights, norms)


PACK_LAYER = (32, 32 + PART)
PACK_HEAD = 32 + 2 * PART
PARCELS = (
    (0, 144, 64), (288, 128, 48), (544, 128, 48), (800, 128, 48),
    (1056, 128, 48), (1312, 128, 48), (1568, 128, 48), (1824, 160, 32),
)
GATHER_ORDER = (
    113000, 115000, 115100, 115200, 115300, 116000, 110000, 122000, 122100, 120030, 122200, 120130, 120230, 114000,
    120330, 121000, 122300, 121100, 121031, 121131, 122010, 122110, 121200, 122210, 121231, 121300, 122310, 121331,
    121010, 120000, 121210, 121110, 120100, 122020, 115400, 120200, 121001, 121310, 120010, 122120, 115500, 120110,
    121101, 121020, 120300, 122220, 115600, 122400, 121011, 120210, 121201, 122320, 115700, 120310, 121301, 121111,
    122500, 121120, 121400, 121220, 120020, 121211, 120430, 122410, 121311, 121320, 122600, 120120, 121500, 122420,
    122510, 120530, 122700, 121021, 121431, 122520, 121410, 120400, 122610, 120220, 121600, 120630, 97000, 121121,
    122620, 121420, 121510, 119000, 121531, 122710, 120500, 120320, 121700, 112000, 120730, 121401, 97100, 121520,
    121221, 122720, 104000, 121610, 121631, 104010, 120600, 120410, 120420, 104020, 120510, 97200, 121620, 104030,
    121321, 121501, 121710, 120700, 104040, 121731, 120520, 104050, 120610, 121720, 97300, 104060, 121601, 121411,
    104070, 121421, 109000, 121511, 120620, 121701, 120710, 102000, 121521, 121611, 97400, 120720, 102010, 121621,
    97500, 121711, 112100, 104100, 121721, 97600, 104110, 104120, 104130, 104140, 97700, 104150, 104160, 104170,
    109100, 102100, 102110, 118000,
)


def nearest(z):
    return (z + 1 - 2 * (z % 2), 2 - z // 2, 3 - 3 * (z // 2), z)


def gather_stages(w_ref, ag_ref, zs, zr, xs, xr, ys, yr, cs, cr):
    z, x, y, c = place()
    me = z * 2 + x
    inner = (z == 1) | (z == 2)
    pair = dev(z + 1 - 2 * (z % 2), x, y, c)
    across = dev(3 - z, x, y, c)
    outward = dev((3 * z + 1) % 4, x, y, c)
    xp, yp, cp = dev(z, 1 - x, y, c), dev(z, x, 1 - y, c), dev(z, x, y, 1 - c)
    near = nearest(z)

    def rc(src, dst, s, r, d):
        return pltpu.make_async_remote_copy(src, dst, s, r, device_id=d, device_id_type=MESH)

    def shard(n, f):
        return near[n] * 2 + (x if f == 0 else 1 - x)

    steps = {}
    always, within = [], []
    others = [(0, 0), (1, 0), (2, 0), (3, 1), (0, 1), (1, 1), (2, 1)]

    def parcel(q, base, half, spare):
        main = pl.ds(mult(base + c * half + y * spare), half - spare)
        extra = pl.ds(mult(base + c * half + y * (half - spare)), spare)
        every = pl.ds(mult(base + c * half), half)

        def at(n, f, rows):
            return ag_ref.at[shard(n, f), rows]

        own = w_ref.at[main]
        to_pair = rc(own, at(3, 0, main), zs.at[q, 0], zr.at[q, 0], pair)
        to_across = rc(own, at(3, 0, main), zs.at[q, 1], zr.at[q, 1], across)
        on = [
            rc(at(0, 0, main), at(0, 0, main), zs.at[q, 2], zr.at[q, 2], across),
            rc(at(1, 0, main), at(1, 0, main), zs.at[q, 3], zr.at[q, 1], outward),
            rc(at(2, 0, main), at(2, 0, main), zs.at[q, 4], zr.at[q, 2], outward),
        ]
        over = [rc(own if n == 3 else at(n, 0, main), at(n, 0, main), xs.at[q, n], xr.at[q, n], xp) for n in range(4)]
        planes, cores = {}, {}
        for n, f in others:
            planes[n, f] = rc(at(n, f, extra), at(n, f, extra), ys.at[q, 2 * n + f], yr.at[q, 2 * n + f], yp)
            cores[n, f] = rc(at(n, f, every), at(n, f, every), cs.at[q, 2 * n + f], cr.at[q, 2 * n + f], cp)
        always.extend([to_pair] + over + list(planes.values()) + list(cores.values()))
        within.extend([to_across] + on)
        landed = [rc(own, at(n, 0, main), zs.at[q, 0], zr.at[q, n], pair) for n in range(3)]

        def issue():
            pl.when(inner)(to_across.start)
            to_pair.start()
            over[3].start()

        def along(n):
            landed[n].wait_recv()
            pl.when(inner)(on[n].start)
            over[n].start()
            planes[n, 0].start()

        def sideways(n):
            over[n].wait_recv()
            planes[n, 1].start()

        def plane(n, f):
            planes[n, f].wait_recv()
            cores[n, f].start()

        def arrived():
            for copy in cores.values():
                copy.wait_recv()

        steps[step_id("s", q)] = (issue,)
        for n in range(3):
            steps[step_id("z", q, n)] = (along, n)
        for n in range(4):
            steps[step_id("x", q, n)] = (sideways, n)
        for n, f in others:
            steps[step_id("y", q, n, f)] = (plane, n, f)
        steps[step_id("a", q)] = (arrived,)

    for q, spec in enumerate(PARCELS):
        parcel(q, *spec)

    def finish():
        for copy in always:
            copy.wait_send()

        @pl.when(inner)
        def _():
            for copy in within:
                copy.wait_send()

    return steps, finish


def request_stages(ask_ref, asks_ref, table_ref, table, picked, rows_s, got, sems, es, er, qs, qr):
    z, x, y, c = place()
    me = z * 2 + x
    g = y * 2 + c
    g2 = (1 - y) * 2 + c
    ep = [(lax.rem(me + k, 8), g) for k in range(8)]
    yp, cp = dev(z, x, 1 - y, c), dev(z, x, y, 1 - c)

    def rc(src, dst, s, r, d):
        return pltpu.make_async_remote_copy(src, dst, s, r, device_id=d, device_id_type=MESH)

    count = rows_s.shape[1]
    to_owner = [rc(ask_ref.at[ep[k][0]], asks_ref.at[g, me], qs.at[k], qr.at[k], ep[k]) for k in range(1, 8)]
    mine = pltpu.make_async_copy(ask_ref.at[me], asks_ref.at[g, me], sems.at[0])
    near = pltpu.make_async_copy(table_ref, table.at[pl.ds(0, table_ref.shape[0])], sems.at[1])
    to_plane = rc(asks_ref.at[g], asks_ref.at[g], qs.at[8], qr.at[8], yp)
    to_core = rc(asks_ref.at[g], asks_ref.at[g], qs.at[9], qr.at[9], cp)
    on_core = rc(asks_ref.at[g2], asks_ref.at[g2], qs.at[10], qr.at[10], cp)
    kept = pltpu.make_async_copy(rows_s.at[me], got.at[me], sems.at[2])
    answers = [rc(rows_s.at[ep[k][0]], got.at[me], es.at[k], er.at[k], ep[k]) for k in range(1, 8)]

    def load():
        near.start()

    def ask():
        for copy in to_owner:
            copy.start()
        mine.start()

    def answer():
        mine.wait()
        for copy in to_owner:
            copy.wait_recv()
        to_plane.start()
        to_core.start()
        wanted = asks_ref[pl.ds(g, 1)].reshape(8, 128).astype(jnp.float32).T
        near.wait()
        depth = table.shape[0] // 5
        rest = table.shape[0] - table_ref.shape[0]
        table[pl.ds(table_ref.shape[0], rest), :] = jnp.zeros((rest, D), jnp.float32)
        picked[...] = jnp.zeros(picked.shape, jnp.float32)
        ramp = lax.broadcasted_iota(jnp.int32, (count, depth), 1).astype(jnp.float32)

        def body(i, carry):
            low = table[pl.ds(pl.multiple_of(i * depth, depth), depth), :].astype(BF)
            shifted = ramp + (i * depth).astype(jnp.float32)
            for r in range(8):
                hot = jnp.where(wanted[:count, r : r + 1] == shifted, 1.0, 0.0).astype(BF)
                picked[r] += dot_nn(hot, low)
            return carry

        lax.fori_loop(0, 5, body, 0)
        rows_s[...] = picked[...].astype(BF)
        kept.start()
        for copy in answers:
            copy.start()

    def relay():
        to_plane.wait_recv()
        on_core.start()

    def take():
        kept.wait()
        for copy in answers:
            copy.wait_recv()

    def finish():
        to_core.wait_recv()
        on_core.wait_recv()
        for copy in answers + to_owner + [to_plane, to_core, on_core]:
            copy.wait_send()

    return load, ask, answer, relay, take, finish


def gather_forward_kernel(
    w_ref, ask_ref, table_ref, key_ref, seg_col_ref, seg_row_ref, valid_ref,
    ag_ref, asks_ref, low_out, qkv_out, lse_out, mix_out, one_out, two_out, unit_ref, pool_ref, zed_ref, norm_ref,
    table, picked, rows_s, got, weights, head, norm_low, low_s, qkv_s, lse_s, mix_s, one_s, two_s, x_s, far, acc,
    zs, zr, xs, xr, ys, yr, cs, cr, sems, es, er, qs, qr, loads, saves,
):
    z, x, y, c = place()
    me = z * 2 + x
    g = y * 2 + c
    tokens = x_s.shape[0]
    tiles = tokens // TILE
    peers = [(lax.rem(me + k, 8), g) for k in range(1, 8)] + [dev(z, x, 1 - y, c), dev(z, x, y, 1 - c)]
    barrier = pltpu.get_barrier_semaphore()
    for peer in peers:
        pl.semaphore_signal(barrier, inc=1, device_id=peer, device_id_type=MESH)
    steps, finish = gather_stages(w_ref, ag_ref, zs, zr, xs, xr, ys, yr, cs, cr)
    load, ask, answer, relay, take, ask_finish = request_stages(
        ask_ref, asks_ref, table_ref, table, picked, rows_s, got, sems, es, er, qs, qr
    )
    own = pltpu.make_async_copy(w_ref, ag_ref.at[me], sems.at[3])

    def loading(slot, rows, count, into):
        return pltpu.make_async_copy(ag_ref.at[:, pl.ds(rows, count)], into, loads.at[slot])

    fetch = {("norm", 0): loading(8, 0, 32, norm_low), ("head", 0): loading(9, PACK_HEAD, 64, head)}
    for layer in range(LAYERS):
        for part in range(4):
            fetch[layer, part] = loading(
                4 * layer + part, PACK_LAYER[layer] + 256 * part, 256, weights.at[layer, :, pl.ds(256 * part, 256)]
            )
    saving = {}
    for layer in range(LAYERS):
        for i, (source, target) in enumerate(
            ((low_s, low_out), (qkv_s, qkv_out), (lse_s, lse_out), (mix_s, mix_out), (one_s, one_out), (two_s, two_out))
        ):
            saving[layer, i] = pltpu.make_async_copy(source.at[layer], target.at[layer], saves.at[layer, i])

    def begin():
        load()
        own.start()

    def arrive(q):
        arrived[q]()
        if q == 0:
            own.wait()
            fetch["norm", 0].start()
        fetch[q // 4, q % 4].start()
        if q == 7:
            fetch["head", 0].start()

    def set_up():
        fill_distance(far, seg_col_ref, seg_row_ref)

    def first_rows():
        take()
        slots = lax.broadcasted_iota(jnp.int32, (tokens, got.shape[0] * got.shape[1]), 1)
        picks = jnp.where(slots == key_ref[...], 1.0, 0.0).astype(BF)
        x_s[...] = dot_nn(picks, got[...].reshape(-1, D))
        fetch["norm", 0].wait()
        norm_ref[...] = jnp.concatenate([norm_low[d, 0:16, 0:64].astype(jnp.float32) for d in range(8)], axis=1)

    def project(layer):
        fetch[layer, 0].wait()

        def body(i, carry):
            rows = pl.ds(pl.multiple_of(i * TILE, TILE), TILE)
            low = x_s[rows, :].astype(BF)
            low_s[layer, rows, :] = low
            for j in range(3):
                qkv_s[layer, rows, j * D : (j + 1) * D] = dot_nn(low, block(weights.at[layer], j * 64)).astype(BF)
            return carry

        lax.fori_loop(0, tiles, body, 0)
        saving[layer, 0].start()
        saving[layer, 1].start()

    def attend_head(layer, head):
        lanes = slice(head * HEAD_DIM, (head + 1) * HEAD_DIM)
        keys = qkv_s[layer, :, D + head * HEAD_DIM : D + (head + 1) * HEAD_DIM]
        vals_t = qkv_s[layer, :, 2 * D + head * HEAD_DIM : 2 * D + (head + 1) * HEAD_DIM].T
        slope = 2.0 ** (-8.0 * (head + 1) / HEADS)
        for i in range(tiles):
            cols = slice(i * TILE, (i + 1) * TILE)
            scores = dot_nt(keys, qkv_s[layer, cols, lanes]) * HEAD_DIM**-0.5 - slope * far[:, cols]
            top = jnp.max(scores, axis=0, keepdims=True)
            raised = jnp.exp(scores - top)
            total = jnp.sum(raised, axis=0, keepdims=True)
            lse_s[layer, head, :, cols] = top + jnp.log(total)
            prob = (raised * (1.0 / total)).astype(BF)
            mix_s[layer, lanes, cols] = dot_nn(vals_t, prob).astype(BF)

    def mix(layer):
        saving[layer, 2].start()
        saving[layer, 3].start()
        acc[...] = dot_tn(mix_s[layer], block(weights.at[layer], 192))

    def feed(layer, i):
        if i == 0:
            for part in (1, 2, 3):
                fetch[layer, part].wait()
        rows = pl.ds(i * TILE, TILE)
        resid = x_s[rows, :] + acc[rows, :]
        one_s[layer, rows, :] = resid
        at = 4 * layer
        scaled, _ = norm_parts(resid)
        hidden = scaled * norm_ref[at : at + 1, :] + norm_ref[at + 1 : at + 2, :]
        low = hidden.astype(BF)
        total = hidden
        for j in range(4):
            gate = dot_nn(low, block(weights.at[layer], 256 + j * 64))
            up = dot_nn(low, block(weights.at[layer], 512 + j * 64))
            bend = jnp.tanh(GELU_SCALE * (gate + GELU_CUBE * gate * gate * gate))
            mid = (0.5 * gate * (1.0 + bend) * up).astype(BF)
            total = total + dot_nn(mid, down_block(weights.at[layer], j))
        two_s[layer, rows, :] = total
        scaled, _ = norm_parts(total)
        x_s[rows, :] = scaled * norm_ref[at + 2 : at + 3, :] + norm_ref[at + 3 : at + 4, :]
        if i == tiles - 1:
            saving[layer, 4].start()
            saving[layer, 5].start()

    def end():
        fetch["head", 0].wait()
        pool_units(x_s, norm_ref, seg_row_ref, valid_ref, head, unit_ref, pool_ref, zed_ref)

    arrived = [steps[step_id("a", q)][0] for q in range(8)]
    for q in range(8):
        steps[step_id("a", q)] = (arrive, q)
    steps[step_id("q")], steps[step_id("n")], steps[step_id("r")] = (ask,), (answer,), (relay,)
    steps[step_id("t")], steps[step_id("w")], steps[step_id("v")] = (set_up,), (first_rows,), (end,)
    for layer in range(LAYERS):
        steps[step_id("p", layer)], steps[step_id("m", layer)] = (project, layer), (mix, layer)
        for head_index in range(HEADS):
            steps[step_id("h", layer, head_index)] = (attend_head, layer, head_index)
        for i in range(tiles):
            steps[step_id("f", layer, i)] = (feed, layer, i)
    begin()
    pl.semaphore_wait(barrier, len(peers))
    for name in GATHER_ORDER:
        fn, *rest = steps.pop(name)
        fn(*rest)
    assert not steps
    finish()
    ask_finish()
    for copy in saving.values():
        copy.wait()


def pool_units(x_s, norm_ref, seg_row_ref, valid_ref, head, unit_ref, pool_ref, zed_ref):
    scaled, _ = norm_parts(x_s[...])
    final = scaled * norm_ref[8:9, :] + norm_ref[9:10, :]
    member = members(seg_row_ref, valid_ref)
    counts = jnp.maximum(jnp.sum(member, axis=1, keepdims=True), 1.0)
    pooled = (exact_dot(member, final) / counts).astype(BF)
    pool_ref[...] = pooled
    zed = dot_nn(pooled, head[...].reshape(D, D))
    zed_ref[...] = zed
    unit = zed * lax.rsqrt(jnp.sum(zed * zed, axis=-1, keepdims=True) + UNIT_EPS)
    for s in range(4):
        for part in range(4):
            unit_ref[4 * s + part : 4 * s + part + 1, :] = unit[s : s + 1, part * 128 : (part + 1) * 128]


def run_gather_forward(packed, asks, embed, key_col, seg_col, seg_row, valid, cid):
    tokens = key_col.shape[0]
    low, full = jnp.bfloat16, jnp.float32
    near = pl.BlockSpec(memory_space=pltpu.VMEM)
    anywhere = pl.BlockSpec(memory_space=pl.ANY)
    shape = jax.ShapeDtypeStruct
    vmem = lambda dims, kind=low: pltpu.VMEM(dims, kind)
    sems = lambda *dims: pltpu.SemaphoreType.DMA(dims)
    padded = -(-embed.shape[0] // 640) * 640
    saved = [
        ((LAYERS, tokens, D), low), ((LAYERS, tokens, 3 * D), low), ((LAYERS, HEADS, 1, tokens), full),
        ((LAYERS, D, tokens), low), ((LAYERS, tokens, D), full), ((LAYERS, tokens, D), full),
    ]
    return pl.pallas_call(
        gather_forward_kernel,
        in_specs=[anywhere, near, anywhere, near, near, near, near],
        out_specs=[anywhere, near] + [anywhere] * 6 + [near] * 4,
        out_shape=[shape((8,) + packed.shape, low), shape((4,) + asks.shape, asks.dtype)]
        + [shape(*v) for v in saved]
        + [shape((16, 128), full), shape((8, D), low), shape((8, D), full), shape((16, D), full)],
        scratch_shapes=[
            vmem((padded, D), full), vmem((8, SLOTS, D), full), vmem((8, SLOTS, D)), vmem((8, SLOTS, D)),
            vmem((LAYERS, 8, PART, D)), vmem((8, 64, D)), vmem((8, 32, D)),
        ]
        + [vmem(*v) for v in saved]
        + [
            vmem((tokens, D), full), vmem((tokens, tokens), full), vmem((tokens, D), full),
            sems(8, 5), sems(8, 3), sems(8, 4), sems(8, 4), sems(8, 8), sems(8, 8), sems(8, 8), sems(8, 8),
            sems(4), sems(8), sems(8), sems(11), sems(11), sems(10), sems(2, 6),
        ],
        compiler_params=pltpu.CompilerParams(collective_id=cid, has_side_effects=True, vmem_limit_bytes=62 * 2**20),
    )(packed, asks, embed, key_col, seg_col, seg_row, valid)


def contrast_kernel(unit_ref, deal_col_ref, deal_row_ref, scale_ref, loss_ref, own_ref, slope_ref, every, ss, rs, ls):
    lin = lax.axis_index("dp") * 4 + lax.axis_index("group")
    peers = [lax.rem(lin + k, 32) for k in range(32)]
    peers = [(p // 4, p % 4) for p in peers]
    entry_barrier(peers[1:])
    copies = [
        pltpu.make_async_remote_copy(
            unit_ref, every.at[lin], ss.at[k], rs.at[k], device_id=peers[k], device_id_type=MESH
        )
        for k in range(1, 32)
    ]
    for copy in copies:
        copy.start()
    own = pltpu.make_async_copy(unit_ref, every.at[lin], ls)
    own.start()
    for copy in copies:
        copy.wait()
    own.wait()
    units = every[...].reshape(512, 128)
    place_at = lax.broadcasted_iota(jnp.int32, (128, 512), 1)
    sorted_units = jnp.concatenate(
        [
            exact_dot(jnp.where(deal_col_ref[...] * 4 + part == place_at, 1.0, 0.0), units)
            for part in range(4)
        ],
        axis=1,
    )
    queries, documents = sorted_units[:64], sorted_units[64:]
    scale = jnp.exp(scale_ref[...])
    logits = scale * exact_dot(queries, documents, ((1,), (1,)))
    row_top = jnp.max(logits, axis=1, keepdims=True)
    row_lse = row_top + jnp.log(jnp.sum(jnp.exp(logits - row_top), axis=1, keepdims=True))
    col_top = jnp.max(logits, axis=0, keepdims=True)
    col_lse = col_top + jnp.log(jnp.sum(jnp.exp(logits - col_top), axis=0, keepdims=True))
    diagonal = jnp.where(
        lax.broadcasted_iota(jnp.int32, (64, 64), 0) == lax.broadcasted_iota(jnp.int32, (64, 64), 1), 1.0, 0.0
    )
    on_diagonal = jnp.sum(logits * diagonal, axis=1, keepdims=True)
    col_sum = jnp.sum(col_lse, axis=1, keepdims=True)
    row_sum = jnp.sum(row_lse, axis=0, keepdims=True)
    loss_ref[...] = 0.5 * (row_sum + col_sum) - jnp.sum(on_diagonal, axis=0, keepdims=True)
    grad_logits = 0.5 * (jnp.exp(logits - row_lse) + jnp.exp(logits - col_lse)) - diagonal
    slope = jnp.sum(grad_logits * logits, axis=1, keepdims=True)
    slope_ref[...] = jnp.sum(slope, axis=0, keepdims=True)
    grad_raw = scale * grad_logits
    grad_queries = exact_dot(grad_raw, documents)
    grad_documents = exact_dot(grad_raw, queries, ((0,), (0,)))
    mine = lax.broadcasted_iota(jnp.int32, (8, 128), 0)
    picks = jnp.where((deal_row_ref[...] == mine + lin * 4) & (mine < 4), 1.0, 0.0)
    own_ref[...] = exact_dot(picks, jnp.concatenate([grad_queries, grad_documents], axis=0))


def run_contrast(unit, deal_order, log_scale, cid):
    sems = pltpu.SemaphoreType.DMA
    one = jax.ShapeDtypeStruct((1, 1), jnp.float32)
    return pl.pallas_call(
        contrast_kernel,
        out_shape=[one, jax.ShapeDtypeStruct((8, D), jnp.float32), one],
        in_specs=[pl.BlockSpec(memory_space=pltpu.VMEM)] * 4,
        out_specs=[pl.BlockSpec(memory_space=pltpu.VMEM)] * 3,
        scratch_shapes=[pltpu.VMEM((32, 16, 128), jnp.float32), sems((32,)), sems((32,)), sems],
        compiler_params=pltpu.CompilerParams(collective_id=cid, has_side_effects=True),
    )(unit, deal_order.reshape(128, 1), deal_order.reshape(1, 128), log_scale.reshape(1, 1))


GRAD_ROWS = 2 * PART + 64
GRAD_LAYER = (0, PART + 64)
GRAD_HEAD = PART
PIECES = tuple(
    (stage, half, spare, at)
    for stage, half, spare, at in (
        (320, 128, 32, GRAD_LAYER[1] + 256), (576, 128, 32, GRAD_LAYER[1] + 512), (832, 128, 32, GRAD_LAYER[1] + 768),
        (0, 160, 32, GRAD_HEAD),
        (320, 128, 32, 256), (576, 128, 32, 512), (832, 128, 32, 768),
        (64, 128, 32, 0),
    )
)


BACKWARD_ORDER = (
    98000, 101100, 102100, 102110, 102120, 102130, 115000, 115100, 115200, 109100, 67000, 67010, 67020, 67030, 104100,
    67040, 67050, 67060, 89000, 67070, 67100, 67110, 89010, 67120, 67130, 67140, 67150, 67160, 89020, 67170, 89030,
    104110, 89040, 89050, 67200, 67210, 88020, 89060, 67220, 67230, 67240, 67250, 89070, 67260, 67270, 88010, 104120,
    89100, 89110, 89120, 104130, 88030, 89130, 89140, 89150, 104140, 89160, 88000, 89170, 104150, 89200, 89210, 88120,
    104160, 89220, 89230, 90000, 89240, 88110, 104170, 89250, 89260, 88130, 89270, 108100, 70000, 115300, 88100,
    88220, 101000, 88210, 90100, 102000, 67300, 88230, 67310, 88200, 67320, 67330, 67340, 67350, 67360, 67370, 70100,
    102010, 89300, 90200, 89310, 89320, 89330, 89340, 102020, 88320, 89350, 89360, 89370, 70200, 102030, 115400,
    115500, 88310, 115600, 88330, 88300, 109000, 67400, 67410, 67420, 67430, 67440, 67450, 67460, 67470, 67500,
    104000, 89400, 67510, 89410, 67520, 67530, 67540, 89420, 67550, 67560, 67570, 67600, 89430, 67610, 67620, 67630,
    89440, 90300, 67640, 89450, 67650, 88420, 67660, 104010, 89460, 89470, 67670, 89500, 88410, 104020, 89510, 89520,
    89530, 88430, 104030, 89540, 89550, 104040, 89560, 88400, 89570, 104050, 89600, 89610, 88520, 104060, 90400,
    89620, 88510, 89630, 104070, 70300, 89640, 89650, 88530, 89660, 108000, 115700, 73000, 69000, 89670, 88500, 70400,
    88620, 67700, 67710, 67720, 88610, 67730, 67740, 67750, 68000, 67760, 67770, 78000, 89700, 89710, 89720, 89730,
    88630, 89740, 69200, 89750, 90500, 69400, 89760, 69600, 69300, 89770, 69500, 69100, 69700, 88600, 70500, 68200,
    68600, 68400, 68700, 68100, 68300, 68500, 88720, 88710, 88730, 90600, 88700, 70600, 90700, 70700, 118000,
)


def sum_stages(stage, out_ref, acc, b1, b2, b3, b4, b5, fin, sems, free):
    cs, cr, ys, yr, xs, xr, zs, zr, as_, ar, fs, fr, ls, os_ = sems
    z, x, y, c = place()
    me = z * 2 + x
    zp = [dev((z + k) % 4, x, y, c) for k in range(4)]
    xp, yp, cp = dev(z, 1 - x, y, c), dev(z, x, 1 - y, c), dev(z, x, y, 1 - c)

    def rc(src, dst, s, r, d):
        return pltpu.make_async_remote_copy(src, dst, s, r, device_id=d, device_id_type=MESH)

    def owner(k, f):
        return ((z + k) % 4) * 2 + (x if f == 0 else 1 - x)

    order = [(k, f) for k in (2, 1, 3, 0) for f in (1, 0)]
    lo, lb, lh, la, l1 = [0], [0], [0], [0], [0]
    for stage_at, half, spare, at in PIECES:
        lo.append(lo[-1] + half)
        lb.append(lb[-1] + spare)
        lh.append(lh[-1] + half - spare)
        la.append(la[-1] + half - 2 * spare)
        l1.append(l1[-1] + half)
    l1 = l1[:4] + l1[:4]

    def add(dst, src, count):
        def body(i, carry):
            at = mult(i * 32)
            into = dst(at)
            into[...] = (into[...].astype(jnp.float32) + src(at)[...].astype(jnp.float32)).astype(BF)
            return carry
        lax.fori_loop(0, count // 32, body, 0)
        if count % 32:
            into = dst(count - 16, 16)
            into[...] = (into[...].astype(jnp.float32) + src(count - 16, 16)[...].astype(jnp.float32)).astype(BF)

    class Piece:
        pass

    pieces = []
    for q, (stage_at, half, spare, at) in enumerate(PIECES):
        p = Piece()
        p.q, p.half, p.spare, p.main = q, half, spare, half - spare
        p.hs = mult(lo[q] + y * spare)
        p.mb = mult(lo[q] + y * p.main)
        p.ob = mult(lo[q] + (1 - y) * p.main)
        p.L, p.C, p.Y, p.X, p.Z = [], [], [], [], []
        for i, (k, f) in enumerate(order):
            s = owner(k, f)
            p.L.append(pltpu.make_async_copy(stage.at[s, pl.ds(mult(stage_at + c * half), half)], acc.at[s, pl.ds(lo[q], half)], ls.at[q, i]))
            p.C.append(rc(stage.at[s, pl.ds(mult(stage_at + (1 - c) * half), half)], b1.at[s, pl.ds(l1[q], half)], cs.at[q, i], cr.at[q, i], cp))
            p.Y.append(rc(acc.at[s, pl.ds(p.ob, spare)], b2.at[s, pl.ds(lb[q], spare)], ys.at[q, i], yr.at[q, i], yp))
        for k in range(4):
            p.X.append(rc(acc.at[owner(k, 1), pl.ds(p.hs, p.main)], b3.at[k, pl.ds(lh[q], p.main)], xs.at[q, k], xr.at[q, k], xp))
            p.Z.append(rc(acc.at[owner(k, 0), pl.ds(p.hs, p.main)], b4.at[k - 1, pl.ds(lh[q], p.main)], zs.at[q, k], zr.at[q, k], zp[k]) if k else None)
        p.aa, p.na = lo[q] + spare, half - 2 * spare
        p.A = rc(fin.at[pl.ds(p.aa, p.na)], b5.at[pl.ds(la[q], p.na)], as_.at[q, 0], ar.at[q, 0], yp)
        p.B = rc(fin.at[pl.ds(p.mb, spare)], fin.at[pl.ds(p.mb, spare)], as_.at[q, 1], ar.at[q, 1], yp)
        p.F = rc(fin.at[pl.ds(lo[q], half)], out_ref.at[pl.ds(mult(at + c * half), half)], fs.at[q], fr.at[q], cp)
        p.O = pltpu.make_async_copy(fin.at[pl.ds(lo[q], half)], out_ref.at[pl.ds(mult(at + c * half), half)], os_.at[q])
        pieces.append(p)

    def issue(q):
        p = pieces[q]
        if q >= 4:
            pl.semaphore_wait(free.at[q - 4], 1)
        for i in range(8):
            p.C[i].start()
            p.L[i].start()

    def core(q, i):
        p = pieces[q]
        s = owner(*order[i])
        p.L[i].wait()
        p.C[i].wait_recv()
        add(lambda a, n=32: acc.at[s, pl.ds(lo[q] + a, n)], lambda a, n=32: b1.at[s, pl.ds(l1[q] + a, n)], p.half)
        p.Y[i].start()
        if i == 7 and q < 4:
            pl.semaphore_signal(free.at[q], inc=1, device_id=cp, device_id_type=MESH)

    def plane(q, i):
        p = pieces[q]
        k, f = order[i]
        s = owner(k, f)
        p.Y[i].wait_recv()
        add(lambda a, n=32: acc.at[s, pl.ds(p.mb + a, n)], lambda a, n=32: b2.at[s, pl.ds(lb[q] + a, n)], p.spare)
        if f == 1:
            p.X[k].start()

    def sideways(q, k):
        p = pieces[q]
        s = owner(k, 0)
        p.X[k].wait_recv()
        add(lambda a, n=32: acc.at[s, pl.ds(p.hs + a, n)], lambda a, n=32: b3.at[k, pl.ds(lh[q] + a, n)], p.main)
        if k:
            p.Z[k].start()

    def along(q):
        p = pieces[q]
        for k in range(1, 4):
            p.Z[k].wait_recv()
        def body(i, carry):
            at = mult(i * 16)
            total = acc[me, pl.ds(p.hs + at, 16)].astype(jnp.float32)
            for k in range(3):
                total += b4[k, pl.ds(lh[q] + at, 16)].astype(jnp.float32)
            fin[pl.ds(p.hs + at, 16)] = total.astype(BF)
            return carry
        lax.fori_loop(0, p.main // 16, body, 0)
        p.A.start()
        p.B.start()

    def last(q):
        p = pieces[q]
        p.A.wait_recv()
        p.A.wait_send()
        add(lambda a, n=32: fin.at[pl.ds(p.aa + a, n)], lambda a, n=32: b5.at[pl.ds(la[q] + a, n)], p.na)
        p.B.wait_recv()
        p.F.start()
        p.O.start()

    steps = {}
    for q in range(8):
        steps[step_id("s", q)], steps[step_id("Z", q)], steps[step_id("F", q)] = (issue, q), (along, q), (last, q)
        for i in range(8):
            steps[step_id("C", q, i)], steps[step_id("Y", q, i)] = (core, q, i), (plane, q, i)
        for k in range(4):
            steps[step_id("X", q, k)] = (sideways, q, k)

    def sent(q):
        for copy in pieces[q].C:
            copy.wait_send()

    def finish():
        for p in pieces:
            p.F.wait()
            p.O.wait()
            p.B.wait_send()
            for copy in p.Y + p.X + p.Z[1:]:
                copy.wait_send()

    return steps, sent, finish


def row_exchange(slots, t_ref, norm_ref, norm_out, nbuf, es, er, el, ns, nr):
    z, x, y, c = place()
    me = z * 2 + x
    g = y * 2 + c
    g2 = (1 - y) * 2 + c
    ep = [(lax.rem(me + k, 8), g) for k in range(8)]
    back = [lax.rem(me + 8 - k, 8) for k in range(8)]
    yp, cp = dev(z, x, 1 - y, c), dev(z, x, y, 1 - c)

    def rc(src, dst, s, r, d):
        return pltpu.make_async_remote_copy(src, dst, s, r, device_id=d, device_id_type=MESH)

    kept = pltpu.make_async_copy(slots.at[me], t_ref.at[g, me], el)
    E = [rc(slots.at[ep[k][0]], t_ref.at[g, me], es.at[0, k], er.at[0, k], ep[k]) for k in range(1, 8)]
    EY = [rc(t_ref.at[g, back[k]], t_ref.at[g, back[k]], es.at[1, k], er.at[1, k], yp) for k in range(8)]
    EC = [rc(t_ref.at[g, back[k]], t_ref.at[g, back[k]], es.at[2, k], er.at[2, k], cp) for k in range(8)]
    ED = [rc(t_ref.at[g2, back[k]], t_ref.at[g2, back[k]], es.at[3, k], er.at[3, k], cp) for k in range(8)]
    NC = rc(norm_ref, nbuf.at[0], ns.at[0], nr.at[0], cp)
    NY = rc(nbuf.at[1], nbuf.at[2], ns.at[1], nr.at[1], yp)

    def issue():
        kept.start()
        for copy in E:
            copy.start()
        NC.start()

    def norms():
        NC.wait_recv()
        nbuf[1] = nbuf[0] + norm_ref[...]
        NY.start()

    def relay(k):
        if k:
            E[k - 1].wait_recv()
        else:
            kept.wait()
        EY[k].start()
        EC[k].start()

    def relay_core(k):
        EY[k].wait_recv()
        ED[k].start()

    def end():
        NY.wait_recv()
        norm_out[...] = nbuf[1] + nbuf[2]
        for copy in EC + ED:
            copy.wait_recv()
        for copy in E + EY + EC + ED + [NC, NY]:
            copy.wait_send()

    steps = {step_id("I"): (issue,), step_id("N"): (norms,), step_id("v"): (end,)}
    for k in range(8):
        steps[step_id("E", k)], steps[step_id("D", k)] = (relay, k), (relay_core, k)
    return steps


def backward_kernel(
    own_ref, zed_ref, pool_ref, seg_col_ref, seg_row_ref, valid_ref, key_ref, norm_ref,
    w_ref, low_in, qkv_in, lse_in, mix_in, one_in, two_in,
    out_ref, t_ref, norm_out, first_ref,
    weights, head, low_ref, qkv_ref, lse_ref, mix_ref, one_ref, two_ref, stage,
    dx, far, acc, two_s, low_s, mid_s, ups, gates, back, norm_s, slots,
    total, b1, b2, b3, b4, b5, fin, nbuf,
    cs, cr, ys, yr, xs, xr, zs, zr, as_, ar, fs, fr, ls, os_, es, er, el, ns, nr, loads, free,
):
    tokens = dx.shape[0]
    tiles = tokens // TILE
    low_type = jnp.bfloat16
    z, x, y, c = place()
    me = z * 2 + x
    g = y * 2 + c
    peers = [(lax.rem(me + k, 8), g) for k in range(1, 8)] + [dev(z, x, 1 - y, c), dev(z, x, y, 1 - c)]
    barrier = pltpu.get_barrier_semaphore()
    for peer in peers:
        pl.semaphore_signal(barrier, inc=1, device_id=peer, device_id_type=MESH)
    steps, sent, finish = sum_stages(
        stage, out_ref, total, b1, b2, b3, b4, b5, fin, (cs, cr, ys, yr, xs, xr, zs, zr, as_, ar, fs, fr, ls, os_), free
    )
    steps |= row_exchange(slots, t_ref, norm_s, norm_out, nbuf, es, er, el, ns, nr)

    def loading(layer):
        base = PACK_LAYER[layer]
        copy = pltpu.make_async_copy
        return {
            "two": copy(two_in.at[layer], two_ref, loads.at[layer, 0]),
            "one": copy(one_in.at[layer], one_ref, loads.at[layer, 1]),
            "feed": copy(w_ref.at[:, pl.ds(base + 256, 768)], weights.at[:, pl.ds(256, 768)], loads.at[layer, 2]),
            "mix": copy(mix_in.at[layer], mix_ref, loads.at[layer, 3]),
            "qkv": copy(qkv_in.at[layer], qkv_ref, loads.at[layer, 4]),
            "lse": copy(lse_in.at[layer], lse_ref, loads.at[layer, 5]),
            "low": copy(low_in.at[layer], low_ref, loads.at[layer, 6]),
            "attend": copy(w_ref.at[:, pl.ds(base, 256)], weights.at[:, pl.ds(0, 256)], loads.at[layer, 7]),
        }

    load = [loading(layer) for layer in range(LAYERS)]
    head_load = pltpu.make_async_copy(w_ref.at[:, pl.ds(PACK_HEAD, 64)], head, loads.at[0, 8])
    head_load.start()
    for copy in load[1].values():
        copy.start()

    def begin():
        fill_distance(far, seg_col_ref, seg_row_ref)
        head_load.wait()
        load[1]["two"].wait()
        zed = zed_ref[...]
        square = jnp.sum(zed * zed, axis=-1, keepdims=True) + UNIT_EPS
        inverse = lax.rsqrt(square)
        own = own_ref[...]
        inner = jnp.sum(own * zed, axis=-1, keepdims=True)
        grad_zed = (inverse * (own - zed * (inner / square))).astype(low_type)
        head_low = head[...].reshape(D, D)
        stage[:, 0:64, :] = dot_tn(pool_ref[...], grad_zed).reshape(8, 64, D).astype(low_type)
        member = members(seg_row_ref, valid_ref)
        counts = jnp.maximum(jnp.sum(member, axis=1, keepdims=True), 1.0)
        grad_pooled = dot_nt(grad_zed, head_low) / counts
        grad_final = exact_dot(member, grad_pooled, ((0,), (0,)))
        stream_scaled, _ = norm_parts(two_ref[...])
        stream = stream_scaled * norm_ref[6:7, :] + norm_ref[7:8, :]
        scaled, inverse = norm_parts(stream)
        norm_s[...] = jnp.zeros(norm_s.shape, jnp.float32)
        norm_s[2, 0:1, :] = jnp.sum(grad_final * scaled, axis=0, keepdims=True)
        norm_s[2, 1:2, :] = jnp.sum(grad_final, axis=0, keepdims=True)
        dx[...] = norm_back(scaled, inverse, grad_final, norm_ref[8:9, :])

    def enter(layer):
        at = 4 * layer
        if layer < LAYERS - 1:
            load[layer]["two"].wait()
        load[layer]["one"].wait()

        def body(i, carry):
            rows = pl.ds(pl.multiple_of(i * TILE, TILE), TILE)
            scaled, inverse = norm_parts(two_ref[rows, :])
            grad = dx[rows, :]
            norm_s[layer, 2:3, :] += jnp.sum(grad * scaled, axis=0, keepdims=True)
            norm_s[layer, 3:4, :] += jnp.sum(grad, axis=0, keepdims=True)
            grad = norm_back(scaled, inverse, grad, norm_ref[at + 2 : at + 3, :])
            acc[rows, :] = grad
            two_s[rows, :] = grad.astype(low_type)
            scaled, _ = norm_parts(one_ref[rows, :])
            hidden = scaled * norm_ref[at : at + 1, :] + norm_ref[at + 1 : at + 2, :]
            low_s[rows, :] = hidden.astype(low_type)
            return carry

        lax.fori_loop(0, tiles, body, 0)
        if layer > 0:
            load[layer - 1]["two"].start()
        load[layer]["feed"].wait()

    def feed(layer, j):
        def body(i, carry):
            rows = pl.ds(pl.multiple_of(i * TILE, TILE), TILE)
            low = low_s[rows, :]
            gate = dot_nn(low, block(weights, 256 + j * 64))
            up = dot_nn(low, block(weights, 512 + j * 64))
            grad_mid = dot_nt(two_s[rows, :], down_block(weights, j))
            value, slope = gelu_parts(gate)
            mid_s[rows, :] = (value * up).astype(low_type)
            grad_gate = (grad_mid * up * slope).astype(low_type)
            grad_up = (grad_mid * value).astype(low_type)
            gates[rows, :] = grad_gate
            ups[rows, :] = grad_up
            acc[rows, :] += dot_nt(grad_gate, block(weights, 256 + j * 64)) + dot_nt(
                grad_up, block(weights, 512 + j * 64)
            )
            return carry

        lax.fori_loop(0, tiles, body, 0)
        if layer < LAYERS - 1 and j == 0:
            for q in range(3):
                sent(q)
        stage[2 * j : 2 * j + 2, 832:1088, :] = dot_tn(mid_s[...], two_s[...]).reshape(2, 256, D).astype(low_type)
        stage[:, 320 + j * 64 : 384 + j * 64, :] = dot_tn(low_s[...], gates[...]).reshape(8, 64, D).astype(low_type)
        stage[:, 576 + j * 64 : 640 + j * 64, :] = dot_tn(low_s[...], ups[...]).reshape(8, 64, D).astype(low_type)

    def middle(layer):
        at = 4 * layer
        if layer > 0:
            load[layer - 1]["feed"].start()
        load[layer]["attend"].wait()
        load[layer]["mix"].wait()

        def body(i, carry):
            rows = pl.ds(pl.multiple_of(i * TILE, TILE), TILE)
            scaled, inverse = norm_parts(one_ref[rows, :])
            grad = acc[rows, :]
            norm_s[layer, 0:1, :] += jnp.sum(grad * scaled, axis=0, keepdims=True)
            norm_s[layer, 1:2, :] += jnp.sum(grad, axis=0, keepdims=True)
            grad = norm_back(scaled, inverse, grad, norm_ref[at : at + 1, :])
            dx[rows, :] = grad
            low = grad.astype(low_type)
            two_s[rows, :] = low
            mid_s[rows, :] = dot_nt(low, block(weights, 192)).astype(low_type)
            return carry

        lax.fori_loop(0, tiles, body, 0)
        if layer > 0:
            load[layer - 1]["one"].start()
        else:
            sent(3)
        stage[:, 256:320, :] = dot_nn(mix_ref[...], two_s[...]).reshape(8, 64, D).astype(low_type)
        load[layer]["qkv"].wait()
        load[layer]["lse"].wait()
        load[layer]["low"].wait()

    def attend_head(layer, head):
        lanes = slice(head * HEAD_DIM, (head + 1) * HEAD_DIM)
        key_lanes = slice(D + head * HEAD_DIM, D + (head + 1) * HEAD_DIM)
        val_lanes = slice(2 * D + head * HEAD_DIM, 2 * D + (head + 1) * HEAD_DIM)
        keys = qkv_ref[:, key_lanes]
        keys_t = keys.T
        vals = qkv_ref[:, val_lanes]
        slope = 2.0 ** (-8.0 * (head + 1) / HEADS)
        grad_vals = None
        grad_keys = None
        for i in range(tiles):
            cols = slice(i * TILE, (i + 1) * TILE)
            query = qkv_ref[cols, lanes]
            grad_mix = mid_s[cols, lanes]
            scores = dot_nt(keys, query) * HEAD_DIM**-0.5 - slope * far[:, cols]
            prob = jnp.exp(scores - lse_ref[head, :, cols])
            grad_prob = dot_nt(vals, grad_mix)
            inner = jnp.sum(prob * grad_prob, axis=0, keepdims=True)
            grad_raw = (prob * (grad_prob - inner) * HEAD_DIM**-0.5).astype(low_type)
            back[cols, lanes] = dot_nn(keys_t, grad_raw).T.astype(low_type)
            value_part = dot_nn(prob.astype(low_type), grad_mix)
            key_part = dot_nn(grad_raw, query)
            grad_vals = value_part if grad_vals is None else grad_vals + value_part
            grad_keys = key_part if grad_keys is None else grad_keys + key_part
        back[:, key_lanes] = grad_keys.astype(low_type)
        back[:, val_lanes] = grad_vals.astype(low_type)

    def leave(layer):
        def body(i, carry):
            rows = pl.ds(pl.multiple_of(i * TILE, TILE), TILE)
            grad = dx[rows, :]
            for j in range(3):
                grad = grad + dot_nt(back[rows, j * D : (j + 1) * D], block(weights, j * 64))
            dx[rows, :] = grad
            return carry

        lax.fori_loop(0, tiles, body, 0)
        for j in range(3):
            stage[:, 64 + j * 64 : 128 + j * 64, :] = (
                dot_tn(low_ref[...], back[:, j * D : (j + 1) * D]).reshape(8, 64, D).astype(low_type)
            )
        if layer > 0:
            for name in ("mix", "qkv", "lse", "low", "attend"):
                load[layer - 1][name].start()
        else:
            first_ref[...] = dx[...].astype(low_type)
            count = slots.shape[1]
            for d in range(8):
                hot = lax.broadcasted_iota(jnp.int32, (count, tokens), 0) + d * count == key_ref[...]
                slots[d] = dot_nn(jnp.where(hot, 1.0, 0.0).astype(low_type), first_ref[...]).astype(low_type)

    steps[step_id("b")] = (begin,)
    for layer in range(LAYERS):
        steps[step_id("e", layer)], steps[step_id("m", layer)], steps[step_id("l", layer)] = (enter, layer), (middle, layer), (leave, layer)
        for j in range(4):
            steps[step_id("f", layer, j)] = (feed, layer, j)
        for head_index in range(HEADS):
            steps[step_id("h", layer, head_index)] = (attend_head, layer, head_index)
    for name in BACKWARD_ORDER:
        if name == step_id("s"):
            pl.semaphore_wait(barrier, len(peers))
        fn, *rest = steps.pop(name)
        fn(*rest)
    assert not steps
    finish()
    for q in range(4, 8):
        sent(q)


def run_backward(own, zed, pool, seg_col, seg_row, valid, key, weights, norms, saved, cid):
    low_x, qkv, lse, mix, one, two = saved
    tokens = low_x.shape[1]
    low = jnp.bfloat16
    full = jnp.float32
    vmem = lambda shape, kind=low: pltpu.VMEM(shape, kind)
    sems = lambda *shape: pltpu.SemaphoreType.DMA(shape)
    half = sum(p[1] for p in PIECES)
    spare = sum(p[2] for p in PIECES)
    near = pl.BlockSpec(memory_space=pltpu.VMEM)
    anywhere = pl.BlockSpec(memory_space=pl.ANY)
    norm_shape = (LAYERS + 1, 8, D)
    square = (tokens, D)
    return pl.pallas_call(
        backward_kernel,
        in_specs=[near] * 8 + [anywhere] * 7,
        out_specs=[anywhere, anywhere, near, near],
        out_shape=[
            jax.ShapeDtypeStruct((GRAD_ROWS, D), low),
            jax.ShapeDtypeStruct((4, 8, SLOTS, D), low),
            jax.ShapeDtypeStruct(norm_shape, full),
            jax.ShapeDtypeStruct(square, low),
        ],
        scratch_shapes=[
            vmem((8, PART, D)), vmem((8, 64, D)), vmem(square), vmem((tokens, 3 * D)), vmem((HEADS, 1, tokens), full),
            vmem((D, tokens)), vmem(square, full), vmem(square, full), vmem((8, PART + 64, D)),
            vmem(square, full), vmem((tokens, tokens), full), vmem(square, full), vmem(square), vmem(square),
            vmem(square), vmem(square), vmem(square), vmem((tokens, 3 * D)), vmem(norm_shape, full), vmem((8, SLOTS, D)),
            vmem((8, half, D)), vmem((8, sum(p[1] for p in PIECES[:4]), D)), vmem((8, spare, D)), vmem((4, half - spare, D)),
            vmem((3, half - spare, D)), vmem((half - 2 * spare, D)), vmem((half, D)), vmem((3,) + norm_shape, full),
            sems(8, 8), sems(8, 8), sems(8, 8), sems(8, 8), sems(8, 4), sems(8, 4), sems(8, 4), sems(8, 4),
            sems(8, 2), sems(8, 2), sems(8), sems(8), sems(8, 8), sems(8), sems(4, 8), sems(4, 8), pltpu.SemaphoreType.DMA,
            sems(2), sems(2), sems(2, 9), pltpu.SemaphoreType.REGULAR((4,)),
        ],
        compiler_params=pltpu.CompilerParams(collective_id=cid, has_side_effects=True, vmem_limit_bytes=63 * 2**20),
    )(own, zed, pool, seg_col, seg_row, valid, key, norms, weights, low_x, qkv, lse, mix, one, two)


def total_kernel(v_ref, o_ref, got, mine, ss, rs, ts, us, ls):
    me = lax.axis_index("dp")
    g = lax.axis_index("group")
    lin = me * 4 + g
    to = [lax.rem(lin + k, 32) for k in range(32)]
    peers = [(p // 4, p % 4) for p in to]
    owners = [(lax.rem(me + k, 8), g) for k in range(8)]
    entry_barrier(peers[1:])
    first = [
        pltpu.make_async_remote_copy(
            v_ref.at[owners[k][0] * 4 + g], got.at[k], ss.at[k], rs.at[k], device_id=owners[k], device_id_type=MESH
        )
        for k in range(1, 8)
    ]
    for copy in first:
        copy.start()
    own = pltpu.make_async_copy(v_ref.at[lin], got.at[0], ls.at[0])
    own.start()
    for copy in first:
        copy.wait()
    own.wait()
    mine[...] = jnp.sum(got[...], axis=0)
    second = [
        pltpu.make_async_remote_copy(
            mine, o_ref.at[lin], ts.at[k], us.at[k], device_id=peers[k], device_id_type=MESH
        )
        for k in range(1, 32)
    ]
    for copy in second:
        copy.start()
    own = pltpu.make_async_copy(mine, o_ref.at[lin], ls.at[1])
    own.start()
    for copy in second:
        copy.wait()
    own.wait()


def total(v, cid):
    sems = pltpu.SemaphoreType.DMA
    return pl.pallas_call(
        total_kernel,
        out_shape=jax.ShapeDtypeStruct(v.shape, v.dtype),
        in_specs=[pl.BlockSpec(memory_space=pltpu.VMEM)], out_specs=pl.BlockSpec(memory_space=pltpu.VMEM),
        scratch_shapes=[
            pltpu.VMEM((8,) + v.shape[1:], v.dtype), pltpu.VMEM(v.shape[1:], v.dtype),
            sems((8,)), sems((8,)), sems((32,)), sems((32,)), sems((2,)),
        ],
        compiler_params=pltpu.CompilerParams(collective_id=cid, has_side_effects=True),
    )(v)


BLOCKS = 28
STEP_AT = 28
SUM_AT = 56
NORM_ROW = 57
ROW_TILE = 512
RATES = (
    RATE_SCALE, RATE_SCALE / D**0.5, RATE_SCALE / D**0.5, RATE_SCALE / (D // 8) ** 0.5,
    RATE_SCALE / D**0.5, RATE_SCALE / FF**0.5,
)


def matrices(layer):
    at = GRAD_LAYER[layer]
    first = 2 + 13 * layer
    return (
        (2, at, 64, 3, first), (3, at + 192, 64, 1, first + 3),
        (4, at + 256, 64, 8, first + 4), (5, at + 768, 256, 1, first + 12),
    )


def turn(row):
    return jnp.broadcast_to(row, (8, row.shape[1])).T[:, 0:1]


def lane_pick(value, lane):
    return jnp.where(lax.broadcasted_iota(jnp.int32, (1, D), 1) == lane, value, 0.0)


def stats_kernel(dense, row_count, *refs):
    *refs, low_hot = refs
    if dense:
        full_ref, grads_ref, norm_ref, table_row_ref, rows_ref, down_ref, *outs = refs
    else:
        slot_ref, slot_rows_ref, grads_ref, norm_ref, table_row_ref, rows_ref, down_ref, *outs = refs
    table_ref, table_row_out, stat_ref, rows_out, down_out = outs
    step = pl.program_id(0)

    def put(at, value):
        stat_ref[at // 3, at % 3 : at % 3 + 1, :] = value

    def add(at, value):
        stat_ref[at // 3, at % 3 : at % 3 + 1, :] += value

    @pl.when(step == 0)
    def _():
        stat_ref[...] = jnp.zeros(stat_ref.shape, jnp.float32)
        for row in range(10):
            put(NORM_ROW + row, norm_ref[row // 4, row % 4 : row % 4 + 1, :])
        sums = jnp.zeros((1, D), jnp.float32)
        rows_out[...] = jnp.zeros(rows_out.shape, jnp.float32)

        def part(first, count, blocks, block_at, old):
            squares = [
                grads_ref[first + j * count : first + (j + 1) * count, :].astype(jnp.float32) ** 2 for j in range(blocks)
            ]
            mean = jnp.sum(functools.reduce(jnp.add, squares), axis=-1, keepdims=True) / (blocks * D)
            new = DECAY_RATE * old + (1.0 - DECAY_RATE) * (mean + STATE_EPS)
            inverse = 1.0 / new
            for j in range(blocks):
                put(block_at + j, jnp.sum(squares[j], axis=0, keepdims=True))
                put(STEP_AT + block_at + j, jnp.sum(squares[j] * inverse, axis=0, keepdims=True))
            return new, jnp.sum(new, axis=0, keepdims=True)

        new, count = part(GRAD_HEAD, 64, 1, 1, rows_ref[:, 6:7])
        rows_out[:, 6:7] = new
        sums += lane_pick(count, 1)
        for layer in range(LAYERS):
            for name, first, rows, blocks, block_at in matrices(layer):
                if name == 5:
                    new, count = part(first, rows, blocks, block_at, down_ref[:, layer : layer + 1])
                    down_out[:, layer : layer + 1] = new
                else:
                    lane = 3 * layer + name - 2
                    new, count = part(first, rows, blocks, block_at, rows_ref[:, lane : lane + 1])
                    rows_out[:, lane : lane + 1] = new
                sums += lane_pick(count, 2 * name - 2 + layer)
        put(SUM_AT, sums)

    index = lax.broadcasted_iota(jnp.int32, (ROW_TILE, 1), 0) + step * ROW_TILE
    if dense:
        grad = jnp.where(index < row_count, full_ref[...], 0.0)
    else:
        high = slot_ref[...] // 64

        @pl.when(step == 0)
        def _():
            low = lax.broadcasted_iota(jnp.int32, low_hot.shape, 0)
            low_hot[...] = jnp.where(low == slot_ref[...] - 64 * high, 1.0, 0.0).astype(jnp.bfloat16)

        picks = jnp.concatenate(
            [
                low_hot[...] * jnp.where(high == step * (ROW_TILE // 64) + i, 1.0, 0.0).astype(jnp.bfloat16)
                for i in range(ROW_TILE // 64)
            ],
            axis=0,
        )
        grad = jnp.dot(picks, slot_rows_ref[...], preferred_element_type=jnp.float32)
    low = grad.astype(jnp.bfloat16)
    table_ref[...] = low
    squares = low.astype(jnp.float32) ** 2
    mean = jnp.mean(squares, axis=-1, keepdims=True)
    mean_row = jnp.broadcast_to(mean, (ROW_TILE, 128)).T[0:1, :]
    new = DECAY_RATE * table_row_ref[...] + (1.0 - DECAY_RATE) * (mean_row + STATE_EPS)
    real = lax.broadcasted_iota(jnp.int32, (1, ROW_TILE), 1) + step * ROW_TILE < row_count
    new = jnp.where(real, new, 1.0)
    table_row_out[...] = new
    add(0, jnp.sum(squares, axis=0, keepdims=True))
    add(STEP_AT, jnp.sum(squares * (1.0 / turn(new)), axis=0, keepdims=True))
    add(SUM_AT, lane_pick(jnp.sum(jnp.where(real, new, 0.0), axis=1, keepdims=True), 0))


def run_stats(dense, heads, grads, norm, table_row, rows, down):
    row_count = table_row.shape[1]
    tile = pl.BlockSpec((ROW_TILE, D), lambda i: (i, 0))
    lane = pl.BlockSpec((1, ROW_TILE), lambda i: (0, i))
    head_specs = [tile] if dense else [whole(v.shape) for v in heads]
    stat = (32, 3, D)
    return pl.pallas_call(
        functools.partial(stats_kernel, dense, row_count),
        grid=(-(-row_count // ROW_TILE),),
        in_specs=head_specs + [whole(grads.shape), whole(norm.shape), lane, whole(rows.shape), whole(down.shape)],
        out_specs=[tile, lane, whole(stat), whole(rows.shape), whole(down.shape)],
        out_shape=[
            jax.ShapeDtypeStruct((row_count, D), jnp.bfloat16), jax.ShapeDtypeStruct(table_row.shape, jnp.float32),
            jax.ShapeDtypeStruct(stat, jnp.float32), jax.ShapeDtypeStruct(rows.shape, jnp.float32),
            jax.ShapeDtypeStruct(down.shape, jnp.float32),
        ],
        scratch_shapes=[pltpu.VMEM((64, 8 if dense else heads[0].shape[1]), jnp.bfloat16)],
        compiler_params=pltpu.CompilerParams(vmem_limit_bytes=48 * 2**20),
    )(*heads, grads, norm, table_row, rows, down)


def update_kernel(
    totals, stat_ref, table_ref, embed_ref, table_row_ref, rows_ref, down_ref, top_cols_ref, cols_ref,
    grads_in, in_in, mix_in, gate_in, low_in, head_in,
    embed_out, table_cols_out, head_cols_out, cols_out, rms_out, in_to, mix_to, gate_to, low_to, head_to,
    factors, grads_ref, in_ref, mix_ref, gate_ref, low_ref, head_ref, loads, stores,
):
    step = pl.program_id(0)
    sources = (grads_in, in_in, mix_in, gate_in, low_in, head_in)
    held = (grads_ref, in_ref, mix_ref, gate_ref, low_ref, head_ref)
    targets = (in_to, mix_to, gate_to, low_to, head_to)
    load = [pltpu.make_async_copy(sources[i], held[i], loads.at[i]) for i in range(6)]
    store = [pltpu.make_async_copy(held[i + 1], targets[i], stores.at[i]) for i in range(5)]

    def stat(at):
        return stat_ref[at // 3, at % 3 : at % 3 + 1, :]

    def mean_of(lane, name):
        return jnp.sum(jnp.where(lax.broadcasted_iota(jnp.int32, (1, D), 1) == lane, stat(SUM_AT), 0.0), axis=1, keepdims=True) / totals[name]

    def columns(block_at, blocks, old, lane, name):
        row_mean = mean_of(lane, name)
        news = []
        steps = 0.0
        for j in range(blocks):
            new = DECAY_RATE * old(j) + (1.0 - DECAY_RATE) * (stat(block_at + j) / totals[name] + STATE_EPS)
            news.append(new)
            steps += jnp.sum(row_mean * stat(STEP_AT + block_at + j) / new, axis=1, keepdims=True)
        rms = jnp.sqrt(steps / (totals[name] * blocks * D))
        scale = -RATES[name] / jnp.maximum(1.0, rms / CLIP_LEVEL)
        return news, row_mean, rms, scale

    @pl.when(step == 0)
    def _():
        for copy in load:
            copy.start()
        news, row_mean, rms, scale = columns(0, 1, lambda j: top_cols_ref[0:1, :], 0, 0)
        table_cols_out[...] = news[0]
        factors[0:1, :] = lax.rsqrt(news[0])
        factors[1:2, :] = jnp.broadcast_to(row_mean, (1, D))
        factors[2:3, :] = jnp.broadcast_to(scale, (1, D))
        factors[3:4, :] = lane_pick(rms, 0)

    @pl.when(step == pl.num_programs(0) - 1)
    def _():
        for copy in load:
            copy.wait()
        all_rms = factors[3:4, :]
        news, row_mean, rms, scale = columns(1, 1, lambda j: top_cols_ref[1:2, :], 1, 1)
        head_cols_out[...] = news[0]
        all_rms += lane_pick(rms, 1)
        row = lax.rsqrt(rows_ref[:, 6:7] / row_mean) * scale
        head_ref[...] = head_ref[...] + grads_ref[GRAD_HEAD : GRAD_HEAD + 64, :].astype(jnp.float32) * row * lax.rsqrt(news[0])
        for layer in range(LAYERS):
            for name, first, rows, blocks, block_at in matrices(layer):
                col_at = (block_at - 2 - 13 * layer) * D
                old = lambda j: cols_ref[layer : layer + 1, col_at + j * D : col_at + (j + 1) * D]
                news, row_mean, rms, scale = columns(block_at, blocks, old, 2 * name - 2 + layer, name)
                all_rms += lane_pick(rms, 2 * name - 2 + layer)
                lane = 3 * layer + name - 2
                state = down_ref[:, layer : layer + 1] if name == 5 else rows_ref[:, lane : lane + 1]
                row = lax.rsqrt(state / row_mean) * scale
                held_ref = (in_ref, mix_ref, gate_ref, low_ref)[name - 2]
                for j in range(blocks):
                    cols_out[layer : layer + 1, col_at + j * D : col_at + (j + 1) * D] = news[j]
                    span = slice(j * D, (j + 1) * D)
                    grad = grads_ref[first + j * rows : first + (j + 1) * rows, :].astype(jnp.float32)
                    held_ref[layer, :, span] = held_ref[layer, :, span] + grad * row * lax.rsqrt(news[j])
        rms_out[...] = all_rms
        for copy in store:
            copy.start()

    row = lax.rsqrt(turn(table_row_ref[...] / factors[1:2, :ROW_TILE])) * factors[2:3, 0:1]
    embed_out[...] = embed_ref[...] + table_ref[...].astype(jnp.float32) * row * factors[0:1, :]

    @pl.when(step == pl.num_programs(0) - 1)
    def _():
        for copy in store:
            copy.wait()


def run_update(totals, stat, table, embed, table_row, grads, rows, down, top_cols, cols, others):
    row_count = embed.shape[0]
    tile = pl.BlockSpec((ROW_TILE, D), lambda i: (i, 0))
    lane = pl.BlockSpec((1, ROW_TILE), lambda i: (0, i))
    shape = lambda v: jax.ShapeDtypeStruct(v.shape, jnp.float32)
    one = jax.ShapeDtypeStruct((1, D), jnp.float32)
    outs = [shape(embed), one, one, shape(cols), one]
    anywhere = pl.BlockSpec(memory_space=pl.ANY)
    return pl.pallas_call(
        functools.partial(update_kernel, totals),
        grid=(-(-row_count // ROW_TILE),),
        in_specs=[whole(stat.shape), tile, tile, lane]
        + [whole(v.shape) for v in (rows, down, top_cols, cols)]
        + [anywhere] * 6,
        out_specs=[tile] + [whole(v.shape) for v in outs[1:]] + [anywhere] * 5,
        out_shape=outs + [shape(v) for v in others],
        scratch_shapes=[pltpu.VMEM((8, D), jnp.float32), pltpu.VMEM(grads.shape, jnp.bfloat16)]
        + [pltpu.VMEM(v.shape, jnp.float32) for v in others]
        + [pltpu.SemaphoreType.DMA((6,)), pltpu.SemaphoreType.DMA((5,))],
        compiler_params=pltpu.CompilerParams(vmem_limit_bytes=62 * 2**20),
    )(stat, table, embed, table_row, rows, down, top_cols, cols, grads, *others)


def fast_shards(
    token_ids,
    seq_lengths,
    valid_mask,
    deal_order,
    log_scale,
    embed_master,
    attn_in,
    attn_out,
    ffn_in,
    ffn_out,
    head_master,
    norm_master,
    embed_rows,
    head_rows,
    layer_rows,
    ffn_out_rows,
    layer_cols,
    embed_head_cols,
    norm_state,
    scale_state,
):
    tokens = token_ids.shape[0]
    shard_rows = embed_master.shape[0]
    my_dp = lax.axis_index("dp")
    position = jnp.arange(tokens, dtype=jnp.int32)
    bounds = jnp.cumsum(seq_lengths[0])
    segment = jnp.sum((position[:, None] >= bounds[None, :]).astype(jnp.int32), axis=1)

    key, wanted, most = slot_plan(token_ids, shard_rows)
    asks = jnp.concatenate(
        [wanted.reshape(8, 1, SLOTS), jnp.broadcast_to(most, (8, 1, 128 - SLOTS))], axis=2
    ).astype(jnp.int32)
    packed = pack_weights(attn_in, attn_out, ffn_in, ffn_out, head_master, norm_master)
    seg_col, seg_row = segment.reshape(-1, 1), segment.reshape(1, -1)
    valid_row = valid_mask.reshape(1, -1)
    weights, asked, *saved, norms = run_gather_forward(
        packed, asks, embed_master, key.reshape(-1, 1), seg_col, seg_row, valid_row, 0
    )
    crowded = jnp.max(asked[:, :, 0, SLOTS:]) >= SLOTS

    def dense_forward(state):
        table = lax.all_gather(embed_master, "dp", axis=0, tiled=True)
        first = jnp.take(table, token_ids, axis=0).astype(jnp.bfloat16)
        return (False, *run_forward(first, seg_col, seg_row, valid_row, weights[:, 32:], norms))

    _, *saved, unit_parts, pooled_low, head_out = lax.while_loop(
        lambda state: state[0], dense_forward, (crowded, *saved)
    )
    loss_value, own_rows, grad_scale = run_contrast(unit_parts, deal_order, log_scale, 1)
    loss_value, grad_scale = loss_value[0, 0], grad_scale[0]
    shard_grads, table_rows, norm_sum, grad_first = run_backward(
        own_rows, head_out, pooled_low, seg_col, seg_row, valid_row, key.reshape(1, -1), weights, norms, saved, 2
    )
    table_slots = asked[:, :, 0, :SLOTS].reshape(1, -1)
    table_row = embed_rows.reshape(1, -1)
    row_state = jnp.pad(
        jnp.concatenate([layer_rows.reshape(6, -1), head_rows.reshape(1, -1)], axis=0), ((0, 1), (0, 0))
    ).T
    shared = (shard_grads, norm_sum, table_row, row_state, ffn_out_rows.T)

    def dense_stats():
        full = jnp.zeros((shard_rows * 8, D), jnp.float32).at[token_ids].add(
            grad_first.astype(jnp.float32)
        )
        full = lax.psum_scatter(full, "dp", scatter_dimension=0, tiled=True)
        return run_stats(True, (lax.psum(full, "group"),), *shared)

    def slot_stats():
        return run_stats(False, (table_slots, table_rows.reshape(-1, D)), *shared)

    table_grad, table_row_new, stats, rows_new, down_new = lax.cond(
        crowded, dense_stats, slot_stats
    )
    sums = total(stats, 3)
    totals = (VOCAB, D, D, D, D, FF)
    (
        new_embed, new_table_cols, new_head_cols, new_cols, rms_row, new_in, new_mix, new_gate, new_low, new_head,
    ) = run_update(
        totals, sums, table_grad, embed_master, table_row_new, shard_grads, rows_new, down_new,
        embed_head_cols, layer_cols, (attn_in, attn_out, ffn_in, ffn_out, head_master),
    )
    norm_grad = sums.reshape(-1, D)[NORM_ROW : NORM_ROW + 10].reshape(2 * LAYERS + 1, 2, D)
    shard_norm = lax.dynamic_slice_in_dim(norm_grad, my_dp * norm_state.shape[2], norm_state.shape[2], 2)
    norm_delta, norm_second = unfactored(shard_norm, norm_state)
    scale_delta, scale_state_new = unfactored(grad_scale, scale_state)
    state_new = rows_new.T
    return (
        loss_value,
        new_embed,
        new_in,
        new_mix,
        new_gate,
        new_low,
        new_head,
        norm_master + norm_delta,
        log_scale + scale_delta,
        table_row_new[0],
        state_new[6],
        state_new[:6].reshape(layer_rows.shape),
        down_new.T,
        new_cols,
        new_table_cols[0],
        new_head_cols[0],
        norm_second,
        scale_state_new,
        rms_row[0, :10],
    )


def solution(mesh):
    in_specs = (
        P(("dp", "group")),
        P(("dp", "group"), None),
        P(("dp", "group")),
        P(),
        P(),
        P("dp", None),
        P(None, "dp", None),
        P(None, "dp", None),
        P(None, "dp", None),
        P(None, "dp", None),
        P("dp", None),
        P(None, None, "dp"),
        P("dp"),
        P("dp"),
        P(None, None, "dp"),
        P(None, "dp"),
        P(),
        P(),
        P(None, None, "dp"),
        P(),
    )
    out_specs = (
        P(),
        P("dp", None),
        P(None, "dp", None),
        P(None, "dp", None),
        P(None, "dp", None),
        P(None, "dp", None),
        P("dp", None),
        P(None, None, "dp"),
        P(),
        P("dp"),
        P("dp"),
        P(None, None, "dp"),
        P(None, "dp"),
        P(),
        P(),
        P(),
        P(None, None, "dp"),
        P(),
        P(),
    )
    body = fast_shards if dict(mesh.shape) == {"dp": 8, "group": 4} else shards
    return jax.shard_map(body, mesh=mesh, in_specs=in_specs, out_specs=out_specs, check_vma=False)
```

```python
import functools

import jax
import jax.numpy as jnp
from jax import lax
from jax.experimental import pallas as pl
from jax.experimental.pallas import tpu as pltpu
from jax.sharding import PartitionSpec as P

D = 512
HEADS = 8
HEAD_DIM = 64
FF = 2048
VOCAB = 30528
LAYERS = 2


NORM_EPS = 1e-06
UNIT_EPS = 1e-06
STATE_EPS = 1e-30
DECAY_RATE = 0.5
CLIP_LEVEL = 0.05
RATE_SCALE = 10.0
NORM_RATE = 0.1


def layer_norm(values, gain_vec, shift_vec):
    center = values - jnp.mean(values, axis=-1, keepdims=True)
    spread = jnp.mean(center * center, axis=-1, keepdims=True)
    return center * lax.rsqrt(spread + NORM_EPS) * gain_vec + shift_vec


def geglu(joined):
    half_width = joined.shape[-1] // 2
    return jax.nn.gelu(joined[:, :half_width]) * joined[:, half_width:]


def alibi_slopes(head_count):
    return 2.0 ** (-8.0 * (jnp.arange(head_count).astype(jnp.float32) + 1.0) / head_count)


def normalize(vectors):
    return vectors * lax.rsqrt(jnp.sum(vectors * vectors, axis=-1, keepdims=True) + UNIT_EPS)


def contrast(unit_all, scale_arg, deal_order):
    pair_count = deal_order.shape[0] // 2
    queries = jnp.take(unit_all, deal_order[:pair_count], axis=0)
    documents = jnp.take(unit_all, deal_order[pair_count:], axis=0)
    logits = jnp.exp(scale_arg[0]) * jnp.matmul(
        queries, documents.T, precision=lax.Precision.HIGHEST
    )
    by_row = jax.nn.logsumexp(logits, axis=1)
    by_column = jax.nn.logsumexp(logits, axis=0)
    return jnp.sum(0.5 * (by_row + by_column) - jnp.diagonal(logits))


def unfactored(grad_full, state):
    state_new = DECAY_RATE * state + (1.0 - DECAY_RATE) * (grad_full * grad_full + STATE_EPS)
    return (-NORM_RATE * grad_full * lax.rsqrt(state_new), state_new)


def block_scores(query_rows, key_all, seg_rows, segment, head_count):
    row_count = query_rows.shape[0]
    raw_scores = jnp.einsum("thc,shc->hts", query_rows, key_all, preferred_element_type=jnp.float32)
    row_pos = jnp.arange(row_count, dtype=jnp.int32)
    col_pos = jnp.arange(key_all.shape[0], dtype=jnp.int32)
    distance = jnp.abs(row_pos[:, None] - col_pos[None, :]).astype(jnp.float32)
    scores = (
        raw_scores * HEAD_DIM ** (-0.5) + -alibi_slopes(head_count)[:, None, None] * distance[None]
    )
    same_seq = seg_rows[:, None] == segment[None, :]
    return jnp.where(same_seq[None], scores, -jnp.inf)


def split_qkv(qkv_low, head_count):
    tokens = qkv_low.shape[0]
    split_heads = qkv_low.reshape(tokens, 3, head_count, qkv_low.shape[1] // (3 * head_count))
    return (split_heads[:, 0], split_heads[:, 1], split_heads[:, 2])


def attend(qkv_low, segment, head_count):
    model_width = qkv_low.shape[1] // 3
    query_all, key_all, value_all = split_qkv(qkv_low, head_count)
    scores = block_scores(query_all, key_all, segment, segment, head_count)
    row_max = jnp.max(scores, axis=-1, keepdims=True)
    exponent = jnp.exp(scores - row_max)
    row_total = jnp.sum(exponent, axis=-1, keepdims=True)
    prob_low = (exponent / row_total).astype(jnp.bfloat16)
    mixed_list = jnp.einsum(
        "hts,shc->thc", prob_low, value_all, preferred_element_type=jnp.float32
    ).reshape(-1, model_width)
    lse_list = row_max[..., 0] + jnp.log(row_total[..., 0])
    return (mixed_list, lse_list)


def attend_back(qkv_low, segment, head_count, lse_all, grad_mixed):
    tokens = qkv_low.shape[0]
    query_all, key_all, value_all = split_qkv(qkv_low, head_count)
    grad_out = grad_mixed.reshape(tokens, head_count, -1)
    block_rows = min(tokens, 512)
    scores = block_scores(query_all, key_all, segment, segment, head_count)
    prob_full = jnp.exp(scores - lse_all[:, 0:block_rows, None])
    grad_value = jnp.einsum(
        "hts,thc->shc", prob_full.astype(jnp.bfloat16), grad_out, preferred_element_type=jnp.float32
    )
    grad_prob = jnp.einsum("thc,shc->hts", grad_out, value_all, preferred_element_type=jnp.float32)
    inner = jnp.sum(prob_full * grad_prob, axis=-1, keepdims=True)
    grad_raw = (prob_full * (grad_prob - inner) * HEAD_DIM ** (-0.5)).astype(jnp.bfloat16)
    query_list = jnp.einsum("hts,shc->thc", grad_raw, key_all, preferred_element_type=jnp.float32)
    grad_key = jnp.einsum("hts,thc->shc", grad_raw, query_all, preferred_element_type=jnp.float32)
    return (
        jnp.stack([query_list, grad_key, grad_value], axis=1)
        .reshape(tokens, -1)
        .astype(jnp.bfloat16)
    )


def shards(
    token_ids,
    seq_lengths,
    valid_mask,
    deal_order,
    log_scale,
    embed_master,
    attn_in,
    attn_out,
    ffn_in,
    ffn_out,
    head_master,
    norm_master,
    embed_rows,
    head_rows,
    layer_rows,
    ffn_out_rows,
    layer_cols,
    embed_head_cols,
    norm_state,
    scale_state,
):
    tokens = token_ids.shape[0]
    model_width = embed_master.shape[1]
    seq_count = seq_lengths.shape[1]
    head_count = HEADS
    position = jnp.arange(tokens, dtype=jnp.int32)
    bounds = jnp.cumsum(seq_lengths[0])
    segment = jnp.sum((position[:, None] >= bounds[None, :]).astype(jnp.int32), axis=1)
    piece_rows = lax.all_gather(embed_master.astype(jnp.bfloat16), "dp", axis=0, tiled=True)
    local_idx = token_ids
    inside = (local_idx >= 0) & (local_idx < piece_rows.shape[0])
    picked = jnp.take(piece_rows, jnp.clip(local_idx, 0, piece_rows.shape[0] - 1), axis=0).astype(
        jnp.float32
    )
    stream = jnp.where(inside[:, None], picked, 0.0)
    w_qkv, w_attn, w_gate_up, w_down, w_head, norm_low = (
        lax.all_gather(attn_in.astype(jnp.bfloat16), "dp", axis=1, tiled=True),
        lax.all_gather(attn_out.astype(jnp.bfloat16), "dp", axis=1, tiled=True),
        lax.all_gather(ffn_in.astype(jnp.bfloat16), "dp", axis=1, tiled=True),
        lax.all_gather(ffn_out.astype(jnp.bfloat16), "dp", axis=1, tiled=True),
        lax.all_gather(head_master.astype(jnp.bfloat16), "dp", axis=0, tiled=True),
        lax.all_gather(norm_master.astype(jnp.bfloat16), "dp", axis=2, tiled=True),
    )
    norms = norm_low.astype(jnp.float32)
    kept_list = []
    for layer_idx in range(LAYERS):
        stream_low = stream.astype(jnp.bfloat16)
        qkv_low = jnp.dot(stream_low, w_qkv[layer_idx], preferred_element_type=jnp.float32).astype(
            jnp.bfloat16
        )
        mixed_heads, lse_all = attend(qkv_low, segment, head_count)
        mixed_low = mixed_heads.astype(jnp.bfloat16)
        resid_one = stream + jnp.dot(
            mixed_low, w_attn[layer_idx], preferred_element_type=jnp.float32
        )
        normed = layer_norm(resid_one, norms[2 * layer_idx, 0], norms[2 * layer_idx, 1])
        normed_low = normed.astype(jnp.bfloat16)
        joined = jnp.dot(normed_low, w_gate_up[layer_idx], preferred_element_type=jnp.float32)
        hidden_low = geglu(joined).astype(jnp.bfloat16)
        resid_two = normed + jnp.dot(
            hidden_low, w_down[layer_idx], preferred_element_type=jnp.float32
        )
        kept_list.append(
            (
                stream_low,
                qkv_low,
                lse_all,
                mixed_low,
                resid_one,
                normed_low,
                joined,
                hidden_low,
                resid_two,
            )
        )
        stream = layer_norm(resid_two, norms[2 * layer_idx + 1, 0], norms[2 * layer_idx + 1, 1])
    final = layer_norm(stream, norms[2 * LAYERS, 0], norms[2 * LAYERS, 1])
    member = (
        (segment[None, :] == jnp.arange(seq_count, dtype=jnp.int32)[:, None])
        & (valid_mask[None, :] > 0)
    ).astype(jnp.float32)
    counts = jnp.maximum(jnp.sum(member, axis=1), 1.0)
    pooled = jnp.matmul(member, final, precision=lax.Precision.HIGHEST) / counts[:, None]
    pooled_low = pooled.astype(jnp.bfloat16)
    head_out = jnp.dot(pooled_low, w_head, preferred_element_type=jnp.float32)
    unit_vecs, unit_back = jax.vjp(normalize, head_out)
    unit_every = lax.all_gather(unit_vecs, ("dp", "group"), axis=0, tiled=True)
    loss_value, loss_back = jax.vjp(
        lambda unit_all, scale_arg: contrast(unit_all, scale_arg, deal_order), unit_every, log_scale
    )
    grad_units, grad_scale = loss_back(jnp.ones_like(loss_value))
    own_rows = lax.dynamic_slice_in_dim(
        grad_units, lax.axis_index(("dp", "group")) * seq_count, seq_count, 0
    )
    grad_head_out = unit_back(own_rows)[0].astype(jnp.bfloat16)
    grad_head = jnp.dot(pooled_low.T, grad_head_out, preferred_element_type=jnp.float32)
    grad_pooled = jnp.dot(grad_head_out, w_head.T, preferred_element_type=jnp.float32)
    grad_final = jnp.matmul(
        member.T, grad_pooled / counts[:, None], precision=lax.Precision.HIGHEST
    )
    final_back = jax.vjp(layer_norm, stream, norms[2 * LAYERS, 0], norms[2 * LAYERS, 1])[1]
    grad_stream, gain_last, shift_last = final_back(grad_final)
    norm_grads = [None] * (2 * LAYERS + 1)
    norm_grads[2 * LAYERS] = jnp.stack([gain_last, shift_last])
    qkv_grads = [None] * LAYERS
    attn_grads = [None] * LAYERS
    gate_grads = [None] * LAYERS
    down_grads = [None] * LAYERS
    for layer_idx in reversed(range(LAYERS)):
        (
            stream_low,
            qkv_low,
            lse_all,
            mixed_low,
            resid_one,
            normed_low,
            joined,
            hidden_low,
            resid_two,
        ) = kept_list[layer_idx]
        norm_two_back = jax.vjp(
            layer_norm, resid_two, norms[2 * layer_idx + 1, 0], norms[2 * layer_idx + 1, 1]
        )[1]
        grad_two, gain_two, shift_two = norm_two_back(grad_stream)
        norm_grads[2 * layer_idx + 1] = jnp.stack([gain_two, shift_two])
        grad_branch = grad_two.astype(jnp.bfloat16)
        down_grads[layer_idx] = jnp.dot(
            hidden_low.T, grad_branch, preferred_element_type=jnp.float32
        )
        grad_hidden = jnp.dot(grad_branch, w_down[layer_idx].T, preferred_element_type=jnp.float32)
        grad_joined = jax.vjp(geglu, joined)[1](grad_hidden)[0].astype(jnp.bfloat16)
        gate_grads[layer_idx] = jnp.dot(
            normed_low.T, grad_joined, preferred_element_type=jnp.float32
        )
        grad_normed = grad_two + jnp.dot(
            grad_joined, w_gate_up[layer_idx].T, preferred_element_type=jnp.float32
        )
        norm_one_back = jax.vjp(
            layer_norm, resid_one, norms[2 * layer_idx, 0], norms[2 * layer_idx, 1]
        )[1]
        grad_one, gain_one, shift_one = norm_one_back(grad_normed)
        norm_grads[2 * layer_idx] = jnp.stack([gain_one, shift_one])
        grad_attended = grad_one.astype(jnp.bfloat16)
        attn_grads[layer_idx] = jnp.dot(
            mixed_low.T, grad_attended, preferred_element_type=jnp.float32
        )
        grad_mixed = jnp.dot(
            grad_attended, w_attn[layer_idx].T, preferred_element_type=jnp.float32
        ).astype(jnp.bfloat16)
        grad_qkv_low = attend_back(qkv_low, segment, head_count, lse_all, grad_mixed)
        qkv_grads[layer_idx] = jnp.dot(
            stream_low.T, grad_qkv_low, preferred_element_type=jnp.float32
        )
        grad_stream = grad_one + jnp.dot(
            grad_qkv_low, w_qkv[layer_idx].T, preferred_element_type=jnp.float32
        )
    row_count = embed_master.shape[0] * lax.axis_size("dp")
    local_idx = token_ids
    inside = (local_idx >= 0) & (local_idx < row_count)
    slot_idx = jnp.where(inside, local_idx, row_count)
    embed_grad = lax.psum_scatter(
        jnp.zeros((row_count, model_width), jnp.float32).at[slot_idx].add(grad_stream, mode="drop"),
        "dp",
        scatter_dimension=0,
        tiled=True,
    )
    grad_qkv = jnp.stack(qkv_grads)
    grad_attn = jnp.stack(attn_grads)
    grad_gate_up = jnp.stack(gate_grads)
    grad_down = jnp.stack(down_grads)
    grad_norm = jnp.stack(norm_grads)
    owned = (
        lax.psum_scatter(grad_qkv, "dp", scatter_dimension=1, tiled=True),
        lax.psum_scatter(grad_attn, "dp", scatter_dimension=1, tiled=True),
        lax.psum_scatter(grad_gate_up, "dp", scatter_dimension=1, tiled=True),
        lax.psum_scatter(grad_down, "dp", scatter_dimension=1, tiled=True),
        lax.psum_scatter(grad_head, "dp", scatter_dimension=0, tiled=True),
        lax.psum_scatter(grad_norm, "dp", scatter_dimension=2, tiled=True),
    )
    shard_qkv, shard_attn, shard_gate_up, shard_down, shard_head, shard_norm, shard_embed = (
        lax.psum((owned[0], owned[1], owned[2], owned[3], owned[4], owned[5], embed_grad), "group")
    )
    grad_list = [
        shard_embed[None],
        shard_head[None],
        shard_qkv,
        shard_attn,
        shard_gate_up,
        shard_down,
    ]
    master_list = [embed_master[None], head_master[None], attn_in, attn_out, ffn_in, ffn_out]
    state_list = [
        embed_rows[None],
        head_rows[None],
        layer_rows[:, 0],
        layer_rows[:, 1],
        layer_rows[:, 2],
        ffn_out_rows,
    ]
    col_list = [
        embed_head_cols[0:1],
        embed_head_cols[1:2],
        layer_cols[:, : 3 * D],
        layer_cols[:, 3 * D : 4 * D],
        layer_cols[:, 4 * D : 4 * D + 2 * FF],
        layer_cols[:, 4 * D + 2 * FF :],
    ]
    total_rows = [VOCAB, D, D, D, D, FF]
    wide_rate = RATE_SCALE / D**0.5
    rates = [
        RATE_SCALE,
        wide_rate,
        wide_rate,
        RATE_SCALE / (D // 8) ** 0.5,
        wide_rate,
        RATE_SCALE / FF**0.5,
    ]
    square_list = [grad_part * grad_part for grad_part in grad_list]
    rows_new = [
        DECAY_RATE * state_list[entry_idx]
        + (1.0 - DECAY_RATE) * (jnp.mean(square_list[entry_idx], axis=-1) + STATE_EPS)
        for entry_idx in range(6)
    ]
    col_parts = jnp.concatenate(
        [jnp.sum(square_part, axis=1).reshape(-1) for square_part in square_list]
    )
    row_parts = jnp.concatenate([jnp.sum(row_part, axis=-1) for row_part in rows_new])
    col_sum, row_sum = lax.psum((col_parts, row_parts), "dp")
    row_means = []
    lead_start = 0
    for entry_idx in range(6):
        lead_count = grad_list[entry_idx].shape[0]
        row_means.append(row_sum[lead_start : lead_start + lead_count] / total_rows[entry_idx])
        lead_start = lead_start + lead_count
    cols_new = []
    steps_all = []
    col_start = 0
    for entry_idx in range(6):
        lead_count = grad_list[entry_idx].shape[0]
        col_width = grad_list[entry_idx].shape[2]
        col_full = col_sum[col_start : col_start + lead_count * col_width].reshape(
            lead_count, col_width
        )
        col_state_new = DECAY_RATE * col_list[entry_idx] + (1.0 - DECAY_RATE) * (
            col_full / total_rows[entry_idx] + STATE_EPS
        )
        cols_new.append(col_state_new)
        steps_all.append(
            grad_list[entry_idx]
            * lax.rsqrt(
                rows_new[entry_idx][:, :, None]
                * col_state_new[:, None, :]
                / row_means[entry_idx][:, None, None]
            )
        )
        col_start = col_start + lead_count * col_width
    step_squares = []
    step_parts = jnp.concatenate(
        [jnp.sum(step_dir * step_dir, axis=(1, 2)) for step_dir in steps_all]
    )
    step_sum = lax.psum(step_parts, "dp")
    lead_start = 0
    for entry_idx in range(6):
        lead_count = grad_list[entry_idx].shape[0]
        step_squares.append(step_sum[lead_start : lead_start + lead_count])
        lead_start = lead_start + lead_count
    new_weights = []
    rms_list = []
    for entry_idx in range(6):
        cell_count = total_rows[entry_idx] * grad_list[entry_idx].shape[2]
        step_rms = jnp.sqrt(step_squares[entry_idx] / cell_count)
        rms_list.append(step_rms)
        delta = (
            -rates[entry_idx]
            * steps_all[entry_idx]
            / jnp.maximum(1.0, step_rms / CLIP_LEVEL)[:, None, None]
        )
        new_weights.append(master_list[entry_idx] + delta)
    norm_delta, norm_second = unfactored(shard_norm, norm_state)
    scale_delta, scale_state_new = unfactored(grad_scale, scale_state)
    return (
        loss_value,
        new_weights[0][0],
        new_weights[2],
        new_weights[3],
        new_weights[4],
        new_weights[5],
        new_weights[1][0],
        norm_master + norm_delta,
        log_scale + scale_delta,
        rows_new[0][0],
        rows_new[1][0],
        jnp.stack([rows_new[2], rows_new[3], rows_new[4]], axis=1),
        rows_new[5],
        jnp.concatenate([cols_new[2], cols_new[3], cols_new[4], cols_new[5]], axis=1),
        cols_new[0][0],
        cols_new[1][0],
        norm_second,
        scale_state_new,
        jnp.concatenate(rms_list),
    )


SLOTS = 80
PART = 1024


MESH = pl.DeviceIdType.MESH
BF=jnp.bfloat16

def place():
    dp = lax.axis_index("dp"); g = lax.axis_index("group")
    return dp // 2, dp % 2, g // 2, g % 2

def dev(z, x, y, c):
    return (z * 2 + x, y * 2 + c)

def entry_barrier(peers):
    bar = pltpu.get_barrier_semaphore()
    for p in peers:
        pl.semaphore_signal(bar, inc=1, device_id=p, device_id_type=MESH)
    pl.semaphore_wait(bar, len(peers))

def mult(v, m=16):
    return pl.multiple_of(v, m)


def slot_plan(token_ids, shard_rows):
    tokens = token_ids.shape[0]
    owner = token_ids // shard_rows
    local = token_ids - owner * shard_rows
    index = jnp.arange(tokens, dtype=jnp.int32)
    same_id = token_ids[:, None] == token_ids[None, :]
    first = jnp.min(jnp.where(same_id, index[None, :], tokens), axis=1)
    leads = first == index
    same_owner = owner[:, None] == owner[None, :]
    slot = jnp.sum(
        (same_owner & leads[None, :] & (index[None, :] < first[:, None])).astype(jnp.int32), axis=1
    )
    key = jnp.where(slot < SLOTS, owner * SLOTS + slot, 8 * SLOTS)
    wanted = jnp.max(
        jnp.where(
            key[:, None] == jnp.arange(8 * SLOTS, dtype=jnp.int32)[None, :], local[:, None], -1
        ),
        axis=0,
    )
    return key, wanted, jnp.max(slot)


def column_blocks(rows):
    lead, count, width = rows.shape
    return (
        rows.reshape(lead, count, width // D, D).transpose(0, 2, 1, 3).reshape(lead, -1, D)
    )


def pack_weights(attn_in, attn_out, ffn_in, ffn_out, head_master, norm_master):
    layers = jnp.concatenate(
        [column_blocks(attn_in), attn_out, column_blocks(ffn_in), ffn_out], axis=1
    ).astype(jnp.bfloat16)
    norm_rows = jnp.pad(
        norm_master.reshape(10, -1).astype(jnp.bfloat16), ((0, 22), (0, D - norm_master.shape[2]))
    )
    return jnp.concatenate(
        [norm_rows, layers.reshape(-1, D), head_master.astype(jnp.bfloat16)], axis=0
    )


def dot_nn(left, right):
    return lax.dot_general(left, right, (((1,), (0,)), ((), ())), preferred_element_type=jnp.float32)


def dot_nt(left, right):
    return lax.dot_general(left, right, (((1,), (1,)), ((), ())), preferred_element_type=jnp.float32)


def dot_tn(left, right):
    return lax.dot_general(left, right, (((0,), (0,)), ((), ())), preferred_element_type=jnp.float32)


def exact_dot(left, right, dims=((1,), (0,))):
    return lax.dot_general(
        left, right, (dims, ((), ())), precision=lax.Precision.HIGHEST, preferred_element_type=jnp.float32
    )


def step_id(kind, first=0, second=0, third=0):
    return ord(kind) * 1000 + first * 100 + second * 10 + third


GELU_SCALE = (2.0 / 3.141592653589793) ** 0.5
GELU_CUBE = 0.044715
TILE = 256


def norm_parts(values):
    center = values - jnp.mean(values, axis=-1, keepdims=True)
    inverse = lax.rsqrt(jnp.mean(center * center, axis=-1, keepdims=True) + NORM_EPS)
    return center * inverse, inverse


def norm_back(scaled, inverse, grad_out, gain):
    grad_scaled = grad_out * gain
    mean_grad = jnp.mean(grad_scaled, axis=-1, keepdims=True)
    mean_both = jnp.mean(grad_scaled * scaled, axis=-1, keepdims=True)
    return inverse * (grad_scaled - mean_grad - scaled * mean_both)


def gelu_parts(value):
    bend = jnp.tanh(GELU_SCALE * (value + GELU_CUBE * value * value * value))
    half = 0.5 * (1.0 + bend)
    slope = half + 0.5 * value * (1.0 - bend * bend) * GELU_SCALE * (1.0 + 3.0 * GELU_CUBE * value * value)
    return value * half, slope


def block(w_ref, start):
    return w_ref[:, start : start + 64, :].reshape(D, D)


def down_block(w_ref, j):
    return w_ref[2 * j : 2 * j + 2, 768:1024, :].reshape(D, D)


def fill_distance(far, seg_col_ref, seg_row_ref):
    tokens = far.shape[0]
    def body(i, carry):
        start = pl.multiple_of(i * 64, 64)
        rows = lax.broadcasted_iota(jnp.int32, (64, tokens), 0) + start
        cols = lax.broadcasted_iota(jnp.int32, (64, tokens), 1)
        gap = jnp.abs(rows - cols).astype(jnp.float32)
        same = seg_col_ref[pl.ds(start, 64), :] == seg_row_ref[...]
        far[pl.ds(start, 64), :] = jnp.where(same, gap, jnp.inf)
        return carry
    lax.fori_loop(0, tokens // 64, body, 0)


def forward_kernel(
    first_ref, seg_col_ref, seg_row_ref, valid_ref, w_ref, head_ref, norm_ref,
    low_ref, qkv_ref, lse_ref, mix_ref, one_ref, two_ref, unit_ref, pool_ref, zed_ref,
    x_s, far, acc,
):
    layer = pl.program_id(0)
    tokens = x_s.shape[0]
    tiles = tokens // TILE

    @pl.when(layer == 0)
    def _():
        x_s[...] = first_ref[...].astype(jnp.float32)
        fill_distance(far, seg_col_ref, seg_row_ref)

    def project(i, carry):
        rows = pl.ds(pl.multiple_of(i * TILE, TILE), TILE)
        low = x_s[rows, :].astype(jnp.bfloat16)
        low_ref[0, rows, :] = low
        for j in range(3):
            qkv_ref[0, rows, j * D : (j + 1) * D] = dot_nn(low, block(w_ref, j * 64)).astype(jnp.bfloat16)
        return carry

    lax.fori_loop(0, tiles, project, 0)
    for head in range(HEADS):
        lanes = slice(head * HEAD_DIM, (head + 1) * HEAD_DIM)
        keys = qkv_ref[0, :, D + head * HEAD_DIM : D + (head + 1) * HEAD_DIM]
        vals_t = qkv_ref[0, :, 2 * D + head * HEAD_DIM : 2 * D + (head + 1) * HEAD_DIM].T
        slope = 2.0 ** (-8.0 * (head + 1) / HEADS)
        for i in range(tiles):
            cols = slice(i * TILE, (i + 1) * TILE)
            scores = dot_nt(keys, qkv_ref[0, cols, lanes]) * HEAD_DIM**-0.5 - slope * far[:, cols]
            top = jnp.max(scores, axis=0, keepdims=True)
            raised = jnp.exp(scores - top)
            total = jnp.sum(raised, axis=0, keepdims=True)
            lse_ref[0, head, :, cols] = top + jnp.log(total)
            prob = (raised * (1.0 / total)).astype(jnp.bfloat16)
            mix_ref[0, lanes, cols] = dot_nn(vals_t, prob).astype(jnp.bfloat16)

    acc[...] = dot_tn(mix_ref[0], block(w_ref, 192))

    def feed(i, carry):
        rows = pl.ds(pl.multiple_of(i * TILE, TILE), TILE)
        resid = x_s[rows, :] + acc[rows, :]
        one_ref[0, rows, :] = resid
        at = 4 * layer
        scaled, _ = norm_parts(resid)
        hidden = scaled * norm_ref[pl.ds(at, 1), :] + norm_ref[pl.ds(at + 1, 1), :]
        low = hidden.astype(jnp.bfloat16)
        total = hidden
        for j in range(4):
            gate = dot_nn(low, block(w_ref, 256 + j * 64))
            up = dot_nn(low, block(w_ref, 512 + j * 64))
            bend = jnp.tanh(GELU_SCALE * (gate + GELU_CUBE * gate * gate * gate))
            mid = (0.5 * gate * (1.0 + bend) * up).astype(jnp.bfloat16)
            total = total + dot_nn(mid, down_block(w_ref, j))
        two_ref[0, rows, :] = total
        scaled, _ = norm_parts(total)
        x_s[rows, :] = scaled * norm_ref[pl.ds(at + 2, 1), :] + norm_ref[pl.ds(at + 3, 1), :]
        return carry

    lax.fori_loop(0, tiles, feed, 0)

    @pl.when(layer == LAYERS - 1)
    def _():
        pool_units(x_s, norm_ref, seg_row_ref, valid_ref, head_ref, unit_ref, pool_ref, zed_ref)


def members(seg_row_ref, valid_ref):
    tokens = seg_row_ref.shape[1]
    slot = lax.broadcasted_iota(jnp.int32, (8, tokens), 0)
    return jnp.where((seg_row_ref[...] == slot) & (valid_ref[...] > 0), 1.0, 0.0)


def whole(shape):
    return pl.BlockSpec(shape, lambda i: (0,) * len(shape))


def run_forward(first, seg_col, seg_row, valid, weights, norms):
    tokens = first.shape[0]
    low = jnp.bfloat16
    layered = lambda *s: pl.BlockSpec((1,) + s, lambda i: (i,) + (0,) * len(s))
    return pl.pallas_call(
        forward_kernel,
        grid=(LAYERS,),
        in_specs=[
            whole((tokens, D)), whole((tokens, 1)), whole((1, tokens)), whole((1, tokens)),
            pl.BlockSpec((8, PART, D), lambda i: (0, i, 0)),
            pl.BlockSpec((8, 64, D), lambda i: (0, 2 * PART // 64, 0)),
            whole(norms.shape),
        ],
        out_specs=[
            layered(tokens, D), layered(tokens, 3 * D), layered(HEADS, 1, tokens), layered(D, tokens),
            layered(tokens, D), layered(tokens, D), whole((16, 128)), whole((8, D)), whole((8, D)),
        ],
        out_shape=[
            jax.ShapeDtypeStruct((LAYERS, tokens, D), low),
            jax.ShapeDtypeStruct((LAYERS, tokens, 3 * D), low),
            jax.ShapeDtypeStruct((LAYERS, HEADS, 1, tokens), jnp.float32),
            jax.ShapeDtypeStruct((LAYERS, D, tokens), low),
            jax.ShapeDtypeStruct((LAYERS, tokens, D), jnp.float32),
            jax.ShapeDtypeStruct((LAYERS, tokens, D), jnp.float32),
            jax.ShapeDtypeStruct((16, 128), jnp.float32),
            jax.ShapeDtypeStruct((8, D), low),
            jax.ShapeDtypeStruct((8, D), jnp.float32),
        ],
        scratch_shapes=[
            pltpu.VMEM((tokens, D), jnp.float32), pltpu.VMEM((tokens, tokens), jnp.float32),
            pltpu.VMEM((tokens, D), jnp.float32),
        ],
        compiler_params=pltpu.CompilerParams(vmem_limit_bytes=60 * 2**20),
    )(first, seg_col, seg_row, valid, weights, weights, norms)


PACK_LAYER = (32, 32 + PART)
PACK_HEAD = 32 + 2 * PART
PARCELS = (
    (0, 144, 64), (288, 128, 48), (544, 128, 48), (800, 128, 48),
    (1056, 128, 48), (1312, 128, 48), (1568, 128, 48), (1824, 160, 32),
)
GATHER_ORDER = (
    113000, 115000, 115100, 115200, 115300, 116000, 110000, 122000, 122100, 120030, 122200, 120130, 120230, 114000,
    120330, 121000, 122300, 121100, 121031, 121131, 122010, 122110, 121200, 122210, 121231, 121300, 122310, 121331,
    121010, 120000, 121210, 121110, 120100, 122020, 115400, 120200, 121001, 121310, 120010, 122120, 115500, 120110,
    121101, 121020, 120300, 122220, 115600, 122400, 121011, 120210, 121201, 122320, 115700, 120310, 121301, 121111,
    122500, 121120, 121400, 121220, 120020, 121211, 120430, 122410, 121311, 121320, 122600, 120120, 121500, 122420,
    122510, 120530, 122700, 121021, 121431, 122520, 121410, 120400, 122610, 120220, 121600, 120630, 97000, 121121,
    122620, 121420, 121510, 119000, 121531, 122710, 120500, 120320, 121700, 112000, 120730, 121401, 97100, 121520,
    121221, 122720, 104000, 121610, 121631, 104010, 120600, 120410, 120420, 104020, 120510, 97200, 121620, 104030,
    121321, 121501, 121710, 120700, 104040, 121731, 120520, 104050, 120610, 121720, 97300, 104060, 121601, 121411,
    104070, 121421, 109000, 121511, 120620, 121701, 120710, 102000, 121521, 121611, 97400, 120720, 102010, 121621,
    97500, 121711, 112100, 104100, 121721, 97600, 104110, 104120, 104130, 104140, 97700, 104150, 104160, 104170,
    109100, 102100, 102110, 118000,
)


def nearest(z):
    return (z + 1 - 2 * (z % 2), 2 - z // 2, 3 - 3 * (z // 2), z)


def gather_stages(w_ref, ag_ref, zs, zr, xs, xr, ys, yr, cs, cr):
    z, x, y, c = place()
    me = z * 2 + x
    inner = (z == 1) | (z == 2)
    pair = dev(z + 1 - 2 * (z % 2), x, y, c)
    across = dev(3 - z, x, y, c)
    outward = dev((3 * z + 1) % 4, x, y, c)
    xp, yp, cp = dev(z, 1 - x, y, c), dev(z, x, 1 - y, c), dev(z, x, y, 1 - c)
    near = nearest(z)

    def rc(src, dst, s, r, d):
        return pltpu.make_async_remote_copy(src, dst, s, r, device_id=d, device_id_type=MESH)

    def shard(n, f):
        return near[n] * 2 + (x if f == 0 else 1 - x)

    steps = {}
    always, within = [], []
    others = [(0, 0), (1, 0), (2, 0), (3, 1), (0, 1), (1, 1), (2, 1)]

    def parcel(q, base, half, spare):
        main = pl.ds(mult(base + c * half + y * spare), half - spare)
        extra = pl.ds(mult(base + c * half + y * (half - spare)), spare)
        every = pl.ds(mult(base + c * half), half)

        def at(n, f, rows):
            return ag_ref.at[shard(n, f), rows]

        own = w_ref.at[main]
        to_pair = rc(own, at(3, 0, main), zs.at[q, 0], zr.at[q, 0], pair)
        to_across = rc(own, at(3, 0, main), zs.at[q, 1], zr.at[q, 1], across)
        on = [
            rc(at(0, 0, main), at(0, 0, main), zs.at[q, 2], zr.at[q, 2], across),
            rc(at(1, 0, main), at(1, 0, main), zs.at[q, 3], zr.at[q, 1], outward),
            rc(at(2, 0, main), at(2, 0, main), zs.at[q, 4], zr.at[q, 2], outward),
        ]
        over = [rc(own if n == 3 else at(n, 0, main), at(n, 0, main), xs.at[q, n], xr.at[q, n], xp) for n in range(4)]
        planes, cores = {}, {}
        for n, f in others:
            planes[n, f] = rc(at(n, f, extra), at(n, f, extra), ys.at[q, 2 * n + f], yr.at[q, 2 * n + f], yp)
            cores[n, f] = rc(at(n, f, every), at(n, f, every), cs.at[q, 2 * n + f], cr.at[q, 2 * n + f], cp)
        always.extend([to_pair] + over + list(planes.values()) + list(cores.values()))
        within.extend([to_across] + on)
        landed = [rc(own, at(n, 0, main), zs.at[q, 0], zr.at[q, n], pair) for n in range(3)]

        def issue():
            pl.when(inner)(to_across.start)
            to_pair.start()
            over[3].start()

        def along(n):
            landed[n].wait_recv()
            pl.when(inner)(on[n].start)
            over[n].start()
            planes[n, 0].start()

        def sideways(n):
            over[n].wait_recv()
            planes[n, 1].start()

        def plane(n, f):
            planes[n, f].wait_recv()
            cores[n, f].start()

        def arrived():
            for copy in cores.values():
                copy.wait_recv()

        steps[step_id("s", q)] = (issue,)
        for n in range(3):
            steps[step_id("z", q, n)] = (along, n)
        for n in range(4):
            steps[step_id("x", q, n)] = (sideways, n)
        for n, f in others:
            steps[step_id("y", q, n, f)] = (plane, n, f)
        steps[step_id("a", q)] = (arrived,)

    for q, spec in enumerate(PARCELS):
        parcel(q, *spec)

    def finish():
        for copy in always:
            copy.wait_send()

        @pl.when(inner)
        def _():
            for copy in within:
                copy.wait_send()

    return steps, finish


def request_stages(ask_ref, asks_ref, table_ref, table, picked, rows_s, got, sems, es, er, qs, qr):
    z, x, y, c = place()
    me = z * 2 + x
    g = y * 2 + c
    g2 = (1 - y) * 2 + c
    ep = [(lax.rem(me + k, 8), g) for k in range(8)]
    yp, cp = dev(z, x, 1 - y, c), dev(z, x, y, 1 - c)

    def rc(src, dst, s, r, d):
        return pltpu.make_async_remote_copy(src, dst, s, r, device_id=d, device_id_type=MESH)

    count = rows_s.shape[1]
    to_owner = [rc(ask_ref.at[ep[k][0]], asks_ref.at[g, me], qs.at[k], qr.at[k], ep[k]) for k in range(1, 8)]
    mine = pltpu.make_async_copy(ask_ref.at[me], asks_ref.at[g, me], sems.at[0])
    near = pltpu.make_async_copy(table_ref, table.at[pl.ds(0, table_ref.shape[0])], sems.at[1])
    to_plane = rc(asks_ref.at[g], asks_ref.at[g], qs.at[8], qr.at[8], yp)
    to_core = rc(asks_ref.at[g], asks_ref.at[g], qs.at[9], qr.at[9], cp)
    on_core = rc(asks_ref.at[g2], asks_ref.at[g2], qs.at[10], qr.at[10], cp)
    kept = pltpu.make_async_copy(rows_s.at[me], got.at[me], sems.at[2])
    answers = [rc(rows_s.at[ep[k][0]], got.at[me], es.at[k], er.at[k], ep[k]) for k in range(1, 8)]

    def load():
        near.start()

    def ask():
        for copy in to_owner:
            copy.start()
        mine.start()

    def answer():
        mine.wait()
        for copy in to_owner:
            copy.wait_recv()
        to_plane.start()
        to_core.start()
        wanted = asks_ref[pl.ds(g, 1)].reshape(8, 128).astype(jnp.float32).T
        near.wait()
        depth = table.shape[0] // 5
        rest = table.shape[0] - table_ref.shape[0]
        table[pl.ds(table_ref.shape[0], rest), :] = jnp.zeros((rest, D), jnp.float32)
        picked[...] = jnp.zeros(picked.shape, jnp.float32)
        ramp = lax.broadcasted_iota(jnp.int32, (count, depth), 1).astype(jnp.float32)

        def body(i, carry):
            low = table[pl.ds(pl.multiple_of(i * depth, depth), depth), :].astype(BF)
            shifted = ramp + (i * depth).astype(jnp.float32)
            for r in range(8):
                hot = jnp.where(wanted[:count, r : r + 1] == shifted, 1.0, 0.0).astype(BF)
                picked[r] += dot_nn(hot, low)
            return carry

        lax.fori_loop(0, 5, body, 0)
        rows_s[...] = picked[...].astype(BF)
        kept.start()
        for copy in answers:
            copy.start()

    def relay():
        to_plane.wait_recv()
        on_core.start()

    def take():
        kept.wait()
        for copy in answers:
            copy.wait_recv()

    def finish():
        to_core.wait_recv()
        on_core.wait_recv()
        for copy in answers + to_owner + [to_plane, to_core, on_core]:
            copy.wait_send()

    return load, ask, answer, relay, take, finish


def gather_forward_kernel(
    w_ref, ask_ref, table_ref, key_ref, seg_col_ref, seg_row_ref, valid_ref,
    ag_ref, asks_ref, low_out, qkv_out, lse_out, mix_out, one_out, two_out, unit_ref, pool_ref, zed_ref, norm_ref,
    table, picked, rows_s, got, weights, head, norm_low, low_s, qkv_s, lse_s, mix_s, one_s, two_s, x_s, far, acc,
    zs, zr, xs, xr, ys, yr, cs, cr, sems, es, er, qs, qr, loads, saves,
):
    z, x, y, c = place()
    me = z * 2 + x
    g = y * 2 + c
    tokens = x_s.shape[0]
    tiles = tokens // TILE
    peers = [(lax.rem(me + k, 8), g) for k in range(1, 8)] + [dev(z, x, 1 - y, c), dev(z, x, y, 1 - c)]
    barrier = pltpu.get_barrier_semaphore()
    for peer in peers:
        pl.semaphore_signal(barrier, inc=1, device_id=peer, device_id_type=MESH)
    steps, finish = gather_stages(w_ref, ag_ref, zs, zr, xs, xr, ys, yr, cs, cr)
    load, ask, answer, relay, take, ask_finish = request_stages(
        ask_ref, asks_ref, table_ref, table, picked, rows_s, got, sems, es, er, qs, qr
    )
    own = pltpu.make_async_copy(w_ref, ag_ref.at[me], sems.at[3])

    def loading(slot, rows, count, into):
        return pltpu.make_async_copy(ag_ref.at[:, pl.ds(rows, count)], into, loads.at[slot])

    fetch = {("norm", 0): loading(8, 0, 32, norm_low), ("head", 0): loading(9, PACK_HEAD, 64, head)}
    for layer in range(LAYERS):
        for part in range(4):
            fetch[layer, part] = loading(
                4 * layer + part, PACK_LAYER[layer] + 256 * part, 256, weights.at[layer, :, pl.ds(256 * part, 256)]
            )
    saving = {}
    for layer in range(LAYERS):
        for i, (source, target) in enumerate(
            ((low_s, low_out), (qkv_s, qkv_out), (lse_s, lse_out), (mix_s, mix_out), (one_s, one_out), (two_s, two_out))
        ):
            saving[layer, i] = pltpu.make_async_copy(source.at[layer], target.at[layer], saves.at[layer, i])

    def begin():
        load()
        own.start()

    def arrive(q):
        arrived[q]()
        if q == 0:
            own.wait()
            fetch["norm", 0].start()
        fetch[q // 4, q % 4].start()
        if q == 7:
            fetch["head", 0].start()

    def set_up():
        fill_distance(far, seg_col_ref, seg_row_ref)

    def first_rows():
        take()
        slots = lax.broadcasted_iota(jnp.int32, (tokens, got.shape[0] * got.shape[1]), 1)
        picks = jnp.where(slots == key_ref[...], 1.0, 0.0).astype(BF)
        x_s[...] = dot_nn(picks, got[...].reshape(-1, D))
        fetch["norm", 0].wait()
        norm_ref[...] = jnp.concatenate([norm_low[d, 0:16, 0:64].astype(jnp.float32) for d in range(8)], axis=1)

    def project(layer):
        fetch[layer, 0].wait()

        def body(i, carry):
            rows = pl.ds(pl.multiple_of(i * TILE, TILE), TILE)
            low = x_s[rows, :].astype(BF)
            low_s[layer, rows, :] = low
            for j in range(3):
                qkv_s[layer, rows, j * D : (j + 1) * D] = dot_nn(low, block(weights.at[layer], j * 64)).astype(BF)
            return carry

        lax.fori_loop(0, tiles, body, 0)
        saving[layer, 0].start()
        saving[layer, 1].start()

    def attend_head(layer, head):
        lanes = slice(head * HEAD_DIM, (head + 1) * HEAD_DIM)
        keys = qkv_s[layer, :, D + head * HEAD_DIM : D + (head + 1) * HEAD_DIM]
        vals_t = qkv_s[layer, :, 2 * D + head * HEAD_DIM : 2 * D + (head + 1) * HEAD_DIM].T
        slope = 2.0 ** (-8.0 * (head + 1) / HEADS)
        for i in range(tiles):
            cols = slice(i * TILE, (i + 1) * TILE)
            scores = dot_nt(keys, qkv_s[layer, cols, lanes]) * HEAD_DIM**-0.5 - slope * far[:, cols]
            top = jnp.max(scores, axis=0, keepdims=True)
            raised = jnp.exp(scores - top)
            total = jnp.sum(raised, axis=0, keepdims=True)
            lse_s[layer, head, :, cols] = top + jnp.log(total)
            prob = (raised * (1.0 / total)).astype(BF)
            mix_s[layer, lanes, cols] = dot_nn(vals_t, prob).astype(BF)

    def mix(layer):
        saving[layer, 2].start()
        saving[layer, 3].start()
        acc[...] = dot_tn(mix_s[layer], block(weights.at[layer], 192))

    def feed(layer, i):
        if i == 0:
            for part in (1, 2, 3):
                fetch[layer, part].wait()
        rows = pl.ds(i * TILE, TILE)
        resid = x_s[rows, :] + acc[rows, :]
        one_s[layer, rows, :] = resid
        at = 4 * layer
        scaled, _ = norm_parts(resid)
        hidden = scaled * norm_ref[at : at + 1, :] + norm_ref[at + 1 : at + 2, :]
        low = hidden.astype(BF)
        total = hidden
        for j in range(4):
            gate = dot_nn(low, block(weights.at[layer], 256 + j * 64))
            up = dot_nn(low, block(weights.at[layer], 512 + j * 64))
            bend = jnp.tanh(GELU_SCALE * (gate + GELU_CUBE * gate * gate * gate))
            mid = (0.5 * gate * (1.0 + bend) * up).astype(BF)
            total = total + dot_nn(mid, down_block(weights.at[layer], j))
        two_s[layer, rows, :] = total
        scaled, _ = norm_parts(total)
        x_s[rows, :] = scaled * norm_ref[at + 2 : at + 3, :] + norm_ref[at + 3 : at + 4, :]
        if i == tiles - 1:
            saving[layer, 4].start()
            saving[layer, 5].start()

    def end():
        fetch["head", 0].wait()
        pool_units(x_s, norm_ref, seg_row_ref, valid_ref, head, unit_ref, pool_ref, zed_ref)

    arrived = [steps[step_id("a", q)][0] for q in range(8)]
    for q in range(8):
        steps[step_id("a", q)] = (arrive, q)
    steps[step_id("q")], steps[step_id("n")], steps[step_id("r")] = (ask,), (answer,), (relay,)
    steps[step_id("t")], steps[step_id("w")], steps[step_id("v")] = (set_up,), (first_rows,), (end,)
    for layer in range(LAYERS):
        steps[step_id("p", layer)], steps[step_id("m", layer)] = (project, layer), (mix, layer)
        for head_index in range(HEADS):
            steps[step_id("h", layer, head_index)] = (attend_head, layer, head_index)
        for i in range(tiles):
            steps[step_id("f", layer, i)] = (feed, layer, i)
    begin()
    pl.semaphore_wait(barrier, len(peers))
    for name in GATHER_ORDER:
        fn, *rest = steps.pop(name)
        fn(*rest)
    assert not steps
    finish()
    ask_finish()
    for copy in saving.values():
        copy.wait()


def pool_units(x_s, norm_ref, seg_row_ref, valid_ref, head, unit_ref, pool_ref, zed_ref):
    scaled, _ = norm_parts(x_s[...])
    final = scaled * norm_ref[8:9, :] + norm_ref[9:10, :]
    member = members(seg_row_ref, valid_ref)
    counts = jnp.maximum(jnp.sum(member, axis=1, keepdims=True), 1.0)
    pooled = (exact_dot(member, final) / counts).astype(BF)
    pool_ref[...] = pooled
    zed = dot_nn(pooled, head[...].reshape(D, D))
    zed_ref[...] = zed
    unit = zed * lax.rsqrt(jnp.sum(zed * zed, axis=-1, keepdims=True) + UNIT_EPS)
    for s in range(4):
        for part in range(4):
            unit_ref[4 * s + part : 4 * s + part + 1, :] = unit[s : s + 1, part * 128 : (part + 1) * 128]


def run_gather_forward(packed, asks, embed, key_col, seg_col, seg_row, valid, cid):
    tokens = key_col.shape[0]
    low, full = jnp.bfloat16, jnp.float32
    near = pl.BlockSpec(memory_space=pltpu.VMEM)
    anywhere = pl.BlockSpec(memory_space=pl.ANY)
    shape = jax.ShapeDtypeStruct
    vmem = lambda dims, kind=low: pltpu.VMEM(dims, kind)
    sems = lambda *dims: pltpu.SemaphoreType.DMA(dims)
    padded = -(-embed.shape[0] // 640) * 640
    saved = [
        ((LAYERS, tokens, D), low), ((LAYERS, tokens, 3 * D), low), ((LAYERS, HEADS, 1, tokens), full),
        ((LAYERS, D, tokens), low), ((LAYERS, tokens, D), full), ((LAYERS, tokens, D), full),
    ]
    return pl.pallas_call(
        gather_forward_kernel,
        in_specs=[anywhere, near, anywhere, near, near, near, near],
        out_specs=[anywhere, near] + [anywhere] * 6 + [near] * 4,
        out_shape=[shape((8,) + packed.shape, low), shape((4,) + asks.shape, asks.dtype)]
        + [shape(*v) for v in saved]
        + [shape((16, 128), full), shape((8, D), low), shape((8, D), full), shape((16, D), full)],
        scratch_shapes=[
            vmem((padded, D), full), vmem((8, SLOTS, D), full), vmem((8, SLOTS, D)), vmem((8, SLOTS, D)),
            vmem((LAYERS, 8, PART, D)), vmem((8, 64, D)), vmem((8, 32, D)),
        ]
        + [vmem(*v) for v in saved]
        + [
            vmem((tokens, D), full), vmem((tokens, tokens), full), vmem((tokens, D), full),
            sems(8, 5), sems(8, 3), sems(8, 4), sems(8, 4), sems(8, 8), sems(8, 8), sems(8, 8), sems(8, 8),
            sems(4), sems(8), sems(8), sems(11), sems(11), sems(10), sems(2, 6),
        ],
        compiler_params=pltpu.CompilerParams(collective_id=cid, has_side_effects=True, vmem_limit_bytes=62 * 2**20),
    )(packed, asks, embed, key_col, seg_col, seg_row, valid)


def contrast_kernel(unit_ref, deal_col_ref, deal_row_ref, scale_ref, loss_ref, own_ref, slope_ref, every, ss, rs, ls):
    lin = lax.axis_index("dp") * 4 + lax.axis_index("group")
    peers = [lax.rem(lin + k, 32) for k in range(32)]
    peers = [(p // 4, p % 4) for p in peers]
    entry_barrier(peers[1:])
    copies = [
        pltpu.make_async_remote_copy(
            unit_ref, every.at[lin], ss.at[k], rs.at[k], device_id=peers[k], device_id_type=MESH
        )
        for k in range(1, 32)
    ]
    for copy in copies:
        copy.start()
    own = pltpu.make_async_copy(unit_ref, every.at[lin], ls)
    own.start()
    for copy in copies:
        copy.wait()
    own.wait()
    units = every[...].reshape(512, 128)
    place_at = lax.broadcasted_iota(jnp.int32, (128, 512), 1)
    sorted_units = jnp.concatenate(
        [
            exact_dot(jnp.where(deal_col_ref[...] * 4 + part == place_at, 1.0, 0.0), units)
            for part in range(4)
        ],
        axis=1,
    )
    queries, documents = sorted_units[:64], sorted_units[64:]
    scale = jnp.exp(scale_ref[...])
    logits = scale * exact_dot(queries, documents, ((1,), (1,)))
    row_top = jnp.max(logits, axis=1, keepdims=True)
    row_lse = row_top + jnp.log(jnp.sum(jnp.exp(logits - row_top), axis=1, keepdims=True))
    col_top = jnp.max(logits, axis=0, keepdims=True)
    col_lse = col_top + jnp.log(jnp.sum(jnp.exp(logits - col_top), axis=0, keepdims=True))
    diagonal = jnp.where(
        lax.broadcasted_iota(jnp.int32, (64, 64), 0) == lax.broadcasted_iota(jnp.int32, (64, 64), 1), 1.0, 0.0
    )
    on_diagonal = jnp.sum(logits * diagonal, axis=1, keepdims=True)
    col_sum = jnp.sum(col_lse, axis=1, keepdims=True)
    row_sum = jnp.sum(row_lse, axis=0, keepdims=True)
    loss_ref[...] = 0.5 * (row_sum + col_sum) - jnp.sum(on_diagonal, axis=0, keepdims=True)
    grad_logits = 0.5 * (jnp.exp(logits - row_lse) + jnp.exp(logits - col_lse)) - diagonal
    slope = jnp.sum(grad_logits * logits, axis=1, keepdims=True)
    slope_ref[...] = jnp.sum(slope, axis=0, keepdims=True)
    grad_raw = scale * grad_logits
    grad_queries = exact_dot(grad_raw, documents)
    grad_documents = exact_dot(grad_raw, queries, ((0,), (0,)))
    mine = lax.broadcasted_iota(jnp.int32, (8, 128), 0)
    picks = jnp.where((deal_row_ref[...] == mine + lin * 4) & (mine < 4), 1.0, 0.0)
    own_ref[...] = exact_dot(picks, jnp.concatenate([grad_queries, grad_documents], axis=0))


def run_contrast(unit, deal_order, log_scale, cid):
    sems = pltpu.SemaphoreType.DMA
    one = jax.ShapeDtypeStruct((1, 1), jnp.float32)
    return pl.pallas_call(
        contrast_kernel,
        out_shape=[one, jax.ShapeDtypeStruct((8, D), jnp.float32), one],
        in_specs=[pl.BlockSpec(memory_space=pltpu.VMEM)] * 4,
        out_specs=[pl.BlockSpec(memory_space=pltpu.VMEM)] * 3,
        scratch_shapes=[pltpu.VMEM((32, 16, 128), jnp.float32), sems((32,)), sems((32,)), sems],
        compiler_params=pltpu.CompilerParams(collective_id=cid, has_side_effects=True),
    )(unit, deal_order.reshape(128, 1), deal_order.reshape(1, 128), log_scale.reshape(1, 1))


GRAD_ROWS = 2 * PART + 64
GRAD_LAYER = (0, PART + 64)
GRAD_HEAD = PART
PIECES = tuple(
    (stage, half, spare, at)
    for stage, half, spare, at in (
        (320, 128, 32, GRAD_LAYER[1] + 256), (576, 128, 32, GRAD_LAYER[1] + 512), (832, 128, 32, GRAD_LAYER[1] + 768),
        (0, 160, 32, GRAD_HEAD),
        (320, 128, 32, 256), (576, 128, 32, 512), (832, 128, 32, 768),
        (64, 128, 32, 0),
    )
)


BACKWARD_ORDER = (
    98000, 101100, 102100, 102110, 102120, 102130, 115000, 115100, 115200, 109100, 67000, 67010, 67020, 67030, 104100,
    67040, 67050, 67060, 89000, 67070, 67100, 67110, 89010, 67120, 67130, 67140, 67150, 67160, 89020, 67170, 89030,
    104110, 89040, 89050, 67200, 67210, 88020, 89060, 67220, 67230, 67240, 67250, 89070, 67260, 67270, 88010, 104120,
    89100, 89110, 89120, 104130, 88030, 89130, 89140, 89150, 104140, 89160, 88000, 89170, 104150, 89200, 89210, 88120,
    104160, 89220, 89230, 90000, 89240, 88110, 104170, 89250, 89260, 88130, 89270, 108100, 70000, 115300, 88100,
    88220, 101000, 88210, 90100, 102000, 67300, 88230, 67310, 88200, 67320, 67330, 67340, 67350, 67360, 67370, 70100,
    102010, 89300, 90200, 89310, 89320, 89330, 89340, 102020, 88320, 89350, 89360, 89370, 70200, 102030, 115400,
    115500, 88310, 115600, 88330, 88300, 109000, 67400, 67410, 67420, 67430, 67440, 67450, 67460, 67470, 67500,
    104000, 89400, 67510, 89410, 67520, 67530, 67540, 89420, 67550, 67560, 67570, 67600, 89430, 67610, 67620, 67630,
    89440, 90300, 67640, 89450, 67650, 88420, 67660, 104010, 89460, 89470, 67670, 89500, 88410, 104020, 89510, 89520,
    89530, 88430, 104030, 89540, 89550, 104040, 89560, 88400, 89570, 104050, 89600, 89610, 88520, 104060, 90400,
    89620, 88510, 89630, 104070, 70300, 89640, 89650, 88530, 89660, 108000, 115700, 73000, 69000, 89670, 88500, 70400,
    88620, 67700, 67710, 67720, 88610, 67730, 67740, 67750, 68000, 67760, 67770, 78000, 89700, 89710, 89720, 89730,
    88630, 89740, 69200, 89750, 90500, 69400, 89760, 69600, 69300, 89770, 69500, 69100, 69700, 88600, 70500, 68200,
    68600, 68400, 68700, 68100, 68300, 68500, 88720, 88710, 88730, 90600, 88700, 70600, 90700, 70700, 118000,
)


def sum_stages(stage, out_ref, acc, b1, b2, b3, b4, b5, fin, sems, free):
    cs, cr, ys, yr, xs, xr, zs, zr, as_, ar, fs, fr, ls, os_ = sems
    z, x, y, c = place()
    me = z * 2 + x
    zp = [dev((z + k) % 4, x, y, c) for k in range(4)]
    xp, yp, cp = dev(z, 1 - x, y, c), dev(z, x, 1 - y, c), dev(z, x, y, 1 - c)

    def rc(src, dst, s, r, d):
        return pltpu.make_async_remote_copy(src, dst, s, r, device_id=d, device_id_type=MESH)

    def owner(k, f):
        return ((z + k) % 4) * 2 + (x if f == 0 else 1 - x)

    order = [(k, f) for k in (2, 1, 3, 0) for f in (1, 0)]
    lo, lb, lh, la, l1 = [0], [0], [0], [0], [0]
    for stage_at, half, spare, at in PIECES:
        lo.append(lo[-1] + half)
        lb.append(lb[-1] + spare)
        lh.append(lh[-1] + half - spare)
        la.append(la[-1] + half - 2 * spare)
        l1.append(l1[-1] + half)
    l1 = l1[:4] + l1[:4]

    def add(dst, src, count):
        def body(i, carry):
            at = mult(i * 32)
            into = dst(at)
            into[...] = (into[...].astype(jnp.float32) + src(at)[...].astype(jnp.float32)).astype(BF)
            return carry
        lax.fori_loop(0, count // 32, body, 0)
        if count % 32:
            into = dst(count - 16, 16)
            into[...] = (into[...].astype(jnp.float32) + src(count - 16, 16)[...].astype(jnp.float32)).astype(BF)

    class Piece:
        pass

    pieces = []
    for q, (stage_at, half, spare, at) in enumerate(PIECES):
        p = Piece()
        p.q, p.half, p.spare, p.main = q, half, spare, half - spare
        p.hs = mult(lo[q] + y * spare)
        p.mb = mult(lo[q] + y * p.main)
        p.ob = mult(lo[q] + (1 - y) * p.main)
        p.L, p.C, p.Y, p.X, p.Z = [], [], [], [], []
        for i, (k, f) in enumerate(order):
            s = owner(k, f)
            p.L.append(pltpu.make_async_copy(stage.at[s, pl.ds(mult(stage_at + c * half), half)], acc.at[s, pl.ds(lo[q], half)], ls.at[q, i]))
            p.C.append(rc(stage.at[s, pl.ds(mult(stage_at + (1 - c) * half), half)], b1.at[s, pl.ds(l1[q], half)], cs.at[q, i], cr.at[q, i], cp))
            p.Y.append(rc(acc.at[s, pl.ds(p.ob, spare)], b2.at[s, pl.ds(lb[q], spare)], ys.at[q, i], yr.at[q, i], yp))
        for k in range(4):
            p.X.append(rc(acc.at[owner(k, 1), pl.ds(p.hs, p.main)], b3.at[k, pl.ds(lh[q], p.main)], xs.at[q, k], xr.at[q, k], xp))
            p.Z.append(rc(acc.at[owner(k, 0), pl.ds(p.hs, p.main)], b4.at[k - 1, pl.ds(lh[q], p.main)], zs.at[q, k], zr.at[q, k], zp[k]) if k else None)
        p.aa, p.na = lo[q] + spare, half - 2 * spare
        p.A = rc(fin.at[pl.ds(p.aa, p.na)], b5.at[pl.ds(la[q], p.na)], as_.at[q, 0], ar.at[q, 0], yp)
        p.B = rc(fin.at[pl.ds(p.mb, spare)], fin.at[pl.ds(p.mb, spare)], as_.at[q, 1], ar.at[q, 1], yp)
        p.F = rc(fin.at[pl.ds(lo[q], half)], out_ref.at[pl.ds(mult(at + c * half), half)], fs.at[q], fr.at[q], cp)
        p.O = pltpu.make_async_copy(fin.at[pl.ds(lo[q], half)], out_ref.at[pl.ds(mult(at + c * half), half)], os_.at[q])
        pieces.append(p)

    def issue(q):
        p = pieces[q]
        if q >= 4:
            pl.semaphore_wait(free.at[q - 4], 1)
        for i in range(8):
            p.C[i].start()
            p.L[i].start()

    def core(q, i):
        p = pieces[q]
        s = owner(*order[i])
        p.L[i].wait()
        p.C[i].wait_recv()
        add(lambda a, n=32: acc.at[s, pl.ds(lo[q] + a, n)], lambda a, n=32: b1.at[s, pl.ds(l1[q] + a, n)], p.half)
        p.Y[i].start()
        if i == 7 and q < 4:
            pl.semaphore_signal(free.at[q], inc=1, device_id=cp, device_id_type=MESH)

    def plane(q, i):
        p = pieces[q]
        k, f = order[i]
        s = owner(k, f)
        p.Y[i].wait_recv()
        add(lambda a, n=32: acc.at[s, pl.ds(p.mb + a, n)], lambda a, n=32: b2.at[s, pl.ds(lb[q] + a, n)], p.spare)
        if f == 1:
            p.X[k].start()

    def sideways(q, k):
        p = pieces[q]
        s = owner(k, 0)
        p.X[k].wait_recv()
        add(lambda a, n=32: acc.at[s, pl.ds(p.hs + a, n)], lambda a, n=32: b3.at[k, pl.ds(lh[q] + a, n)], p.main)
        if k:
            p.Z[k].start()

    def along(q):
        p = pieces[q]
        for k in range(1, 4):
            p.Z[k].wait_recv()
        def body(i, carry):
            at = mult(i * 16)
            total = acc[me, pl.ds(p.hs + at, 16)].astype(jnp.float32)
            for k in range(3):
                total += b4[k, pl.ds(lh[q] + at, 16)].astype(jnp.float32)
            fin[pl.ds(p.hs + at, 16)] = total.astype(BF)
            return carry
        lax.fori_loop(0, p.main // 16, body, 0)
        p.A.start()
        p.B.start()

    def last(q):
        p = pieces[q]
        p.A.wait_recv()
        p.A.wait_send()
        add(lambda a, n=32: fin.at[pl.ds(p.aa + a, n)], lambda a, n=32: b5.at[pl.ds(la[q] + a, n)], p.na)
        p.B.wait_recv()
        p.F.start()
        p.O.start()

    steps = {}
    for q in range(8):
        steps[step_id("s", q)], steps[step_id("Z", q)], steps[step_id("F", q)] = (issue, q), (along, q), (last, q)
        for i in range(8):
            steps[step_id("C", q, i)], steps[step_id("Y", q, i)] = (core, q, i), (plane, q, i)
        for k in range(4):
            steps[step_id("X", q, k)] = (sideways, q, k)

    def sent(q):
        for copy in pieces[q].C:
            copy.wait_send()

    def finish():
        for p in pieces:
            p.F.wait()
            p.O.wait()
            p.B.wait_send()
            for copy in p.Y + p.X + p.Z[1:]:
                copy.wait_send()

    return steps, sent, finish


def row_exchange(slots, t_ref, norm_ref, norm_out, nbuf, es, er, el, ns, nr):
    z, x, y, c = place()
    me = z * 2 + x
    g = y * 2 + c
    g2 = (1 - y) * 2 + c
    ep = [(lax.rem(me + k, 8), g) for k in range(8)]
    back = [lax.rem(me + 8 - k, 8) for k in range(8)]
    yp, cp = dev(z, x, 1 - y, c), dev(z, x, y, 1 - c)

    def rc(src, dst, s, r, d):
        return pltpu.make_async_remote_copy(src, dst, s, r, device_id=d, device_id_type=MESH)

    kept = pltpu.make_async_copy(slots.at[me], t_ref.at[g, me], el)
    E = [rc(slots.at[ep[k][0]], t_ref.at[g, me], es.at[0, k], er.at[0, k], ep[k]) for k in range(1, 8)]
    EY = [rc(t_ref.at[g, back[k]], t_ref.at[g, back[k]], es.at[1, k], er.at[1, k], yp) for k in range(8)]
    EC = [rc(t_ref.at[g, back[k]], t_ref.at[g, back[k]], es.at[2, k], er.at[2, k], cp) for k in range(8)]
    ED = [rc(t_ref.at[g2, back[k]], t_ref.at[g2, back[k]], es.at[3, k], er.at[3, k], cp) for k in range(8)]
    NC = rc(norm_ref, nbuf.at[0], ns.at[0], nr.at[0], cp)
    NY = rc(nbuf.at[1], nbuf.at[2], ns.at[1], nr.at[1], yp)

    def issue():
        kept.start()
        for copy in E:
            copy.start()
        NC.start()

    def norms():
        NC.wait_recv()
        nbuf[1] = nbuf[0] + norm_ref[...]
        NY.start()

    def relay(k):
        if k:
            E[k - 1].wait_recv()
        else:
            kept.wait()
        EY[k].start()
        EC[k].start()

    def relay_core(k):
        EY[k].wait_recv()
        ED[k].start()

    def end():
        NY.wait_recv()
        norm_out[...] = nbuf[1] + nbuf[2]
        for copy in EC + ED:
            copy.wait_recv()
        for copy in E + EY + EC + ED + [NC, NY]:
            copy.wait_send()

    steps = {step_id("I"): (issue,), step_id("N"): (norms,), step_id("v"): (end,)}
    for k in range(8):
        steps[step_id("E", k)], steps[step_id("D", k)] = (relay, k), (relay_core, k)
    return steps


def backward_kernel(
    own_ref, zed_ref, pool_ref, seg_col_ref, seg_row_ref, valid_ref, key_ref, norm_ref,
    w_ref, low_in, qkv_in, lse_in, mix_in, one_in, two_in,
    out_ref, t_ref, norm_out, first_ref,
    weights, head, low_ref, qkv_ref, lse_ref, mix_ref, one_ref, two_ref, stage,
    dx, far, acc, two_s, low_s, mid_s, ups, gates, back, norm_s, slots,
    total, b1, b2, b3, b4, b5, fin, nbuf,
    cs, cr, ys, yr, xs, xr, zs, zr, as_, ar, fs, fr, ls, os_, es, er, el, ns, nr, loads, free,
):
    tokens = dx.shape[0]
    tiles = tokens // TILE
    low_type = jnp.bfloat16
    z, x, y, c = place()
    me = z * 2 + x
    g = y * 2 + c
    peers = [(lax.rem(me + k, 8), g) for k in range(1, 8)] + [dev(z, x, 1 - y, c), dev(z, x, y, 1 - c)]
    barrier = pltpu.get_barrier_semaphore()
    for peer in peers:
        pl.semaphore_signal(barrier, inc=1, device_id=peer, device_id_type=MESH)
    steps, sent, finish = sum_stages(
        stage, out_ref, total, b1, b2, b3, b4, b5, fin, (cs, cr, ys, yr, xs, xr, zs, zr, as_, ar, fs, fr, ls, os_), free
    )
    steps |= row_exchange(slots, t_ref, norm_s, norm_out, nbuf, es, er, el, ns, nr)

    def loading(layer):
        base = PACK_LAYER[layer]
        copy = pltpu.make_async_copy
        return {
            "two": copy(two_in.at[layer], two_ref, loads.at[layer, 0]),
            "one": copy(one_in.at[layer], one_ref, loads.at[layer, 1]),
            "feed": copy(w_ref.at[:, pl.ds(base + 256, 768)], weights.at[:, pl.ds(256, 768)], loads.at[layer, 2]),
            "mix": copy(mix_in.at[layer], mix_ref, loads.at[layer, 3]),
            "qkv": copy(qkv_in.at[layer], qkv_ref, loads.at[layer, 4]),
            "lse": copy(lse_in.at[layer], lse_ref, loads.at[layer, 5]),
            "low": copy(low_in.at[layer], low_ref, loads.at[layer, 6]),
            "attend": copy(w_ref.at[:, pl.ds(base, 256)], weights.at[:, pl.ds(0, 256)], loads.at[layer, 7]),
        }

    load = [loading(layer) for layer in range(LAYERS)]
    head_load = pltpu.make_async_copy(w_ref.at[:, pl.ds(PACK_HEAD, 64)], head, loads.at[0, 8])
    head_load.start()
    for copy in load[1].values():
        copy.start()

    def begin():
        fill_distance(far, seg_col_ref, seg_row_ref)
        head_load.wait()
        load[1]["two"].wait()
        zed = zed_ref[...]
        square = jnp.sum(zed * zed, axis=-1, keepdims=True) + UNIT_EPS
        inverse = lax.rsqrt(square)
        own = own_ref[...]
        inner = jnp.sum(own * zed, axis=-1, keepdims=True)
        grad_zed = (inverse * (own - zed * (inner / square))).astype(low_type)
        head_low = head[...].reshape(D, D)
        stage[:, 0:64, :] = dot_tn(pool_ref[...], grad_zed).reshape(8, 64, D).astype(low_type)
        member = members(seg_row_ref, valid_ref)
        counts = jnp.maximum(jnp.sum(member, axis=1, keepdims=True), 1.0)
        grad_pooled = dot_nt(grad_zed, head_low) / counts
        grad_final = exact_dot(member, grad_pooled, ((0,), (0,)))
        stream_scaled, _ = norm_parts(two_ref[...])
        stream = stream_scaled * norm_ref[6:7, :] + norm_ref[7:8, :]
        scaled, inverse = norm_parts(stream)
        norm_s[...] = jnp.zeros(norm_s.shape, jnp.float32)
        norm_s[2, 0:1, :] = jnp.sum(grad_final * scaled, axis=0, keepdims=True)
        norm_s[2, 1:2, :] = jnp.sum(grad_final, axis=0, keepdims=True)
        dx[...] = norm_back(scaled, inverse, grad_final, norm_ref[8:9, :])

    def enter(layer):
        at = 4 * layer
        if layer < LAYERS - 1:
            load[layer]["two"].wait()
        load[layer]["one"].wait()

        def body(i, carry):
            rows = pl.ds(pl.multiple_of(i * TILE, TILE), TILE)
            scaled, inverse = norm_parts(two_ref[rows, :])
            grad = dx[rows, :]
            norm_s[layer, 2:3, :] += jnp.sum(grad * scaled, axis=0, keepdims=True)
            norm_s[layer, 3:4, :] += jnp.sum(grad, axis=0, keepdims=True)
            grad = norm_back(scaled, inverse, grad, norm_ref[at + 2 : at + 3, :])
            acc[rows, :] = grad
            two_s[rows, :] = grad.astype(low_type)
            scaled, _ = norm_parts(one_ref[rows, :])
            hidden = scaled * norm_ref[at : at + 1, :] + norm_ref[at + 1 : at + 2, :]
            low_s[rows, :] = hidden.astype(low_type)
            return carry

        lax.fori_loop(0, tiles, body, 0)
        if layer > 0:
            load[layer - 1]["two"].start()
        load[layer]["feed"].wait()

    def feed(layer, j):
        def body(i, carry):
            rows = pl.ds(pl.multiple_of(i * TILE, TILE), TILE)
            low = low_s[rows, :]
            gate = dot_nn(low, block(weights, 256 + j * 64))
            up = dot_nn(low, block(weights, 512 + j * 64))
            grad_mid = dot_nt(two_s[rows, :], down_block(weights, j))
            value, slope = gelu_parts(gate)
            mid_s[rows, :] = (value * up).astype(low_type)
            grad_gate = (grad_mid * up * slope).astype(low_type)
            grad_up = (grad_mid * value).astype(low_type)
            gates[rows, :] = grad_gate
            ups[rows, :] = grad_up
            acc[rows, :] += dot_nt(grad_gate, block(weights, 256 + j * 64)) + dot_nt(
                grad_up, block(weights, 512 + j * 64)
            )
            return carry

        lax.fori_loop(0, tiles, body, 0)
        if layer < LAYERS - 1 and j == 0:
            for q in range(3):
                sent(q)
        stage[2 * j : 2 * j + 2, 832:1088, :] = dot_tn(mid_s[...], two_s[...]).reshape(2, 256, D).astype(low_type)
        stage[:, 320 + j * 64 : 384 + j * 64, :] = dot_tn(low_s[...], gates[...]).reshape(8, 64, D).astype(low_type)
        stage[:, 576 + j * 64 : 640 + j * 64, :] = dot_tn(low_s[...], ups[...]).reshape(8, 64, D).astype(low_type)

    def middle(layer):
        at = 4 * layer
        if layer > 0:
            load[layer - 1]["feed"].start()
        load[layer]["attend"].wait()
        load[layer]["mix"].wait()

        def body(i, carry):
            rows = pl.ds(pl.multiple_of(i * TILE, TILE), TILE)
            scaled, inverse = norm_parts(one_ref[rows, :])
            grad = acc[rows, :]
            norm_s[layer, 0:1, :] += jnp.sum(grad * scaled, axis=0, keepdims=True)
            norm_s[layer, 1:2, :] += jnp.sum(grad, axis=0, keepdims=True)
            grad = norm_back(scaled, inverse, grad, norm_ref[at : at + 1, :])
            dx[rows, :] = grad
            low = grad.astype(low_type)
            two_s[rows, :] = low
            mid_s[rows, :] = dot_nt(low, block(weights, 192)).astype(low_type)
            return carry

        lax.fori_loop(0, tiles, body, 0)
        if layer > 0:
            load[layer - 1]["one"].start()
        else:
            sent(3)
        stage[:, 256:320, :] = dot_nn(mix_ref[...], two_s[...]).reshape(8, 64, D).astype(low_type)
        load[layer]["qkv"].wait()
        load[layer]["lse"].wait()
        load[layer]["low"].wait()

    def attend_head(layer, head):
        lanes = slice(head * HEAD_DIM, (head + 1) * HEAD_DIM)
        key_lanes = slice(D + head * HEAD_DIM, D + (head + 1) * HEAD_DIM)
        val_lanes = slice(2 * D + head * HEAD_DIM, 2 * D + (head + 1) * HEAD_DIM)
        keys = qkv_ref[:, key_lanes]
        keys_t = keys.T
        vals = qkv_ref[:, val_lanes]
        slope = 2.0 ** (-8.0 * (head + 1) / HEADS)
        grad_vals = None
        grad_keys = None
        for i in range(tiles):
            cols = slice(i * TILE, (i + 1) * TILE)
            query = qkv_ref[cols, lanes]
            grad_mix = mid_s[cols, lanes]
            scores = dot_nt(keys, query) * HEAD_DIM**-0.5 - slope * far[:, cols]
            prob = jnp.exp(scores - lse_ref[head, :, cols])
            grad_prob = dot_nt(vals, grad_mix)
            inner = jnp.sum(prob * grad_prob, axis=0, keepdims=True)
            grad_raw = (prob * (grad_prob - inner) * HEAD_DIM**-0.5).astype(low_type)
            back[cols, lanes] = dot_nn(keys_t, grad_raw).T.astype(low_type)
            value_part = dot_nn(prob.astype(low_type), grad_mix)
            key_part = dot_nn(grad_raw, query)
            grad_vals = value_part if grad_vals is None else grad_vals + value_part
            grad_keys = key_part if grad_keys is None else grad_keys + key_part
        back[:, key_lanes] = grad_keys.astype(low_type)
        back[:, val_lanes] = grad_vals.astype(low_type)

    def leave(layer):
        def body(i, carry):
            rows = pl.ds(pl.multiple_of(i * TILE, TILE), TILE)
            grad = dx[rows, :]
            for j in range(3):
                grad = grad + dot_nt(back[rows, j * D : (j + 1) * D], block(weights, j * 64))
            dx[rows, :] = grad
            return carry

        lax.fori_loop(0, tiles, body, 0)
        for j in range(3):
            stage[:, 64 + j * 64 : 128 + j * 64, :] = (
                dot_tn(low_ref[...], back[:, j * D : (j + 1) * D]).reshape(8, 64, D).astype(low_type)
            )
        if layer > 0:
            for name in ("mix", "qkv", "lse", "low", "attend"):
                load[layer - 1][name].start()
        else:
            first_ref[...] = dx[...].astype(low_type)
            count = slots.shape[1]
            for d in range(8):
                hot = lax.broadcasted_iota(jnp.int32, (count, tokens), 0) + d * count == key_ref[...]
                slots[d] = dot_nn(jnp.where(hot, 1.0, 0.0).astype(low_type), first_ref[...]).astype(low_type)

    steps[step_id("b")] = (begin,)
    for layer in range(LAYERS):
        steps[step_id("e", layer)], steps[step_id("m", layer)], steps[step_id("l", layer)] = (enter, layer), (middle, layer), (leave, layer)
        for j in range(4):
            steps[step_id("f", layer, j)] = (feed, layer, j)
        for head_index in range(HEADS):
            steps[step_id("h", layer, head_index)] = (attend_head, layer, head_index)
    for name in BACKWARD_ORDER:
        if name == step_id("s"):
            pl.semaphore_wait(barrier, len(peers))
        fn, *rest = steps.pop(name)
        fn(*rest)
    assert not steps
    finish()
    for q in range(4, 8):
        sent(q)


def run_backward(own, zed, pool, seg_col, seg_row, valid, key, weights, norms, saved, cid):
    low_x, qkv, lse, mix, one, two = saved
    tokens = low_x.shape[1]
    low = jnp.bfloat16
    full = jnp.float32
    vmem = lambda shape, kind=low: pltpu.VMEM(shape, kind)
    sems = lambda *shape: pltpu.SemaphoreType.DMA(shape)
    half = sum(p[1] for p in PIECES)
    spare = sum(p[2] for p in PIECES)
    near = pl.BlockSpec(memory_space=pltpu.VMEM)
    anywhere = pl.BlockSpec(memory_space=pl.ANY)
    norm_shape = (LAYERS + 1, 8, D)
    square = (tokens, D)
    return pl.pallas_call(
        backward_kernel,
        in_specs=[near] * 8 + [anywhere] * 7,
        out_specs=[anywhere, anywhere, near, near],
        out_shape=[
            jax.ShapeDtypeStruct((GRAD_ROWS, D), low),
            jax.ShapeDtypeStruct((4, 8, SLOTS, D), low),
            jax.ShapeDtypeStruct(norm_shape, full),
            jax.ShapeDtypeStruct(square, low),
        ],
        scratch_shapes=[
            vmem((8, PART, D)), vmem((8, 64, D)), vmem(square), vmem((tokens, 3 * D)), vmem((HEADS, 1, tokens), full),
            vmem((D, tokens)), vmem(square, full), vmem(square, full), vmem((8, PART + 64, D)),
            vmem(square, full), vmem((tokens, tokens), full), vmem(square, full), vmem(square), vmem(square),
            vmem(square), vmem(square), vmem(square), vmem((tokens, 3 * D)), vmem(norm_shape, full), vmem((8, SLOTS, D)),
            vmem((8, half, D)), vmem((8, sum(p[1] for p in PIECES[:4]), D)), vmem((8, spare, D)), vmem((4, half - spare, D)),
            vmem((3, half - spare, D)), vmem((half - 2 * spare, D)), vmem((half, D)), vmem((3,) + norm_shape, full),
            sems(8, 8), sems(8, 8), sems(8, 8), sems(8, 8), sems(8, 4), sems(8, 4), sems(8, 4), sems(8, 4),
            sems(8, 2), sems(8, 2), sems(8), sems(8), sems(8, 8), sems(8), sems(4, 8), sems(4, 8), pltpu.SemaphoreType.DMA,
            sems(2), sems(2), sems(2, 9), pltpu.SemaphoreType.REGULAR((4,)),
        ],
        compiler_params=pltpu.CompilerParams(collective_id=cid, has_side_effects=True, vmem_limit_bytes=63 * 2**20),
    )(own, zed, pool, seg_col, seg_row, valid, key, norms, weights, low_x, qkv, lse, mix, one, two)


def total_kernel(v_ref, o_ref, got, mine, ss, rs, ts, us, ls):
    me = lax.axis_index("dp")
    g = lax.axis_index("group")
    lin = me * 4 + g
    to = [lax.rem(lin + k, 32) for k in range(32)]
    peers = [(p // 4, p % 4) for p in to]
    owners = [(lax.rem(me + k, 8), g) for k in range(8)]
    entry_barrier(peers[1:])
    first = [
        pltpu.make_async_remote_copy(
            v_ref.at[owners[k][0] * 4 + g], got.at[k], ss.at[k], rs.at[k], device_id=owners[k], device_id_type=MESH
        )
        for k in range(1, 8)
    ]
    for copy in first:
        copy.start()
    own = pltpu.make_async_copy(v_ref.at[lin], got.at[0], ls.at[0])
    own.start()
    for copy in first:
        copy.wait()
    own.wait()
    mine[...] = jnp.sum(got[...], axis=0)
    second = [
        pltpu.make_async_remote_copy(
            mine, o_ref.at[lin], ts.at[k], us.at[k], device_id=peers[k], device_id_type=MESH
        )
        for k in range(1, 32)
    ]
    for copy in second:
        copy.start()
    own = pltpu.make_async_copy(mine, o_ref.at[lin], ls.at[1])
    own.start()
    for copy in second:
        copy.wait()
    own.wait()


def total(v, cid):
    sems = pltpu.SemaphoreType.DMA
    return pl.pallas_call(
        total_kernel,
        out_shape=jax.ShapeDtypeStruct(v.shape, v.dtype),
        in_specs=[pl.BlockSpec(memory_space=pltpu.VMEM)], out_specs=pl.BlockSpec(memory_space=pltpu.VMEM),
        scratch_shapes=[
            pltpu.VMEM((8,) + v.shape[1:], v.dtype), pltpu.VMEM(v.shape[1:], v.dtype),
            sems((8,)), sems((8,)), sems((32,)), sems((32,)), sems((2,)),
        ],
        compiler_params=pltpu.CompilerParams(collective_id=cid, has_side_effects=True),
    )(v)


BLOCKS = 28
STEP_AT = 28
SUM_AT = 56
NORM_ROW = 57
ROW_TILE = 1024
STAT_TILE = 1024
RATES = (
    RATE_SCALE, RATE_SCALE / D**0.5, RATE_SCALE / D**0.5, RATE_SCALE / (D // 8) ** 0.5,
    RATE_SCALE / D**0.5, RATE_SCALE / FF**0.5,
)


def matrices(layer):
    at = GRAD_LAYER[layer]
    first = 2 + 13 * layer
    return (
        (2, at, 64, 3, first), (3, at + 192, 64, 1, first + 3),
        (4, at + 256, 64, 8, first + 4), (5, at + 768, 256, 1, first + 12),
    )


def turn(row):
    return jnp.broadcast_to(row, (8, row.shape[1])).T[:, 0:1]


def lane_pick(value, lane):
    return jnp.where(lax.broadcasted_iota(jnp.int32, (1, D), 1) == lane, value, 0.0)


def stats_kernel(dense, row_count, *refs):
    *refs, low_hot = refs
    if dense:
        full_ref, grads_ref, norm_ref, table_row_ref, rows_ref, down_ref, *outs = refs
    else:
        slot_ref, slot_rows_ref, grads_ref, norm_ref, table_row_ref, rows_ref, down_ref, *outs = refs
    table_ref, table_row_out, stat_ref, rows_out, down_out = outs
    step = pl.program_id(0)

    def put(at, value):
        stat_ref[at // 3, at % 3 : at % 3 + 1, :] = value

    def add(at, value):
        stat_ref[at // 3, at % 3 : at % 3 + 1, :] += value

    @pl.when(step == 0)
    def _():
        stat_ref[...] = jnp.zeros(stat_ref.shape, jnp.float32)
        for row in range(10):
            put(NORM_ROW + row, norm_ref[row // 4, row % 4 : row % 4 + 1, :])
        sums = jnp.zeros((1, D), jnp.float32)
        rows_out[...] = jnp.zeros(rows_out.shape, jnp.float32)

        def part(first, count, blocks, block_at, old):
            squares = [
                grads_ref[first + j * count : first + (j + 1) * count, :].astype(jnp.float32) ** 2 for j in range(blocks)
            ]
            mean = jnp.sum(functools.reduce(jnp.add, squares), axis=-1, keepdims=True) / (blocks * D)
            new = DECAY_RATE * old + (1.0 - DECAY_RATE) * (mean + STATE_EPS)
            inverse = 1.0 / new
            for j in range(blocks):
                put(block_at + j, jnp.sum(squares[j], axis=0, keepdims=True))
                put(STEP_AT + block_at + j, jnp.sum(squares[j] * inverse, axis=0, keepdims=True))
            return new, jnp.sum(new, axis=0, keepdims=True)

        new, count = part(GRAD_HEAD, 64, 1, 1, rows_ref[:, 6:7])
        rows_out[:, 6:7] = new
        sums += lane_pick(count, 1)
        for layer in range(LAYERS):
            for name, first, rows, blocks, block_at in matrices(layer):
                if name == 5:
                    new, count = part(first, rows, blocks, block_at, down_ref[:, layer : layer + 1])
                    down_out[:, layer : layer + 1] = new
                else:
                    lane = 3 * layer + name - 2
                    new, count = part(first, rows, blocks, block_at, rows_ref[:, lane : lane + 1])
                    rows_out[:, lane : lane + 1] = new
                sums += lane_pick(count, 2 * name - 2 + layer)
        put(SUM_AT, sums)

    index = lax.broadcasted_iota(jnp.int32, (STAT_TILE, 1), 0) + step * STAT_TILE
    if dense:
        grad = jnp.where(index < row_count, full_ref[...], 0.0)
    else:
        high = slot_ref[...] // 64

        @pl.when(step == 0)
        def _():
            low = lax.broadcasted_iota(jnp.int32, low_hot.shape, 0)
            low_hot[...] = jnp.where(low == slot_ref[...] - 64 * high, 1.0, 0.0).astype(jnp.bfloat16)

        picks = jnp.concatenate(
            [
                low_hot[...] * jnp.where(high == step * (STAT_TILE // 64) + i, 1.0, 0.0).astype(jnp.bfloat16)
                for i in range(STAT_TILE // 64)
            ],
            axis=0,
        )
        grad = jnp.dot(picks, slot_rows_ref[...], preferred_element_type=jnp.float32)
    low = grad.astype(jnp.bfloat16)
    table_ref[...] = low
    squares = low.astype(jnp.float32) ** 2
    mean = jnp.mean(squares, axis=-1, keepdims=True)
    mean_row = jnp.broadcast_to(mean, (STAT_TILE, 128)).T[0:1, :]
    new = DECAY_RATE * table_row_ref[...] + (1.0 - DECAY_RATE) * (mean_row + STATE_EPS)
    real = lax.broadcasted_iota(jnp.int32, (1, STAT_TILE), 1) + step * STAT_TILE < row_count
    new = jnp.where(real, new, 1.0)
    table_row_out[...] = new
    add(0, jnp.sum(squares, axis=0, keepdims=True))
    add(STEP_AT, jnp.sum(squares * (1.0 / turn(new)), axis=0, keepdims=True))
    add(SUM_AT, lane_pick(jnp.sum(jnp.where(real, new, 0.0), axis=1, keepdims=True), 0))


def run_stats(dense, heads, grads, norm, table_row, rows, down):
    row_count = table_row.shape[1]
    tile = pl.BlockSpec((STAT_TILE, D), lambda i: (i, 0))
    lane = pl.BlockSpec((1, STAT_TILE), lambda i: (0, i))
    head_specs = [tile] if dense else [whole(v.shape) for v in heads]
    stat = (32, 3, D)
    return pl.pallas_call(
        functools.partial(stats_kernel, dense, row_count),
        grid=(-(-row_count // STAT_TILE),),
        in_specs=head_specs + [whole(grads.shape), whole(norm.shape), lane, whole(rows.shape), whole(down.shape)],
        out_specs=[tile, lane, whole(stat), whole(rows.shape), whole(down.shape)],
        out_shape=[
            jax.ShapeDtypeStruct((row_count, D), jnp.bfloat16), jax.ShapeDtypeStruct(table_row.shape, jnp.float32),
            jax.ShapeDtypeStruct(stat, jnp.float32), jax.ShapeDtypeStruct(rows.shape, jnp.float32),
            jax.ShapeDtypeStruct(down.shape, jnp.float32),
        ],
        scratch_shapes=[pltpu.VMEM((64, 8 if dense else heads[0].shape[1]), jnp.bfloat16)],
        compiler_params=pltpu.CompilerParams(vmem_limit_bytes=48 * 2**20),
    )(*heads, grads, norm, table_row, rows, down)


def update_kernel(
    totals, stat_ref, table_ref, embed_ref, table_row_ref, rows_ref, down_ref, top_cols_ref, cols_ref,
    grads_in, in_in, mix_in, gate_in, low_in, head_in,
    embed_out, table_cols_out, head_cols_out, cols_out, rms_out, in_to, mix_to, gate_to, low_to, head_to,
    factors, grads_ref, in_ref, mix_ref, gate_ref, low_ref, head_ref, loads, stores,
):
    step = pl.program_id(0)
    sources = (grads_in, in_in, mix_in, gate_in, low_in, head_in)
    held = (grads_ref, in_ref, mix_ref, gate_ref, low_ref, head_ref)
    targets = (in_to, mix_to, gate_to, low_to, head_to)
    load = [pltpu.make_async_copy(sources[i], held[i], loads.at[i]) for i in range(6)]
    store = [pltpu.make_async_copy(held[i + 1], targets[i], stores.at[i]) for i in range(5)]

    def stat(at):
        return stat_ref[at // 3, at % 3 : at % 3 + 1, :]

    def mean_of(lane, name):
        return jnp.sum(jnp.where(lax.broadcasted_iota(jnp.int32, (1, D), 1) == lane, stat(SUM_AT), 0.0), axis=1, keepdims=True) / totals[name]

    def columns(block_at, blocks, old, lane, name):
        row_mean = mean_of(lane, name)
        news = []
        steps = 0.0
        for j in range(blocks):
            new = DECAY_RATE * old(j) + (1.0 - DECAY_RATE) * (stat(block_at + j) / totals[name] + STATE_EPS)
            news.append(new)
            steps += jnp.sum(row_mean * stat(STEP_AT + block_at + j) / new, axis=1, keepdims=True)
        rms = jnp.sqrt(steps / (totals[name] * blocks * D))
        scale = -RATES[name] / jnp.maximum(1.0, rms / CLIP_LEVEL)
        return news, row_mean, rms, scale

    @pl.when(step == 0)
    def _():
        for copy in load:
            copy.start()
        news, row_mean, rms, scale = columns(0, 1, lambda j: top_cols_ref[0:1, :], 0, 0)
        table_cols_out[...] = news[0]
        factors[0:1, :] = lax.rsqrt(news[0])
        factors[1:2, :] = jnp.broadcast_to(row_mean, (1, D))
        factors[2:3, :] = jnp.broadcast_to(scale, (1, D))
        factors[3:4, :] = lane_pick(rms, 0)

    @pl.when(step == pl.num_programs(0) - 1)
    def _():
        for copy in load:
            copy.wait()
        all_rms = factors[3:4, :]
        news, row_mean, rms, scale = columns(1, 1, lambda j: top_cols_ref[1:2, :], 1, 1)
        head_cols_out[...] = news[0]
        all_rms += lane_pick(rms, 1)
        row = lax.rsqrt(rows_ref[:, 6:7] / row_mean) * scale
        head_ref[...] = head_ref[...] + grads_ref[GRAD_HEAD : GRAD_HEAD + 64, :].astype(jnp.float32) * row * lax.rsqrt(news[0])
        for layer in range(LAYERS):
            for name, first, rows, blocks, block_at in matrices(layer):
                col_at = (block_at - 2 - 13 * layer) * D
                old = lambda j: cols_ref[layer : layer + 1, col_at + j * D : col_at + (j + 1) * D]
                news, row_mean, rms, scale = columns(block_at, blocks, old, 2 * name - 2 + layer, name)
                all_rms += lane_pick(rms, 2 * name - 2 + layer)
                lane = 3 * layer + name - 2
                state = down_ref[:, layer : layer + 1] if name == 5 else rows_ref[:, lane : lane + 1]
                row = lax.rsqrt(state / row_mean) * scale
                held_ref = (in_ref, mix_ref, gate_ref, low_ref)[name - 2]
                for j in range(blocks):
                    cols_out[layer : layer + 1, col_at + j * D : col_at + (j + 1) * D] = news[j]
                    span = slice(j * D, (j + 1) * D)
                    grad = grads_ref[first + j * rows : first + (j + 1) * rows, :].astype(jnp.float32)
                    held_ref[layer, :, span] = held_ref[layer, :, span] + grad * row * lax.rsqrt(news[j])
        rms_out[...] = all_rms
        for copy in store:
            copy.start()

    row = lax.rsqrt(turn(table_row_ref[...] / factors[1:2, 0:1])) * factors[2:3, 0:1]
    embed_out[...] = embed_ref[...] + table_ref[...].astype(jnp.float32) * row * factors[0:1, :]

    @pl.when(step == pl.num_programs(0) - 1)
    def _():
        for copy in store:
            copy.wait()


def run_update(totals, stat, table, embed, table_row, grads, rows, down, top_cols, cols, others):
    row_count = embed.shape[0]
    tile = pl.BlockSpec((ROW_TILE, D), lambda i: (i, 0))
    lane = pl.BlockSpec((1, ROW_TILE), lambda i: (0, i))
    shape = lambda v: jax.ShapeDtypeStruct(v.shape, jnp.float32)
    one = jax.ShapeDtypeStruct((1, D), jnp.float32)
    outs = [shape(embed), one, one, shape(cols), one]
    anywhere = pl.BlockSpec(memory_space=pl.ANY)
    return pl.pallas_call(
        functools.partial(update_kernel, totals),
        grid=(-(-row_count // ROW_TILE),),
        in_specs=[whole(stat.shape), tile, tile, lane]
        + [whole(v.shape) for v in (rows, down, top_cols, cols)]
        + [anywhere] * 6,
        out_specs=[tile] + [whole(v.shape) for v in outs[1:]] + [anywhere] * 5,
        out_shape=outs + [shape(v) for v in others],
        scratch_shapes=[pltpu.VMEM((8, D), jnp.float32), pltpu.VMEM(grads.shape, jnp.bfloat16)]
        + [pltpu.VMEM(v.shape, jnp.float32) for v in others]
        + [pltpu.SemaphoreType.DMA((6,)), pltpu.SemaphoreType.DMA((5,))],
        compiler_params=pltpu.CompilerParams(vmem_limit_bytes=62 * 2**20),
    )(stat, table, embed, table_row, rows, down, top_cols, cols, grads, *others)


def fast_shards(
    token_ids,
    seq_lengths,
    valid_mask,
    deal_order,
    log_scale,
    embed_master,
    attn_in,
    attn_out,
    ffn_in,
    ffn_out,
    head_master,
    norm_master,
    embed_rows,
    head_rows,
    layer_rows,
    ffn_out_rows,
    layer_cols,
    embed_head_cols,
    norm_state,
    scale_state,
):
    tokens = token_ids.shape[0]
    shard_rows = embed_master.shape[0]
    my_dp = lax.axis_index("dp")
    position = jnp.arange(tokens, dtype=jnp.int32)
    segment = jnp.zeros_like(position)
    bound = 0
    for s in range(seq_lengths.shape[1]):
        bound = bound + seq_lengths[0, s]
        segment = segment + (position >= bound).astype(jnp.int32)

    key, wanted, most = slot_plan(token_ids, shard_rows)
    asks = jnp.concatenate(
        [wanted.reshape(8, 1, SLOTS), jnp.broadcast_to(most, (8, 1, 128 - SLOTS))], axis=2
    ).astype(jnp.int32)
    packed = pack_weights(attn_in, attn_out, ffn_in, ffn_out, head_master, norm_master)
    seg_col, seg_row = segment.reshape(-1, 1), segment.reshape(1, -1)
    valid_row = valid_mask.reshape(1, -1)
    weights, asked, *saved, norms = run_gather_forward(
        packed, asks, embed_master, key.reshape(-1, 1), seg_col, seg_row, valid_row, 0
    )
    crowded = jnp.max(asked[:, :, 0, SLOTS:]) >= SLOTS

    def dense_forward(state):
        table = lax.all_gather(embed_master, "dp", axis=0, tiled=True)
        first = jnp.take(table, token_ids, axis=0).astype(jnp.bfloat16)
        return (False, *run_forward(first, seg_col, seg_row, valid_row, weights[:, 32:], norms))

    _, *saved, unit_parts, pooled_low, head_out = lax.while_loop(
        lambda state: state[0], dense_forward, (crowded, *saved)
    )
    loss_value, own_rows, grad_scale = run_contrast(unit_parts, deal_order, log_scale, 1)
    loss_value, grad_scale = loss_value[0, 0], grad_scale[0]
    shard_grads, table_rows, norm_sum, grad_first = run_backward(
        own_rows, head_out, pooled_low, seg_col, seg_row, valid_row, key.reshape(1, -1), weights, norms, saved, 2
    )
    table_slots = asked[:, :, 0, :SLOTS].reshape(1, -1)
    table_row = embed_rows.reshape(1, -1)
    row_state = jnp.pad(
        jnp.concatenate([layer_rows.reshape(6, -1), head_rows.reshape(1, -1)], axis=0), ((0, 1), (0, 0))
    ).T
    shared = (shard_grads, norm_sum, table_row, row_state, ffn_out_rows.T)

    def dense_stats():
        full = jnp.zeros((shard_rows * 8, D), jnp.float32).at[token_ids].add(
            grad_first.astype(jnp.float32)
        )
        full = lax.psum_scatter(full, "dp", scatter_dimension=0, tiled=True)
        return run_stats(True, (lax.psum(full, "group"),), *shared)

    def slot_stats():
        return run_stats(False, (table_slots, table_rows.reshape(-1, D)), *shared)

    table_grad, table_row_new, stats, rows_new, down_new = lax.cond(
        crowded, dense_stats, slot_stats
    )
    sums = total(stats, 3)
    totals = (VOCAB, D, D, D, D, FF)
    (
        new_embed, new_table_cols, new_head_cols, new_cols, rms_row, new_in, new_mix, new_gate, new_low, new_head,
    ) = run_update(
        totals, sums, table_grad, embed_master, table_row_new, shard_grads, rows_new, down_new,
        embed_head_cols, layer_cols, (attn_in, attn_out, ffn_in, ffn_out, head_master),
    )
    norm_grad = sums.reshape(-1, D)[NORM_ROW : NORM_ROW + 10].reshape(2 * LAYERS + 1, 2, D)
    shard_norm = lax.dynamic_slice_in_dim(norm_grad, my_dp * norm_state.shape[2], norm_state.shape[2], 2)
    norm_delta, norm_second = unfactored(shard_norm, norm_state)
    scale_delta, scale_state_new = unfactored(grad_scale, scale_state)
    state_new = rows_new.T
    return (
        loss_value,
        new_embed,
        new_in,
        new_mix,
        new_gate,
        new_low,
        new_head,
        norm_master + norm_delta,
        log_scale + scale_delta,
        table_row_new[0],
        state_new[6],
        state_new[:6].reshape(layer_rows.shape),
        down_new.T,
        new_cols,
        new_table_cols[0],
        new_head_cols[0],
        norm_second,
        scale_state_new,
        rms_row[0, :10],
    )


def solution(mesh):
    in_specs = (
        P(("dp", "group")),
        P(("dp", "group"), None),
        P(("dp", "group")),
        P(),
        P(),
        P("dp", None),
        P(None, "dp", None),
        P(None, "dp", None),
        P(None, "dp", None),
        P(None, "dp", None),
        P("dp", None),
        P(None, None, "dp"),
        P("dp"),
        P("dp"),
        P(None, None, "dp"),
        P(None, "dp"),
        P(),
        P(),
        P(None, None, "dp"),
        P(),
    )
    out_specs = (
        P(),
        P("dp", None),
        P(None, "dp", None),
        P(None, "dp", None),
        P(None, "dp", None),
        P(None, "dp", None),
        P("dp", None),
        P(None, None, "dp"),
        P(),
        P("dp"),
        P("dp"),
        P(None, None, "dp"),
        P(None, "dp"),
        P(),
        P(),
        P(),
        P(None, None, "dp"),
        P(),
        P(),
    )
    body = fast_shards if dict(mesh.shape) == {"dp": 8, "group": 4} else shards
    return jax.shard_map(body, mesh=mesh, in_specs=in_specs, out_specs=out_specs, check_vma=False)
```
